32 devices in a mesh: dp: 8 (over y, x, core), tensor: 4 (over z).
Axes of the slice: x: 2, y: 2, z: 4, core: 2. Of those that a mesh axis runs over, the one named last changes fastest.
Arguments:
- tokens: bfloat16 [8192, 2048], P('dp'), may hold values from -6 to 6
- cotangent: bfloat16 [8192, 2048], P('dp'), may hold values from -6 to 6
- attention_norm_gain: bfloat16 [2048], replicated, may hold values from 0.099609375 to 1.8984375
- query_key_value_weight: bfloat16 [2048, 3, 2048], P('dp', None, 'tensor'), may hold values from -0.125 to 0.125
- query_key_value_bias: bfloat16 [3, 2048], P(None, 'tensor'), may hold values from -0.59765625 to 0.59765625
- output_projection_weight: bfloat16 [2048, 2048], P('dp', 'tensor'), may hold values from -2 to 2
- feedforward_norm_gain: bfloat16 [2048], replicated, may hold values from 0.099609375 to 1.8984375
- router_matrix: bfloat16 [2048, 16], P('dp'), may hold values from -0.0625 to 0.0625
- shared_expert_gate_weight: bfloat16 [2048], P('dp'), may hold values from -0.125 to 0.125
- routed_gate_up_weight: bfloat16 [2048, 16, 2, 1408], P('dp', None, None, 'tensor'), may hold values from -0.125 to 0.125
- routed_down_weight: bfloat16 [2048, 16, 1408], P('dp', None, 'tensor'), may hold values from -4 to 4
- shared_expert_gate_up_weight: bfloat16 [2048, 2, 5632], P('dp', None, 'tensor'), may hold values from -0.125 to 0.125
- shared_expert_down_weight: bfloat16 [2048, 5632], P('dp', 'tensor'), may hold values from -0.25 to 0.25
- routes: int32 [8192, 4], P('dp'), may hold values from 0 to 15, all different within a row; in each aligned block of 1024 rows (0 to 1023, 1024 to 2047, ...) at most 384 rows name the same one
- sequence_adapter_index: int32 [8], P('dp'), may hold values from 0 to 7
- picture_piece_starts: int32 [8, 2], P('dp'), may hold values from 0 to 768, as said below
- adapter_query_key_value_lower: bfloat16 [8, 2048, 16], replicated, may hold values from -0.125 to 0.125
- adapter_query_key_value_upper: bfloat16 [8, 16, 3, 2048], P(None, None, None, 'tensor'), may hold values from -0.375 to 0.375
- adapter_output_lower: bfloat16 [8, 2048, 16], P(None, 'tensor'), may hold values from -2 to 2
- adapter_output_upper: bfloat16 [8, 16, 2048], replicated, may hold values from -0.375 to 0.375
- adapter_shared_up_lower: bfloat16 [8, 2048, 16], replicated, may hold values from -0.125 to 0.125
- adapter_shared_up_upper: bfloat16 [8, 16, 2, 5632], P(None, None, None, 'tensor'), may hold values from -0.375 to 0.375
- adapter_shared_down_lower: bfloat16 [8, 5632, 16], P(None, 'tensor'), may hold values from -0.078125 to 0.078125
- adapter_shared_down_upper: bfloat16 [8, 16, 2048], replicated, may hold values from -0.75 to 0.75
Outputs:
- output: bfloat16 [8192, 2048], P('dp')
- grad_tokens: bfloat16 [8192, 2048], P('dp')
- grad_qkv_a: float32 [8, 2048, 16], replicated
- grad_qkv_b: float32 [8, 16, 3, 2048], P(None, None, None, 'tensor')
- grad_out_a: float32 [8, 2048, 16], P(None, 'tensor')
- grad_out_b: float32 [8, 16, 2048], replicated
- grad_up_a: float32 [8, 2048, 16], replicated
- grad_up_b: float32 [8, 16, 2, 5632], P(None, None, None, 'tensor')
- grad_down_a: float32 [8, 5632, 16], P(None, 'tensor')
- grad_down_b: float32 [8, 16, 2048], replicated
The draws below stay inside these ranges and needn't reach their ends.
Inputs may be any that keep to these rules, and one draw needn't show every extreme that they name: `routes`: in each sequence no expert is named by more than 384 of the sequence's pairs. `picture_piece_starts`: in each sequence the pieces are in rising order, do not intersect, and each of their 256 tokens lies inside the sequence.
All inputs are finite; a program needn't handle non-finite values.
Results may differ from the reference program's by a relative error of at most 0.02.
Values may be sent and summed in bfloat16 or wider, within the bound.
A program may use at most 512 MiB of HBM per device.

```python
import math
import jax
import jax.numpy as jnp
import numpy as np
from jax import lax

MODEL_WIDTH = 2048
HEAD_COUNT = 16
HEAD_SIZE = 128
FE = 1408
SHARED_HIDDEN = 5632
TOP = 4
EXPERTS = 16
ADAPTER_RANK = 16
ADAPTER_SETS = 8
PIECE = 256
PIECES = 2
LEN = 1024
SEQS = 8
TOKENS = 8192
CAP = 384


def draw_picture_piece_starts(key, part):
    key = jax.random.fold_in(key, 11)
    spacing = LEN // PIECES
    offset_key, low_key, high_key = jax.random.split(key, 3)
    offsets = jax.random.randint(offset_key, (SEQS, PIECES), 0, spacing - PIECE + 1, dtype=jnp.int32)
    first_seq = jax.random.randint(low_key, (), 0, SEQS, dtype=jnp.int32)
    last_seq = jax.random.randint(high_key, (), 0, SEQS, dtype=jnp.int32)
    seq_ids = jnp.arange(SEQS, dtype=jnp.int32)[:, None]
    piece_ids = jnp.arange(PIECES, dtype=jnp.int32)[None, :]
    offsets = jnp.where((seq_ids == first_seq) & (piece_ids == 0), 0, offsets)
    offsets = jnp.where((seq_ids == last_seq) & (piece_ids == PIECES - 1), spacing - PIECE, offsets)
    return (offsets + piece_ids * spacing).astype(jnp.int32)


def touch_ends(array, key, low, high):
    longest = array.shape.index(max(array.shape))
    spots = []
    for shift in (0, 1):
        where = [jax.random.randint(jax.random.fold_in(key, axis), (), 0, length) for axis, length in enumerate(array.shape)]
        where[longest] = (where[longest] + shift) % array.shape[longest]
        spots.append(tuple(where))
    return array.at[spots[0]].set(low).at[spots[1]].set(high)


def block_scale(key, shape, shards, low, top_value):
    def one(dim, blocks):
        draws = jax.random.uniform(jax.random.fold_in(jax.random.fold_in(key, 6), dim), (blocks,), jnp.float32, low / len(shards), top_value / len(shards))
        return jnp.repeat(jnp.exp(draws), shape[dim] // blocks).reshape((-1,) + (1,) * (len(shape) - dim - 1))

    level = one(*shards[0])
    for cut in shards[1:]:
        level = level * one(*cut)
    return level


def assign_block(stream_key, own, number, rows, amount, top, limit, slope):
    sequence = jax.random.permutation(stream_key, amount)
    packed, common = portions_of(amount, rows * top, limit, slope, True), portions_of(amount, rows * top, limit, slope, False)
    places = jnp.arange(amount)

    def named(lengths, rotation):
        used = int((lengths > 0).sum())
        fixed = max(1, used // 4)
        moved = fixed + (places - fixed + rotation * (used - fixed)) % max(1, amount - fixed)
        return jnp.zeros((amount,), jnp.int32).at[sequence[jnp.where(places < fixed, places, moved)]].set(jnp.asarray(lengths, jnp.int32))

    lengths = jnp.where(number % 4 == 0, named(packed, number // 4), named(common, number - number // 4 - 1))
    mixed = jax.random.permutation(jax.random.fold_in(own, 3), amount)
    donor, receiver = mixed[0:amount // 2 * 2:2], mixed[1:amount // 2 * 2:2]
    room = jnp.minimum(lengths[donor] - 1, limit - lengths[receiver]) // 2
    room = jnp.where((donor == sequence[0]) | (receiver == sequence[0]) | (lengths[receiver] == 0), 0, jnp.maximum(room, 0))
    moved = jax.random.randint(jax.random.fold_in(own, 4), (amount // 2,), 0, 1 << 20) % (room + 1)
    lengths = lengths.at[donor].add(-moved).at[receiver].add(moved)
    items = jnp.searchsorted(jnp.cumsum(lengths), jnp.arange(rows * top), side="right").astype(jnp.int32)
    table = items.reshape(top, rows).T
    table = table[jax.random.permutation(jax.random.fold_in(own, 1), rows)]
    rotation = jax.random.randint(jax.random.fold_in(own, 2), (rows, 1), 0, top)
    return jnp.take_along_axis(table, (jnp.arange(top)[None, :] + rotation) % top, axis=1)


def portions_of(amount, total, reach, skew, full):
    loads = [(1 << 20) // math.isqrt(rank ** skew) + 1 for rank in range(1, amount + 1)]
    largest = reach if full else min(reach, max(-(-total // amount), total * loads[0] // sum(loads)))
    least = 1 if total - largest >= amount - 1 else 0
    given, surplus = [largest] + [least] * (amount - 1), total - largest - least * (amount - 1)
    while surplus > 0:
        free = [i for i in range(1, amount) if given[i] < largest] or [i for i in range(1, amount) if given[i] < reach]
        pool, budget = sum([loads[i] for i in free]), surplus
        for i in free:
            more = min(reach - given[i], max(1, budget * loads[i] // pool), surplus)
            given[i] = given[i] + more
            surplus = surplus - more
    return np.array(given)


def scatter_about(rng, shape, scale, bound, shards=(), kind=jnp.bfloat16):
    values = scale * jax.random.normal(rng, shape, jnp.float32)
    if shards:
        values = values * block_scale(rng, shape, shards, -0.22, 0.18)
    return jnp.clip(values, -bound, bound).astype(kind)


def setup_inputs(seed: int = 0) -> dict:
    streams_of = jax.random.split(jax.random.key(seed), 25)
    tokens = scatter_about(streams_of[0], (TOKENS, MODEL_WIDTH), 1.0, 6.0, ((0, 8),))
    cotangent = scatter_about(streams_of[1], (TOKENS, MODEL_WIDTH), 1.0, 6.0, ((0, 8),))
    attention_norm_gain = jnp.clip(1.0 + 0.18 * jax.random.normal(streams_of[2], (MODEL_WIDTH,), jnp.float32), 0.099609375, 1.8984375).astype(jnp.bfloat16)
    query_key_value_weight = scatter_about(streams_of[3], (MODEL_WIDTH, 3, HEAD_COUNT * HEAD_SIZE), MODEL_WIDTH ** -0.5, 0.125, ((0, 8), (2, 4)))
    query_key_value_bias = scatter_about(streams_of[4], (3, HEAD_COUNT * HEAD_SIZE), 0.1, 0.59765625, ((1, 4),))
    output_projection_weight = scatter_about(streams_of[5], (MODEL_WIDTH, HEAD_COUNT * HEAD_SIZE), (max(HEAD_COUNT * HEAD_SIZE // 256, 1)) ** -0.5, 2.0, ((0, 8), (1, 4)))
    feedforward_norm_gain = jnp.clip(1.0 + 0.18 * jax.random.normal(streams_of[6], (MODEL_WIDTH,), jnp.float32), 0.099609375, 1.8984375).astype(jnp.bfloat16)
    router_matrix = scatter_about(streams_of[7], (MODEL_WIDTH, EXPERTS), (4 * MODEL_WIDTH) ** -0.5, 0.0625, ((0, 8),))
    shared_expert_gate_weight = scatter_about(streams_of[8], (MODEL_WIDTH,), MODEL_WIDTH ** -0.5, 0.125, ((0, 8),))
    routed_gate_up_weight = scatter_about(streams_of[9], (MODEL_WIDTH, EXPERTS, 2, FE), MODEL_WIDTH ** -0.5, 0.125, ((0, 8), (3, 4)))
    routed_down_weight = scatter_about(streams_of[10], (MODEL_WIDTH, EXPERTS, FE), (max(FE // 512, 1)) ** -0.5, 4.0, ((0, 8), (2, 4)))
    shared_expert_gate_up_weight = scatter_about(streams_of[11], (MODEL_WIDTH, 2, SHARED_HIDDEN), MODEL_WIDTH ** -0.5, 0.125, ((0, 8), (2, 4)))
    shared_expert_down_weight = scatter_about(streams_of[12], (MODEL_WIDTH, SHARED_HIDDEN), (SHARED_HIDDEN // 12) ** -0.5, 0.25, ((0, 8), (1, 4)))
    routes_keys = jax.random.split(jax.random.fold_in(streams_of[13], 1), TOKENS // LEN)
    routes_turns = jax.random.permutation(jax.random.fold_in(streams_of[13], 3), TOKENS // LEN)
    routes = jax.vmap(lambda own, number: assign_block(jax.random.fold_in(streams_of[13], 2), own, number, LEN, EXPERTS, TOP, CAP, 1))(routes_keys, routes_turns).reshape((TOKENS, TOP))
    sequence_adapter_index = touch_ends(jax.random.randint(streams_of[14], (SEQS,), 0, ADAPTER_SETS), jax.random.fold_in(streams_of[14], 1), 0, ADAPTER_SETS - 1).astype(jnp.int32)
    picture_piece_starts = draw_picture_piece_starts(jax.random.fold_in(streams_of[24], 71), 0)
    adapter_query_key_value_lower = scatter_about(streams_of[16], (ADAPTER_SETS, MODEL_WIDTH, ADAPTER_RANK), MODEL_WIDTH ** -0.5, 0.125)
    adapter_query_key_value_upper = scatter_about(streams_of[17], (ADAPTER_SETS, ADAPTER_RANK, 3, HEAD_COUNT * HEAD_SIZE), (16 * ADAPTER_RANK) ** -0.5, 0.375, ((3, 4),))
    adapter_output_lower = scatter_about(streams_of[18], (ADAPTER_SETS, HEAD_COUNT * HEAD_SIZE, ADAPTER_RANK), (max(HEAD_COUNT * HEAD_SIZE // 256, 1)) ** -0.5, 2.0, ((1, 4),))
    adapter_output_upper = scatter_about(streams_of[19], (ADAPTER_SETS, ADAPTER_RANK, MODEL_WIDTH), (16 * ADAPTER_RANK) ** -0.5, 0.375)
    adapter_shared_up_lower = scatter_about(streams_of[20], (ADAPTER_SETS, MODEL_WIDTH, ADAPTER_RANK), MODEL_WIDTH ** -0.5, 0.125)
    adapter_shared_up_upper = scatter_about(streams_of[21], (ADAPTER_SETS, ADAPTER_RANK, 2, SHARED_HIDDEN), (16 * ADAPTER_RANK) ** -0.5, 0.375, ((3, 4),))
    adapter_shared_down_lower = scatter_about(streams_of[22], (ADAPTER_SETS, SHARED_HIDDEN, ADAPTER_RANK), SHARED_HIDDEN ** -0.5, 0.078125, ((1, 4),))
    adapter_shared_down_upper = scatter_about(streams_of[23], (ADAPTER_SETS, ADAPTER_RANK, MODEL_WIDTH), (4 * ADAPTER_RANK) ** -0.5, 0.75)
    return dict(tokens=tokens, cotangent=cotangent, attention_norm_gain=attention_norm_gain, query_key_value_weight=query_key_value_weight, query_key_value_bias=query_key_value_bias, output_projection_weight=output_projection_weight, feedforward_norm_gain=feedforward_norm_gain, router_matrix=router_matrix, shared_expert_gate_weight=shared_expert_gate_weight, routed_gate_up_weight=routed_gate_up_weight, routed_down_weight=routed_down_weight, shared_expert_gate_up_weight=shared_expert_gate_up_weight, shared_expert_down_weight=shared_expert_down_weight, routes=routes, sequence_adapter_index=sequence_adapter_index, picture_piece_starts=picture_piece_starts, adapter_query_key_value_lower=adapter_query_key_value_lower, adapter_query_key_value_upper=adapter_query_key_value_upper, adapter_output_lower=adapter_output_lower, adapter_output_upper=adapter_output_upper, adapter_shared_up_lower=adapter_shared_up_lower, adapter_shared_up_upper=adapter_shared_up_upper, adapter_shared_down_lower=adapter_shared_down_lower, adapter_shared_down_upper=adapter_shared_down_upper)


EPSILON = 1e-06
THETA = 1000000.0
ADAPTER_SCALE = 2.0
MASKED = -1e+30
HIGHEST = lax.Precision.HIGHEST

@jax.custom_vjp
def low(v):
    return lax.optimization_barrier(v.astype(jnp.bfloat16)).astype(jnp.float32)

@jax.custom_vjp
def low_back(v):
    return v

def low_keep(v):
    return (low(v), None)

def low_pass(kept, grad):
    return (grad,)

def back_keep(v):
    return (v, None)

def back_low(kept, grad):
    return (low(grad),)
low.defvjp(low_keep, low_pass)
low_back.defvjp(back_keep, back_low)

def dense(left_side, right_side):
    return jnp.dot(left_side, right_side, precision=HIGHEST)

def rms_scale(values, gain_values):
    return values * lax.rsqrt(lax.optimization_barrier(jnp.mean(values * values, axis=1, keepdims=True)) + EPSILON) * gain_values

def rope_tables(length):
    half_size = HEAD_SIZE // 2
    frequency = THETA ** (-jnp.arange(half_size, dtype=jnp.float32) * 2.0 / HEAD_SIZE)
    angles = jnp.arange(length, dtype=jnp.float32)[:, None] * frequency[None, :]
    return (jnp.concatenate([jnp.cos(angles)] * 2, axis=1), jnp.concatenate([jnp.sin(angles)] * 2, axis=1))

def rotate(values, cosine, sine_table):
    half_size = values.shape[-1] // 2
    turned = jnp.concatenate([-values[..., half_size:], values[..., :half_size]], axis=-1)
    return values * cosine[:, None, :] + turned * sine_table[:, None, :]

def piece_index(positions, starts):
    inside = (positions[:, None] >= starts[None, :]) & (positions[:, None] < starts[None, :] + PIECE)
    labels = jnp.arange(PIECES, dtype=jnp.int32)[None, :] + 1
    return lax.optimization_barrier(jnp.sum(jnp.where(inside, labels, 0), axis=1)) - 1

def visible(row_positions, col_positions, starts):
    row_piece = piece_index(row_positions, starts)
    col_piece = piece_index(col_positions, starts)
    causal = col_positions[None, :] <= row_positions[:, None]
    together = (row_piece[:, None] == col_piece[None, :]) & (row_piece[:, None] >= 0)
    return causal | together

def slot_table(routes, length):
    flat_routes = routes.reshape(-1)
    hit_table = (flat_routes[:, None] == jnp.arange(EXPERTS, dtype=jnp.int32)[None, :]).astype(jnp.int32)
    earlier = jnp.cumsum(hit_table, axis=0) - hit_table
    slot_index = (flat_routes * CAP + lax.optimization_barrier(jnp.sum(earlier * hit_table, axis=1))).astype(jnp.int32)
    pair_tokens = jnp.arange(length * TOP, dtype=jnp.int32) // TOP
    slot_owner = jnp.full((EXPERTS * CAP,), length, jnp.int32).at[slot_index].set(pair_tokens)
    return (slot_index, slot_owner)

def layer(tokens_f, adapter_bundle, frozen, routes, starts):
    attention_norm_gain, query_key_value_weight, query_key_value_bias, output_projection_weight, feedforward_norm_gain, router_matrix, shared_expert_gate_weight, routed_gate_up_weight, routed_down_weight, shared_expert_gate_up_weight, shared_expert_down_weight = frozen
    qkv_a, qkv_b, out_a, out_b, up_a, up_b, down_a, down_b = adapter_bundle
    length = tokens_f.shape[0]
    normed = low(rms_scale(tokens_f, attention_norm_gain))
    mid_qkv = low_back(low(dense(normed, qkv_a)))
    qkv = jnp.einsum('td,dsf->tsf', normed, query_key_value_weight, precision=HIGHEST) + query_key_value_bias
    qkv = low_back(qkv + ADAPTER_SCALE * jnp.einsum('tr,rsf->tsf', mid_qkv, qkv_b, precision=HIGHEST))
    cosine, sine_table = rope_tables(length)
    query = low(rotate(qkv[:, 0].reshape(length, HEAD_COUNT, HEAD_SIZE), cosine, sine_table))
    keys = low(rotate(qkv[:, 1].reshape(length, HEAD_COUNT, HEAD_SIZE), cosine, sine_table))
    values = low(qkv[:, 2].reshape(length, HEAD_COUNT, HEAD_SIZE))
    block_rows = min(length, 512)
    positions = jnp.arange(length, dtype=jnp.int32)

    def attend(offset):
        row_positions = lax.dynamic_slice_in_dim(positions, offset, block_rows)
        query_rows = lax.dynamic_slice_in_dim(query, offset, block_rows)
        scores = low_back(jnp.einsum('qhd,khd->hqk', query_rows, keys, precision=HIGHEST) * HEAD_SIZE ** (-0.5))
        scores = jnp.where(visible(row_positions, positions, starts)[None], scores, MASKED)
        weights_att = low(jax.nn.softmax(scores, axis=-1))
        return jnp.einsum('hqk,khd->qhd', weights_att, values, precision=HIGHEST)
    offsets = jnp.arange(length // block_rows, dtype=jnp.int32) * block_rows
    attended = lax.map(jax.checkpoint(attend), offsets).reshape(length, HEAD_COUNT * HEAD_SIZE)
    attended = low_back(low(attended))
    mid_out = low_back(low(dense(attended, out_a)))
    hidden = tokens_f + low_back(dense(attended, output_projection_weight.T) + ADAPTER_SCALE * dense(mid_out, out_b))
    normed_two = low(rms_scale(hidden, feedforward_norm_gain))
    logits = low_back(dense(normed_two, router_matrix))
    gates = jnp.take_along_axis(jax.nn.softmax(logits, axis=-1), routes, axis=1)
    slot_index, slot_owner = slot_table(routes, length)
    padded = jnp.concatenate([normed_two, jnp.zeros((1, MODEL_WIDTH), jnp.float32)], axis=0)
    dispatched = padded[slot_owner].reshape(EXPERTS, CAP, MODEL_WIDTH)
    gate_up = low_back(jnp.einsum('ecd,dexf->ecxf', dispatched, routed_gate_up_weight, precision=HIGHEST))
    act = low(jax.nn.silu(gate_up[:, :, 0]) * gate_up[:, :, 1])
    expert_out = low_back(jnp.einsum('ecf,def->ecd', act, routed_down_weight, precision=HIGHEST))
    picked = expert_out.reshape(EXPERTS * CAP, MODEL_WIDTH)[slot_index].reshape(length, TOP, MODEL_WIDTH)
    routed = lax.optimization_barrier(jnp.sum(gates[:, :, None] * picked, axis=1))
    shared_gate = jax.nn.sigmoid(low_back(dense(normed_two, shared_expert_gate_weight[:, None]))[:, 0])
    mid_up = low_back(low(dense(normed_two, up_a)))
    shared_gu = jnp.einsum('td,dxf->txf', normed_two, shared_expert_gate_up_weight, precision=HIGHEST)
    shared_gu = low_back(shared_gu + ADAPTER_SCALE * jnp.einsum('tr,rxf->txf', mid_up, up_b, precision=HIGHEST))
    shared_act = low(jax.nn.silu(shared_gu[:, 0]) * shared_gu[:, 1])
    mid_down = low_back(low(dense(shared_act, down_a)))
    shared_out = low_back(dense(shared_act, shared_expert_down_weight.T) + ADAPTER_SCALE * dense(mid_down, down_b))
    return hidden + routed + shared_gate[:, None] * shared_out

def broadcast_expand(adapter_entry):
    return adapter_entry.astype(jnp.float32)

def reference(tokens, cotangent, attention_norm_gain, query_key_value_weight, query_key_value_bias, output_projection_weight, feedforward_norm_gain, router_matrix, shared_expert_gate_weight, routed_gate_up_weight, routed_down_weight, shared_expert_gate_up_weight, shared_expert_down_weight, routes, sequence_adapter_index, picture_piece_starts, adapter_query_key_value_lower, adapter_query_key_value_upper, adapter_output_lower, adapter_output_upper, adapter_shared_up_lower, adapter_shared_up_upper, adapter_shared_down_lower, adapter_shared_down_upper):
    frozen = tuple((broadcast_expand(adapter_entry) for adapter_entry in (attention_norm_gain, query_key_value_weight, query_key_value_bias, output_projection_weight, feedforward_norm_gain, router_matrix, shared_expert_gate_weight, routed_gate_up_weight, routed_down_weight, shared_expert_gate_up_weight, shared_expert_down_weight)))
    adapter_bundle = tuple((broadcast_expand(adapter_entry) for adapter_entry in (adapter_query_key_value_lower, adapter_query_key_value_upper, adapter_output_lower, adapter_output_upper, adapter_shared_up_lower, adapter_shared_up_upper, adapter_shared_down_lower, adapter_shared_down_upper)))

    def one_sequence(running, inputs):
        seq_tokens, seq_cot, seq_routes, seq_set, seq_starts = inputs
        selected_experts = tuple((lax.dynamic_index_in_dim(adapter_entry, seq_set, 0, keepdims=False) for adapter_entry in adapter_bundle))

        def forward(token_values, picked_sets):
            return layer(token_values, picked_sets, frozen, seq_routes, seq_starts)
        result, pull = jax.vjp(forward, broadcast_expand(seq_tokens), selected_experts)
        grad_token, grad_sets = pull(broadcast_expand(seq_cot))
        marker = (jnp.arange(ADAPTER_SETS, dtype=jnp.int32) == seq_set).astype(jnp.float32)
        running = tuple((total_grad + marker.reshape((ADAPTER_SETS,) + (1,) * gradient.ndim) * gradient[None] for total_grad, gradient in zip(running, grad_sets)))
        return (running, (result.astype(jnp.bfloat16), grad_token.astype(jnp.bfloat16)))
    initial = tuple((jnp.zeros_like(adapter_entry) for adapter_entry in adapter_bundle))
    inputs = (tokens.reshape(SEQS, LEN, MODEL_WIDTH), cotangent.reshape(SEQS, LEN, MODEL_WIDTH), routes.reshape(SEQS, LEN, TOP), sequence_adapter_index, picture_piece_starts)
    totals, (outputs, grads_tok) = lax.scan(one_sequence, initial, inputs)
    return (outputs.reshape(TOKENS, MODEL_WIDTH), grads_tok.reshape(TOKENS, MODEL_WIDTH), totals[0], totals[1], totals[2], totals[3], totals[4], totals[5], totals[6], totals[7])
```

```python
import functools

import jax
import jax.numpy as jnp
from jax import lax
from jax.experimental import pallas as pl
from jax.experimental.pallas import tpu as pltpu
from jax.sharding import PartitionSpec as P

HEAD_SIZE = 128
TOP = 4
EXPERTS = 16
ADAPTER_SETS = 8
PIECE = 256


EPSILON = 1e-06
THETA = 1000000.0
ADAPTER_SCALE = 2.0
MASKED = -1e30
MESH = pl.DeviceIdType.MESH
SUM_CHUNKS = 16
EXPERT_PARTS = 4


def matmul(left_side, right_side):
    return jnp.dot(left_side, right_side, preferred_element_type=jnp.float32)


def contract_last(left_side, right_side):
    return lax.dot_general(
        left_side, right_side, (((1,), (1,)), ((), ())), preferred_element_type=jnp.float32
    )


def contract_first(left_side, right_side):
    return lax.dot_general(
        left_side, right_side, (((0,), (0,)), ((), ())), preferred_element_type=jnp.float32
    )


def to_low(values):
    return values.astype(jnp.bfloat16)


def rms_scale(values, gain_values):
    return (
        values * lax.rsqrt(jnp.mean(values * values, axis=1, keepdims=True) + EPSILON) * gain_values
    )


def rope_tables(length):
    half_size = HEAD_SIZE // 2
    frequency = THETA ** (-jnp.arange(half_size, dtype=jnp.float32) * 2.0 / HEAD_SIZE)
    angles = jnp.arange(length, dtype=jnp.float32)[:, None] * frequency[None, :]
    return (
        jnp.concatenate([jnp.cos(angles)] * 2, axis=1),
        jnp.concatenate([jnp.sin(angles)] * 2, axis=1),
    )


def rotate(values, cosine, sine_table):
    half_size = values.shape[-1] // 2
    turned = jnp.concatenate([-values[..., half_size:], values[..., :half_size]], axis=-1)
    return values * cosine[:, None, :] + turned * sine_table[:, None, :]


def piece_index(positions, starts):
    inside = (positions[:, None] >= starts[None, :]) & (
        positions[:, None] < starts[None, :] + PIECE
    )
    labels = jnp.arange(starts.shape[0], dtype=jnp.int32)[None, :] + 1
    return jnp.sum(jnp.where(inside, labels, 0), axis=1) - 1


def visible(row_positions, col_positions, starts):
    row_piece = piece_index(row_positions, starts)
    col_piece = piece_index(col_positions, starts)
    causal = col_positions[None, :] <= row_positions[:, None]
    together = (row_piece[:, None] == col_piece[None, :]) & (row_piece[:, None] >= 0)
    return causal | together


def line_sum_kernel(
    chunks, part_ref, total_ref, from_end, pair_sum, from_pair, semaphores
):
    place = lax.axis_index("tensor")
    rows = part_ref.shape[0] // chunks
    inner = (place == 1) | (place == 2)
    end = (place == 0) | (place == 3)
    mate = jnp.where(place < 2, 1 - place, 5 - place)
    other = jnp.where(inner, 3 - place, place)
    barrier = pltpu.get_barrier_semaphore()
    pl.semaphore_signal(barrier, inc=1, device_id={"tensor": mate}, device_id_type=MESH)

    @pl.when(inner)
    def _():
        pl.semaphore_signal(barrier, inc=1, device_id={"tensor": other}, device_id_type=MESH)
        pl.semaphore_wait(barrier, 2)

    @pl.when(end)
    def _():
        pl.semaphore_wait(barrier, 1)

    def span(chunk):
        return pl.ds(pl.multiple_of(chunk * rows, rows), rows)

    def copy(source, target, chunk, lane, device):
        return pltpu.make_async_remote_copy(
            source.at[span(chunk)],
            target.at[span(chunk)],
            semaphores.at[2 * lane, chunk],
            semaphores.at[2 * lane + 1, chunk],
            device_id={"tensor": device},
            device_id_type=MESH,
        )

    def inward(chunk):
        return copy(part_ref, from_end, chunk, 0, mate)

    def across(chunk):
        return copy(pair_sum, from_pair, chunk, 1, other)

    def outward(chunk):
        return copy(total_ref, total_ref, chunk, 2, mate)

    def add(left_ref, right_ref, out_ref, chunk):
        out_ref[span(chunk)] = to_low(
            left_ref[span(chunk)].astype(jnp.float32) + right_ref[span(chunk)].astype(jnp.float32)
        )

    @pl.when(end)
    def _():
        @pl.loop(0, chunks)
        def _(chunk):
            inward(chunk).start()

        @pl.loop(0, chunks)
        def _(chunk):
            inward(chunk).wait_send()

        @pl.loop(0, chunks)
        def _(chunk):
            outward(chunk).wait_recv()

    @pl.when(inner)
    def _():
        @pl.loop(0, chunks + 1)
        def _(step):
            @pl.when(step < chunks)
            def _():
                inward(step).wait_recv()
                add(part_ref, from_end, pair_sum, step)
                across(step).start()

            @pl.when(step > 0)
            def _():
                across(step - 1).wait_recv()
                add(pair_sum, from_pair, total_ref, step - 1)
                outward(step - 1).start()

        @pl.loop(0, chunks)
        def _(chunk):
            across(chunk).wait_send()
            outward(chunk).wait_send()


def tensor_sum(part, number):
    if lax.axis_size("tensor") != 4:
        return lax.psum(part.astype(jnp.float32), "tensor")
    total = pl.pallas_call(
        functools.partial(line_sum_kernel, SUM_CHUNKS),
        out_shape=jax.ShapeDtypeStruct(part.shape, jnp.bfloat16),
        in_specs=[pl.BlockSpec(memory_space=pltpu.VMEM)],
        out_specs=pl.BlockSpec(memory_space=pltpu.VMEM),
        scratch_shapes=[pltpu.VMEM(part.shape, jnp.bfloat16)] * 3
        + [pltpu.SemaphoreType.DMA((6, SUM_CHUNKS))],
        compiler_params=pltpu.CompilerParams(
            collective_id=number, has_side_effects=True, vmem_limit_bytes=40 * 2**20
        ),
        cost_estimate=pl.CostEstimate(flops=0, bytes_accessed=300 * 2**20, transcendentals=0),
    )(to_low(part))
    return total.astype(jnp.float32)


def summed(wide_part, narrow_part, number):
    width, small = wide_part.shape[1], narrow_part.shape[1]
    pad = jnp.zeros((wide_part.shape[0], 128 - small), jnp.bfloat16)
    total = tensor_sum(
        jnp.concatenate([to_low(wide_part), to_low(narrow_part), pad], axis=1), number
    )
    return total[:, :width], total[:, width : width + small]


def swiglu(paired):
    return jax.nn.silu(paired[..., 0, :]) * paired[..., 1, :]


def gathered(weight):
    return lax.all_gather(weight, "dp", axis=0, tiled=True)


def body(
    tokens,
    cotangent,
    attention_norm_gain,
    query_key_value_weight,
    query_key_value_bias,
    output_projection_weight,
    feedforward_norm_gain,
    router_matrix,
    shared_expert_gate_weight,
    routed_gate_up_weight,
    routed_down_weight,
    shared_expert_gate_up_weight,
    shared_expert_down_weight,
    routes,
    sequence_adapter_index,
    picture_piece_starts,
    adapter_query_key_value_lower,
    adapter_query_key_value_upper,
    adapter_output_lower,
    adapter_output_upper,
    adapter_shared_up_lower,
    adapter_shared_up_upper,
    adapter_shared_down_lower,
    adapter_shared_down_upper,
):
    length, width = tokens.shape
    heads_here = query_key_value_weight.shape[2] // HEAD_SIZE
    set_id = sequence_adapter_index[0]
    starts = picture_piece_starts[0]

    def selected_experts(adapter_entry):
        return lax.dynamic_index_in_dim(adapter_entry, set_id, 0, keepdims=False)

    qkv_a, qkv_b, out_a, out_b = (
        selected_experts(adapter_query_key_value_lower),
        selected_experts(adapter_query_key_value_upper),
        selected_experts(adapter_output_lower),
        selected_experts(adapter_output_upper),
    )
    up_a, up_b, down_a, down_b = (
        selected_experts(adapter_shared_up_lower),
        selected_experts(adapter_shared_up_upper),
        selected_experts(adapter_shared_down_lower),
        selected_experts(adapter_shared_down_upper),
    )
    gain_attn_f = attention_norm_gain.astype(jnp.float32)
    gain_ffn_f = feedforward_norm_gain.astype(jnp.float32)
    tokens_f = tokens.astype(jnp.float32)
    normed = to_low(rms_scale(tokens_f, gain_attn_f))
    mid_qkv = to_low(matmul(normed, qkv_a))
    columns = normed
    qkv_rows = gathered(query_key_value_weight)
    qkv_sum = jnp.einsum(
        "tr,rsf->tsf",
        columns,
        qkv_rows,
        preferred_element_type=jnp.float32,
    )
    qkv_sum = qkv_sum + query_key_value_bias.astype(jnp.float32)
    qkv_sum = qkv_sum + ADAPTER_SCALE * jnp.einsum(
        "tr,rsf->tsf", mid_qkv, qkv_b, preferred_element_type=jnp.float32
    )
    cosine, sine_table = rope_tables(length)

    def position(raw_values):
        query_part = rotate(
            raw_values[:, 0].reshape(length, heads_here, HEAD_SIZE), cosine, sine_table
        )
        keys_part = rotate(
            raw_values[:, 1].reshape(length, heads_here, HEAD_SIZE), cosine, sine_table
        )
        return (query_part, keys_part)

    (query_f, keys_f), rope_pull = jax.vjp(position, qkv_sum)
    query = to_low(query_f)
    keys = to_low(keys_f)
    values = to_low(qkv_sum[:, 2].reshape(length, heads_here, HEAD_SIZE))
    block_rows = min(length, 512)
    score_scale = HEAD_SIZE ** (-0.5)
    positions = jnp.arange(length, dtype=jnp.int32)
    attended_parts = []
    logsum_parts = []
    for offset in range(0, length, block_rows):
        allowed = visible(positions[offset : offset + block_rows], positions, starts)
        scores = (
            jnp.einsum(
                "qhd,khd->hqk",
                query[offset : offset + block_rows],
                keys,
                preferred_element_type=jnp.float32,
            )
            * score_scale
        )
        scores = jnp.where(allowed[None], scores, MASKED)
        highest = jnp.max(scores, axis=-1, keepdims=True)
        weights_exp = jnp.exp(scores - highest)
        row_totals = jnp.sum(weights_exp, axis=-1, keepdims=True)
        attended_parts.append(
            jnp.einsum(
                "hqk,khd->qhd",
                to_low(weights_exp / row_totals),
                values,
                preferred_element_type=jnp.float32,
            )
        )
        logsum_parts.append(highest + jnp.log(row_totals))
    attended = to_low(jnp.concatenate(attended_parts, axis=0).reshape(length, -1))
    output_rows = gathered(output_projection_weight)
    branch_part = contract_last(attended, output_rows)
    branch_here, mid_out_here_f = summed(branch_part, matmul(attended, out_a), 1)
    mid_out_here = to_low(mid_out_here_f)
    hidden_here = tokens_f + branch_here + ADAPTER_SCALE * matmul(mid_out_here, out_b)
    normed_two_here_f, norm_ffn_pull = jax.vjp(
        lambda rows: rms_scale(rows, gain_ffn_f), hidden_here
    )
    normed_two_here = to_low(normed_two_here_f)
    normed_two, mid_out = (normed_two_here, mid_out_here)
    cot_f = cotangent.astype(jnp.float32)
    down_rows = gathered(routed_down_weight)
    sdown_rows = gathered(shared_expert_down_weight)
    shared_rows = gathered(shared_expert_gate_up_weight)
    small_rows = gathered(
        jnp.concatenate(
            [
                router_matrix,
                shared_expert_gate_weight[:, None],
                jnp.full_like(shared_expert_gate_weight, set_id)[:, None],
            ],
            axis=1,
        )
    )
    router_full, gate_full = small_rows[:, :EXPERTS], small_rows[:, EXPERTS]
    router_probs = jax.nn.softmax(matmul(normed_two, router_full), axis=-1)
    shared_gate = jax.nn.sigmoid(matmul(normed_two, gate_full))
    expert_ids = jnp.arange(EXPERTS, dtype=jnp.int32)
    chosen = jnp.sum(
        (routes[:, :, None] == expert_ids[None, None, :]).astype(jnp.float32), axis=1
    )
    gate_table = (router_probs * chosen).T

    mid_up = to_low(matmul(normed_two, up_a))
    shared_gu = jnp.einsum(
        "tr,rxf->txf", normed_two, shared_rows, preferred_element_type=jnp.float32
    ) + ADAPTER_SCALE * jnp.einsum("tr,rxf->txf", mid_up, up_b, preferred_element_type=jnp.float32)
    shared_act_f, shared_pull = jax.vjp(swiglu, shared_gu)
    shared_act = to_low(shared_act_f)
    shared_cols = contract_last(shared_act, sdown_rows)
    shared_gate_part = jnp.sum(cot_f * shared_cols, axis=1)
    grad_shared = to_low(shared_gate[:, None] * cot_f)
    grad_mid_down = to_low(ADAPTER_SCALE * contract_last(grad_shared, down_b))
    grad_shared_act = matmul(grad_shared, sdown_rows) + contract_last(grad_mid_down, down_a)
    grad_shared_gu = to_low(shared_pull(grad_shared_act)[0])
    grad_mid_up_part = ADAPTER_SCALE * jnp.einsum(
        "txf,rxf->tr", grad_shared_gu, up_b, preferred_element_type=jnp.float32
    )
    grad_up_b_local = ADAPTER_SCALE * jnp.einsum(
        "tr,txf->rxf", mid_up, grad_shared_gu, preferred_element_type=jnp.float32
    )
    grad_down_a_local = contract_first(shared_act, grad_mid_down)
    combined_part = shared_gate[:, None] * shared_cols
    normed_two_part = jnp.einsum(
        "txf,rxf->tr", grad_shared_gu, shared_rows, preferred_element_type=jnp.float32
    )

    grad_act_open = jnp.einsum(
        "ref,tr->eft", down_rows, cotangent, preferred_element_type=jnp.float32
    )
    gate_grad_parts = []
    share = EXPERTS // EXPERT_PARTS
    for first in range(0, EXPERTS, share):
        some = slice(first, first + share)
        up_rows = gathered(routed_gate_up_weight[:, some])
        gate_up = jnp.einsum(
            "rexf,tr->exft", up_rows, normed_two, preferred_element_type=jnp.float32
        )
        gate_half, up_half = gate_up[:, 0], gate_up[:, 1]
        squashed = jax.nn.sigmoid(gate_half)
        act = to_low(gate_half * squashed * up_half).astype(jnp.float32)
        gate_rows = gate_table[some, None, :]
        open_part = grad_act_open[some]
        gate_grad_parts.append(jnp.sum(act * open_part, axis=1))
        grad_act = gate_rows * open_part
        grad_gate_up = to_low(
            jnp.stack(
                [
                    grad_act * up_half * squashed * (1.0 + gate_half * (1.0 - squashed)),
                    grad_act * gate_half * squashed,
                ],
                axis=1,
            )
        )
        combined_part = combined_part + jnp.einsum(
            "eft,ref->tr",
            to_low(gate_rows * act),
            down_rows[:, some],
            preferred_element_type=jnp.float32,
        )
        normed_two_part = normed_two_part + jnp.einsum(
            "exft,rexf->tr", grad_gate_up, up_rows, preferred_element_type=jnp.float32
        )
    gate_grad_part = jnp.concatenate(gate_grad_parts, axis=0).T
    narrow_part = jnp.concatenate(
        [gate_grad_part, shared_gate_part[:, None], grad_mid_up_part], axis=1
    )
    grad_normed_two, narrow_sum = summed(normed_two_part, narrow_part, 2)
    combined_here, mid_down_here_f = summed(combined_part, matmul(shared_act, down_a), 3)
    mid_down = to_low(mid_down_here_f)
    extra_here = ADAPTER_SCALE * matmul(mid_down, down_b)
    output = to_low(hidden_here + combined_here + shared_gate[:, None] * extra_here)
    grad_down_b_local = ADAPTER_SCALE * contract_first(mid_down, grad_shared)
    grad_probs = chosen * narrow_sum[:, :EXPERTS]
    grad_logits = to_low(
        router_probs * (grad_probs - jnp.sum(router_probs * grad_probs, axis=1, keepdims=True))
    )
    shared_gate_grad = narrow_sum[:, EXPERTS] + jnp.sum(cot_f * extra_here, axis=1)
    grad_gate_logit = to_low(shared_gate_grad * shared_gate * (1.0 - shared_gate))
    grad_mid_up_here = to_low(narrow_sum[:, EXPERTS + 1 :])
    grad_normed_two = grad_normed_two + contract_last(grad_logits, router_full)
    grad_normed_two = (
        grad_normed_two
        + grad_gate_logit.astype(jnp.float32)[:, None] * gate_full.astype(jnp.float32)[None, :]
    )
    grad_normed_two = grad_normed_two + contract_last(grad_mid_up_here, up_a)
    grad_hidden = cot_f + norm_ffn_pull(grad_normed_two)[0]
    grad_branch_here = to_low(grad_hidden)
    grad_branch, grad_mid_up = (grad_branch_here, grad_mid_up_here)
    grad_up_a_local = contract_first(normed_two, grad_mid_up)
    grad_mid_out = to_low(ADAPTER_SCALE * contract_last(grad_branch, out_b))
    grad_out_b_local = ADAPTER_SCALE * contract_first(mid_out, grad_branch)
    columns = grad_branch
    grad_att_sum = matmul(
        columns, output_rows
    )
    grad_attended = to_low(grad_att_sum + contract_last(grad_mid_out, out_a)).reshape(
        length, heads_here, HEAD_SIZE
    )
    grad_out_a_local = contract_first(attended, grad_mid_out)
    grad_keys = jnp.zeros((length, heads_here, HEAD_SIZE), jnp.float32)
    grad_values = jnp.zeros((length, heads_here, HEAD_SIZE), jnp.float32)
    grad_query_parts = []
    for block_number, offset in enumerate(range(0, length, block_rows)):
        query_rows = query[offset : offset + block_rows]
        allowed = visible(positions[offset : offset + block_rows], positions, starts)
        scores = (
            jnp.einsum("qhd,khd->hqk", query_rows, keys, preferred_element_type=jnp.float32)
            * score_scale
        )
        scores = jnp.where(allowed[None], scores, MASKED)
        probs_f = jnp.exp(scores - logsum_parts[block_number])
        grad_rows = grad_attended[offset : offset + block_rows]
        grad_values = grad_values + jnp.einsum(
            "hqk,qhd->khd", to_low(probs_f), grad_rows, preferred_element_type=jnp.float32
        )
        grad_probs_att = jnp.einsum(
            "qhd,khd->hqk", grad_rows, values, preferred_element_type=jnp.float32
        )
        grad_scores = to_low(
            probs_f * (grad_probs_att - jnp.sum(probs_f * grad_probs_att, axis=-1, keepdims=True))
        )
        grad_query_parts.append(
            jnp.einsum("hqk,khd->qhd", grad_scores, keys, preferred_element_type=jnp.float32)
            * score_scale
        )
        grad_keys = (
            grad_keys
            + jnp.einsum(
                "hqk,qhd->khd", grad_scores, query_rows, preferred_element_type=jnp.float32
            )
            * score_scale
        )
    grad_query = jnp.concatenate(grad_query_parts, axis=0)
    grad_raw = rope_pull((grad_query, grad_keys))[0]
    grad_raw = grad_raw.at[:, 2].set(grad_values.reshape(length, -1))
    grad_qkv = to_low(grad_raw)
    grad_mid_qkv_part = ADAPTER_SCALE * jnp.einsum(
        "tsf,rsf->tr", grad_qkv, qkv_b, preferred_element_type=jnp.float32
    )
    grad_qkv_b_local = ADAPTER_SCALE * jnp.einsum(
        "tr,tsf->rsf", mid_qkv, grad_qkv, preferred_element_type=jnp.float32
    )
    normed_part = jnp.einsum(
        "tsf,rsf->tr",
        grad_qkv,
        qkv_rows,
        preferred_element_type=jnp.float32,
    )
    grad_normed, grad_mid_qkv_f = summed(normed_part, grad_mid_qkv_part, 4)
    grad_mid_qkv_here = to_low(grad_mid_qkv_f)
    grad_normed = grad_normed + contract_last(grad_mid_qkv_here, qkv_a)
    norm_attn_pull = jax.vjp(lambda rows: rms_scale(rows, gain_attn_f), tokens_f)[1]
    grad_tokens_here = to_low(grad_hidden + norm_attn_pull(grad_normed)[0])
    grad_tokens, grad_mid_qkv = (grad_tokens_here, grad_mid_qkv_here)
    grad_qkv_a_local = contract_first(normed, grad_mid_qkv)
    everyone = small_rows[:: small_rows.shape[0] // lax.axis_size("dp"), EXPERTS + 1]
    marker = to_low(
        jnp.arange(ADAPTER_SETS, dtype=jnp.int32)[:, None] == everyone.astype(jnp.int32)[None, :]
    )

    def adapter_sums(local_grads):
        sizes = [local_grad.size for local_grad in local_grads]
        flat = jnp.concatenate([to_low(local_grad).reshape(-1) for local_grad in local_grads])
        rows = lax.all_gather(flat[None], "dp", axis=0, tiled=True)
        totals = matmul(marker, rows)
        results, start = [], 0
        for local_grad, size in zip(local_grads, sizes):
            results.append(
                totals[:, start : start + size].reshape((ADAPTER_SETS,) + local_grad.shape)
            )
            start += size
        return results

    early = adapter_sums(
        [
            grad_out_a_local,
            grad_out_b_local,
            grad_up_a_local,
            grad_up_b_local,
            grad_down_a_local,
            grad_down_b_local,
        ]
    )
    late = adapter_sums([grad_qkv_b_local, grad_qkv_a_local])
    adapter_totals = [late[1], late[0]] + early
    return (
        output,
        grad_tokens,
        adapter_totals[0],
        adapter_totals[1],
        adapter_totals[2],
        adapter_totals[3],
        adapter_totals[4],
        adapter_totals[5],
        adapter_totals[6],
        adapter_totals[7],
    )


def solution(mesh):
    return jax.shard_map(
        body,
        mesh=mesh,
        in_specs=(
            P("dp", None),
            P("dp", None),
            P(),
            P("dp", None, "tensor"),
            P(None, "tensor"),
            P("dp", "tensor"),
            P(),
            P("dp", None),
            P("dp"),
            P("dp", None, None, "tensor"),
            P("dp", None, "tensor"),
            P("dp", None, "tensor"),
            P("dp", "tensor"),
            P("dp", None),
            P("dp"),
            P("dp", None),
            P(),
            P(None, None, None, "tensor"),
            P(None, "tensor", None),
            P(),
            P(),
            P(None, None, None, "tensor"),
            P(None, "tensor", None),
            P(),
        ),
        out_specs=(
            P("dp", None),
            P("dp", None),
            P(),
            P(None, None, None, "tensor"),
            P(None, "tensor", None),
            P(),
            P(),
            P(None, None, None, "tensor"),
            P(None, "tensor", None),
            P(),
        ),
        check_vma=False,
    )
```

```python
import functools

import jax
import jax.numpy as jnp
from jax import lax
from jax.experimental import pallas as pl
from jax.experimental.pallas import tpu as pltpu
from jax.sharding import PartitionSpec as P

HEAD_SIZE = 128
TOP = 4
EXPERTS = 16
ADAPTER_SETS = 8
PIECE = 256


EPSILON = 1e-06
THETA = 1000000.0
ADAPTER_SCALE = 2.0
MASKED = -1e30
MESH = pl.DeviceIdType.MESH
SUM_CHUNKS = 16
AHEAD = 2
PAIR = 2
EXPERT_PARTS = (8, 4, 4)


def matmul(left_side, right_side):
    return jnp.dot(left_side, right_side, preferred_element_type=jnp.float32)


def contract_last(left_side, right_side):
    return lax.dot_general(
        left_side, right_side, (((1,), (1,)), ((), ())), preferred_element_type=jnp.float32
    )


def contract_first(left_side, right_side):
    return lax.dot_general(
        left_side, right_side, (((0,), (0,)), ((), ())), preferred_element_type=jnp.float32
    )


def to_low(values):
    return values.astype(jnp.bfloat16)


def rms_scale(values, gain_values):
    return (
        values * lax.rsqrt(jnp.mean(values * values, axis=1, keepdims=True) + EPSILON) * gain_values
    )


def rope_tables(length):
    half_size = HEAD_SIZE // 2
    frequency = THETA ** (-jnp.arange(half_size, dtype=jnp.float32) * 2.0 / HEAD_SIZE)
    angles = jnp.arange(length, dtype=jnp.float32)[:, None] * frequency[None, :]
    return (
        jnp.concatenate([jnp.cos(angles)] * 2, axis=1),
        jnp.concatenate([jnp.sin(angles)] * 2, axis=1),
    )


def rotate(values, cosine, sine_table):
    half_size = values.shape[-1] // 2
    turned = jnp.concatenate([-values[..., half_size:], values[..., :half_size]], axis=-1)
    return values * cosine[:, None, :] + turned * sine_table[:, None, :]


def piece_index(positions, starts):
    inside = (positions[:, None] >= starts[None, :]) & (
        positions[:, None] < starts[None, :] + PIECE
    )
    labels = jnp.arange(starts.shape[0], dtype=jnp.int32)[None, :] + 1
    return jnp.sum(jnp.where(inside, labels, 0), axis=1) - 1


def visible(row_positions, col_positions, starts):
    row_piece = piece_index(row_positions, starts)
    col_piece = piece_index(col_positions, starts)
    causal = col_positions[None, :] <= row_positions[:, None]
    together = (row_piece[:, None] == col_piece[None, :]) & (row_piece[:, None] >= 0)
    return causal | together


def line_sum_steps(chunks, part_ref, total_ref, from_end, pair_sum, from_pair, semaphores):
    place = lax.axis_index("tensor")
    rows = part_ref.shape[0] // chunks
    inner = (place == 1) | (place == 2)
    end = (place == 0) | (place == 3)
    mate = jnp.where(place < 2, 1 - place, 5 - place)
    other = jnp.where(inner, 3 - place, place)

    def span(chunk):
        return pl.ds(pl.multiple_of(chunk * rows, rows), rows)

    def copy(source, target, chunk, lane, device):
        return pltpu.make_async_remote_copy(
            source.at[span(chunk)],
            target.at[span(chunk)],
            semaphores.at[2 * lane, chunk],
            semaphores.at[2 * lane + 1, chunk],
            device_id={"tensor": device},
            device_id_type=MESH,
        )

    def inward(chunk):
        return copy(part_ref, from_end, chunk, 0, mate)

    def across(chunk):
        return copy(pair_sum, from_pair, chunk, 1, other)

    def outward(chunk):
        return copy(total_ref, total_ref, chunk, 2, mate)

    def add(left_ref, right_ref, out_ref, chunk):
        out_ref[span(chunk)] = to_low(
            left_ref[span(chunk)].astype(jnp.float32) + right_ref[span(chunk)].astype(jnp.float32)
        )

    def greet(extra):
        barrier = pltpu.get_barrier_semaphore()
        pl.semaphore_signal(barrier, inc=1, device_id={"tensor": mate}, device_id_type=MESH)

        @pl.when(inner)
        def _():
            pl.semaphore_signal(barrier, inc=1, device_id={"tensor": other}, device_id_type=MESH)
            pl.semaphore_wait(barrier, 2 + extra)

        @pl.when(end)
        def _():
            pl.semaphore_wait(barrier, 1 + extra)

    def begin():
        @pl.when(end)
        def _():
            @pl.loop(0, chunks)
            def _(chunk):
                inward(chunk).start()

    def advance(step):
        @pl.when(inner & (step < chunks))
        def _():
            inward(step).wait_recv()
            add(part_ref, from_end, pair_sum, step)
            across(step).start()

        @pl.when(inner & (step > 0) & (step <= chunks))
        def _():
            across(step - 1).wait_recv()
            add(pair_sum, from_pair, total_ref, step - 1)
            outward(step - 1).start()

    def finish():
        @pl.when(end)
        def _():
            @pl.loop(0, chunks)
            def _(chunk):
                inward(chunk).wait_send()
                outward(chunk).wait_recv()

        @pl.when(inner)
        def _():
            @pl.loop(0, chunks)
            def _(chunk):
                across(chunk).wait_send()
                outward(chunk).wait_send()

    return greet, begin, advance, finish


def plane_gather_steps(pieces, block_ref, whole_ref, semaphores, local_semaphore):
    spot = lax.axis_index("dp")
    depth = block_ref.shape[1]
    rows = block_ref.shape[0] // pieces
    core_mate = spot + 1 - 2 * (spot % 2)
    x_mate = spot + 2 - 4 * ((spot // 2) % 2)
    y_mate = spot + 4 - 8 * (spot // 4)
    x_y_mate = x_mate + 4 - 8 * (spot // 4)
    lanes = {
        "core": (spot, core_mate, 0, 1),
        "x": (spot, x_mate, 0, 1),
        "y": (spot, y_mate, 0, 1),
        "x_core": (x_mate, core_mate, 0, 1),
        "x_y": (x_mate, y_mate, 0, 2),
        "y_core": (y_mate, core_mate, 0, 1),
        "y_x": (y_mate, x_mate, 1, 2),
        "xy_core": (x_y_mate, core_mate, 0, 2),
        "yx_core": (x_y_mate, core_mate, 1, 2),
    }
    order = list(lanes)

    def send(name, piece):
        owner, device, part, parts = lanes[name]
        lane = order.index(name)
        span = pl.ds(
            pl.multiple_of(piece * rows + part * (rows // parts), rows // parts), rows // parts
        )
        columns = pl.ds(pl.multiple_of(owner * depth, depth), depth)
        target = whole_ref.at[span, columns]
        source = block_ref.at[span] if name in ("core", "x", "y") else target
        return pltpu.make_async_remote_copy(
            source,
            target,
            semaphores.at[2 * lane, piece],
            semaphores.at[2 * lane + 1, piece],
            device_id={"dp": device},
            device_id_type=MESH,
        )

    def own():
        columns = pl.ds(pl.multiple_of(spot * depth, depth), depth)
        return pltpu.make_async_copy(block_ref, whole_ref.at[:, columns], local_semaphore)

    def greet():
        barrier = pltpu.get_barrier_semaphore()
        for device in (core_mate, x_mate, y_mate):
            pl.semaphore_signal(barrier, inc=1, device_id={"dp": device}, device_id_type=MESH)

    def begin():
        own().start()

    def advance(step):
        @pl.when(step < pieces)
        def _():
            for name in ("x", "y", "core"):
                send(name, step).start()

        @pl.when((step >= AHEAD) & (step < pieces + AHEAD))
        def _():
            piece = step - AHEAD
            send("x", piece).wait_recv()
            send("x_y", piece).start()
            send("x_core", piece).start()
            send("y", piece).wait_recv()
            send("y_x", piece).start()
            send("y_core", piece).start()

        @pl.when((step >= 2 * AHEAD) & (step < pieces + 2 * AHEAD))
        def _():
            piece = step - 2 * AHEAD
            send("x_y", piece).wait_recv()
            send("xy_core", piece).start()
            send("y_x", piece).wait_recv()
            send("yx_core", piece).start()

    def finish():
        own().wait()

        @pl.loop(0, pieces)
        def _(piece):
            for name in order:
                send(name, piece).wait_send()
            for name in ("core", "x_core", "y_core", "xy_core", "yx_core"):
                send(name, piece).wait_recv()

    return greet, begin, advance, finish


def line_sum_kernel(chunks, part_ref, total_ref, from_end, pair_sum, from_pair, semaphores):
    greet, begin, advance, finish = line_sum_steps(
        chunks, part_ref, total_ref, from_end, pair_sum, from_pair, semaphores
    )
    greet(0)
    begin()

    @pl.loop(0, chunks + 1)
    def _(step):
        advance(step)

    finish()


def sum_gather_kernel(
    chunks,
    pieces,
    part_ref,
    block_ref,
    total_ref,
    whole_ref,
    from_end,
    pair_sum,
    from_pair,
    semaphores,
    gather_semaphores,
    local_semaphore,
):
    greet, begin, advance, finish = line_sum_steps(
        chunks, part_ref, total_ref, from_end, pair_sum, from_pair, semaphores
    )
    gather_greet, gather_begin, gather_advance, gather_finish = plane_gather_steps(
        pieces, block_ref, whole_ref, gather_semaphores, local_semaphore.at[0]
    )
    gather_greet()
    greet(3)
    begin()
    gather_begin()

    @pl.loop(0, max(chunks + 1, pieces + 2 * AHEAD))
    def _(step):
        gather_advance(step)
        advance(step)

    gather_finish()
    finish()


def on_line():
    return lax.axis_size("tensor") == 4


def in_plane():
    return lax.axis_size("dp") == 8


def tensor_sum(part, number):
    if not on_line():
        return lax.psum(part.astype(jnp.float32), "tensor")
    total = pl.pallas_call(
        functools.partial(line_sum_kernel, SUM_CHUNKS),
        out_shape=jax.ShapeDtypeStruct(part.shape, jnp.bfloat16),
        in_specs=[pl.BlockSpec(memory_space=pltpu.VMEM)],
        out_specs=pl.BlockSpec(memory_space=pltpu.VMEM),
        scratch_shapes=[pltpu.VMEM(part.shape, jnp.bfloat16)] * 3
        + [pltpu.SemaphoreType.DMA((6, SUM_CHUNKS))],
        compiler_params=pltpu.CompilerParams(
            collective_id=number, has_side_effects=True, vmem_limit_bytes=40 * 2**20
        ),
        cost_estimate=pl.CostEstimate(flops=0, bytes_accessed=300 * 2**20, transcendentals=0),
    )(part)
    return total.astype(jnp.float32)


def packed(wide_part, narrow_part):
    pad = jnp.zeros((wide_part.shape[0], 128 - narrow_part.shape[1]), jnp.bfloat16)
    return jnp.concatenate([to_low(wide_part), to_low(narrow_part), pad], axis=1)


def summed(wide_part, narrow_part, number):
    width, small = wide_part.shape[1], narrow_part.shape[1]
    total = tensor_sum(packed(wide_part, narrow_part), number)
    return total[:, :width], total[:, width : width + small]


def summed_and_gathered(wide_part, narrow_part, block, number):
    if not (on_line() and in_plane()):
        whole = lax.all_gather(block, "dp", axis=1, tiled=True)
        return summed(wide_part, narrow_part, number) + (whole,)
    width, small = wide_part.shape[1], narrow_part.shape[1]
    part = packed(wide_part, narrow_part)
    pieces = EXPERTS
    total, whole = pl.pallas_call(
        functools.partial(sum_gather_kernel, SUM_CHUNKS, pieces),
        out_shape=[
            jax.ShapeDtypeStruct(part.shape, jnp.bfloat16),
            jax.ShapeDtypeStruct((block.shape[0], 8 * block.shape[1]), jnp.bfloat16),
        ],
        in_specs=[pl.BlockSpec(memory_space=pltpu.VMEM), pl.BlockSpec(memory_space=pltpu.HBM)],
        out_specs=[pl.BlockSpec(memory_space=pltpu.VMEM), pl.BlockSpec(memory_space=pltpu.HBM)],
        scratch_shapes=[pltpu.VMEM(part.shape, jnp.bfloat16)] * 3
        + [
            pltpu.SemaphoreType.DMA((6, SUM_CHUNKS)),
            pltpu.SemaphoreType.DMA((18, pieces)),
            pltpu.SemaphoreType.DMA((1,)),
        ],
        compiler_params=pltpu.CompilerParams(
            collective_id=number, has_side_effects=True, vmem_limit_bytes=40 * 2**20
        ),
        cost_estimate=pl.CostEstimate(flops=0, bytes_accessed=360 * 2**20, transcendentals=0),
    )(part, block)
    total = total.astype(jnp.float32)
    return total[:, :width], total[:, width : width + small], whole


def experts_kernel(
    tile,
    inputs_ref,
    cotangent_ref,
    gate_ref,
    up_ref,
    down_ref,
    out_start,
    grad_start,
    out_ref,
    grad_ref,
    gate_grad_ref,
    act_rows,
    grad_rows,
    semaphores,
):
    @pl.when(pl.program_id(0) == 0)
    def _():
        loads = [
            pltpu.make_async_copy(out_start, out_ref, semaphores.at[0]),
            pltpu.make_async_copy(grad_start, grad_ref, semaphores.at[1]),
        ]
        for load in loads:
            load.start()
        for load in loads:
            load.wait()

    pair = gate_ref.shape[1]
    hidden = down_ref.shape[1] // pair

    @pl.loop(0, inputs_ref.shape[1] // tile)
    def _(index):
        column = pl.ds(pl.multiple_of(index * tile, tile), tile)
        inputs = inputs_ref[:, column]
        cotangents = cotangent_ref[:, column]
        for member in range(pair):
            gate_from, up_from = 2 * hidden * member, 2 * hidden * member + hidden
            gate_up = matmul(up_ref[0, gate_from : gate_from + 2 * hidden], inputs)
            open_part = matmul(down_ref[0, hidden * member : hidden * (member + 1)], cotangents)
            gate_half, up_half = gate_up[:hidden], gate_up[hidden:]
            squashed = 1.0 / (1.0 + jnp.exp(-gate_half))
            act = to_low(gate_half * squashed * up_half).astype(jnp.float32)
            gate_row = gate_ref[0, member : member + 1, column]
            gate_grad_ref[0, member : member + 1, column] = jnp.sum(
                act * open_part, axis=0, keepdims=True
            )
            act_rows[hidden * member : hidden * (member + 1)] = to_low(gate_row * act)
            grad_act = gate_row * open_part
            grad_rows[gate_from : gate_from + hidden] = to_low(
                grad_act * up_half * squashed * (1.0 + gate_half * (1.0 - squashed))
            )
            grad_rows[up_from : up_from + hidden] = to_low(grad_act * gate_half * squashed)
        out_ref[column] += contract_first(act_rows[...], down_ref[0])
        grad_ref[column] += contract_first(grad_rows[...], up_ref[0])


def experts_step(inputs, cotangents, gates, up_rows, down_rows, out_start, grad_start, first):
    groups, pair, length = up_rows.shape[0], gates.shape[1], inputs.shape[1]
    width, hidden = inputs.shape[0], down_rows.shape[1] // gates.shape[1]
    tile = min(512, length)
    once = pl.Buffered(1)

    def still(shape):
        return pl.BlockSpec(shape, lambda group: (0, 0), pipeline_mode=once)

    return pl.pallas_call(
        functools.partial(experts_kernel, tile),
        grid=(groups,),
        in_specs=[
            still((width, length)),
            still((width, length)),
            pl.BlockSpec((1, pair, length), lambda group: (group + first, 0, 0)),
            pl.BlockSpec((1, 2 * pair * hidden, width), lambda group: (group, 0, 0)),
            pl.BlockSpec((1, pair * hidden, width), lambda group: (group + first, 0, 0)),
            pl.BlockSpec(memory_space=pltpu.HBM),
            pl.BlockSpec(memory_space=pltpu.HBM),
        ],
        out_specs=[
            still((length, width)),
            still((length, width)),
            pl.BlockSpec((1, pair, length), lambda group: (group, 0, 0)),
        ],
        out_shape=[
            jax.ShapeDtypeStruct((length, width), jnp.float32),
            jax.ShapeDtypeStruct((length, width), jnp.float32),
            jax.ShapeDtypeStruct((groups, pair, length), jnp.float32),
        ],
        scratch_shapes=[
            pltpu.VMEM((pair * hidden, tile), jnp.bfloat16),
            pltpu.VMEM((2 * pair * hidden, tile), jnp.bfloat16),
            pltpu.SemaphoreType.DMA((2,)),
        ],
        compiler_params=pltpu.CompilerParams(
            vmem_limit_bytes=60 * 2**20, dimension_semantics=("arbitrary",)
        ),
        cost_estimate=pl.CostEstimate(
            flops=18 * groups * pair * hidden * width * length,
            bytes_accessed=64 * 2**20,
            transcendentals=0,
        ),
    )(inputs, cotangents, gates, up_rows, down_rows, out_start, grad_start)


def swiglu(paired):
    return jax.nn.silu(paired[..., 0, :]) * paired[..., 1, :]


def gathered(weight):
    return lax.all_gather(weight, "dp", axis=0, tiled=True)


def body(
    tokens,
    cotangent,
    attention_norm_gain,
    query_key_value_weight,
    query_key_value_bias,
    output_projection_weight,
    feedforward_norm_gain,
    router_matrix,
    shared_expert_gate_weight,
    routed_gate_up_weight,
    routed_down_weight,
    shared_expert_gate_up_weight,
    shared_expert_down_weight,
    routes,
    sequence_adapter_index,
    picture_piece_starts,
    adapter_query_key_value_lower,
    adapter_query_key_value_upper,
    adapter_output_lower,
    adapter_output_upper,
    adapter_shared_up_lower,
    adapter_shared_up_upper,
    adapter_shared_down_lower,
    adapter_shared_down_upper,
):
    length, width = tokens.shape
    heads_here = query_key_value_weight.shape[2] // HEAD_SIZE
    set_id = sequence_adapter_index[0]
    starts = picture_piece_starts[0]

    def selected_experts(adapter_entry):
        return lax.dynamic_index_in_dim(adapter_entry, set_id, 0, keepdims=False)

    qkv_a, qkv_b, out_a, out_b = (
        selected_experts(adapter_query_key_value_lower),
        selected_experts(adapter_query_key_value_upper),
        selected_experts(adapter_output_lower),
        selected_experts(adapter_output_upper),
    )
    up_a, up_b, down_a, down_b = (
        selected_experts(adapter_shared_up_lower),
        selected_experts(adapter_shared_up_upper),
        selected_experts(adapter_shared_down_lower),
        selected_experts(adapter_shared_down_upper),
    )
    gain_attn_f = attention_norm_gain.astype(jnp.float32)
    gain_ffn_f = feedforward_norm_gain.astype(jnp.float32)
    tokens_f = tokens.astype(jnp.float32)
    normed = to_low(rms_scale(tokens_f, gain_attn_f))
    mid_qkv = to_low(matmul(normed, qkv_a))
    columns = normed
    attention_rows = gathered(
        jnp.concatenate([query_key_value_weight, output_projection_weight[:, None]], axis=1)
    )
    qkv_rows, output_rows = attention_rows[:, :3], attention_rows[:, 3]
    qkv_sum = jnp.einsum(
        "tr,rsf->tsf",
        columns,
        qkv_rows,
        preferred_element_type=jnp.float32,
    )
    qkv_sum = qkv_sum + query_key_value_bias.astype(jnp.float32)
    qkv_sum = qkv_sum + ADAPTER_SCALE * jnp.einsum(
        "tr,rsf->tsf", mid_qkv, qkv_b, preferred_element_type=jnp.float32
    )
    cosine, sine_table = rope_tables(length)

    def position(raw_values):
        query_part = rotate(
            raw_values[:, 0].reshape(length, heads_here, HEAD_SIZE), cosine, sine_table
        )
        keys_part = rotate(
            raw_values[:, 1].reshape(length, heads_here, HEAD_SIZE), cosine, sine_table
        )
        return (query_part, keys_part)

    (query_f, keys_f), rope_pull = jax.vjp(position, qkv_sum)
    query = to_low(query_f)
    keys = to_low(keys_f)
    values = to_low(qkv_sum[:, 2].reshape(length, heads_here, HEAD_SIZE))
    block_rows = min(length, 512)
    score_scale = HEAD_SIZE ** (-0.5)
    positions = jnp.arange(length, dtype=jnp.int32)
    attended_parts = []
    logsum_parts = []
    for offset in range(0, length, block_rows):
        allowed = visible(positions[offset : offset + block_rows], positions, starts)
        scores = (
            jnp.einsum(
                "qhd,khd->hqk",
                query[offset : offset + block_rows],
                keys,
                preferred_element_type=jnp.float32,
            )
            * score_scale
        )
        scores = jnp.where(allowed[None], scores, MASKED)
        highest = jnp.max(scores, axis=-1, keepdims=True)
        weights_exp = jnp.exp(scores - highest)
        row_totals = jnp.sum(weights_exp, axis=-1, keepdims=True)
        attended_parts.append(
            jnp.einsum(
                "hqk,khd->qhd",
                to_low(weights_exp / row_totals),
                values,
                preferred_element_type=jnp.float32,
            )
        )
        logsum_parts.append(highest + jnp.log(row_totals))
    attended = to_low(jnp.concatenate(attended_parts, axis=0).reshape(length, -1))
    branch_part = contract_last(attended, output_rows)
    down_block = jnp.transpose(routed_down_weight, (1, 2, 0))
    branch_here, mid_out_here_f, down_rows = summed_and_gathered(
        branch_part,
        matmul(attended, out_a),
        down_block.reshape(-1, down_block.shape[2]),
        1,
    )
    mid_out_here = to_low(mid_out_here_f)
    hidden_here = tokens_f + branch_here + ADAPTER_SCALE * matmul(mid_out_here, out_b)
    normed_two_here_f, norm_ffn_pull = jax.vjp(
        lambda rows: rms_scale(rows, gain_ffn_f), hidden_here
    )
    normed_two_here = to_low(normed_two_here_f)
    normed_two, mid_out = (normed_two_here, mid_out_here)
    cot_f = cotangent.astype(jnp.float32)
    shared_three = gathered(
        jnp.concatenate([shared_expert_gate_up_weight, shared_expert_down_weight[:, None]], axis=1)
    )
    shared_rows, sdown_rows = shared_three[:, :2], shared_three[:, 2]
    small_rows = gathered(
        jnp.concatenate(
            [
                router_matrix,
                shared_expert_gate_weight[:, None],
                jnp.full_like(shared_expert_gate_weight, set_id)[:, None],
            ],
            axis=1,
        )
    )
    router_full, gate_full = small_rows[:, :EXPERTS], small_rows[:, EXPERTS]
    router_probs = jax.nn.softmax(matmul(normed_two, router_full), axis=-1)
    shared_gate = jax.nn.sigmoid(matmul(normed_two, gate_full))
    expert_ids = jnp.arange(EXPERTS, dtype=jnp.int32)
    chosen = jnp.sum(
        (routes[:, :, None] == expert_ids[None, None, :]).astype(jnp.float32), axis=1
    )
    gate_table = (router_probs * chosen).T

    mid_up = to_low(matmul(normed_two, up_a))
    shared_gu = jnp.einsum(
        "tr,rxf->txf", normed_two, shared_rows, preferred_element_type=jnp.float32
    ) + ADAPTER_SCALE * jnp.einsum("tr,rxf->txf", mid_up, up_b, preferred_element_type=jnp.float32)
    shared_act_f, shared_pull = jax.vjp(swiglu, shared_gu)
    shared_act = to_low(shared_act_f)
    shared_cols = contract_last(shared_act, sdown_rows)
    shared_gate_part = jnp.sum(cot_f * shared_cols, axis=1)
    grad_shared = to_low(shared_gate[:, None] * cot_f)
    grad_mid_down = to_low(ADAPTER_SCALE * contract_last(grad_shared, down_b))
    grad_shared_act = matmul(grad_shared, sdown_rows) + contract_last(grad_mid_down, down_a)
    grad_shared_gu = to_low(shared_pull(grad_shared_act)[0])
    grad_mid_up_part = ADAPTER_SCALE * jnp.einsum(
        "txf,rxf->tr", grad_shared_gu, up_b, preferred_element_type=jnp.float32
    )
    grad_up_b_local = ADAPTER_SCALE * jnp.einsum(
        "tr,txf->rxf", mid_up, grad_shared_gu, preferred_element_type=jnp.float32
    )
    grad_down_a_local = contract_first(grad_mid_down, shared_act)
    combined_part = shared_gate[:, None] * shared_cols
    normed_two_part = jnp.einsum(
        "txf,rxf->tr", grad_shared_gu, shared_rows, preferred_element_type=jnp.float32
    )

    up_block = jnp.transpose(routed_gate_up_weight, (1, 2, 3, 0))
    inputs_t, cotangents_t = normed_two.T, cotangent.T
    gates = gate_table.reshape(EXPERTS // PAIR, PAIR, length)
    down_rows = down_rows.reshape(EXPERTS // PAIR, -1, width)
    gate_grad_parts = []
    first = 0
    for count in EXPERT_PARTS:
        up_rows = lax.all_gather(up_block[first : first + count], "dp", axis=3, tiled=True)
        combined_part, normed_two_part, gate_grads = experts_step(
            inputs_t,
            cotangents_t,
            gates,
            up_rows.reshape(count // PAIR, -1, width),
            down_rows,
            combined_part,
            normed_two_part,
            first // PAIR,
        )
        gate_grad_parts.append(gate_grads.reshape(count, length))
        first += count
    gate_grad_part = jnp.concatenate(gate_grad_parts, axis=0).T
    narrow_part = jnp.concatenate(
        [gate_grad_part, shared_gate_part[:, None], grad_mid_up_part], axis=1
    )
    grad_normed_two, narrow_sum = summed(normed_two_part, narrow_part, 2)
    combined_here, mid_down_here_f = summed(combined_part, matmul(shared_act, down_a), 3)
    mid_down = to_low(mid_down_here_f)
    extra_here = ADAPTER_SCALE * matmul(mid_down, down_b)
    output = to_low(hidden_here + combined_here + shared_gate[:, None] * extra_here)
    grad_down_b_local = ADAPTER_SCALE * contract_first(mid_down, grad_shared)
    grad_probs = chosen * narrow_sum[:, :EXPERTS]
    grad_logits = to_low(
        router_probs * (grad_probs - jnp.sum(router_probs * grad_probs, axis=1, keepdims=True))
    )
    shared_gate_grad = narrow_sum[:, EXPERTS] + jnp.sum(cot_f * extra_here, axis=1)
    grad_gate_logit = to_low(shared_gate_grad * shared_gate * (1.0 - shared_gate))
    grad_mid_up_here = to_low(narrow_sum[:, EXPERTS + 1 :])
    grad_normed_two = grad_normed_two + contract_last(grad_logits, router_full)
    grad_normed_two = (
        grad_normed_two
        + grad_gate_logit.astype(jnp.float32)[:, None] * gate_full.astype(jnp.float32)[None, :]
    )
    grad_normed_two = grad_normed_two + contract_last(grad_mid_up_here, up_a)
    grad_hidden = cot_f + norm_ffn_pull(grad_normed_two)[0]
    grad_branch_here = to_low(grad_hidden)
    grad_branch, grad_mid_up = (grad_branch_here, grad_mid_up_here)
    grad_up_a_local = contract_first(grad_mid_up, normed_two)
    grad_mid_out = to_low(ADAPTER_SCALE * contract_last(grad_branch, out_b))
    grad_out_b_local = ADAPTER_SCALE * contract_first(mid_out, grad_branch)
    columns = grad_branch
    grad_att_sum = matmul(
        columns, output_rows
    )
    grad_attended = to_low(grad_att_sum + contract_last(grad_mid_out, out_a)).reshape(
        length, heads_here, HEAD_SIZE
    )
    grad_out_a_local = contract_first(grad_mid_out, attended)
    grad_keys = jnp.zeros((length, heads_here, HEAD_SIZE), jnp.float32)
    grad_values = jnp.zeros((length, heads_here, HEAD_SIZE), jnp.float32)
    grad_query_parts = []
    for block_number, offset in enumerate(range(0, length, block_rows)):
        query_rows = query[offset : offset + block_rows]
        allowed = visible(positions[offset : offset + block_rows], positions, starts)
        scores = (
            jnp.einsum("qhd,khd->hqk", query_rows, keys, preferred_element_type=jnp.float32)
            * score_scale
        )
        scores = jnp.where(allowed[None], scores, MASKED)
        probs_f = jnp.exp(scores - logsum_parts[block_number])
        grad_rows = grad_attended[offset : offset + block_rows]
        grad_values = grad_values + jnp.einsum(
            "hqk,qhd->khd", to_low(probs_f), grad_rows, preferred_element_type=jnp.float32
        )
        grad_probs_att = jnp.einsum(
            "qhd,khd->hqk", grad_rows, values, preferred_element_type=jnp.float32
        )
        grad_scores = to_low(
            probs_f * (grad_probs_att - jnp.sum(probs_f * grad_probs_att, axis=-1, keepdims=True))
        )
        grad_query_parts.append(
            jnp.einsum("hqk,khd->qhd", grad_scores, keys, preferred_element_type=jnp.float32)
            * score_scale
        )
        grad_keys = (
            grad_keys
            + jnp.einsum(
                "hqk,qhd->khd", grad_scores, query_rows, preferred_element_type=jnp.float32
            )
            * score_scale
        )
    grad_query = jnp.concatenate(grad_query_parts, axis=0)
    grad_raw = rope_pull((grad_query, grad_keys))[0]
    grad_raw = grad_raw.at[:, 2].set(grad_values.reshape(length, -1))
    grad_qkv = to_low(grad_raw)
    grad_mid_qkv_part = ADAPTER_SCALE * jnp.einsum(
        "tsf,rsf->tr", grad_qkv, qkv_b, preferred_element_type=jnp.float32
    )
    grad_qkv_b_local = ADAPTER_SCALE * jnp.einsum(
        "tr,tsf->rsf", mid_qkv, grad_qkv, preferred_element_type=jnp.float32
    )
    normed_part = jnp.einsum(
        "tsf,rsf->tr",
        grad_qkv,
        qkv_rows,
        preferred_element_type=jnp.float32,
    )
    grad_normed, grad_mid_qkv_f = summed(normed_part, grad_mid_qkv_part, 4)
    grad_mid_qkv_here = to_low(grad_mid_qkv_f)
    grad_normed = grad_normed + contract_last(grad_mid_qkv_here, qkv_a)
    norm_attn_pull = jax.vjp(lambda rows: rms_scale(rows, gain_attn_f), tokens_f)[1]
    grad_tokens_here = to_low(grad_hidden + norm_attn_pull(grad_normed)[0])
    grad_tokens, grad_mid_qkv = (grad_tokens_here, grad_mid_qkv_here)
    grad_qkv_a_local = contract_first(grad_mid_qkv, normed)
    everyone = small_rows[:: small_rows.shape[0] // lax.axis_size("dp"), EXPERTS + 1]
    marker = to_low(
        jnp.arange(ADAPTER_SETS, dtype=jnp.int32)[:, None] == everyone.astype(jnp.int32)[None, :]
    )

    def adapter_sums(local_grads):
        sizes = [local_grad.shape[1] for local_grad in local_grads]
        flat = jnp.concatenate([to_low(local_grad) for local_grad in local_grads], axis=1)
        rows = lax.all_gather(flat, "dp", axis=0, tiled=False)
        totals = jnp.einsum("cj,jrn->crn", marker, rows, preferred_element_type=jnp.float32)
        results, start = [], 0
        for size in sizes:
            results.append(totals[:, :, start : start + size])
            start += size
        return results

    def flipped(total):
        return jnp.swapaxes(total, 1, 2)

    def opened(total, count):
        return total.reshape(total.shape[0], total.shape[1], count, -1)

    total_out_a, total_out_b, total_up_a, total_up_b, total_down_a, total_down_b = adapter_sums(
        [
            grad_out_a_local,
            grad_out_b_local,
            grad_up_a_local,
            grad_up_b_local.reshape(grad_up_b_local.shape[0], -1),
            grad_down_a_local,
            grad_down_b_local,
        ]
    )
    total_qkv_b, total_qkv_a = adapter_sums(
        [grad_qkv_b_local.reshape(grad_qkv_b_local.shape[0], -1), grad_qkv_a_local]
    )
    return (
        output,
        grad_tokens,
        flipped(total_qkv_a),
        opened(total_qkv_b, 3),
        flipped(total_out_a),
        total_out_b,
        flipped(total_up_a),
        opened(total_up_b, 2),
        flipped(total_down_a),
        total_down_b,
    )


def solution(mesh):
    return jax.shard_map(
        body,
        mesh=mesh,
        in_specs=(
            P("dp", None),
            P("dp", None),
            P(),
            P("dp", None, "tensor"),
            P(None, "tensor"),
            P("dp", "tensor"),
            P(),
            P("dp", None),
            P("dp"),
            P("dp", None, None, "tensor"),
            P("dp", None, "tensor"),
            P("dp", None, "tensor"),
            P("dp", "tensor"),
            P("dp", None),
            P("dp"),
            P("dp", None),
            P(),
            P(None, None, None, "tensor"),
            P(None, "tensor", None),
            P(),
            P(),
            P(None, None, None, "tensor"),
            P(None, "tensor", None),
            P(),
        ),
        out_specs=(
            P("dp", None),
            P("dp", None),
            P(),
            P(None, None, None, "tensor"),
            P(None, "tensor", None),
            P(),
            P(),
            P(None, None, None, "tensor"),
            P(None, "tensor", None),
            P(),
        ),
        check_vma=False,
    )
```

```python
import functools

import jax
import jax.numpy as jnp
from jax import lax
from jax.experimental import pallas as pl
from jax.experimental.pallas import tpu as pltpu
from jax.sharding import PartitionSpec as P

HEAD_SIZE = 128
TOP = 4
EXPERTS = 16
ADAPTER_SETS = 8
PIECE = 256


EPSILON = 1e-06
THETA = 1000000.0
ADAPTER_SCALE = 2.0
MASKED = -1e30
QUERY_ROWS = 256
NARROW = 128
MESH = pl.DeviceIdType.MESH
SUM_CHUNKS = 16
AHEAD = 2
GATHER_PIECES = 16
PAIR = 2
EXPERT_PARTS = (8, 4, 4)


def matmul(left_side, right_side):
    return jnp.dot(left_side, right_side, preferred_element_type=jnp.float32)


def contract_last(left_side, right_side):
    return lax.dot_general(
        left_side, right_side, (((1,), (1,)), ((), ())), preferred_element_type=jnp.float32
    )


def contract_first(left_side, right_side):
    return lax.dot_general(
        left_side, right_side, (((0,), (0,)), ((), ())), preferred_element_type=jnp.float32
    )


def to_low(values):
    return values.astype(jnp.bfloat16)


def rms_scale(values, gain_values):
    return (
        values * lax.rsqrt(jnp.mean(values * values, axis=1, keepdims=True) + EPSILON) * gain_values
    )


def rope_tables(length):
    half_size = HEAD_SIZE // 2
    frequency = THETA ** (-jnp.arange(half_size, dtype=jnp.float32) * 2.0 / HEAD_SIZE)
    angles = jnp.arange(length, dtype=jnp.float32)[:, None] * frequency[None, :]
    return (
        jnp.concatenate([jnp.cos(angles)] * 2, axis=1),
        jnp.concatenate([jnp.sin(angles)] * 2, axis=1),
    )


def piece_index(positions, starts):
    inside = (positions[:, None] >= starts[None, :]) & (
        positions[:, None] < starts[None, :] + PIECE
    )
    labels = jnp.arange(starts.shape[0], dtype=jnp.int32)[None, :] + 1
    return jnp.sum(jnp.where(inside, labels, 0), axis=1) - 1


def line_sum_steps(
    chunks, wide_ref, narrow_ref, total_ref, part_ref, from_end, pair_sum, from_pair, semaphores
):
    place = lax.axis_index("tensor")
    width = wide_ref.shape[1]
    rows = part_ref.shape[0] // chunks
    inner = (place == 1) | (place == 2)
    end = (place == 0) | (place == 3)
    mate = jnp.where(place < 2, 1 - place, 5 - place)
    other = jnp.where(inner, 3 - place, place)

    def span(chunk):
        return pl.ds(pl.multiple_of(chunk * rows, rows), rows)

    def copy(source, target, chunk, lane, device):
        return pltpu.make_async_remote_copy(
            source.at[span(chunk)],
            target.at[span(chunk)],
            semaphores.at[2 * lane, chunk],
            semaphores.at[2 * lane + 1, chunk],
            device_id={"tensor": device},
            device_id_type=MESH,
        )

    def inward(chunk):
        return copy(part_ref, from_end, chunk, 0, mate)

    def across(chunk):
        return copy(pair_sum, from_pair, chunk, 1, other)

    def outward(chunk):
        return copy(total_ref, total_ref, chunk, 2, mate)

    def add(left_ref, right_ref, out_ref, chunk):
        out_ref[span(chunk)] = to_low(
            left_ref[span(chunk)].astype(jnp.float32) + right_ref[span(chunk)].astype(jnp.float32)
        )

    def stage(chunk):
        part_ref[span(chunk), :width] = to_low(wide_ref[span(chunk)])
        if narrow_ref is not None:
            part_ref[span(chunk), width:] = narrow_ref[span(chunk)]

    def greet(extra):
        barrier = pltpu.get_barrier_semaphore()
        pl.semaphore_signal(barrier, inc=1, device_id={"tensor": mate}, device_id_type=MESH)

        @pl.when(inner)
        def _():
            pl.semaphore_signal(barrier, inc=1, device_id={"tensor": other}, device_id_type=MESH)
            pl.semaphore_wait(barrier, 2 + extra)

        @pl.when(end)
        def _():
            pl.semaphore_wait(barrier, 1 + extra)

    def begin():
        @pl.when(end)
        def _():
            @pl.loop(0, chunks)
            def _(chunk):
                stage(chunk)
                inward(chunk).start()

    def advance(step):
        @pl.when(inner & (step < chunks))
        def _():
            stage(step)
            inward(step).wait_recv()
            add(part_ref, from_end, pair_sum, step)
            across(step).start()

        @pl.when(inner & (step > 0) & (step <= chunks))
        def _():
            across(step - 1).wait_recv()
            add(pair_sum, from_pair, total_ref, step - 1)
            outward(step - 1).start()

    def finish():
        @pl.when(end)
        def _():
            @pl.loop(0, chunks)
            def _(chunk):
                inward(chunk).wait_send()
                outward(chunk).wait_recv()

        @pl.when(inner)
        def _():
            @pl.loop(0, chunks)
            def _(chunk):
                across(chunk).wait_send()
                outward(chunk).wait_send()

    return greet, begin, advance, finish


def plane_gather_steps(pieces, block_ref, whole_ref, semaphores, local_semaphore):
    spot = lax.axis_index("dp")
    depth = block_ref.shape[1]
    rows = block_ref.shape[0] // pieces
    core_mate = spot + 1 - 2 * (spot % 2)
    x_mate = spot + 2 - 4 * ((spot // 2) % 2)
    y_mate = spot + 4 - 8 * (spot // 4)
    x_y_mate = x_mate + 4 - 8 * (spot // 4)
    lanes = {
        "core": (spot, core_mate, 0, 1),
        "x": (spot, x_mate, 0, 1),
        "y": (spot, y_mate, 0, 1),
        "x_core": (x_mate, core_mate, 0, 1),
        "x_y": (x_mate, y_mate, 0, 2),
        "y_core": (y_mate, core_mate, 0, 1),
        "y_x": (y_mate, x_mate, 1, 2),
        "xy_core": (x_y_mate, core_mate, 0, 2),
        "yx_core": (x_y_mate, core_mate, 1, 2),
    }
    order = list(lanes)

    def send(name, piece):
        owner, device, part, parts = lanes[name]
        lane = order.index(name)
        span = pl.ds(
            pl.multiple_of(piece * rows + part * (rows // parts), rows // parts), rows // parts
        )
        columns = pl.ds(pl.multiple_of(owner * depth, depth), depth)
        target = whole_ref.at[span, columns]
        source = block_ref.at[span] if name in ("core", "x", "y") else target
        return pltpu.make_async_remote_copy(
            source,
            target,
            semaphores.at[2 * lane, piece],
            semaphores.at[2 * lane + 1, piece],
            device_id={"dp": device},
            device_id_type=MESH,
        )

    def own():
        columns = pl.ds(pl.multiple_of(spot * depth, depth), depth)
        return pltpu.make_async_copy(block_ref, whole_ref.at[:, columns], local_semaphore)

    def greet():
        barrier = pltpu.get_barrier_semaphore()
        for device in (core_mate, x_mate, y_mate):
            pl.semaphore_signal(barrier, inc=1, device_id={"dp": device}, device_id_type=MESH)

    def begin():
        own().start()

    def advance(step):
        @pl.when(step < pieces)
        def _():
            for name in ("x", "y", "core"):
                send(name, step).start()

        @pl.when((step >= AHEAD) & (step < pieces + AHEAD))
        def _():
            piece = step - AHEAD
            send("x", piece).wait_recv()
            send("x_y", piece).start()
            send("x_core", piece).start()
            send("y", piece).wait_recv()
            send("y_x", piece).start()
            send("y_core", piece).start()

        @pl.when((step >= 2 * AHEAD) & (step < pieces + 2 * AHEAD))
        def _():
            piece = step - 2 * AHEAD
            send("x_y", piece).wait_recv()
            send("xy_core", piece).start()
            send("y_x", piece).wait_recv()
            send("yx_core", piece).start()

    def finish():
        own().wait()

        @pl.loop(0, pieces)
        def _(piece):
            for name in order:
                send(name, piece).wait_send()
            for name in ("core", "x_core", "y_core", "xy_core", "yx_core"):
                send(name, piece).wait_recv()

    return greet, begin, advance, finish


def line_sum_kernel(chunks, *refs):
    greet, begin, advance, finish = line_sum_steps(chunks, *refs)
    greet(0)
    begin()

    @pl.loop(0, chunks + 1)
    def _(step):
        advance(step)

    finish()


def sum_gather_kernel(
    chunks, pieces, wide_ref, narrow_ref, block_ref, total_ref, whole_ref, *scratch
):
    greet, begin, advance, finish = line_sum_steps(
        chunks, wide_ref, narrow_ref, total_ref, *scratch[:5]
    )
    gather_semaphores, local_semaphore = scratch[5:]
    gather_greet, gather_begin, gather_advance, gather_finish = plane_gather_steps(
        pieces, block_ref, whole_ref, gather_semaphores, local_semaphore.at[0]
    )
    gather_greet()
    greet(3)
    begin()
    gather_begin()

    @pl.loop(0, max(chunks + 1, pieces + 2 * AHEAD))
    def _(step):
        gather_advance(step)
        advance(step)

    gather_finish()
    finish()


def attend_back_sum_kernel(chunks, wide_ref, *refs):
    inputs, (total_ref, grad_qkv_ref), scratch = refs[:8], refs[8:10], refs[10:]
    greet, begin, advance, finish = line_sum_steps(
        chunks, wide_ref, None, total_ref, *scratch[:5]
    )
    head_block = attend_back_steps(*inputs, grad_qkv_ref, *scratch[5:])
    length, heads_width = inputs[0].shape
    heads, blocks = heads_width // HEAD_SIZE, length // QUERY_ROWS
    greet(0)
    begin()

    @pl.loop(0, heads)
    def _(head):
        for block in range(blocks):
            advance(head * blocks + block)
            head_block(head, block * QUERY_ROWS)

    @pl.loop(heads * blocks, max(heads * blocks, chunks + 1))
    def _(step):
        advance(step)

    finish()


def on_line():
    return lax.axis_size("tensor") == 4


def in_plane():
    return lax.axis_size("dp") == 8


def in_vmem(count):
    return [pl.BlockSpec(memory_space=pltpu.VMEM)] * count


def sum_scratch(shape):
    return [pltpu.VMEM(shape, jnp.bfloat16)] * 4 + [pltpu.SemaphoreType.DMA((6, SUM_CHUNKS))]


def narrowed(narrow_part):
    pad = jnp.zeros((narrow_part.shape[0], NARROW - narrow_part.shape[1]), jnp.bfloat16)
    return jnp.concatenate([to_low(narrow_part), pad], axis=1)


def parts_of(total, wide_part, narrow_part):
    width, small = wide_part.shape[1], narrow_part.shape[1]
    total = total.astype(jnp.float32)
    return total[:, :width], total[:, width : width + small]


def summed(wide_part, narrow_part, number):
    if not on_line():
        return lax.psum((wide_part, narrow_part), "tensor")
    shape = (wide_part.shape[0], wide_part.shape[1] + NARROW)
    total = pl.pallas_call(
        functools.partial(line_sum_kernel, SUM_CHUNKS),
        out_shape=jax.ShapeDtypeStruct(shape, jnp.bfloat16),
        in_specs=in_vmem(2),
        out_specs=pl.BlockSpec(memory_space=pltpu.VMEM),
        scratch_shapes=sum_scratch(shape),
        compiler_params=pltpu.CompilerParams(
            collective_id=number, has_side_effects=True, vmem_limit_bytes=48 * 2**20
        ),
        cost_estimate=pl.CostEstimate(flops=0, bytes_accessed=300 * 2**20, transcendentals=0),
    )(wide_part, narrowed(narrow_part))
    return parts_of(total, wide_part, narrow_part)


def summed_and_gathered(wide_part, narrow_part, block, number):
    if not (on_line() and in_plane()):
        whole = lax.all_gather(block, "dp", axis=1, tiled=True)
        return summed(wide_part, narrow_part, number) + (whole,)
    shape = (wide_part.shape[0], wide_part.shape[1] + NARROW)
    pieces = GATHER_PIECES
    total, whole = pl.pallas_call(
        functools.partial(sum_gather_kernel, SUM_CHUNKS, pieces),
        out_shape=[
            jax.ShapeDtypeStruct(shape, jnp.bfloat16),
            jax.ShapeDtypeStruct((block.shape[0], 8 * block.shape[1]), jnp.bfloat16),
        ],
        in_specs=in_vmem(2) + [pl.BlockSpec(memory_space=pltpu.HBM)],
        out_specs=[pl.BlockSpec(memory_space=pltpu.VMEM), pl.BlockSpec(memory_space=pltpu.HBM)],
        scratch_shapes=sum_scratch(shape)
        + [pltpu.SemaphoreType.DMA((18, pieces)), pltpu.SemaphoreType.DMA((1,))],
        compiler_params=pltpu.CompilerParams(
            collective_id=number, has_side_effects=True, vmem_limit_bytes=48 * 2**20
        ),
        cost_estimate=pl.CostEstimate(flops=0, bytes_accessed=360 * 2**20, transcendentals=0),
    )(wide_part, narrowed(narrow_part), block)
    return parts_of(total, wide_part, narrow_part) + (whole,)


def block_mask(first, rows, extent, row_piece_ref, col_piece_ref):
    row_place = lax.broadcasted_iota(jnp.int32, (rows, extent), 0) + first
    col_place = lax.broadcasted_iota(jnp.int32, (rows, extent), 1)
    row_piece = row_piece_ref[first : first + rows, 0:1]
    together = (row_piece == col_piece_ref[0:1, :extent]) & (row_piece >= 0)
    return (col_place <= row_place) | together


def block_probs(query_rows, keys, allowed):
    scores = jnp.where(allowed, contract_last(query_rows, keys) * HEAD_SIZE**-0.5, MASKED)
    raised = jnp.exp(scores - jnp.max(scores, axis=1, keepdims=True))
    return raised * (1.0 / jnp.sum(raised, axis=1, keepdims=True))


def half_turn(values, signed_sine):
    return pltpu.roll(values, HEAD_SIZE // 2, 1) * signed_sine


def attend_kernel(
    qkv_ref,
    cosine_ref,
    sine_ref,
    row_piece_ref,
    col_piece_ref,
    query_ref,
    keys_ref,
    values_ref,
    attended_ref,
):
    length = qkv_ref.shape[1]

    @pl.loop(0, qkv_ref.shape[2] // HEAD_SIZE)
    def _(head):
        column = pl.ds(pl.multiple_of(head * HEAD_SIZE, HEAD_SIZE), HEAD_SIZE)
        for source, target in ((0, query_ref), (1, keys_ref)):
            raw = qkv_ref[source, :, column]
            target[:, column] = to_low(raw * cosine_ref[...] + half_turn(raw, sine_ref[...]))
        values_ref[:, column] = to_low(qkv_ref[2, :, column])
        for first in range(0, length, QUERY_ROWS):
            extent = min(length, first + QUERY_ROWS + PIECE)
            allowed = block_mask(first, QUERY_ROWS, extent, row_piece_ref, col_piece_ref)
            probs = block_probs(
                query_ref[first : first + QUERY_ROWS, column], keys_ref[:extent, column], allowed
            )
            attended_ref[first : first + QUERY_ROWS, column] = to_low(
                matmul(to_low(probs), values_ref[:extent, column])
            )


def attend(qkv, cosine, signed_sine, row_piece, col_piece):
    length, heads_width = qkv.shape[1:]
    shape = jax.ShapeDtypeStruct((length, heads_width), jnp.bfloat16)
    return pl.pallas_call(
        attend_kernel,
        out_shape=[shape] * 4,
        in_specs=[pl.BlockSpec(memory_space=pltpu.VMEM)] * 5,
        out_specs=[pl.BlockSpec(memory_space=pltpu.VMEM)] * 4,
        compiler_params=pltpu.CompilerParams(vmem_limit_bytes=48 * 2**20),
        cost_estimate=pl.CostEstimate(
            flops=4 * length * length * heads_width,
            bytes_accessed=16 * 2**20,
            transcendentals=length * length * heads_width // HEAD_SIZE,
        ),
    )(qkv, cosine, signed_sine, row_piece, col_piece)


def attend_back_steps(
    query_ref,
    keys_ref,
    values_ref,
    grad_ref,
    cosine_ref,
    sine_ref,
    row_piece_ref,
    col_piece_ref,
    grad_qkv_ref,
    grad_keys,
    grad_values,
):
    length = query_ref.shape[0]

    def turned_back(grad, first):
        span = slice(first, first + grad.shape[0])
        scaled = grad * HEAD_SIZE**-0.5
        return to_low(scaled * cosine_ref[span] - half_turn(scaled, sine_ref[span]))

    def head_block(head, first):
        column = pl.ds(pl.multiple_of(head * HEAD_SIZE, HEAD_SIZE), HEAD_SIZE)
        span = slice(first, first + QUERY_ROWS)
        extent = min(length, first + QUERY_ROWS + PIECE)
        if first == 0:
            grad_keys[...] = jnp.zeros_like(grad_keys)
            grad_values[...] = jnp.zeros_like(grad_values)
        allowed = block_mask(first, QUERY_ROWS, extent, row_piece_ref, col_piece_ref)
        query_rows = query_ref[span, column]
        keys = keys_ref[:extent, column]
        grad_rows = grad_ref[span, column]
        probs = block_probs(query_rows, keys, allowed)
        grad_probs = contract_last(grad_rows, values_ref[:extent, column])
        shift = jnp.sum(probs * grad_probs, axis=1, keepdims=True)
        grad_scores = to_low(probs * (grad_probs - shift))
        grad_values[:extent] += contract_first(to_low(probs), grad_rows)
        grad_keys[:extent] += contract_first(grad_scores, query_rows)
        grad_qkv_ref[0, span, column] = turned_back(matmul(grad_scores, keys), first)
        if first + QUERY_ROWS >= length:
            grad_qkv_ref[1, :, column] = turned_back(grad_keys[...], 0)
            grad_qkv_ref[2, :, column] = to_low(grad_values[...])

    return head_block


def attend_back_kernel(*refs):
    head_block = attend_back_steps(*refs)

    @pl.loop(0, refs[0].shape[1] // HEAD_SIZE)
    def _(head):
        for first in range(0, refs[0].shape[0], QUERY_ROWS):
            head_block(head, first)


def attend_back(query, keys, values, grads, cosine, signed_sine, row_piece, col_piece):
    length, heads_width = query.shape
    return pl.pallas_call(
        attend_back_kernel,
        out_shape=jax.ShapeDtypeStruct((3, length, heads_width), jnp.bfloat16),
        in_specs=[pl.BlockSpec(memory_space=pltpu.VMEM)] * 8,
        out_specs=pl.BlockSpec(memory_space=pltpu.VMEM),
        scratch_shapes=[pltpu.VMEM((length, HEAD_SIZE), jnp.float32)] * 2,
        compiler_params=pltpu.CompilerParams(vmem_limit_bytes=48 * 2**20),
        cost_estimate=pl.CostEstimate(
            flops=10 * length * length * heads_width,
            bytes_accessed=16 * 2**20,
            transcendentals=length * length * heads_width // HEAD_SIZE,
        ),
    )(query, keys, values, grads, cosine, signed_sine, row_piece, col_piece)


def summed_and_attended_back(wide_part, attention_inputs, number):
    if not on_line():
        return lax.psum(wide_part, "tensor"), attend_back(*attention_inputs)
    shape = wide_part.shape
    length, heads_width = attention_inputs[0].shape
    return pl.pallas_call(
        functools.partial(attend_back_sum_kernel, SUM_CHUNKS),
        out_shape=[
            jax.ShapeDtypeStruct(shape, jnp.bfloat16),
            jax.ShapeDtypeStruct((3, length, heads_width), jnp.bfloat16),
        ],
        in_specs=in_vmem(1 + len(attention_inputs)),
        out_specs=in_vmem(2),
        scratch_shapes=sum_scratch(shape) + [pltpu.VMEM((length, HEAD_SIZE), jnp.float32)] * 2,
        compiler_params=pltpu.CompilerParams(
            collective_id=number, has_side_effects=True, vmem_limit_bytes=58 * 2**20
        ),
        cost_estimate=pl.CostEstimate(flops=0, bytes_accessed=300 * 2**20, transcendentals=0),
    )(wide_part, *attention_inputs)


def experts_kernel(
    tile,
    inputs_ref,
    cotangent_ref,
    gate_ref,
    up_ref,
    down_ref,
    out_start,
    grad_start,
    out_ref,
    grad_ref,
    gate_grad_ref,
    act_rows,
    grad_rows,
    semaphores,
):
    @pl.when(pl.program_id(0) == 0)
    def _():
        loads = [
            pltpu.make_async_copy(out_start, out_ref, semaphores.at[0]),
            pltpu.make_async_copy(grad_start, grad_ref, semaphores.at[1]),
        ]
        for load in loads:
            load.start()
        for load in loads:
            load.wait()

    pair = gate_ref.shape[1]
    hidden = down_ref.shape[1] // pair

    @pl.loop(0, inputs_ref.shape[1] // tile)
    def _(index):
        column = pl.ds(pl.multiple_of(index * tile, tile), tile)
        inputs = inputs_ref[:, column]
        cotangents = cotangent_ref[:, column]
        for member in range(pair):
            gate_from, up_from = 2 * hidden * member, 2 * hidden * member + hidden
            gate_up = matmul(up_ref[0, gate_from : gate_from + 2 * hidden], inputs)
            open_part = matmul(down_ref[0, hidden * member : hidden * (member + 1)], cotangents)
            gate_half, up_half = gate_up[:hidden], gate_up[hidden:]
            squashed = 1.0 / (1.0 + jnp.exp(-gate_half))
            act = to_low(gate_half * squashed * up_half).astype(jnp.float32)
            gate_row = gate_ref[0, member : member + 1, column]
            gate_grad_ref[0, member : member + 1, column] = jnp.sum(
                act * open_part, axis=0, keepdims=True
            )
            act_rows[hidden * member : hidden * (member + 1)] = to_low(gate_row * act)
            grad_act = gate_row * open_part
            grad_rows[gate_from : gate_from + hidden] = to_low(
                grad_act * up_half * squashed * (1.0 + gate_half * (1.0 - squashed))
            )
            grad_rows[up_from : up_from + hidden] = to_low(grad_act * gate_half * squashed)
        out_ref[column] += contract_first(act_rows[...], down_ref[0])
        grad_ref[column] += contract_first(grad_rows[...], up_ref[0])


def experts_step(inputs, cotangents, gates, up_rows, down_rows, out_start, grad_start, first):
    groups, pair, length = up_rows.shape[0], gates.shape[1], inputs.shape[1]
    width, hidden = inputs.shape[0], down_rows.shape[1] // gates.shape[1]
    tile = min(512, length)
    once = pl.Buffered(1)

    def still(shape):
        return pl.BlockSpec(shape, lambda group: (0, 0), pipeline_mode=once)

    return pl.pallas_call(
        functools.partial(experts_kernel, tile),
        grid=(groups,),
        in_specs=[
            still((width, length)),
            still((width, length)),
            pl.BlockSpec((1, pair, length), lambda group: (group, 0, 0)),
            pl.BlockSpec((1, 2 * pair * hidden, width), lambda group: (group, 0, 0)),
            pl.BlockSpec((1, pair * hidden, width), lambda group: (group + first, 0, 0)),
            pl.BlockSpec(memory_space=pltpu.HBM),
            pl.BlockSpec(memory_space=pltpu.HBM),
        ],
        out_specs=[
            still((length, width)),
            still((length, width)),
            pl.BlockSpec((1, pair, length), lambda group: (group, 0, 0)),
        ],
        out_shape=[
            jax.ShapeDtypeStruct((length, width), jnp.float32),
            jax.ShapeDtypeStruct((length, width), jnp.float32),
            jax.ShapeDtypeStruct((groups, pair, length), jnp.float32),
        ],
        scratch_shapes=[
            pltpu.VMEM((pair * hidden, tile), jnp.bfloat16),
            pltpu.VMEM((2 * pair * hidden, tile), jnp.bfloat16),
            pltpu.SemaphoreType.DMA((2,)),
        ],
        compiler_params=pltpu.CompilerParams(
            vmem_limit_bytes=60 * 2**20, dimension_semantics=("arbitrary",)
        ),
        cost_estimate=pl.CostEstimate(
            flops=18 * groups * pair * hidden * width * length,
            bytes_accessed=64 * 2**20,
            transcendentals=0,
        ),
    )(inputs, cotangents, gates, up_rows, down_rows, out_start, grad_start)


def swiglu(paired):
    return jax.nn.silu(paired[..., 0, :]) * paired[..., 1, :]


def gathered(weight):
    return lax.all_gather(weight, "dp", axis=0, tiled=True)


def body(
    tokens,
    cotangent,
    attention_norm_gain,
    query_key_value_weight,
    query_key_value_bias,
    output_projection_weight,
    feedforward_norm_gain,
    router_matrix,
    shared_expert_gate_weight,
    routed_gate_up_weight,
    routed_down_weight,
    shared_expert_gate_up_weight,
    shared_expert_down_weight,
    routes,
    sequence_adapter_index,
    picture_piece_starts,
    adapter_query_key_value_lower,
    adapter_query_key_value_upper,
    adapter_output_lower,
    adapter_output_upper,
    adapter_shared_up_lower,
    adapter_shared_up_upper,
    adapter_shared_down_lower,
    adapter_shared_down_upper,
):
    length, width = tokens.shape
    set_id = sequence_adapter_index[0]
    starts = picture_piece_starts[0]

    def selected_experts(adapter_entry):
        return lax.dynamic_index_in_dim(adapter_entry, set_id, 0, keepdims=False)

    qkv_a, qkv_b, out_a, out_b = (
        selected_experts(adapter_query_key_value_lower),
        selected_experts(adapter_query_key_value_upper),
        selected_experts(adapter_output_lower),
        selected_experts(adapter_output_upper),
    )
    up_a, up_b, down_a, down_b = (
        selected_experts(adapter_shared_up_lower),
        selected_experts(adapter_shared_up_upper),
        selected_experts(adapter_shared_down_lower),
        selected_experts(adapter_shared_down_upper),
    )
    gain_attn_f = attention_norm_gain.astype(jnp.float32)
    gain_ffn_f = feedforward_norm_gain.astype(jnp.float32)
    tokens_f = tokens.astype(jnp.float32)
    normed = to_low(rms_scale(tokens_f, gain_attn_f))
    mid_qkv = to_low(matmul(normed, qkv_a))
    attention_rows = gathered(
        jnp.concatenate([query_key_value_weight, output_projection_weight[:, None]], axis=1)
    )
    qkv_rows, output_rows = attention_rows[:, :3], attention_rows[:, 3]
    qkv_sum = jnp.einsum("tr,rsf->stf", normed, qkv_rows, preferred_element_type=jnp.float32)
    qkv_sum = qkv_sum + query_key_value_bias.astype(jnp.float32)[:, None, :]
    qkv_sum = qkv_sum + ADAPTER_SCALE * jnp.einsum(
        "tr,rsf->stf", mid_qkv, qkv_b, preferred_element_type=jnp.float32
    )
    cosine, sine_table = rope_tables(length)
    signs = jnp.where(jnp.arange(HEAD_SIZE) < HEAD_SIZE // 2, -1.0, 1.0)
    piece_ids = piece_index(jnp.arange(length, dtype=jnp.int32), starts)
    places = (cosine, sine_table * signs[None, :], piece_ids[:, None], piece_ids[None, :])
    query, keys, values, attended = attend(qkv_sum, *places)
    branch_part = contract_last(attended, output_rows)
    down_block = jnp.transpose(routed_down_weight, (1, 2, 0))
    early = EXPERT_PARTS[0]
    branch_here, mid_out_here_f, down_early = summed_and_gathered(
        branch_part,
        matmul(attended, out_a),
        down_block[:early].reshape(-1, down_block.shape[2]),
        1,
    )
    down_late = lax.all_gather(down_block[early:], "dp", axis=2, tiled=True)
    mid_out_here = to_low(mid_out_here_f)
    hidden_here = tokens_f + branch_here + ADAPTER_SCALE * matmul(mid_out_here, out_b)
    normed_two_here_f, norm_ffn_pull = jax.vjp(
        lambda rows: rms_scale(rows, gain_ffn_f), hidden_here
    )
    normed_two_here = to_low(normed_two_here_f)
    normed_two, mid_out = (normed_two_here, mid_out_here)
    cot_f = cotangent.astype(jnp.float32)
    shared_three = gathered(
        jnp.concatenate([shared_expert_gate_up_weight, shared_expert_down_weight[:, None]], axis=1)
    )
    shared_rows, sdown_rows = shared_three[:, :2], shared_three[:, 2]
    small_rows = gathered(
        jnp.concatenate(
            [
                router_matrix,
                shared_expert_gate_weight[:, None],
                jnp.full_like(shared_expert_gate_weight, set_id)[:, None],
            ],
            axis=1,
        )
    )
    router_full, gate_full = small_rows[:, :EXPERTS], small_rows[:, EXPERTS]
    router_probs = jax.nn.softmax(matmul(normed_two, router_full), axis=-1)
    shared_gate = jax.nn.sigmoid(matmul(normed_two, gate_full))
    expert_ids = jnp.arange(EXPERTS, dtype=jnp.int32)
    chosen = jnp.sum(
        (routes[:, :, None] == expert_ids[None, None, :]).astype(jnp.float32), axis=1
    )
    gate_table = (router_probs * chosen).T

    mid_up = to_low(matmul(normed_two, up_a))
    shared_gu = jnp.einsum(
        "tr,rxf->txf", normed_two, shared_rows, preferred_element_type=jnp.float32
    ) + ADAPTER_SCALE * jnp.einsum("tr,rxf->txf", mid_up, up_b, preferred_element_type=jnp.float32)
    shared_act_f, shared_pull = jax.vjp(swiglu, shared_gu)
    shared_act = to_low(shared_act_f)
    shared_cols = contract_last(shared_act, sdown_rows)
    shared_gate_part = jnp.sum(cot_f * shared_cols, axis=1)
    grad_shared = to_low(shared_gate[:, None] * cot_f)
    cotangent_down = ADAPTER_SCALE * contract_last(cotangent, down_b)
    grad_mid_down = to_low(ADAPTER_SCALE * contract_last(grad_shared, down_b))
    grad_shared_act = matmul(grad_shared, sdown_rows) + contract_last(grad_mid_down, down_a)
    grad_shared_gu = to_low(shared_pull(grad_shared_act)[0])
    grad_mid_up_part = ADAPTER_SCALE * jnp.einsum(
        "txf,rxf->tr", grad_shared_gu, up_b, preferred_element_type=jnp.float32
    )
    grad_up_b_local = ADAPTER_SCALE * jnp.einsum(
        "tr,txf->rxf", mid_up, grad_shared_gu, preferred_element_type=jnp.float32
    )
    grad_down_a_local = contract_first(grad_mid_down, shared_act)
    combined_part = shared_gate[:, None] * shared_cols
    normed_two_part = jnp.einsum(
        "txf,rxf->tr", grad_shared_gu, shared_rows, preferred_element_type=jnp.float32
    )

    up_block = jnp.transpose(routed_gate_up_weight, (1, 2, 3, 0))
    inputs_t, cotangents_t = normed_two.T, cotangent.T
    gates = gate_table.reshape(EXPERTS // PAIR, PAIR, length)
    down_early = down_early.reshape(early // PAIR, -1, width)
    down_late = down_late.reshape((EXPERTS - early) // PAIR, -1, width)
    gate_grad_parts = []
    first = 0
    for count in EXPERT_PARTS:
        up_rows = lax.all_gather(up_block[first : first + count], "dp", axis=3, tiled=True)
        combined_part, normed_two_part, gate_grads = experts_step(
            inputs_t,
            cotangents_t,
            gates[first // PAIR : (first + count) // PAIR],
            up_rows.reshape(count // PAIR, -1, width),
            down_early if first < early else down_late,
            combined_part,
            normed_two_part,
            (first if first < early else first - early) // PAIR,
        )
        gate_grad_parts.append(gate_grads.reshape(count, length))
        first += count
    gate_grad_part = jnp.concatenate(gate_grad_parts, axis=0).T
    narrow_part = jnp.concatenate(
        [
            gate_grad_part,
            shared_gate_part[:, None],
            grad_mid_up_part,
            matmul(shared_act, down_a),
        ],
        axis=1,
    )
    grad_normed_two, narrow_sum = summed(normed_two_part, narrow_part, 2)
    rank = up_a.shape[1]
    mid_down = to_low(narrow_sum[:, EXPERTS + 1 + rank :])
    grad_mid_up = to_low(narrow_sum[:, EXPERTS + 1 : EXPERTS + 1 + rank])
    grad_probs = chosen * narrow_sum[:, :EXPERTS]
    grad_logits = to_low(
        router_probs * (grad_probs - jnp.sum(router_probs * grad_probs, axis=1, keepdims=True))
    )
    shared_gate_grad = narrow_sum[:, EXPERTS] + jnp.sum(
        mid_down.astype(jnp.float32) * cotangent_down, axis=1
    )
    grad_gate_logit = to_low(shared_gate_grad * shared_gate * (1.0 - shared_gate))
    grad_normed_two = grad_normed_two + contract_last(
        jnp.concatenate([grad_logits, grad_gate_logit[:, None], grad_mid_up], axis=1),
        jnp.concatenate([router_full, gate_full[:, None], up_a], axis=1),
    )
    grad_hidden = cot_f + norm_ffn_pull(grad_normed_two)[0]
    grad_branch = to_low(grad_hidden)
    grad_mid_out = to_low(ADAPTER_SCALE * contract_last(grad_branch, out_b))
    grad_attended = to_low(
        matmul(grad_branch, output_rows) + contract_last(grad_mid_out, out_a)
    )
    combined_here, grad_qkv = summed_and_attended_back(
        combined_part, (query, keys, values, grad_attended) + places, 3
    )
    extra_here = ADAPTER_SCALE * matmul(mid_down, down_b)
    output = to_low(hidden_here + combined_here + shared_gate[:, None] * extra_here)
    grad_down_b_local = ADAPTER_SCALE * contract_first(mid_down, grad_shared)
    grad_up_a_local = contract_first(grad_mid_up, normed_two)
    grad_out_b_local = ADAPTER_SCALE * contract_first(mid_out, grad_branch)
    grad_out_a_local = contract_first(grad_mid_out, attended)
    grad_mid_qkv_part = ADAPTER_SCALE * jnp.einsum(
        "stf,rsf->tr", grad_qkv, qkv_b, preferred_element_type=jnp.float32
    )
    grad_qkv_b_local = ADAPTER_SCALE * jnp.einsum(
        "tr,stf->rsf", mid_qkv, grad_qkv, preferred_element_type=jnp.float32
    )
    normed_part = jnp.einsum(
        "stf,rsf->tr",
        grad_qkv,
        qkv_rows,
        preferred_element_type=jnp.float32,
    )
    grad_normed, grad_mid_qkv_f = summed(normed_part, grad_mid_qkv_part, 4)
    grad_mid_qkv_here = to_low(grad_mid_qkv_f)
    grad_normed = grad_normed + contract_last(grad_mid_qkv_here, qkv_a)
    norm_attn_pull = jax.vjp(lambda rows: rms_scale(rows, gain_attn_f), tokens_f)[1]
    grad_tokens_here = to_low(grad_hidden + norm_attn_pull(grad_normed)[0])
    grad_tokens, grad_mid_qkv = (grad_tokens_here, grad_mid_qkv_here)
    grad_qkv_a_local = contract_first(grad_mid_qkv, normed)
    everyone = small_rows[:: small_rows.shape[0] // lax.axis_size("dp"), EXPERTS + 1]
    marker = to_low(
        jnp.arange(ADAPTER_SETS, dtype=jnp.int32)[:, None] == everyone.astype(jnp.int32)[None, :]
    )

    def adapter_sums(local_grads):
        sizes = [local_grad.shape[1] for local_grad in local_grads]
        flat = jnp.concatenate([to_low(local_grad) for local_grad in local_grads], axis=1)
        rows = lax.all_gather(flat, "dp", axis=0, tiled=False)
        totals = jnp.einsum("cj,jrn->crn", marker, rows, preferred_element_type=jnp.float32)
        results, start = [], 0
        for size in sizes:
            results.append(totals[:, :, start : start + size])
            start += size
        return results

    def flipped(total):
        return jnp.swapaxes(total, 1, 2)

    def opened(total, count):
        return total.reshape(total.shape[0], total.shape[1], count, -1)

    total_out_a, total_out_b, total_up_a, total_up_b, total_down_a, total_down_b = adapter_sums(
        [
            grad_out_a_local,
            grad_out_b_local,
            grad_up_a_local,
            grad_up_b_local.reshape(grad_up_b_local.shape[0], -1),
            grad_down_a_local,
            grad_down_b_local,
        ]
    )
    total_qkv_b, total_qkv_a = adapter_sums(
        [grad_qkv_b_local.reshape(grad_qkv_b_local.shape[0], -1), grad_qkv_a_local]
    )
    return (
        output,
        grad_tokens,
        flipped(total_qkv_a),
        opened(total_qkv_b, 3),
        flipped(total_out_a),
        total_out_b,
        flipped(total_up_a),
        opened(total_up_b, 2),
        flipped(total_down_a),
        total_down_b,
    )


def solution(mesh):
    return jax.shard_map(
        body,
        mesh=mesh,
        in_specs=(
            P("dp", None),
            P("dp", None),
            P(),
            P("dp", None, "tensor"),
            P(None, "tensor"),
            P("dp", "tensor"),
            P(),
            P("dp", None),
            P("dp"),
            P("dp", None, None, "tensor"),
            P("dp", None, "tensor"),
            P("dp", None, "tensor"),
            P("dp", "tensor"),
            P("dp", None),
            P("dp"),
            P("dp", None),
            P(),
            P(None, None, None, "tensor"),
            P(None, "tensor", None),
            P(),
            P(),
            P(None, None, None, "tensor"),
            P(None, "tensor", None),
            P(),
        ),
        out_specs=(
            P("dp", None),
            P("dp", None),
            P(),
            P(None, None, None, "tensor"),
            P(None, "tensor", None),
            P(),
            P(),
            P(None, None, None, "tensor"),
            P(None, "tensor", None),
            P(),
        ),
        check_vma=False,
    )
```

```python
import functools

import jax
import jax.numpy as jnp
from jax import lax
from jax.experimental import pallas as pl
from jax.experimental.pallas import tpu as pltpu
from jax.sharding import PartitionSpec as P

HEAD_SIZE = 128
TOP = 4
EXPERTS = 16
ADAPTER_SETS = 8
PIECE = 256


EPSILON = 1e-06
THETA = 1000000.0
ADAPTER_SCALE = 2.0
MASKED = -1e30
QUERY_ROWS = 256
NARROW = 128
MESH = pl.DeviceIdType.MESH
SUM_CHUNKS = 16
AHEAD = 2
EXPERT_PARTS = (8, 4, 4)


def matmul(left_side, right_side):
    return jnp.dot(left_side, right_side, preferred_element_type=jnp.float32)


def contract_last(left_side, right_side):
    return lax.dot_general(
        left_side, right_side, (((1,), (1,)), ((), ())), preferred_element_type=jnp.float32
    )


def contract_first(left_side, right_side):
    return lax.dot_general(
        left_side, right_side, (((0,), (0,)), ((), ())), preferred_element_type=jnp.float32
    )


def to_low(values):
    return values.astype(jnp.bfloat16)


def rms_scale(values, gain_values):
    return (
        values * lax.rsqrt(jnp.mean(values * values, axis=1, keepdims=True) + EPSILON) * gain_values
    )


def rope_tables(length):
    half_size = HEAD_SIZE // 2
    frequency = THETA ** (-jnp.arange(half_size, dtype=jnp.float32) * 2.0 / HEAD_SIZE)
    angles = jnp.arange(length, dtype=jnp.float32)[:, None] * frequency[None, :]
    return (
        jnp.concatenate([jnp.cos(angles)] * 2, axis=1),
        jnp.concatenate([jnp.sin(angles)] * 2, axis=1),
    )


def piece_index(positions, starts):
    inside = (positions[:, None] >= starts[None, :]) & (
        positions[:, None] < starts[None, :] + PIECE
    )
    labels = jnp.arange(starts.shape[0], dtype=jnp.int32)[None, :] + 1
    return jnp.sum(jnp.where(inside, labels, 0), axis=1) - 1


def line_sum_steps(
    chunks, wide_ref, narrow_ref, total_ref, part_ref, from_end, pair_sum, from_pair, semaphores
):
    place = lax.axis_index("tensor")
    width = wide_ref.shape[1]
    rows = part_ref.shape[0] // chunks
    inner = (place == 1) | (place == 2)
    end = (place == 0) | (place == 3)
    mate = jnp.where(place < 2, 1 - place, 5 - place)
    other = jnp.where(inner, 3 - place, place)

    def span(chunk):
        return pl.ds(pl.multiple_of(chunk * rows, rows), rows)

    def copy(source, target, chunk, lane, device):
        return pltpu.make_async_remote_copy(
            source.at[span(chunk)],
            target.at[span(chunk)],
            semaphores.at[2 * lane, chunk],
            semaphores.at[2 * lane + 1, chunk],
            device_id={"tensor": device},
            device_id_type=MESH,
        )

    def inward(chunk):
        return copy(part_ref, from_end, chunk, 0, mate)

    def across(chunk):
        return copy(pair_sum, from_pair, chunk, 1, other)

    def outward(chunk):
        return copy(total_ref, total_ref, chunk, 2, mate)

    def add(left_ref, right_ref, out_ref, chunk):
        out_ref[span(chunk)] = to_low(
            left_ref[span(chunk)].astype(jnp.float32) + right_ref[span(chunk)].astype(jnp.float32)
        )

    def stage(chunk):
        part_ref[span(chunk), :width] = to_low(wide_ref[span(chunk)])
        if narrow_ref is not None:
            part_ref[span(chunk), width:] = narrow_ref[span(chunk)]

    def greet(extra):
        barrier = pltpu.get_barrier_semaphore()
        pl.semaphore_signal(barrier, inc=1, device_id={"tensor": mate}, device_id_type=MESH)

        @pl.when(inner)
        def _():
            pl.semaphore_signal(barrier, inc=1, device_id={"tensor": other}, device_id_type=MESH)
            pl.semaphore_wait(barrier, 2 + extra)

        @pl.when(end)
        def _():
            pl.semaphore_wait(barrier, 1 + extra)

    def begin():
        @pl.when(end)
        def _():
            @pl.loop(0, chunks)
            def _(chunk):
                stage(chunk)
                inward(chunk).start()

    def advance(step):
        @pl.when(inner & (step < chunks))
        def _():
            stage(step)
            inward(step).wait_recv()
            add(part_ref, from_end, pair_sum, step)
            across(step).start()

        @pl.when(inner & (step > 0) & (step <= chunks))
        def _():
            across(step - 1).wait_recv()
            add(pair_sum, from_pair, total_ref, step - 1)
            outward(step - 1).start()

    def finish():
        @pl.when(end)
        def _():
            @pl.loop(0, chunks)
            def _(chunk):
                inward(chunk).wait_send()
                outward(chunk).wait_recv()

        @pl.when(inner)
        def _():
            @pl.loop(0, chunks)
            def _(chunk):
                across(chunk).wait_send()
                outward(chunk).wait_send()

    return greet, begin, advance, finish


def plane_gather_steps(pieces, block_ref, whole_ref, semaphores, local_semaphore):
    spot = lax.axis_index("dp")
    depth = block_ref.shape[1]
    rows = block_ref.shape[0] // pieces
    core_mate = spot + 1 - 2 * (spot % 2)
    x_mate = spot + 2 - 4 * ((spot // 2) % 2)
    y_mate = spot + 4 - 8 * (spot // 4)
    x_y_mate = x_mate + 4 - 8 * (spot // 4)
    lanes = {
        "core": (spot, core_mate, 0, 1),
        "x": (spot, x_mate, 0, 1),
        "y": (spot, y_mate, 0, 1),
        "x_core": (x_mate, core_mate, 0, 1),
        "x_y": (x_mate, y_mate, 0, 2),
        "y_core": (y_mate, core_mate, 0, 1),
        "y_x": (y_mate, x_mate, 1, 2),
        "xy_core": (x_y_mate, core_mate, 0, 2),
        "yx_core": (x_y_mate, core_mate, 1, 2),
    }
    order = list(lanes)

    def send(name, piece):
        owner, device, part, parts = lanes[name]
        lane = order.index(name)
        span = pl.ds(
            pl.multiple_of(piece * rows + part * (rows // parts), rows // parts), rows // parts
        )
        columns = pl.ds(pl.multiple_of(owner * depth, depth), depth)
        target = whole_ref.at[span, columns]
        source = block_ref.at[span] if name in ("core", "x", "y") else target
        return pltpu.make_async_remote_copy(
            source,
            target,
            semaphores.at[2 * lane, piece],
            semaphores.at[2 * lane + 1, piece],
            device_id={"dp": device},
            device_id_type=MESH,
        )

    def own():
        columns = pl.ds(pl.multiple_of(spot * depth, depth), depth)
        return pltpu.make_async_copy(block_ref, whole_ref.at[:, columns], local_semaphore)

    def greet():
        barrier = pltpu.get_barrier_semaphore()
        for device in (core_mate, x_mate, y_mate):
            pl.semaphore_signal(barrier, inc=1, device_id={"dp": device}, device_id_type=MESH)

    def begin():
        own().start()

    def advance(step):
        @pl.when(step < pieces)
        def _():
            for name in ("x", "y", "core"):
                send(name, step).start()

        @pl.when((step >= AHEAD) & (step < pieces + AHEAD))
        def _():
            piece = step - AHEAD
            send("x", piece).wait_recv()
            send("x_y", piece).start()
            send("x_core", piece).start()
            send("y", piece).wait_recv()
            send("y_x", piece).start()
            send("y_core", piece).start()

        @pl.when((step >= 2 * AHEAD) & (step < pieces + 2 * AHEAD))
        def _():
            piece = step - 2 * AHEAD
            send("x_y", piece).wait_recv()
            send("xy_core", piece).start()
            send("y_x", piece).wait_recv()
            send("yx_core", piece).start()

    def arrive(piece):
        @pl.when(piece == 0)
        def _():
            own().wait()

        for name in ("core", "x_core", "y_core", "xy_core", "yx_core"):
            send(name, piece).wait_recv()

    def finish():
        @pl.loop(0, pieces)
        def _(piece):
            for name in order:
                send(name, piece).wait_send()

    return greet, begin, advance, arrive, finish


def line_sum_kernel(chunks, *refs):
    greet, begin, advance, finish = line_sum_steps(chunks, *refs)
    greet(0)
    begin()

    @pl.loop(0, chunks + 1)
    def _(step):
        advance(step)

    finish()


def sum_gather_kernel(
    chunks,
    pieces,
    wide_ref,
    narrow_ref,
    block_ref,
    cotangent_ref,
    total_ref,
    whole_ref,
    open_ref,
    *scratch,
):
    greet, begin, advance, finish = line_sum_steps(
        chunks, wide_ref, narrow_ref, total_ref, *scratch[:5]
    )
    gather_semaphores, local_semaphores, piece_rows, open_rows = scratch[5:]
    gather_greet, gather_begin, gather_advance, gather_arrive, gather_finish = plane_gather_steps(
        pieces, block_ref, whole_ref, gather_semaphores, local_semaphores.at[0]
    )
    rows = piece_rows.shape[1]

    def load(piece):
        slot = piece % 2
        span = pl.ds(pl.multiple_of(piece * rows, rows), rows)
        return pltpu.make_async_copy(
            whole_ref.at[span], piece_rows.at[slot], local_semaphores.at[1 + slot]
        )

    def store(piece):
        slot = piece % 2
        span = pl.ds(pl.multiple_of(piece * rows, rows), rows)
        return pltpu.make_async_copy(
            open_rows.at[slot], open_ref.at[span], local_semaphores.at[3 + slot]
        )

    gather_greet()
    greet(3)
    begin()
    gather_begin()

    @pl.loop(0, max(chunks + 1, pieces + 3 * AHEAD + 1))
    def _(step):
        gather_advance(step)
        advance(step)

        @pl.when((step >= 3 * AHEAD) & (step < pieces + 3 * AHEAD))
        def _():
            gather_arrive(step - 3 * AHEAD)
            load(step - 3 * AHEAD).start()

        @pl.when((step > 3 * AHEAD) & (step <= pieces + 3 * AHEAD))
        def _():
            piece = step - 3 * AHEAD - 1
            load(piece).wait()

            @pl.when(piece >= 2)
            def _():
                store(piece - 2).wait()

            open_rows[piece % 2] = to_low(matmul(piece_rows[piece % 2], cotangent_ref[...]))
            store(piece).start()

    store(pieces - 2).wait()
    store(pieces - 1).wait()
    gather_finish()
    finish()


def sum_down_kernel(
    chunks,
    wide_ref,
    narrow_ref,
    start_ref,
    down_ref,
    *refs,
):
    act_refs, (total_ref, out_ref), scratch = refs[:-11], refs[-11:-9], refs[-9:]
    greet, begin, advance, finish = line_sum_steps(
        chunks, wide_ref, narrow_ref, total_ref, *scratch[:5]
    )
    semaphores, act_rows, down_rows, out_rows = scratch[5:]
    rows = act_rows.shape[1]
    blocks = down_ref.shape[0] // rows

    def load_down(block):
        slot = block % 2
        span = pl.ds(pl.multiple_of(block * rows, rows), rows)
        return pltpu.make_async_copy(
            down_ref.at[span], down_rows.at[slot], semaphores.at[1, slot]
        )

    def load_act(act_ref, block, slot):
        span = pl.ds(pl.multiple_of(block * rows, rows), rows)
        return pltpu.make_async_copy(act_ref.at[span], act_rows.at[slot], semaphores.at[0, slot])

    def load_start(block):
        load_down(block).start()
        first = 0
        for act_ref in act_refs:
            count = act_ref.shape[0] // rows
            from_here = block - first

            @pl.when((from_here >= 0) & (from_here < count))
            def _():
                load_act(act_ref, from_here, block % 2).start()

            first += count

    def load_wait(block):
        load_down(block).wait()
        load_act(act_refs[0], 0, block % 2).wait()

    first = pltpu.make_async_copy(start_ref, out_rows, semaphores.at[2, 0])
    first.start()
    load_start(0)
    greet(0)
    begin()
    first.wait()

    @pl.loop(0, max(blocks, chunks + 1))
    def _(step):
        advance(step)

        @pl.when(step < blocks)
        def _():
            @pl.when(step + 1 < blocks)
            def _():
                load_start(step + 1)

            load_wait(step)
            tile = min(256, out_rows.shape[0])

            @pl.loop(0, out_rows.shape[0] // tile)
            def _(index):
                span = pl.ds(pl.multiple_of(index * tile, tile), tile)
                out_rows[span] += contract_first(
                    act_rows[step % 2, :, span], down_rows[step % 2]
                )

    out_ref[...] = to_low(out_rows[...])
    finish()


def attend_back_sum_kernel(chunks, wide_ref, *refs):
    inputs, (total_ref, grad_qkv_ref), scratch = refs[:8], refs[8:10], refs[10:]
    greet, begin, advance, finish = line_sum_steps(
        chunks, wide_ref, None, total_ref, *scratch[:5]
    )
    head_block = attend_back_steps(*inputs, grad_qkv_ref, *scratch[5:])
    length, heads_width = inputs[0].shape
    heads, blocks = heads_width // HEAD_SIZE, length // QUERY_ROWS
    greet(0)
    begin()

    @pl.loop(0, heads)
    def _(head):
        for block in range(blocks):
            advance(head * blocks + block)
            head_block(head, block * QUERY_ROWS)

    @pl.loop(heads * blocks, max(heads * blocks, chunks + 1))
    def _(step):
        advance(step)

    finish()


def on_line():
    return lax.axis_size("tensor") == 4


def in_plane():
    return lax.axis_size("dp") == 8


def in_vmem(count):
    return [pl.BlockSpec(memory_space=pltpu.VMEM)] * count


def sum_scratch(shape):
    return [pltpu.VMEM(shape, jnp.bfloat16)] * 4 + [pltpu.SemaphoreType.DMA((6, SUM_CHUNKS))]


def narrowed(narrow_part):
    pad = jnp.zeros((narrow_part.shape[0], NARROW - narrow_part.shape[1]), jnp.bfloat16)
    return jnp.concatenate([to_low(narrow_part), pad], axis=1)


def parts_of(total, wide_part, narrow_part):
    width, small = wide_part.shape[1], narrow_part.shape[1]
    total = total.astype(jnp.float32)
    return total[:, :width], total[:, width : width + small]


def summed(wide_part, narrow_part, number):
    if not on_line():
        return lax.psum((wide_part, narrow_part), "tensor")
    shape = (wide_part.shape[0], wide_part.shape[1] + NARROW)
    total = pl.pallas_call(
        functools.partial(line_sum_kernel, SUM_CHUNKS),
        out_shape=jax.ShapeDtypeStruct(shape, jnp.bfloat16),
        in_specs=in_vmem(2),
        out_specs=pl.BlockSpec(memory_space=pltpu.VMEM),
        scratch_shapes=sum_scratch(shape),
        compiler_params=pltpu.CompilerParams(
            collective_id=number, has_side_effects=True, vmem_limit_bytes=48 * 2**20
        ),
        cost_estimate=pl.CostEstimate(flops=0, bytes_accessed=300 * 2**20, transcendentals=0),
    )(wide_part, narrowed(narrow_part))
    return parts_of(total, wide_part, narrow_part)


def summed_and_gathered(wide_part, narrow_part, block, cotangents, number):
    length, width = wide_part.shape
    if not (on_line() and in_plane()):
        whole = lax.all_gather(block, "dp", axis=1, tiled=True)
        open_rows = to_low(matmul(whole, cotangents))
        return summed(wide_part, narrow_part, number) + (whole, open_rows)
    shape = (length, width + NARROW)
    pieces = EXPERTS
    rows = block.shape[0] // pieces
    in_hbm = pl.BlockSpec(memory_space=pltpu.HBM)
    total, whole, open_rows = pl.pallas_call(
        functools.partial(sum_gather_kernel, SUM_CHUNKS, pieces),
        out_shape=[
            jax.ShapeDtypeStruct(shape, jnp.bfloat16),
            jax.ShapeDtypeStruct((block.shape[0], width), jnp.bfloat16),
            jax.ShapeDtypeStruct((block.shape[0], length), jnp.bfloat16),
        ],
        in_specs=in_vmem(2) + [in_hbm] + in_vmem(1),
        out_specs=in_vmem(1) + [in_hbm] * 2,
        scratch_shapes=sum_scratch(shape)
        + [
            pltpu.SemaphoreType.DMA((18, pieces)),
            pltpu.SemaphoreType.DMA((5,)),
            pltpu.VMEM((2, rows, width), jnp.bfloat16),
            pltpu.VMEM((2, rows, length), jnp.bfloat16),
        ],
        compiler_params=pltpu.CompilerParams(
            collective_id=number, has_side_effects=True, vmem_limit_bytes=58 * 2**20
        ),
        cost_estimate=pl.CostEstimate(flops=0, bytes_accessed=360 * 2**20, transcendentals=0),
    )(wide_part, narrowed(narrow_part), block, cotangents)
    return parts_of(total, wide_part, narrow_part) + (whole, open_rows)


def summed_and_down(wide_part, narrow_part, start, act_parts, down_rows, number):
    length, width = wide_part.shape
    if not on_line():
        out = start + contract_first(jnp.concatenate(act_parts, axis=0), down_rows)
        return summed(wide_part, narrow_part, number) + (out,)
    shape = (length, width + NARROW)
    rows = 2 * down_rows.shape[0] // EXPERTS
    in_hbm = pl.BlockSpec(memory_space=pltpu.HBM)
    total, out = pl.pallas_call(
        functools.partial(sum_down_kernel, SUM_CHUNKS),
        out_shape=[
            jax.ShapeDtypeStruct(shape, jnp.bfloat16),
            jax.ShapeDtypeStruct((length, width), jnp.bfloat16),
        ],
        in_specs=in_vmem(2) + [in_hbm] * (2 + len(act_parts)),
        out_specs=in_vmem(2),
        scratch_shapes=sum_scratch(shape)
        + [
            pltpu.SemaphoreType.DMA((3, 2)),
            pltpu.VMEM((2, rows, length), jnp.bfloat16),
            pltpu.VMEM((2, rows, width), jnp.bfloat16),
            pltpu.VMEM((length, width), jnp.float32),
        ],
        compiler_params=pltpu.CompilerParams(
            collective_id=number, has_side_effects=True, vmem_limit_bytes=58 * 2**20
        ),
        cost_estimate=pl.CostEstimate(flops=0, bytes_accessed=300 * 2**20, transcendentals=0),
    )(wide_part, narrowed(narrow_part), start, down_rows, *act_parts)
    return parts_of(total, wide_part, narrow_part) + (out,)


def block_mask(first, rows, extent, row_piece_ref, col_piece_ref):
    row_place = lax.broadcasted_iota(jnp.int32, (rows, extent), 0) + first
    col_place = lax.broadcasted_iota(jnp.int32, (rows, extent), 1)
    row_piece = row_piece_ref[first : first + rows, 0:1]
    together = (row_piece == col_piece_ref[0:1, :extent]) & (row_piece >= 0)
    return (col_place <= row_place) | together


def block_probs(query_rows, keys, allowed):
    scores = jnp.where(allowed, contract_last(query_rows, keys) * HEAD_SIZE**-0.5, MASKED)
    raised = jnp.exp(scores - jnp.max(scores, axis=1, keepdims=True))
    return raised * (1.0 / jnp.sum(raised, axis=1, keepdims=True))


def half_turn(values, signed_sine):
    return pltpu.roll(values, HEAD_SIZE // 2, 1) * signed_sine


def attend_kernel(
    qkv_ref,
    cosine_ref,
    sine_ref,
    row_piece_ref,
    col_piece_ref,
    query_ref,
    keys_ref,
    values_ref,
    attended_ref,
):
    length = qkv_ref.shape[1]

    @pl.loop(0, qkv_ref.shape[2] // HEAD_SIZE)
    def _(head):
        column = pl.ds(pl.multiple_of(head * HEAD_SIZE, HEAD_SIZE), HEAD_SIZE)
        for source, target in ((0, query_ref), (1, keys_ref)):
            raw = qkv_ref[source, :, column]
            target[:, column] = to_low(raw * cosine_ref[...] + half_turn(raw, sine_ref[...]))
        values_ref[:, column] = to_low(qkv_ref[2, :, column])
        for first in range(0, length, QUERY_ROWS):
            extent = min(length, first + QUERY_ROWS + PIECE)
            allowed = block_mask(first, QUERY_ROWS, extent, row_piece_ref, col_piece_ref)
            probs = block_probs(
                query_ref[first : first + QUERY_ROWS, column], keys_ref[:extent, column], allowed
            )
            attended_ref[first : first + QUERY_ROWS, column] = to_low(
                matmul(to_low(probs), values_ref[:extent, column])
            )


def attend(qkv, cosine, signed_sine, row_piece, col_piece):
    length, heads_width = qkv.shape[1:]
    shape = jax.ShapeDtypeStruct((length, heads_width), jnp.bfloat16)
    return pl.pallas_call(
        attend_kernel,
        out_shape=[shape] * 4,
        in_specs=[pl.BlockSpec(memory_space=pltpu.VMEM)] * 5,
        out_specs=[pl.BlockSpec(memory_space=pltpu.VMEM)] * 4,
        compiler_params=pltpu.CompilerParams(vmem_limit_bytes=48 * 2**20),
        cost_estimate=pl.CostEstimate(
            flops=4 * length * length * heads_width,
            bytes_accessed=16 * 2**20,
            transcendentals=length * length * heads_width // HEAD_SIZE,
        ),
    )(qkv, cosine, signed_sine, row_piece, col_piece)


def attend_back_steps(
    query_ref,
    keys_ref,
    values_ref,
    grad_ref,
    cosine_ref,
    sine_ref,
    row_piece_ref,
    col_piece_ref,
    grad_qkv_ref,
    grad_keys,
    grad_values,
):
    length = query_ref.shape[0]

    def turned_back(grad, first):
        span = slice(first, first + grad.shape[0])
        scaled = grad * HEAD_SIZE**-0.5
        return to_low(scaled * cosine_ref[span] - half_turn(scaled, sine_ref[span]))

    def head_block(head, first):
        column = pl.ds(pl.multiple_of(head * HEAD_SIZE, HEAD_SIZE), HEAD_SIZE)
        span = slice(first, first + QUERY_ROWS)
        extent = min(length, first + QUERY_ROWS + PIECE)
        if first == 0:
            grad_keys[...] = jnp.zeros_like(grad_keys)
            grad_values[...] = jnp.zeros_like(grad_values)
        allowed = block_mask(first, QUERY_ROWS, extent, row_piece_ref, col_piece_ref)
        query_rows = query_ref[span, column]
        keys = keys_ref[:extent, column]
        grad_rows = grad_ref[span, column]
        probs = block_probs(query_rows, keys, allowed)
        grad_probs = contract_last(grad_rows, values_ref[:extent, column])
        shift = jnp.sum(probs * grad_probs, axis=1, keepdims=True)
        grad_scores = to_low(probs * (grad_probs - shift))
        grad_values[:extent] += contract_first(to_low(probs), grad_rows)
        grad_keys[:extent] += contract_first(grad_scores, query_rows)
        grad_qkv_ref[0, span, column] = turned_back(matmul(grad_scores, keys), first)
        if first + QUERY_ROWS >= length:
            grad_qkv_ref[1, :, column] = turned_back(grad_keys[...], 0)
            grad_qkv_ref[2, :, column] = to_low(grad_values[...])

    return head_block


def attend_back_kernel(*refs):
    head_block = attend_back_steps(*refs)

    @pl.loop(0, refs[0].shape[1] // HEAD_SIZE)
    def _(head):
        for first in range(0, refs[0].shape[0], QUERY_ROWS):
            head_block(head, first)


def attend_back(query, keys, values, grads, cosine, signed_sine, row_piece, col_piece):
    length, heads_width = query.shape
    return pl.pallas_call(
        attend_back_kernel,
        out_shape=jax.ShapeDtypeStruct((3, length, heads_width), jnp.bfloat16),
        in_specs=[pl.BlockSpec(memory_space=pltpu.VMEM)] * 8,
        out_specs=pl.BlockSpec(memory_space=pltpu.VMEM),
        scratch_shapes=[pltpu.VMEM((length, HEAD_SIZE), jnp.float32)] * 2,
        compiler_params=pltpu.CompilerParams(vmem_limit_bytes=48 * 2**20),
        cost_estimate=pl.CostEstimate(
            flops=10 * length * length * heads_width,
            bytes_accessed=16 * 2**20,
            transcendentals=length * length * heads_width // HEAD_SIZE,
        ),
    )(query, keys, values, grads, cosine, signed_sine, row_piece, col_piece)


def summed_and_attended_back(wide_part, attention_inputs, number):
    if not on_line():
        return lax.psum(wide_part, "tensor"), attend_back(*attention_inputs)
    shape = wide_part.shape
    length, heads_width = attention_inputs[0].shape
    return pl.pallas_call(
        functools.partial(attend_back_sum_kernel, SUM_CHUNKS),
        out_shape=[
            jax.ShapeDtypeStruct(shape, jnp.bfloat16),
            jax.ShapeDtypeStruct((3, length, heads_width), jnp.bfloat16),
        ],
        in_specs=in_vmem(1 + len(attention_inputs)),
        out_specs=in_vmem(2),
        scratch_shapes=sum_scratch(shape) + [pltpu.VMEM((length, HEAD_SIZE), jnp.float32)] * 2,
        compiler_params=pltpu.CompilerParams(
            collective_id=number, has_side_effects=True, vmem_limit_bytes=58 * 2**20
        ),
        cost_estimate=pl.CostEstimate(flops=0, bytes_accessed=300 * 2**20, transcendentals=0),
    )(wide_part, *attention_inputs)


def experts_kernel(
    inputs_ref,
    gate_ref,
    up_ref,
    open_ref,
    grad_start,
    grad_ref,
    act_ref,
    gate_grad_ref,
    grad_rows,
    semaphore,
):
    @pl.when(pl.program_id(0) == 0)
    def _():
        load = pltpu.make_async_copy(grad_start, grad_ref, semaphore.at[0])
        load.start()
        load.wait()

    hidden = open_ref.shape[1]
    gate_up = matmul(up_ref[0], inputs_ref[...])
    open_part = open_ref[0].astype(jnp.float32)
    gate_half, up_half = gate_up[:hidden], gate_up[hidden:]
    squashed = 1.0 / (1.0 + jnp.exp(-gate_half))
    act = to_low(gate_half * squashed * up_half).astype(jnp.float32)
    gate_row = gate_ref[0]
    gate_grad_ref[0] = jnp.sum(act * open_part, axis=0, keepdims=True)
    act_ref[0] = to_low(gate_row * act)
    grad_act = gate_row * open_part
    grad_rows[:hidden] = to_low(
        grad_act * up_half * squashed * (1.0 + gate_half * (1.0 - squashed))
    )
    grad_rows[hidden:] = to_low(grad_act * gate_half * squashed)
    grad_ref[...] += contract_first(grad_rows[...], up_ref[0])


def experts_step(inputs, gates, up_rows, open_rows, grad_start, first):
    count, length, width = up_rows.shape[0], inputs.shape[1], inputs.shape[0]
    hidden = open_rows.shape[1]
    once = pl.Buffered(1)

    def still(shape):
        return pl.BlockSpec(shape, lambda expert: (0, 0), pipeline_mode=once)

    def here(rows):
        return pl.BlockSpec((1, rows, length), lambda expert: (expert, 0, 0))

    def ahead(rows):
        return pl.BlockSpec((1, rows, length), lambda expert: (expert + first, 0, 0))

    return pl.pallas_call(
        experts_kernel,
        grid=(count,),
        in_specs=[
            still((width, length)),
            ahead(1),
            pl.BlockSpec((1, 2 * hidden, width), lambda expert: (expert, 0, 0)),
            ahead(hidden),
            pl.BlockSpec(memory_space=pltpu.HBM),
        ],
        out_specs=[still((length, width)), here(hidden), here(1)],
        out_shape=[
            jax.ShapeDtypeStruct((length, width), jnp.float32),
            jax.ShapeDtypeStruct((count, hidden, length), jnp.bfloat16),
            jax.ShapeDtypeStruct((count, 1, length), jnp.float32),
        ],
        scratch_shapes=[
            pltpu.VMEM((2 * hidden, length), jnp.bfloat16),
            pltpu.SemaphoreType.DMA((1,)),
        ],
        compiler_params=pltpu.CompilerParams(
            vmem_limit_bytes=58 * 2**20, dimension_semantics=("arbitrary",)
        ),
        cost_estimate=pl.CostEstimate(
            flops=12 * count * hidden * width * length,
            bytes_accessed=32 * 2**20,
            transcendentals=0,
        ),
    )(inputs, gates, up_rows, open_rows, grad_start)


def swiglu(paired):
    return jax.nn.silu(paired[..., 0, :]) * paired[..., 1, :]


def gathered(weight):
    return lax.all_gather(weight, "dp", axis=0, tiled=True)


def body(
    tokens,
    cotangent,
    attention_norm_gain,
    query_key_value_weight,
    query_key_value_bias,
    output_projection_weight,
    feedforward_norm_gain,
    router_matrix,
    shared_expert_gate_weight,
    routed_gate_up_weight,
    routed_down_weight,
    shared_expert_gate_up_weight,
    shared_expert_down_weight,
    routes,
    sequence_adapter_index,
    picture_piece_starts,
    adapter_query_key_value_lower,
    adapter_query_key_value_upper,
    adapter_output_lower,
    adapter_output_upper,
    adapter_shared_up_lower,
    adapter_shared_up_upper,
    adapter_shared_down_lower,
    adapter_shared_down_upper,
):
    length, width = tokens.shape
    set_id = sequence_adapter_index[0]
    starts = picture_piece_starts[0]

    def selected_experts(adapter_entry):
        return lax.dynamic_index_in_dim(adapter_entry, set_id, 0, keepdims=False)

    qkv_a, qkv_b, out_a, out_b = (
        selected_experts(adapter_query_key_value_lower),
        selected_experts(adapter_query_key_value_upper),
        selected_experts(adapter_output_lower),
        selected_experts(adapter_output_upper),
    )
    up_a, up_b, down_a, down_b = (
        selected_experts(adapter_shared_up_lower),
        selected_experts(adapter_shared_up_upper),
        selected_experts(adapter_shared_down_lower),
        selected_experts(adapter_shared_down_upper),
    )
    gain_attn_f = attention_norm_gain.astype(jnp.float32)
    gain_ffn_f = feedforward_norm_gain.astype(jnp.float32)
    tokens_f = tokens.astype(jnp.float32)
    normed = to_low(rms_scale(tokens_f, gain_attn_f))
    mid_qkv = to_low(matmul(normed, qkv_a))
    attention_rows = gathered(
        jnp.concatenate([query_key_value_weight, output_projection_weight[:, None]], axis=1)
    )
    qkv_rows, output_rows = attention_rows[:, :3], attention_rows[:, 3]
    qkv_sum = jnp.einsum("tr,rsf->stf", normed, qkv_rows, preferred_element_type=jnp.float32)
    qkv_sum = qkv_sum + query_key_value_bias.astype(jnp.float32)[:, None, :]
    qkv_sum = qkv_sum + ADAPTER_SCALE * jnp.einsum(
        "tr,rsf->stf", mid_qkv, qkv_b, preferred_element_type=jnp.float32
    )
    cosine, sine_table = rope_tables(length)
    signs = jnp.where(jnp.arange(HEAD_SIZE) < HEAD_SIZE // 2, -1.0, 1.0)
    piece_ids = piece_index(jnp.arange(length, dtype=jnp.int32), starts)
    places = (cosine, sine_table * signs[None, :], piece_ids[:, None], piece_ids[None, :])
    query, keys, values, attended = attend(qkv_sum, *places)
    branch_part = contract_last(attended, output_rows)
    down_block = jnp.transpose(routed_down_weight, (1, 2, 0))
    branch_here, mid_out_here_f, down_rows, open_rows = summed_and_gathered(
        branch_part,
        matmul(attended, out_a),
        down_block.reshape(-1, down_block.shape[2]),
        cotangent.T,
        1,
    )
    mid_out = to_low(mid_out_here_f)
    hidden_here = tokens_f + branch_here + ADAPTER_SCALE * matmul(mid_out, out_b)
    normed_two_here_f, norm_ffn_pull = jax.vjp(
        lambda rows: rms_scale(rows, gain_ffn_f), hidden_here
    )
    normed_two_here = to_low(normed_two_here_f)
    normed_two = normed_two_here
    cot_f = cotangent.astype(jnp.float32)
    shared_three = gathered(
        jnp.concatenate([shared_expert_gate_up_weight, shared_expert_down_weight[:, None]], axis=1)
    )
    shared_rows, sdown_rows = shared_three[:, :2], shared_three[:, 2]
    small_rows = gathered(
        jnp.concatenate(
            [
                router_matrix,
                shared_expert_gate_weight[:, None],
                jnp.full_like(shared_expert_gate_weight, set_id)[:, None],
            ],
            axis=1,
        )
    )
    router_full, gate_full = small_rows[:, :EXPERTS], small_rows[:, EXPERTS]
    router_probs = jax.nn.softmax(matmul(normed_two, router_full), axis=-1)
    shared_gate = jax.nn.sigmoid(matmul(normed_two, gate_full))
    expert_ids = jnp.arange(EXPERTS, dtype=jnp.int32)
    chosen = jnp.sum(
        (routes[:, :, None] == expert_ids[None, None, :]).astype(jnp.float32), axis=1
    )
    gate_table = (router_probs * chosen).T

    mid_up = to_low(matmul(normed_two, up_a))
    shared_gu = jnp.einsum(
        "tr,rxf->txf", normed_two, shared_rows, preferred_element_type=jnp.float32
    ) + ADAPTER_SCALE * jnp.einsum("tr,rxf->txf", mid_up, up_b, preferred_element_type=jnp.float32)
    shared_act_f, shared_pull = jax.vjp(swiglu, shared_gu)
    shared_act = to_low(shared_act_f)
    shared_cols = contract_last(shared_act, sdown_rows)
    shared_gate_part = jnp.sum(cot_f * shared_cols, axis=1)
    grad_shared = to_low(shared_gate[:, None] * cot_f)
    cotangent_down = ADAPTER_SCALE * contract_last(cotangent, down_b)
    grad_mid_down = to_low(ADAPTER_SCALE * contract_last(grad_shared, down_b))
    grad_shared_act = matmul(grad_shared, sdown_rows) + contract_last(grad_mid_down, down_a)
    grad_shared_gu = to_low(shared_pull(grad_shared_act)[0])
    grad_mid_up_part = ADAPTER_SCALE * jnp.einsum(
        "txf,rxf->tr", grad_shared_gu, up_b, preferred_element_type=jnp.float32
    )
    grad_up_b_local = ADAPTER_SCALE * jnp.einsum(
        "tr,txf->rxf", mid_up, grad_shared_gu, preferred_element_type=jnp.float32
    )
    grad_down_a_local = contract_first(grad_mid_down, shared_act)
    combined_part = shared_gate[:, None] * shared_cols
    normed_two_part = jnp.einsum(
        "txf,rxf->tr", grad_shared_gu, shared_rows, preferred_element_type=jnp.float32
    )

    up_block = jnp.transpose(routed_gate_up_weight, (1, 2, 3, 0))
    inputs_t = normed_two.T
    gates = gate_table.reshape(EXPERTS, 1, length)
    open_rows = open_rows.reshape(EXPERTS, -1, length)
    gate_grad_parts = []
    act_parts = []
    first = 0
    for count in EXPERT_PARTS:
        up_rows = lax.all_gather(up_block[first : first + count], "dp", axis=3, tiled=True)
        normed_two_part, act_part, gate_grads = experts_step(
            inputs_t,
            gates,
            up_rows.reshape(count, -1, width),
            open_rows,
            normed_two_part,
            first,
        )
        act_parts.append(act_part.reshape(-1, length))
        gate_grad_parts.append(gate_grads.reshape(count, length))
        first += count
    gate_grad_part = jnp.concatenate(gate_grad_parts, axis=0).T
    narrow_part = jnp.concatenate(
        [
            gate_grad_part,
            shared_gate_part[:, None],
            grad_mid_up_part,
            matmul(shared_act, down_a),
        ],
        axis=1,
    )
    grad_normed_two, narrow_sum, combined_part = summed_and_down(
        normed_two_part, narrow_part, combined_part, act_parts, down_rows, 2
    )
    rank = up_a.shape[1]
    mid_down = to_low(narrow_sum[:, EXPERTS + 1 + rank :])
    grad_mid_up = to_low(narrow_sum[:, EXPERTS + 1 : EXPERTS + 1 + rank])
    grad_probs = chosen * narrow_sum[:, :EXPERTS]
    grad_logits = to_low(
        router_probs * (grad_probs - jnp.sum(router_probs * grad_probs, axis=1, keepdims=True))
    )
    shared_gate_grad = narrow_sum[:, EXPERTS] + jnp.sum(
        mid_down.astype(jnp.float32) * cotangent_down, axis=1
    )
    grad_gate_logit = to_low(shared_gate_grad * shared_gate * (1.0 - shared_gate))
    grad_normed_two = grad_normed_two + contract_last(
        jnp.concatenate([grad_logits, grad_gate_logit[:, None], grad_mid_up], axis=1),
        jnp.concatenate([router_full, gate_full[:, None], up_a], axis=1),
    )
    grad_hidden = cot_f + norm_ffn_pull(grad_normed_two)[0]
    grad_branch = to_low(grad_hidden)
    grad_mid_out = to_low(ADAPTER_SCALE * contract_last(grad_branch, out_b))
    grad_attended = to_low(
        matmul(grad_branch, output_rows) + contract_last(grad_mid_out, out_a)
    )
    combined_here, grad_qkv = summed_and_attended_back(
        combined_part, (query, keys, values, grad_attended) + places, 3
    )
    extra_here = ADAPTER_SCALE * matmul(mid_down, down_b)
    output = to_low(hidden_here + combined_here + shared_gate[:, None] * extra_here)
    grad_down_b_local = ADAPTER_SCALE * contract_first(mid_down, grad_shared)
    grad_up_a_local = contract_first(grad_mid_up, normed_two)
    grad_out_b_local = ADAPTER_SCALE * contract_first(mid_out, grad_branch)
    grad_out_a_local = contract_first(grad_mid_out, attended)
    grad_mid_qkv_part = ADAPTER_SCALE * jnp.einsum(
        "stf,rsf->tr", grad_qkv, qkv_b, preferred_element_type=jnp.float32
    )
    grad_qkv_b_local = ADAPTER_SCALE * jnp.einsum(
        "tr,stf->rsf", mid_qkv, grad_qkv, preferred_element_type=jnp.float32
    )
    normed_part = jnp.einsum(
        "stf,rsf->tr",
        grad_qkv,
        qkv_rows,
        preferred_element_type=jnp.float32,
    )
    grad_normed, grad_mid_qkv_f = summed(normed_part, grad_mid_qkv_part, 4)
    grad_mid_qkv_here = to_low(grad_mid_qkv_f)
    grad_normed = grad_normed + contract_last(grad_mid_qkv_here, qkv_a)
    norm_attn_pull = jax.vjp(lambda rows: rms_scale(rows, gain_attn_f), tokens_f)[1]
    grad_tokens_here = to_low(grad_hidden + norm_attn_pull(grad_normed)[0])
    grad_tokens, grad_mid_qkv = (grad_tokens_here, grad_mid_qkv_here)
    grad_qkv_a_local = contract_first(grad_mid_qkv, normed)
    everyone = small_rows[:: small_rows.shape[0] // lax.axis_size("dp"), EXPERTS + 1]
    marker = to_low(
        jnp.arange(ADAPTER_SETS, dtype=jnp.int32)[:, None] == everyone.astype(jnp.int32)[None, :]
    )

    def adapter_sums(local_grads):
        sizes = [local_grad.shape[1] for local_grad in local_grads]
        flat = jnp.concatenate([to_low(local_grad) for local_grad in local_grads], axis=1)
        rows = lax.all_gather(flat, "dp", axis=0, tiled=False)
        totals = jnp.einsum("cj,jrn->crn", marker, rows, preferred_element_type=jnp.float32)
        results, start = [], 0
        for size in sizes:
            results.append(totals[:, :, start : start + size])
            start += size
        return results

    def flipped(total):
        return jnp.swapaxes(total, 1, 2)

    def opened(total, count):
        return total.reshape(total.shape[0], total.shape[1], count, -1)

    total_out_a, total_out_b, total_up_a, total_up_b, total_down_a, total_down_b = adapter_sums(
        [
            grad_out_a_local,
            grad_out_b_local,
            grad_up_a_local,
            grad_up_b_local.reshape(grad_up_b_local.shape[0], -1),
            grad_down_a_local,
            grad_down_b_local,
        ]
    )
    total_qkv_b, total_qkv_a = adapter_sums(
        [grad_qkv_b_local.reshape(grad_qkv_b_local.shape[0], -1), grad_qkv_a_local]
    )
    return (
        output,
        grad_tokens,
        flipped(total_qkv_a),
        opened(total_qkv_b, 3),
        flipped(total_out_a),
        total_out_b,
        flipped(total_up_a),
        opened(total_up_b, 2),
        flipped(total_down_a),
        total_down_b,
    )


def solution(mesh):
    return jax.shard_map(
        body,
        mesh=mesh,
        in_specs=(
            P("dp", None),
            P("dp", None),
            P(),
            P("dp", None, "tensor"),
            P(None, "tensor"),
            P("dp", "tensor"),
            P(),
            P("dp", None),
            P("dp"),
            P("dp", None, None, "tensor"),
            P("dp", None, "tensor"),
            P("dp", None, "tensor"),
            P("dp", "tensor"),
            P("dp", None),
            P("dp"),
            P("dp", None),
            P(),
            P(None, None, None, "tensor"),
            P(None, "tensor", None),
            P(),
            P(),
            P(None, None, None, "tensor"),
            P(None, "tensor", None),
            P(),
        ),
        out_specs=(
            P("dp", None),
            P("dp", None),
            P(),
            P(None, None, None, "tensor"),
            P(None, "tensor", None),
            P(),
            P(),
            P(None, None, None, "tensor"),
            P(None, "tensor", None),
            P(),
        ),
        check_vma=False,
    )
```

```python
import functools

import jax
import jax.numpy as jnp
from jax import lax
from jax.experimental import pallas as pl
from jax.experimental.pallas import tpu as pltpu
from jax.sharding import PartitionSpec as P

HEAD_SIZE = 128
TOP = 4
EXPERTS = 16
ADAPTER_SETS = 8
PIECE = 256


EPSILON = 1e-06
THETA = 1000000.0
ADAPTER_SCALE = 2.0
MASKED = -1e30
QUERY_ROWS = 256
NARROW = 128
MESH = pl.DeviceIdType.MESH
SUM_CHUNKS = 16
AHEAD = 2
SHARED = 4
HALVES = 2


def matmul(left_side, right_side):
    return jnp.dot(left_side, right_side, preferred_element_type=jnp.float32)


def contract_last(left_side, right_side):
    return lax.dot_general(
        left_side, right_side, (((1,), (1,)), ((), ())), preferred_element_type=jnp.float32
    )


def contract_first(left_side, right_side):
    return lax.dot_general(
        left_side, right_side, (((0,), (0,)), ((), ())), preferred_element_type=jnp.float32
    )


def to_low(values):
    return values.astype(jnp.bfloat16)


def rms_scale(values, gain_values):
    return (
        values * lax.rsqrt(jnp.mean(values * values, axis=1, keepdims=True) + EPSILON) * gain_values
    )


def rope_tables(length):
    half_size = HEAD_SIZE // 2
    frequency = THETA ** (-jnp.arange(half_size, dtype=jnp.float32) * 2.0 / HEAD_SIZE)
    angles = jnp.arange(length, dtype=jnp.float32)[:, None] * frequency[None, :]
    return (
        jnp.concatenate([jnp.cos(angles)] * 2, axis=1),
        jnp.concatenate([jnp.sin(angles)] * 2, axis=1),
    )


def piece_index(positions, starts):
    inside = (positions[:, None] >= starts[None, :]) & (
        positions[:, None] < starts[None, :] + PIECE
    )
    labels = jnp.arange(starts.shape[0], dtype=jnp.int32)[None, :] + 1
    return jnp.sum(jnp.where(inside, labels, 0), axis=1) - 1


def line_sum_steps(
    chunks, wide_ref, narrow_ref, total_ref, part_ref, from_end, pair_sum, from_pair, semaphores
):
    place = lax.axis_index("tensor")
    width = wide_ref.shape[1]
    rows = part_ref.shape[0] // chunks
    inner = (place == 1) | (place == 2)
    end = (place == 0) | (place == 3)
    mate = jnp.where(place < 2, 1 - place, 5 - place)
    other = jnp.where(inner, 3 - place, place)

    def span(chunk):
        return pl.ds(pl.multiple_of(chunk * rows, rows), rows)

    def copy(source, target, chunk, lane, device):
        return pltpu.make_async_remote_copy(
            source.at[span(chunk)],
            target.at[span(chunk)],
            semaphores.at[2 * lane, chunk],
            semaphores.at[2 * lane + 1, chunk],
            device_id={"tensor": device},
            device_id_type=MESH,
        )

    def inward(chunk):
        return copy(part_ref, from_end, chunk, 0, mate)

    def across(chunk):
        return copy(pair_sum, from_pair, chunk, 1, other)

    def outward(chunk):
        return copy(total_ref, total_ref, chunk, 2, mate)

    def add(left_ref, right_ref, out_ref, chunk):
        out_ref[span(chunk)] = to_low(
            left_ref[span(chunk)].astype(jnp.float32) + right_ref[span(chunk)].astype(jnp.float32)
        )

    def stage(chunk):
        part_ref[span(chunk), :width] = to_low(wide_ref[span(chunk)])
        if narrow_ref is not None:
            part_ref[span(chunk), width:] = narrow_ref[span(chunk)]

    def greet(extra):
        barrier = pltpu.get_barrier_semaphore()
        pl.semaphore_signal(barrier, inc=1, device_id={"tensor": mate}, device_id_type=MESH)

        @pl.when(inner)
        def _():
            pl.semaphore_signal(barrier, inc=1, device_id={"tensor": other}, device_id_type=MESH)
            pl.semaphore_wait(barrier, 2 + extra)

        @pl.when(end)
        def _():
            pl.semaphore_wait(barrier, 1 + extra)

    def begin():
        @pl.when(end)
        def _():
            @pl.loop(0, chunks)
            def _(chunk):
                stage(chunk)
                inward(chunk).start()

    def advance(step):
        @pl.when(inner & (step < chunks))
        def _():
            stage(step)
            inward(step).wait_recv()
            add(part_ref, from_end, pair_sum, step)
            across(step).start()

        @pl.when(inner & (step > 0) & (step <= chunks))
        def _():
            across(step - 1).wait_recv()
            add(pair_sum, from_pair, total_ref, step - 1)
            outward(step - 1).start()

    def finish():
        @pl.when(end)
        def _():
            @pl.loop(0, chunks)
            def _(chunk):
                inward(chunk).wait_send()
                outward(chunk).wait_recv()

        @pl.when(inner)
        def _():
            @pl.loop(0, chunks)
            def _(chunk):
                across(chunk).wait_send()
                outward(chunk).wait_send()

    return greet, begin, advance, finish


def plane_gather_steps(pieces, block_ref, whole_ref, semaphores, local_semaphore):
    spot = lax.axis_index("dp")
    depth = block_ref.shape[1]
    rows = block_ref.shape[0] // pieces
    core_mate = spot + 1 - 2 * (spot % 2)
    x_mate = spot + 2 - 4 * ((spot // 2) % 2)
    y_mate = spot + 4 - 8 * (spot // 4)
    x_y_mate = x_mate + 4 - 8 * (spot // 4)
    lanes = {
        "core": (spot, core_mate, 0, 1),
        "x": (spot, x_mate, 0, 1),
        "y": (spot, y_mate, 0, 1),
        "x_core": (x_mate, core_mate, 0, 1),
        "x_y": (x_mate, y_mate, 0, 2),
        "y_core": (y_mate, core_mate, 0, 1),
        "y_x": (y_mate, x_mate, 1, 2),
        "xy_core": (x_y_mate, core_mate, 0, 2),
        "yx_core": (x_y_mate, core_mate, 1, 2),
    }
    order = list(lanes)

    def send(name, piece):
        owner, device, part, parts = lanes[name]
        lane = order.index(name)
        span = pl.ds(
            pl.multiple_of(piece * rows + part * (rows // parts), rows // parts), rows // parts
        )
        columns = pl.ds(pl.multiple_of(owner * depth, depth), depth)
        target = whole_ref.at[span, columns]
        source = block_ref.at[span] if name in ("core", "x", "y") else target
        return pltpu.make_async_remote_copy(
            source,
            target,
            semaphores.at[2 * lane, piece],
            semaphores.at[2 * lane + 1, piece],
            device_id={"dp": device},
            device_id_type=MESH,
        )

    def own():
        columns = pl.ds(pl.multiple_of(spot * depth, depth), depth)
        return pltpu.make_async_copy(block_ref, whole_ref.at[:, columns], local_semaphore)

    def greet():
        barrier = pltpu.get_barrier_semaphore()
        for device in (core_mate, x_mate, y_mate):
            pl.semaphore_signal(barrier, inc=1, device_id={"dp": device}, device_id_type=MESH)

    def begin():
        own().start()

    def launch(piece):
        @pl.when((piece >= 0) & (piece < pieces))
        def _():
            for name in ("x", "y", "core"):
                send(name, piece).start()

    def forward(piece):
        @pl.when((piece >= 0) & (piece < pieces))
        def _():
            send("x", piece).wait_recv()
            send("x_y", piece).start()
            send("x_core", piece).start()
            send("y", piece).wait_recv()
            send("y_x", piece).start()
            send("y_core", piece).start()

    def hand_over(piece):
        @pl.when((piece >= 0) & (piece < pieces))
        def _():
            send("x_y", piece).wait_recv()
            send("xy_core", piece).start()
            send("y_x", piece).wait_recv()
            send("yx_core", piece).start()

    def advance(step):
        launch(step)
        forward(step - AHEAD)
        hand_over(step - 2 * AHEAD)

    def arrive(piece):
        @pl.when(piece == 0)
        def _():
            own().wait()

        for name in ("core", "x_core", "y_core", "xy_core", "yx_core"):
            send(name, piece).wait_recv()

    def finish():
        @pl.loop(0, pieces)
        def _(piece):
            for name in order:
                send(name, piece).wait_send()

    return greet, begin, advance, arrive, finish, (launch, forward, hand_over)


def line_sum_kernel(chunks, *refs):
    greet, begin, advance, finish = line_sum_steps(chunks, *refs)
    greet(0)
    begin()

    @pl.loop(0, chunks + 1)
    def _(step):
        advance(step)

    finish()


def sum_gather_kernel(
    chunks,
    pieces,
    wide_ref,
    narrow_ref,
    block_ref,
    cotangent_ref,
    total_ref,
    whole_ref,
    open_ref,
    *scratch,
):
    greet, begin, advance, finish = line_sum_steps(
        chunks, wide_ref, narrow_ref, total_ref, *scratch[:5]
    )
    gather_semaphores, local_semaphores, piece_rows, open_rows = scratch[5:]
    gather_greet, gather_begin, gather_advance, gather_arrive, gather_finish, _ = (
        plane_gather_steps(
            pieces, block_ref, whole_ref, gather_semaphores, local_semaphores.at[0]
        )
    )
    rows = piece_rows.shape[1]

    def load(piece):
        slot = piece % 2
        span = pl.ds(pl.multiple_of(piece * rows, rows), rows)
        return pltpu.make_async_copy(
            whole_ref.at[span], piece_rows.at[slot], local_semaphores.at[1 + slot]
        )

    def store(piece):
        slot = piece % 2
        span = pl.ds(pl.multiple_of(piece * rows, rows), rows)
        return pltpu.make_async_copy(
            open_rows.at[slot], open_ref.at[span], local_semaphores.at[3 + slot]
        )

    gather_greet()
    greet(3)
    begin()
    gather_begin()

    @pl.loop(0, max(chunks + 1, pieces + 3 * AHEAD + 1))
    def _(step):
        gather_advance(step)
        advance(step)

        @pl.when((step >= 3 * AHEAD) & (step < pieces + 3 * AHEAD))
        def _():
            gather_arrive(step - 3 * AHEAD)
            load(step - 3 * AHEAD).start()

        @pl.when((step > 3 * AHEAD) & (step <= pieces + 3 * AHEAD))
        def _():
            piece = step - 3 * AHEAD - 1
            load(piece).wait()

            @pl.when(piece >= 2)
            def _():
                store(piece - 2).wait()

            open_rows[piece % 2] = to_low(matmul(piece_rows[piece % 2], cotangent_ref[...]))
            store(piece).start()

    store(pieces - 2).wait()
    store(pieces - 1).wait()
    gather_finish()
    finish()


def sum_down_kernel(
    chunks, wide_ref, narrow_ref, act_ref, down_ref, total_ref, out_ref, *scratch
):
    greet, begin, advance, finish = line_sum_steps(
        chunks, wide_ref, narrow_ref, total_ref, *scratch[:5]
    )
    semaphores, act_rows, down_rows, out_rows = scratch[5:]
    rows = act_rows.shape[1]
    blocks = down_ref.shape[0] // rows

    def loads(block):
        slot = block % 2
        span = pl.ds(pl.multiple_of(block * rows, rows), rows)
        return [
            pltpu.make_async_copy(act_ref.at[span], act_rows.at[slot], semaphores.at[0, slot]),
            pltpu.make_async_copy(down_ref.at[span], down_rows.at[slot], semaphores.at[1, slot]),
        ]

    for load in loads(0):
        load.start()
    greet(0)
    begin()
    out_rows[...] = jnp.zeros_like(out_rows)

    @pl.loop(0, max(blocks, chunks + 1))
    def _(step):
        advance(step)

        @pl.when(step < blocks)
        def _():
            @pl.when(step + 1 < blocks)
            def _():
                for load in loads(step + 1):
                    load.start()

            for load in loads(step):
                load.wait()
            tile = min(256, out_rows.shape[0])

            @pl.loop(0, out_rows.shape[0] // tile)
            def _(index):
                span = pl.ds(pl.multiple_of(index * tile, tile), tile)
                out_rows[span] += contract_first(
                    act_rows[step % 2, :, span], down_rows[step % 2]
                )

    out_ref[...] = to_low(out_rows[...])
    finish()


def attend_back_sum_kernel(chunks, wide_ref, *refs):
    inputs, (total_ref, grad_qkv_ref), scratch = refs[:8], refs[8:10], refs[10:]
    greet, begin, advance, finish = line_sum_steps(
        chunks, wide_ref, None, total_ref, *scratch[:5]
    )
    head_block = attend_back_steps(*inputs, grad_qkv_ref, *scratch[5:])
    length, heads_width = inputs[0].shape
    heads, blocks = heads_width // HEAD_SIZE, length // QUERY_ROWS
    greet(0)
    begin()

    @pl.loop(0, heads)
    def _(head):
        for block in range(blocks):
            advance(head * blocks + block)
            head_block(head, block * QUERY_ROWS)

    @pl.loop(heads * blocks, max(heads * blocks, chunks + 1))
    def _(step):
        advance(step)

    finish()


def on_line():
    return lax.axis_size("tensor") == 4


def in_plane():
    return lax.axis_size("dp") == 8


def in_vmem(count):
    return [pl.BlockSpec(memory_space=pltpu.VMEM)] * count


def in_hbm(count):
    return [pl.BlockSpec(memory_space=pltpu.HBM)] * count


def sum_scratch(shape):
    return [pltpu.VMEM(shape, jnp.bfloat16)] * 4 + [pltpu.SemaphoreType.DMA((6, SUM_CHUNKS))]


def narrowed(narrow_part):
    pad = jnp.zeros((narrow_part.shape[0], NARROW - narrow_part.shape[1]), jnp.bfloat16)
    return jnp.concatenate([to_low(narrow_part), pad], axis=1)


def parts_of(total, wide_part, narrow_part):
    width, small = wide_part.shape[1], narrow_part.shape[1]
    total = total.astype(jnp.float32)
    return total[:, :width], total[:, width : width + small]


def summed(wide_part, narrow_part, number):
    if not on_line():
        return lax.psum((wide_part, narrow_part), "tensor")
    shape = (wide_part.shape[0], wide_part.shape[1] + NARROW)
    total = pl.pallas_call(
        functools.partial(line_sum_kernel, SUM_CHUNKS),
        out_shape=jax.ShapeDtypeStruct(shape, jnp.bfloat16),
        in_specs=in_vmem(2),
        out_specs=pl.BlockSpec(memory_space=pltpu.VMEM),
        scratch_shapes=sum_scratch(shape),
        compiler_params=pltpu.CompilerParams(
            collective_id=number, has_side_effects=True, vmem_limit_bytes=48 * 2**20
        ),
        cost_estimate=pl.CostEstimate(flops=0, bytes_accessed=300 * 2**20, transcendentals=0),
    )(wide_part, narrowed(narrow_part))
    return parts_of(total, wide_part, narrow_part)


def summed_and_gathered(wide_part, narrow_part, block, cotangents, number):
    length, width = wide_part.shape
    if not (on_line() and in_plane()):
        whole = lax.all_gather(block, "dp", axis=1, tiled=True)
        open_rows = to_low(matmul(whole, cotangents))
        return summed(wide_part, narrow_part, number) + (whole, open_rows)
    shape = (length, width + NARROW)
    pieces = SHARED + EXPERTS
    rows = block.shape[0] // pieces
    total, whole, open_rows = pl.pallas_call(
        functools.partial(sum_gather_kernel, SUM_CHUNKS, pieces),
        out_shape=[
            jax.ShapeDtypeStruct(shape, jnp.bfloat16),
            jax.ShapeDtypeStruct((block.shape[0], width), jnp.bfloat16),
            jax.ShapeDtypeStruct((block.shape[0], length), jnp.bfloat16),
        ],
        in_specs=in_vmem(2) + in_hbm(1) + in_vmem(1),
        out_specs=in_vmem(1) + in_hbm(2),
        scratch_shapes=sum_scratch(shape)
        + [
            pltpu.SemaphoreType.DMA((18, pieces)),
            pltpu.SemaphoreType.DMA((5,)),
            pltpu.VMEM((2, rows, width), jnp.bfloat16),
            pltpu.VMEM((2, rows, length), jnp.bfloat16),
        ],
        compiler_params=pltpu.CompilerParams(
            collective_id=number, has_side_effects=True, vmem_limit_bytes=58 * 2**20
        ),
        cost_estimate=pl.CostEstimate(flops=0, bytes_accessed=360 * 2**20, transcendentals=0),
    )(wide_part, narrowed(narrow_part), block, cotangents)
    return parts_of(total, wide_part, narrow_part) + (whole, open_rows)


def summed_and_down(wide_part, narrow_part, act_rows, down_rows, number):
    length, width = wide_part.shape
    if not on_line():
        out = contract_first(act_rows, down_rows)
        return summed(wide_part, narrow_part, number) + (out,)
    shape = (length, width + NARROW)
    rows = 2 * down_rows.shape[0] // (SHARED + EXPERTS)
    total, out = pl.pallas_call(
        functools.partial(sum_down_kernel, SUM_CHUNKS),
        out_shape=[
            jax.ShapeDtypeStruct(shape, jnp.bfloat16),
            jax.ShapeDtypeStruct((length, width), jnp.bfloat16),
        ],
        in_specs=in_vmem(2) + in_hbm(2),
        out_specs=in_vmem(2),
        scratch_shapes=sum_scratch(shape)
        + [
            pltpu.SemaphoreType.DMA((2, 2)),
            pltpu.VMEM((2, rows, length), jnp.bfloat16),
            pltpu.VMEM((2, rows, width), jnp.bfloat16),
            pltpu.VMEM((length, width), jnp.float32),
        ],
        compiler_params=pltpu.CompilerParams(
            collective_id=number, has_side_effects=True, vmem_limit_bytes=58 * 2**20
        ),
        cost_estimate=pl.CostEstimate(flops=0, bytes_accessed=300 * 2**20, transcendentals=0),
    )(wide_part, narrowed(narrow_part), act_rows, down_rows)
    return parts_of(total, wide_part, narrow_part) + (out,)


def block_mask(first, rows, extent, row_piece_ref, col_piece_ref):
    row_place = lax.broadcasted_iota(jnp.int32, (rows, extent), 0) + first
    col_place = lax.broadcasted_iota(jnp.int32, (rows, extent), 1)
    row_piece = row_piece_ref[first : first + rows, 0:1]
    together = (row_piece == col_piece_ref[0:1, :extent]) & (row_piece >= 0)
    return (col_place <= row_place) | together


def block_probs(query_rows, keys, allowed):
    scores = jnp.where(allowed, contract_last(query_rows, keys) * HEAD_SIZE**-0.5, MASKED)
    raised = jnp.exp(scores - jnp.max(scores, axis=1, keepdims=True))
    return raised * (1.0 / jnp.sum(raised, axis=1, keepdims=True))


def half_turn(values, signed_sine):
    return pltpu.roll(values, HEAD_SIZE // 2, 1) * signed_sine


def attend_kernel(
    qkv_ref,
    cosine_ref,
    sine_ref,
    row_piece_ref,
    col_piece_ref,
    query_ref,
    keys_ref,
    values_ref,
    attended_ref,
):
    length = qkv_ref.shape[1]

    @pl.loop(0, qkv_ref.shape[2] // HEAD_SIZE)
    def _(head):
        column = pl.ds(pl.multiple_of(head * HEAD_SIZE, HEAD_SIZE), HEAD_SIZE)
        for source, target in ((0, query_ref), (1, keys_ref)):
            raw = qkv_ref[source, :, column]
            target[:, column] = to_low(raw * cosine_ref[...] + half_turn(raw, sine_ref[...]))
        values_ref[:, column] = to_low(qkv_ref[2, :, column])
        for first in range(0, length, QUERY_ROWS):
            extent = min(length, first + QUERY_ROWS + PIECE)
            allowed = block_mask(first, QUERY_ROWS, extent, row_piece_ref, col_piece_ref)
            probs = block_probs(
                query_ref[first : first + QUERY_ROWS, column], keys_ref[:extent, column], allowed
            )
            attended_ref[first : first + QUERY_ROWS, column] = to_low(
                matmul(to_low(probs), values_ref[:extent, column])
            )


def attend(qkv, cosine, signed_sine, row_piece, col_piece):
    length, heads_width = qkv.shape[1:]
    shape = jax.ShapeDtypeStruct((length, heads_width), jnp.bfloat16)
    return pl.pallas_call(
        attend_kernel,
        out_shape=[shape] * 4,
        in_specs=[pl.BlockSpec(memory_space=pltpu.VMEM)] * 5,
        out_specs=[pl.BlockSpec(memory_space=pltpu.VMEM)] * 4,
        compiler_params=pltpu.CompilerParams(vmem_limit_bytes=48 * 2**20),
        cost_estimate=pl.CostEstimate(
            flops=4 * length * length * heads_width,
            bytes_accessed=16 * 2**20,
            transcendentals=length * length * heads_width // HEAD_SIZE,
        ),
    )(qkv, cosine, signed_sine, row_piece, col_piece)


def attend_back_steps(
    query_ref,
    keys_ref,
    values_ref,
    grad_ref,
    cosine_ref,
    sine_ref,
    row_piece_ref,
    col_piece_ref,
    grad_qkv_ref,
    grad_keys,
    grad_values,
):
    length = query_ref.shape[0]

    def turned_back(grad, first):
        span = slice(first, first + grad.shape[0])
        scaled = grad * HEAD_SIZE**-0.5
        return to_low(scaled * cosine_ref[span] - half_turn(scaled, sine_ref[span]))

    def head_block(head, first):
        column = pl.ds(pl.multiple_of(head * HEAD_SIZE, HEAD_SIZE), HEAD_SIZE)
        span = slice(first, first + QUERY_ROWS)
        extent = min(length, first + QUERY_ROWS + PIECE)
        if first == 0:
            grad_keys[...] = jnp.zeros_like(grad_keys)
            grad_values[...] = jnp.zeros_like(grad_values)
        allowed = block_mask(first, QUERY_ROWS, extent, row_piece_ref, col_piece_ref)
        query_rows = query_ref[span, column]
        keys = keys_ref[:extent, column]
        grad_rows = grad_ref[span, column]
        probs = block_probs(query_rows, keys, allowed)
        grad_probs = contract_last(grad_rows, values_ref[:extent, column])
        shift = jnp.sum(probs * grad_probs, axis=1, keepdims=True)
        grad_scores = to_low(probs * (grad_probs - shift))
        grad_values[:extent] += contract_first(to_low(probs), grad_rows)
        grad_keys[:extent] += contract_first(grad_scores, query_rows)
        grad_qkv_ref[0, span, column] = turned_back(matmul(grad_scores, keys), first)
        if first + QUERY_ROWS >= length:
            grad_qkv_ref[1, :, column] = turned_back(grad_keys[...], 0)
            grad_qkv_ref[2, :, column] = to_low(grad_values[...])

    return head_block


def attend_back_kernel(*refs):
    head_block = attend_back_steps(*refs)

    @pl.loop(0, refs[0].shape[1] // HEAD_SIZE)
    def _(head):
        for first in range(0, refs[0].shape[0], QUERY_ROWS):
            head_block(head, first)


def attend_back(query, keys, values, grads, cosine, signed_sine, row_piece, col_piece):
    length, heads_width = query.shape
    return pl.pallas_call(
        attend_back_kernel,
        out_shape=jax.ShapeDtypeStruct((3, length, heads_width), jnp.bfloat16),
        in_specs=[pl.BlockSpec(memory_space=pltpu.VMEM)] * 8,
        out_specs=pl.BlockSpec(memory_space=pltpu.VMEM),
        scratch_shapes=[pltpu.VMEM((length, HEAD_SIZE), jnp.float32)] * 2,
        compiler_params=pltpu.CompilerParams(vmem_limit_bytes=48 * 2**20),
        cost_estimate=pl.CostEstimate(
            flops=10 * length * length * heads_width,
            bytes_accessed=16 * 2**20,
            transcendentals=length * length * heads_width // HEAD_SIZE,
        ),
    )(query, keys, values, grads, cosine, signed_sine, row_piece, col_piece)


def summed_and_attended_back(wide_part, attention_inputs, number):
    if not on_line():
        return lax.psum(wide_part, "tensor"), attend_back(*attention_inputs)
    shape = wide_part.shape
    length, heads_width = attention_inputs[0].shape
    return pl.pallas_call(
        functools.partial(attend_back_sum_kernel, SUM_CHUNKS),
        out_shape=[
            jax.ShapeDtypeStruct(shape, jnp.bfloat16),
            jax.ShapeDtypeStruct((3, length, heads_width), jnp.bfloat16),
        ],
        in_specs=in_vmem(1 + len(attention_inputs)),
        out_specs=in_vmem(2),
        scratch_shapes=sum_scratch(shape) + [pltpu.VMEM((length, HEAD_SIZE), jnp.float32)] * 2,
        compiler_params=pltpu.CompilerParams(
            collective_id=number, has_side_effects=True, vmem_limit_bytes=58 * 2**20
        ),
        cost_estimate=pl.CostEstimate(flops=0, bytes_accessed=300 * 2**20, transcendentals=0),
    )(wide_part, *attention_inputs)


def hidden_step(gate_up, open_part, gate_row, extra):
    hidden = open_part.shape[0]
    gate_half, up_half = gate_up[:hidden], gate_up[hidden:]
    squashed = 1.0 / (1.0 + jnp.exp(-gate_half))
    act = to_low(gate_half * squashed * up_half)
    act_f = act.astype(jnp.float32)
    gate_grad = jnp.sum(act_f * open_part, axis=0, keepdims=True)
    grad_act = gate_row * open_part
    if extra is not None:
        grad_act = grad_act + extra
    grad_gate = to_low(grad_act * up_half * squashed * (1.0 + gate_half * (1.0 - squashed)))
    grad_up = to_low(grad_act * gate_half * squashed)
    return act, to_low(gate_row * act_f), gate_grad, grad_gate, grad_up


def experts_kernel(
    pieces,
    inputs_ref,
    gate_ref,
    mid_up_ref,
    grad_mid_ref,
    up_extra_ref,
    down_extra_ref,
    shared_up_ref,
    block_ref,
    open_ref,
    grad_ref,
    gate_grad_ref,
    mid_down_ref,
    grad_mid_up_ref,
    grad_down_a_ref,
    grad_up_b_ref,
    act_ref,
    whole_ref,
    grad_total,
    up_rows,
    open_rows,
    act_rows,
    grad_rows,
    gather_semaphores,
    semaphores,
):
    greet, begin, _, arrive, finish, (launch, forward, hand_over) = plane_gather_steps(
        pieces, block_ref, whole_ref, gather_semaphores, semaphores.at[0, 0]
    )
    hidden = open_rows.shape[1]
    count = SHARED + EXPERTS
    each = pieces // EXPERTS

    def span(expert, rows):
        return pl.ds(pl.multiple_of(expert * rows, rows), rows)

    def load_open(expert):
        slot = expert % 2
        return pltpu.make_async_copy(
            open_ref.at[span(expert, hidden)], open_rows.at[slot], semaphores.at[1, slot]
        )

    def load_shared(expert):
        slot = expert % 2
        return pltpu.make_async_copy(
            shared_up_ref.at[span(expert, 2 * hidden)], up_rows.at[slot], semaphores.at[2, slot]
        )

    def load_routed(expert):
        slot = expert % 2
        return pltpu.make_async_copy(
            whole_ref.at[span(expert - SHARED, 2 * hidden)],
            up_rows.at[slot],
            semaphores.at[2, slot],
        )

    def store_act(expert):
        slot = expert % 2
        return pltpu.make_async_copy(
            act_rows.at[slot], act_ref.at[span(expert, hidden)], semaphores.at[3, slot]
        )

    def advance(expert):
        for part in range(each):
            launch(each * expert + part)
        for part in range(each):
            forward(each * (expert - 2) + part + 1)
        for part in range(each):
            hand_over(each * (expert - 3) + part + 1)

        @pl.when(expert + 1 < count)
        def _():
            load_open(expert + 1).start()

        @pl.when(expert + 1 < SHARED)
        def _():
            load_shared(expert + 1).start()

        @pl.when((expert + 1 >= SHARED) & (expert + 1 < count))
        def _():
            for part in range(each):
                arrive(each * (expert + 1 - SHARED) + part)
            load_routed(expert + 1).start()

        load_open(expert).wait()
        load_shared(0 * expert + expert % 2).wait()

        @pl.when(expert >= 2)
        def _():
            store_act(expert - 2).wait()

    def compute(expert, shared):
        slot = expert % 2
        gate_up = matmul(up_rows[slot], inputs_ref[...])
        extra = None
        if shared:
            gate_up = gate_up + matmul(up_extra_ref[expert], mid_up_ref[...])
            extra = matmul(down_extra_ref[expert], grad_mid_ref[...])
        act, act_gated, gate_grad, grad_gate, grad_up = hidden_step(
            gate_up,
            open_rows[slot].astype(jnp.float32),
            gate_ref[pl.ds(expert, 1)],
            extra,
        )
        gate_grad_ref[pl.ds(expert, 1)] = gate_grad
        act_rows[slot] = act_gated
        grad_rows[:hidden] = grad_gate
        grad_rows[hidden:] = grad_up
        store_act(expert).start()
        grad_total[...] += contract_first(grad_rows[...], up_rows[slot])
        if shared:
            mid_down_ref[...] += contract_first(down_extra_ref[expert], act)
            grad_mid_up_ref[...] += contract_first(up_extra_ref[expert], grad_rows[...])
            grad_down_a_ref[expert] = contract_last(grad_mid_ref[...], act)
            grad_up_b_ref[expert] = ADAPTER_SCALE * contract_last(mid_up_ref[...], grad_rows[...])

    greet()
    pl.semaphore_wait(pltpu.get_barrier_semaphore(), 3)
    begin()
    load_open(0).start()
    load_shared(0).start()
    grad_total[...] = jnp.zeros_like(grad_total)
    mid_down_ref[...] = jnp.zeros_like(mid_down_ref)
    grad_mid_up_ref[...] = jnp.zeros_like(grad_mid_up_ref)

    @pl.loop(0, SHARED)
    def _(expert):
        advance(expert)
        compute(expert, True)

    @pl.loop(SHARED, count)
    def _(expert):
        advance(expert)
        compute(expert, False)

    grad_ref[...] = to_low(grad_total[...])
    store_act(count - 2).wait()
    store_act(count - 1).wait()
    finish()


def experts_plain(inputs, gates, mid_up, grad_mid, up_extra, down_extra, up_rows, open_rows):
    count, length = gates.shape
    hidden = open_rows.shape[0] // count
    width = inputs.shape[0]
    grad_total = jnp.zeros((length, width), jnp.float32)
    act_parts, gate_grads, down_parts, up_parts = [], [], [], []
    mid_down = jnp.zeros((NARROW, length), jnp.float32)
    grad_mid_up = jnp.zeros((NARROW, length), jnp.float32)
    for expert in range(count):
        weights = up_rows[2 * hidden * expert : 2 * hidden * (expert + 1)]
        gate_up = matmul(weights, inputs)
        extra = None
        if expert < SHARED:
            gate_up = gate_up + matmul(up_extra[expert], mid_up)
            extra = matmul(down_extra[expert], grad_mid)
        act, act_gated, gate_grad, grad_gate, grad_up = hidden_step(
            gate_up,
            open_rows[hidden * expert : hidden * (expert + 1)].astype(jnp.float32),
            gates[expert : expert + 1],
            extra,
        )
        grad = jnp.concatenate([grad_gate, grad_up], axis=0)
        act_parts.append(act_gated)
        gate_grads.append(gate_grad)
        grad_total = grad_total + contract_first(grad, weights)
        if expert < SHARED:
            mid_down = mid_down + contract_first(down_extra[expert], act)
            grad_mid_up = grad_mid_up + contract_first(up_extra[expert], grad)
            down_parts.append(contract_last(grad_mid, act))
            up_parts.append(ADAPTER_SCALE * contract_last(mid_up, grad))
    return (
        grad_total,
        jnp.concatenate(gate_grads, axis=0),
        mid_down,
        grad_mid_up,
        jnp.stack(down_parts),
        jnp.stack(up_parts),
        jnp.concatenate(act_parts, axis=0),
    )


def experts_step(
    inputs, gates, mid_up, grad_mid, up_extra, down_extra, shared_up, block, open_rows, number
):
    width, length = inputs.shape
    count = SHARED + EXPERTS
    hidden = open_rows.shape[0] // count
    if not in_plane():
        whole = lax.all_gather(block, "dp", axis=1, tiled=True)
        up_rows = jnp.concatenate([shared_up, whole], axis=0)
        return experts_plain(
            inputs, gates, mid_up, grad_mid, up_extra, down_extra, up_rows, open_rows
        )
    pieces = HALVES * EXPERTS
    return pl.pallas_call(
        functools.partial(experts_kernel, pieces),
        in_specs=in_vmem(6) + in_hbm(3),
        out_specs=in_vmem(6) + in_hbm(2),
        out_shape=[
            jax.ShapeDtypeStruct((length, width), jnp.bfloat16),
            jax.ShapeDtypeStruct((count, length), jnp.float32),
            jax.ShapeDtypeStruct((NARROW, length), jnp.float32),
            jax.ShapeDtypeStruct((NARROW, length), jnp.float32),
            jax.ShapeDtypeStruct((SHARED, NARROW, hidden), jnp.float32),
            jax.ShapeDtypeStruct((SHARED, NARROW, 2 * hidden), jnp.float32),
            jax.ShapeDtypeStruct((count * hidden, length), jnp.bfloat16),
            jax.ShapeDtypeStruct((EXPERTS * 2 * hidden, width), jnp.bfloat16),
        ],
        scratch_shapes=[
            pltpu.VMEM((length, width), jnp.float32),
            pltpu.VMEM((2, 2 * hidden, width), jnp.bfloat16),
            pltpu.VMEM((2, hidden, length), jnp.bfloat16),
            pltpu.VMEM((2, hidden, length), jnp.bfloat16),
            pltpu.VMEM((2 * hidden, length), jnp.bfloat16),
            pltpu.SemaphoreType.DMA((18, pieces)),
            pltpu.SemaphoreType.DMA((4, 2)),
        ],
        compiler_params=pltpu.CompilerParams(
            collective_id=number, has_side_effects=True, vmem_limit_bytes=60 * 2**20
        ),
        cost_estimate=pl.CostEstimate(flops=0, bytes_accessed=600 * 2**20, transcendentals=0),
    )(inputs, gates, mid_up, grad_mid, up_extra, down_extra, shared_up, block, open_rows)[:7]


def gathered(weight):
    return lax.all_gather(weight, "dp", axis=0, tiled=True)


def body(
    tokens,
    cotangent,
    attention_norm_gain,
    query_key_value_weight,
    query_key_value_bias,
    output_projection_weight,
    feedforward_norm_gain,
    router_matrix,
    shared_expert_gate_weight,
    routed_gate_up_weight,
    routed_down_weight,
    shared_expert_gate_up_weight,
    shared_expert_down_weight,
    routes,
    sequence_adapter_index,
    picture_piece_starts,
    adapter_query_key_value_lower,
    adapter_query_key_value_upper,
    adapter_output_lower,
    adapter_output_upper,
    adapter_shared_up_lower,
    adapter_shared_up_upper,
    adapter_shared_down_lower,
    adapter_shared_down_upper,
):
    length, width = tokens.shape
    set_id = sequence_adapter_index[0]
    starts = picture_piece_starts[0]

    def selected_experts(adapter_entry):
        return lax.dynamic_index_in_dim(adapter_entry, set_id, 0, keepdims=False)

    qkv_a, qkv_b, out_a, out_b = (
        selected_experts(adapter_query_key_value_lower),
        selected_experts(adapter_query_key_value_upper),
        selected_experts(adapter_output_lower),
        selected_experts(adapter_output_upper),
    )
    up_a, up_b, down_a, down_b = (
        selected_experts(adapter_shared_up_lower),
        selected_experts(adapter_shared_up_upper),
        selected_experts(adapter_shared_down_lower),
        selected_experts(adapter_shared_down_upper),
    )
    gain_attn_f = attention_norm_gain.astype(jnp.float32)
    gain_ffn_f = feedforward_norm_gain.astype(jnp.float32)
    tokens_f = tokens.astype(jnp.float32)
    normed = to_low(rms_scale(tokens_f, gain_attn_f))
    mid_qkv = to_low(matmul(normed, qkv_a))
    attention_rows = gathered(
        jnp.concatenate([query_key_value_weight, output_projection_weight[:, None]], axis=1)
    )
    qkv_rows, output_rows = attention_rows[:, :3], attention_rows[:, 3]
    qkv_sum = jnp.einsum("tr,rsf->stf", normed, qkv_rows, preferred_element_type=jnp.float32)
    qkv_sum = qkv_sum + query_key_value_bias.astype(jnp.float32)[:, None, :]
    qkv_sum = qkv_sum + ADAPTER_SCALE * jnp.einsum(
        "tr,rsf->stf", mid_qkv, qkv_b, preferred_element_type=jnp.float32
    )
    cosine, sine_table = rope_tables(length)
    signs = jnp.where(jnp.arange(HEAD_SIZE) < HEAD_SIZE // 2, -1.0, 1.0)
    piece_ids = piece_index(jnp.arange(length, dtype=jnp.int32), starts)
    places = (cosine, sine_table * signs[None, :], piece_ids[:, None], piece_ids[None, :])
    query, keys, values, attended = attend(qkv_sum, *places)
    branch_part = contract_last(attended, output_rows)
    down_block = jnp.transpose(routed_down_weight, (1, 2, 0))
    depth = down_block.shape[2]
    down_block = jnp.concatenate(
        [shared_expert_down_weight.T, down_block.reshape(-1, depth)], axis=0
    )
    branch_here, mid_out_here_f, down_rows, open_rows = summed_and_gathered(
        branch_part,
        matmul(attended, out_a),
        down_block,
        cotangent.T,
        1,
    )
    mid_out = to_low(mid_out_here_f)
    hidden_here = tokens_f + branch_here + ADAPTER_SCALE * matmul(mid_out, out_b)
    normed_two_here_f, norm_ffn_pull = jax.vjp(
        lambda rows: rms_scale(rows, gain_ffn_f), hidden_here
    )
    normed_two_here = to_low(normed_two_here_f)
    normed_two = normed_two_here
    cot_f = cotangent.astype(jnp.float32)
    small_rows = gathered(
        jnp.concatenate(
            [
                router_matrix,
                shared_expert_gate_weight[:, None],
                jnp.full_like(shared_expert_gate_weight, set_id)[:, None],
            ],
            axis=1,
        )
    )
    router_full, gate_full = small_rows[:, :EXPERTS], small_rows[:, EXPERTS]
    router_probs = jax.nn.softmax(matmul(normed_two, router_full), axis=-1)
    shared_gate = jax.nn.sigmoid(matmul(normed_two, gate_full))
    expert_ids = jnp.arange(EXPERTS, dtype=jnp.int32)
    chosen = jnp.sum(
        (routes[:, :, None] == expert_ids[None, None, :]).astype(jnp.float32), axis=1
    )
    gates = jnp.concatenate(
        [jnp.broadcast_to(shared_gate[None], (SHARED, length)), (router_probs * chosen).T], axis=0
    )
    hidden = shared_expert_down_weight.shape[1] // SHARED
    rank = up_a.shape[1]

    def fill(rows):
        return jnp.pad(to_low(rows), ((0, NARROW - rows.shape[0]), (0, 0)))

    def fill_last(rows):
        return jnp.pad(to_low(rows), ((0, 0), (0, 0), (0, NARROW - rows.shape[2])))

    cotangent_down = ADAPTER_SCALE * contract_last(cotangent, down_b)
    mid_up = to_low(matmul(normed_two, up_a))
    grad_mid_down = shared_gate[:, None] * cotangent_down
    up_extra = ADAPTER_SCALE * up_b.reshape(rank, 2, SHARED, hidden).transpose(2, 1, 3, 0)
    shared_block = shared_expert_gate_up_weight.reshape(-1, 2, SHARED, hidden)
    shared_up = lax.all_gather(
        shared_block.transpose(2, 1, 3, 0).reshape(-1, depth), "dp", axis=1, tiled=True
    )
    up_block = jnp.transpose(routed_gate_up_weight, (1, 2, 3, 0))
    (
        normed_two_part,
        gate_grads,
        mid_down_part,
        grad_mid_up_part,
        grad_down_a_parts,
        grad_up_b_parts,
        act_rows,
    ) = experts_step(
        normed_two.T,
        gates,
        fill(mid_up.T),
        fill(grad_mid_down.T),
        fill_last(up_extra.reshape(SHARED, 2 * hidden, rank)),
        fill_last(down_a.reshape(SHARED, hidden, rank)),
        shared_up,
        up_block.reshape(-1, depth),
        open_rows,
        5,
    )
    grad_down_a_local = grad_down_a_parts[:, :rank].transpose(1, 0, 2).reshape(rank, -1)
    grad_up_b_local = (
        grad_up_b_parts[:, :rank]
        .reshape(SHARED, rank, 2, hidden)
        .transpose(1, 2, 0, 3)
        .reshape(rank, 2, -1)
    )
    narrow_part = jnp.concatenate(
        [
            gate_grads[SHARED:],
            jnp.sum(gate_grads[:SHARED], axis=0, keepdims=True),
            grad_mid_up_part[:rank],
            mid_down_part[:rank],
        ],
        axis=0,
    ).T
    grad_normed_two, narrow_sum, combined_part = summed_and_down(
        normed_two_part, narrow_part, act_rows, down_rows, 2
    )
    mid_down = to_low(narrow_sum[:, EXPERTS + 1 + rank :])
    grad_mid_up = to_low(narrow_sum[:, EXPERTS + 1 : EXPERTS + 1 + rank])
    grad_probs = chosen * narrow_sum[:, :EXPERTS]
    grad_logits = to_low(
        router_probs * (grad_probs - jnp.sum(router_probs * grad_probs, axis=1, keepdims=True))
    )
    shared_gate_grad = narrow_sum[:, EXPERTS] + jnp.sum(
        mid_down.astype(jnp.float32) * cotangent_down, axis=1
    )
    grad_gate_logit = to_low(shared_gate_grad * shared_gate * (1.0 - shared_gate))
    grad_normed_two = grad_normed_two + contract_last(
        jnp.concatenate([grad_logits, grad_gate_logit[:, None], grad_mid_up], axis=1),
        jnp.concatenate([router_full, gate_full[:, None], up_a], axis=1),
    )
    grad_hidden = cot_f + norm_ffn_pull(grad_normed_two)[0]
    grad_branch = to_low(grad_hidden)
    grad_mid_out = to_low(ADAPTER_SCALE * contract_last(grad_branch, out_b))
    grad_attended = to_low(
        matmul(grad_branch, output_rows) + contract_last(grad_mid_out, out_a)
    )
    combined_here, grad_qkv = summed_and_attended_back(
        combined_part, (query, keys, values, grad_attended) + places, 3
    )
    extra_here = ADAPTER_SCALE * matmul(mid_down, down_b)
    output = to_low(hidden_here + combined_here + shared_gate[:, None] * extra_here)
    grad_down_b_local = ADAPTER_SCALE * contract_first(
        to_low(shared_gate[:, None] * mid_down.astype(jnp.float32)), cotangent
    )
    grad_up_a_local = contract_first(grad_mid_up, normed_two)
    grad_out_b_local = ADAPTER_SCALE * contract_first(mid_out, grad_branch)
    grad_out_a_local = contract_first(grad_mid_out, attended)
    grad_mid_qkv_part = ADAPTER_SCALE * jnp.einsum(
        "stf,rsf->tr", grad_qkv, qkv_b, preferred_element_type=jnp.float32
    )
    grad_qkv_b_local = ADAPTER_SCALE * jnp.einsum(
        "tr,stf->rsf", mid_qkv, grad_qkv, preferred_element_type=jnp.float32
    )
    normed_part = jnp.einsum(
        "stf,rsf->tr",
        grad_qkv,
        qkv_rows,
        preferred_element_type=jnp.float32,
    )
    grad_normed, grad_mid_qkv_f = summed(normed_part, grad_mid_qkv_part, 4)
    grad_mid_qkv_here = to_low(grad_mid_qkv_f)
    grad_normed = grad_normed + contract_last(grad_mid_qkv_here, qkv_a)
    norm_attn_pull = jax.vjp(lambda rows: rms_scale(rows, gain_attn_f), tokens_f)[1]
    grad_tokens_here = to_low(grad_hidden + norm_attn_pull(grad_normed)[0])
    grad_tokens, grad_mid_qkv = (grad_tokens_here, grad_mid_qkv_here)
    grad_qkv_a_local = contract_first(grad_mid_qkv, normed)
    everyone = small_rows[:: small_rows.shape[0] // lax.axis_size("dp"), EXPERTS + 1]
    marker = to_low(
        jnp.arange(ADAPTER_SETS, dtype=jnp.int32)[:, None] == everyone.astype(jnp.int32)[None, :]
    )

    def adapter_sums(local_grads):
        sizes = [local_grad.shape[1] for local_grad in local_grads]
        flat = jnp.concatenate([to_low(local_grad) for local_grad in local_grads], axis=1)
        rows = lax.all_gather(flat, "dp", axis=0, tiled=False)
        totals = jnp.einsum("cj,jrn->crn", marker, rows, preferred_element_type=jnp.float32)
        results, start = [], 0
        for size in sizes:
            results.append(totals[:, :, start : start + size])
            start += size
        return results

    def flipped(total):
        return jnp.swapaxes(total, 1, 2)

    def opened(total, count):
        return total.reshape(total.shape[0], total.shape[1], count, -1)

    total_out_a, total_out_b, total_up_a, total_up_b, total_down_a, total_down_b = adapter_sums(
        [
            grad_out_a_local,
            grad_out_b_local,
            grad_up_a_local,
            grad_up_b_local.reshape(grad_up_b_local.shape[0], -1),
            grad_down_a_local,
            grad_down_b_local,
        ]
    )
    total_qkv_b, total_qkv_a = adapter_sums(
        [grad_qkv_b_local.reshape(grad_qkv_b_local.shape[0], -1), grad_qkv_a_local]
    )
    return (
        output,
        grad_tokens,
        flipped(total_qkv_a),
        opened(total_qkv_b, 3),
        flipped(total_out_a),
        total_out_b,
        flipped(total_up_a),
        opened(total_up_b, 2),
        flipped(total_down_a),
        total_down_b,
    )


def solution(mesh):
    return jax.shard_map(
        body,
        mesh=mesh,
        in_specs=(
            P("dp", None),
            P("dp", None),
            P(),
            P("dp", None, "tensor"),
            P(None, "tensor"),
            P("dp", "tensor"),
            P(),
            P("dp", None),
            P("dp"),
            P("dp", None, None, "tensor"),
            P("dp", None, "tensor"),
            P("dp", None, "tensor"),
            P("dp", "tensor"),
            P("dp", None),
            P("dp"),
            P("dp", None),
            P(),
            P(None, None, None, "tensor"),
            P(None, "tensor", None),
            P(),
            P(),
            P(None, None, None, "tensor"),
            P(None, "tensor", None),
            P(),
        ),
        out_specs=(
            P("dp", None),
            P("dp", None),
            P(),
            P(None, None, None, "tensor"),
            P(None, "tensor", None),
            P(),
            P(),
            P(None, None, None, "tensor"),
            P(None, "tensor", None),
            P(),
        ),
        check_vma=False,
    )
```

```python
import functools

import jax
import jax.numpy as jnp
from jax import lax
from jax.experimental import pallas as pl
from jax.experimental.pallas import tpu as pltpu
from jax.sharding import PartitionSpec as P

HEAD_SIZE = 128
TOP = 4
EXPERTS = 16
ADAPTER_SETS = 8
PIECE = 256


EPSILON = 1e-06
THETA = 1000000.0
ADAPTER_SCALE = 2.0
MASKED = -1e30
QUERY_ROWS = 256
NARROW = 128
MESH = pl.DeviceIdType.MESH
SUM_CHUNKS = 16
AHEAD = 2
SHARED = 4
HALVES = 2


def matmul(left_side, right_side):
    return jnp.dot(left_side, right_side, preferred_element_type=jnp.float32)


def contract_last(left_side, right_side):
    return lax.dot_general(
        left_side, right_side, (((1,), (1,)), ((), ())), preferred_element_type=jnp.float32
    )


def contract_first(left_side, right_side):
    return lax.dot_general(
        left_side, right_side, (((0,), (0,)), ((), ())), preferred_element_type=jnp.float32
    )


def to_low(values):
    return values.astype(jnp.bfloat16)


def rms_scale(values, gain_values):
    return (
        values * lax.rsqrt(jnp.mean(values * values, axis=1, keepdims=True) + EPSILON) * gain_values
    )


def rope_tables(length):
    half_size = HEAD_SIZE // 2
    frequency = THETA ** (-jnp.arange(half_size, dtype=jnp.float32) * 2.0 / HEAD_SIZE)
    angles = jnp.arange(length, dtype=jnp.float32)[:, None] * frequency[None, :]
    return (
        jnp.concatenate([jnp.cos(angles)] * 2, axis=1),
        jnp.concatenate([jnp.sin(angles)] * 2, axis=1),
    )


def piece_index(positions, starts):
    inside = (positions[:, None] >= starts[None, :]) & (
        positions[:, None] < starts[None, :] + PIECE
    )
    labels = jnp.arange(starts.shape[0], dtype=jnp.int32)[None, :] + 1
    return jnp.sum(jnp.where(inside, labels, 0), axis=1) - 1


def line_sum_steps(
    chunks, wide_ref, narrow_ref, total_ref, part_ref, from_end, pair_sum, from_pair, semaphores
):
    place = lax.axis_index("tensor")
    width = wide_ref.shape[1]
    rows = part_ref.shape[0] // chunks
    inner = (place == 1) | (place == 2)
    end = (place == 0) | (place == 3)
    mate = jnp.where(place < 2, 1 - place, 5 - place)
    other = jnp.where(inner, 3 - place, place)

    def span(chunk):
        return pl.ds(pl.multiple_of(chunk * rows, rows), rows)

    def copy(source, target, chunk, lane, device):
        return pltpu.make_async_remote_copy(
            source.at[span(chunk)],
            target.at[span(chunk)],
            semaphores.at[2 * lane, chunk],
            semaphores.at[2 * lane + 1, chunk],
            device_id={"tensor": device},
            device_id_type=MESH,
        )

    def inward(chunk):
        return copy(part_ref, from_end, chunk, 0, mate)

    def across(chunk):
        return copy(pair_sum, from_pair, chunk, 1, other)

    def outward(chunk):
        return copy(total_ref, total_ref, chunk, 2, mate)

    def add(left_ref, right_ref, out_ref, chunk):
        out_ref[span(chunk)] = to_low(
            left_ref[span(chunk)].astype(jnp.float32) + right_ref[span(chunk)].astype(jnp.float32)
        )

    def stage(chunk):
        part_ref[span(chunk), :width] = to_low(wide_ref[span(chunk)])
        if narrow_ref is not None:
            part_ref[span(chunk), width:] = narrow_ref[span(chunk)]

    def greet(extra):
        barrier = pltpu.get_barrier_semaphore()
        pl.semaphore_signal(barrier, inc=1, device_id={"tensor": mate}, device_id_type=MESH)

        @pl.when(inner)
        def _():
            pl.semaphore_signal(barrier, inc=1, device_id={"tensor": other}, device_id_type=MESH)
            pl.semaphore_wait(barrier, 2 + extra)

        @pl.when(end)
        def _():
            pl.semaphore_wait(barrier, 1 + extra)

    def begin():
        @pl.when(end)
        def _():
            @pl.loop(0, chunks)
            def _(chunk):
                stage(chunk)
                inward(chunk).start()

    def advance(step):
        @pl.when(inner & (step < chunks))
        def _():
            stage(step)
            inward(step).wait_recv()
            add(part_ref, from_end, pair_sum, step)
            across(step).start()

        @pl.when(inner & (step > 0) & (step <= chunks))
        def _():
            across(step - 1).wait_recv()
            add(pair_sum, from_pair, total_ref, step - 1)
            outward(step - 1).start()

    def finish():
        @pl.when(end)
        def _():
            @pl.loop(0, chunks)
            def _(chunk):
                inward(chunk).wait_send()
                outward(chunk).wait_recv()

        @pl.when(inner)
        def _():
            @pl.loop(0, chunks)
            def _(chunk):
                across(chunk).wait_send()
                outward(chunk).wait_send()

    return greet, begin, advance, finish


def plane_gather_steps(pieces, block_ref, whole_ref, semaphores, local_semaphore):
    spot = lax.axis_index("dp")
    depth = block_ref.shape[1]
    rows = block_ref.shape[0] // pieces
    core_mate = spot + 1 - 2 * (spot % 2)
    x_mate = spot + 2 - 4 * ((spot // 2) % 2)
    y_mate = spot + 4 - 8 * (spot // 4)
    x_y_mate = x_mate + 4 - 8 * (spot // 4)
    lanes = {
        "core": (spot, core_mate, 0, 1),
        "x": (spot, x_mate, 0, 1),
        "y": (spot, y_mate, 0, 1),
        "x_core": (x_mate, core_mate, 0, 1),
        "x_y": (x_mate, y_mate, 0, 2),
        "y_core": (y_mate, core_mate, 0, 1),
        "y_x": (y_mate, x_mate, 1, 2),
        "xy_core": (x_y_mate, core_mate, 0, 2),
        "yx_core": (x_y_mate, core_mate, 1, 2),
    }
    order = list(lanes)

    def send(name, piece):
        owner, device, part, parts = lanes[name]
        lane = order.index(name)
        span = pl.ds(
            pl.multiple_of(piece * rows + part * (rows // parts), rows // parts), rows // parts
        )
        columns = pl.ds(pl.multiple_of(owner * depth, depth), depth)
        target = whole_ref.at[span, columns]
        source = block_ref.at[span] if name in ("core", "x", "y") else target
        return pltpu.make_async_remote_copy(
            source,
            target,
            semaphores.at[2 * lane, piece],
            semaphores.at[2 * lane + 1, piece],
            device_id={"dp": device},
            device_id_type=MESH,
        )

    def own():
        columns = pl.ds(pl.multiple_of(spot * depth, depth), depth)
        return pltpu.make_async_copy(block_ref, whole_ref.at[:, columns], local_semaphore)

    def greet():
        barrier = pltpu.get_barrier_semaphore()
        for device in (core_mate, x_mate, y_mate):
            pl.semaphore_signal(barrier, inc=1, device_id={"dp": device}, device_id_type=MESH)

    def launch(piece):
        @pl.when((piece >= 0) & (piece < pieces))
        def _():
            for name in ("x", "y", "core"):
                send(name, piece).start()

    def forward(piece):
        @pl.when((piece >= 0) & (piece < pieces))
        def _():
            send("x", piece).wait_recv()
            send("x_y", piece).start()
            send("x_core", piece).start()
            send("y", piece).wait_recv()
            send("y_x", piece).start()
            send("y_core", piece).start()

    def hand_over(piece):
        @pl.when((piece >= 0) & (piece < pieces))
        def _():
            send("x_y", piece).wait_recv()
            send("xy_core", piece).start()
            send("y_x", piece).wait_recv()
            send("yx_core", piece).start()

    def advance(step):
        launch(step)
        forward(step - AHEAD)
        hand_over(step - 2 * AHEAD)

    def load(first, count, target, semaphore):
        span = pl.ds(pl.multiple_of(first, rows), count)

        def columns(owner):
            return pl.ds(pl.multiple_of(owner * depth, depth), depth)

        here = columns(spot)
        copies = [pltpu.make_async_copy(block_ref.at[span], target.at[:, here], semaphore)]
        for shift in range(1, 8):
            there = columns((spot + shift) % 8)
            copies.append(
                pltpu.make_async_copy(
                    whole_ref.at[span, there], target.at[:, there], semaphore
                )
            )
        return copies

    def load_wait(count, target, semaphore):
        pltpu.make_async_copy(whole_ref.at[pl.ds(0, count)], target, semaphore).wait()

    def arrive(piece):
        for name in ("core", "x_core", "y_core", "xy_core", "yx_core"):
            send(name, piece).wait_recv()

    def finish():
        @pl.loop(0, pieces)
        def _(piece):
            for name in order:
                send(name, piece).wait_send()

    return greet, advance, arrive, finish, own, load, load_wait, (launch, forward, hand_over)


def line_sum_kernel(chunks, *refs):
    greet, begin, advance, finish = line_sum_steps(chunks, *refs)
    greet(0)
    begin()

    @pl.loop(0, chunks + 1)
    def _(step):
        advance(step)

    finish()


def sum_gather_kernel(
    chunks,
    pieces,
    wide_ref,
    narrow_ref,
    block_ref,
    cotangent_ref,
    total_ref,
    whole_ref,
    open_ref,
    *scratch,
):
    greet, begin, advance, finish = line_sum_steps(
        chunks, wide_ref, narrow_ref, total_ref, *scratch[:5]
    )
    gather_semaphores, local_semaphores, piece_rows, open_rows = scratch[5:]
    gather_greet, gather_advance, gather_arrive, gather_finish, own, load, load_wait, _ = (
        plane_gather_steps(
            pieces, block_ref, whole_ref, gather_semaphores, local_semaphores.at[0]
        )
    )
    rows = piece_rows.shape[1]

    def store(piece):
        slot = piece % 2
        span = pl.ds(pl.multiple_of(piece * rows, rows), rows)
        return pltpu.make_async_copy(
            open_rows.at[slot], open_ref.at[span], local_semaphores.at[3 + slot]
        )

    gather_greet()
    greet(3)
    begin()
    own().start()

    @pl.loop(0, max(chunks + 1, pieces + 3 * AHEAD + 1))
    def _(step):
        gather_advance(step)
        advance(step)

        @pl.when((step >= 3 * AHEAD) & (step < pieces + 3 * AHEAD))
        def _():
            piece = step - 3 * AHEAD
            gather_arrive(piece)
            slot = piece % 2
            for copy in load(piece * rows, rows, piece_rows.at[slot], local_semaphores.at[1 + slot]):
                copy.start()

        @pl.when((step > 3 * AHEAD) & (step <= pieces + 3 * AHEAD))
        def _():
            piece = step - 3 * AHEAD - 1
            slot = piece % 2
            load_wait(rows, piece_rows.at[slot], local_semaphores.at[1 + slot])

            @pl.when(piece >= 2)
            def _():
                store(piece - 2).wait()

            open_rows[piece % 2] = to_low(matmul(piece_rows[piece % 2], cotangent_ref[...]))
            store(piece).start()

    store(pieces - 2).wait()
    store(pieces - 1).wait()
    own().wait()
    gather_finish()
    finish()


def sum_down_kernel(
    chunks, wide_ref, narrow_ref, act_ref, down_ref, total_ref, out_ref, *scratch
):
    greet, begin, advance, finish = line_sum_steps(
        chunks, wide_ref, narrow_ref, total_ref, *scratch[:5]
    )
    semaphores, act_rows, down_rows, out_rows = scratch[5:]
    rows = act_rows.shape[1]
    blocks = down_ref.shape[0] // rows

    def loads(block):
        slot = block % 2
        span = pl.ds(pl.multiple_of(block * rows, rows), rows)
        return [
            pltpu.make_async_copy(act_ref.at[span], act_rows.at[slot], semaphores.at[0, slot]),
            pltpu.make_async_copy(down_ref.at[span], down_rows.at[slot], semaphores.at[1, slot]),
        ]

    for load in loads(0):
        load.start()
    greet(0)
    begin()
    out_rows[...] = jnp.zeros_like(out_rows)

    @pl.loop(0, max(blocks, chunks + 1))
    def _(step):
        advance(step)

        @pl.when(step < blocks)
        def _():
            @pl.when(step + 1 < blocks)
            def _():
                for load in loads(step + 1):
                    load.start()

            for load in loads(step):
                load.wait()
            tile = min(256, out_rows.shape[0])

            @pl.loop(0, out_rows.shape[0] // tile)
            def _(index):
                span = pl.ds(pl.multiple_of(index * tile, tile), tile)
                out_rows[span] += contract_first(
                    act_rows[step % 2, :, span], down_rows[step % 2]
                )

    out_ref[...] = to_low(out_rows[...])
    finish()


def attend_back_sum_kernel(chunks, wide_ref, *refs):
    inputs, (total_ref, grad_qkv_ref), scratch = refs[:8], refs[8:10], refs[10:]
    greet, begin, advance, finish = line_sum_steps(
        chunks, wide_ref, None, total_ref, *scratch[:5]
    )
    head_block = attend_back_steps(*inputs, grad_qkv_ref, *scratch[5:])
    length, heads_width = inputs[0].shape
    heads, blocks = heads_width // HEAD_SIZE, length // QUERY_ROWS
    greet(0)
    begin()

    @pl.loop(0, heads)
    def _(head):
        for block in range(blocks):
            advance(head * blocks + block)
            head_block(head, block * QUERY_ROWS)

    @pl.loop(heads * blocks, max(heads * blocks, chunks + 1))
    def _(step):
        advance(step)

    finish()


def on_line():
    return lax.axis_size("tensor") == 4


def in_plane():
    return lax.axis_size("dp") == 8


def in_vmem(count):
    return [pl.BlockSpec(memory_space=pltpu.VMEM)] * count


def in_hbm(count):
    return [pl.BlockSpec(memory_space=pltpu.HBM)] * count


def sum_scratch(shape):
    return [pltpu.VMEM(shape, jnp.bfloat16)] * 4 + [pltpu.SemaphoreType.DMA((6, SUM_CHUNKS))]


def narrowed(narrow_part):
    pad = jnp.zeros((narrow_part.shape[0], NARROW - narrow_part.shape[1]), jnp.bfloat16)
    return jnp.concatenate([to_low(narrow_part), pad], axis=1)


def parts_of(total, wide_part, narrow_part):
    width, small = wide_part.shape[1], narrow_part.shape[1]
    total = total.astype(jnp.float32)
    return total[:, :width], total[:, width : width + small]


def summed(wide_part, narrow_part, number):
    if not on_line():
        return lax.psum((wide_part, narrow_part), "tensor")
    shape = (wide_part.shape[0], wide_part.shape[1] + NARROW)
    total = pl.pallas_call(
        functools.partial(line_sum_kernel, SUM_CHUNKS),
        out_shape=jax.ShapeDtypeStruct(shape, jnp.bfloat16),
        in_specs=in_vmem(2),
        out_specs=pl.BlockSpec(memory_space=pltpu.VMEM),
        scratch_shapes=sum_scratch(shape),
        compiler_params=pltpu.CompilerParams(
            collective_id=number, has_side_effects=True, vmem_limit_bytes=48 * 2**20
        ),
        cost_estimate=pl.CostEstimate(flops=0, bytes_accessed=300 * 2**20, transcendentals=0),
    )(wide_part, narrowed(narrow_part))
    return parts_of(total, wide_part, narrow_part)


def summed_and_gathered(wide_part, narrow_part, block, cotangents, number):
    length, width = wide_part.shape
    if not (on_line() and in_plane()):
        whole = lax.all_gather(block, "dp", axis=1, tiled=True)
        open_rows = to_low(matmul(whole, cotangents))
        return summed(wide_part, narrow_part, number) + (whole, open_rows)
    shape = (length, width + NARROW)
    pieces = SHARED + EXPERTS
    rows = block.shape[0] // pieces
    total, whole, open_rows = pl.pallas_call(
        functools.partial(sum_gather_kernel, SUM_CHUNKS, pieces),
        out_shape=[
            jax.ShapeDtypeStruct(shape, jnp.bfloat16),
            jax.ShapeDtypeStruct((block.shape[0], width), jnp.bfloat16),
            jax.ShapeDtypeStruct((block.shape[0], length), jnp.bfloat16),
        ],
        in_specs=in_vmem(2) + in_hbm(1) + in_vmem(1),
        out_specs=in_vmem(1) + in_hbm(2),
        scratch_shapes=sum_scratch(shape)
        + [
            pltpu.SemaphoreType.DMA((18, pieces)),
            pltpu.SemaphoreType.DMA((5,)),
            pltpu.VMEM((2, rows, width), jnp.bfloat16),
            pltpu.VMEM((2, rows, length), jnp.bfloat16),
        ],
        compiler_params=pltpu.CompilerParams(
            collective_id=number, has_side_effects=True, vmem_limit_bytes=58 * 2**20
        ),
        cost_estimate=pl.CostEstimate(flops=0, bytes_accessed=360 * 2**20, transcendentals=0),
    )(wide_part, narrowed(narrow_part), block, cotangents)
    return parts_of(total, wide_part, narrow_part) + (whole, open_rows)


def summed_and_down(wide_part, narrow_part, act_rows, down_rows, number):
    length, width = wide_part.shape
    if not on_line():
        out = contract_first(act_rows, down_rows)
        return summed(wide_part, narrow_part, number) + (out,)
    shape = (length, width + NARROW)
    rows = 2 * down_rows.shape[0] // (SHARED + EXPERTS)
    total, out = pl.pallas_call(
        functools.partial(sum_down_kernel, SUM_CHUNKS),
        out_shape=[
            jax.ShapeDtypeStruct(shape, jnp.bfloat16),
            jax.ShapeDtypeStruct((length, width), jnp.bfloat16),
        ],
        in_specs=in_vmem(2) + in_hbm(2),
        out_specs=in_vmem(2),
        scratch_shapes=sum_scratch(shape)
        + [
            pltpu.SemaphoreType.DMA((2, 2)),
            pltpu.VMEM((2, rows, length), jnp.bfloat16),
            pltpu.VMEM((2, rows, width), jnp.bfloat16),
            pltpu.VMEM((length, width), jnp.float32),
        ],
        compiler_params=pltpu.CompilerParams(
            collective_id=number, has_side_effects=True, vmem_limit_bytes=58 * 2**20
        ),
        cost_estimate=pl.CostEstimate(flops=0, bytes_accessed=300 * 2**20, transcendentals=0),
    )(wide_part, narrowed(narrow_part), act_rows, down_rows)
    return parts_of(total, wide_part, narrow_part) + (out,)


def block_mask(first, rows, extent, row_piece_ref, col_piece_ref):
    row_place = lax.broadcasted_iota(jnp.int32, (rows, extent), 0) + first
    col_place = lax.broadcasted_iota(jnp.int32, (rows, extent), 1)
    row_piece = row_piece_ref[first : first + rows, 0:1]
    together = (row_piece == col_piece_ref[0:1, :extent]) & (row_piece >= 0)
    return (col_place <= row_place) | together


def block_probs(query_rows, keys, allowed):
    scores = jnp.where(allowed, contract_last(query_rows, keys) * HEAD_SIZE**-0.5, MASKED)
    raised = jnp.exp(scores - jnp.max(scores, axis=1, keepdims=True))
    return raised * (1.0 / jnp.sum(raised, axis=1, keepdims=True))


def half_turn(values, signed_sine):
    return pltpu.roll(values, HEAD_SIZE // 2, 1) * signed_sine


def attend_kernel(
    qkv_ref,
    cosine_ref,
    sine_ref,
    row_piece_ref,
    col_piece_ref,
    query_ref,
    keys_ref,
    values_ref,
    attended_ref,
):
    length = qkv_ref.shape[1]

    @pl.loop(0, qkv_ref.shape[2] // HEAD_SIZE)
    def _(head):
        column = pl.ds(pl.multiple_of(head * HEAD_SIZE, HEAD_SIZE), HEAD_SIZE)
        for source, target in ((0, query_ref), (1, keys_ref)):
            raw = qkv_ref[source, :, column]
            target[:, column] = to_low(raw * cosine_ref[...] + half_turn(raw, sine_ref[...]))
        values_ref[:, column] = to_low(qkv_ref[2, :, column])
        for first in range(0, length, QUERY_ROWS):
            extent = min(length, first + QUERY_ROWS + PIECE)
            allowed = block_mask(first, QUERY_ROWS, extent, row_piece_ref, col_piece_ref)
            probs = block_probs(
                query_ref[first : first + QUERY_ROWS, column], keys_ref[:extent, column], allowed
            )
            attended_ref[first : first + QUERY_ROWS, column] = to_low(
                matmul(to_low(probs), values_ref[:extent, column])
            )


def attend(qkv, cosine, signed_sine, row_piece, col_piece):
    length, heads_width = qkv.shape[1:]
    shape = jax.ShapeDtypeStruct((length, heads_width), jnp.bfloat16)
    return pl.pallas_call(
        attend_kernel,
        out_shape=[shape] * 4,
        in_specs=[pl.BlockSpec(memory_space=pltpu.VMEM)] * 5,
        out_specs=[pl.BlockSpec(memory_space=pltpu.VMEM)] * 4,
        compiler_params=pltpu.CompilerParams(vmem_limit_bytes=48 * 2**20),
        cost_estimate=pl.CostEstimate(
            flops=4 * length * length * heads_width,
            bytes_accessed=16 * 2**20,
            transcendentals=length * length * heads_width // HEAD_SIZE,
        ),
    )(qkv, cosine, signed_sine, row_piece, col_piece)


def attend_back_steps(
    query_ref,
    keys_ref,
    values_ref,
    grad_ref,
    cosine_ref,
    sine_ref,
    row_piece_ref,
    col_piece_ref,
    grad_qkv_ref,
    grad_keys,
    grad_values,
):
    length = query_ref.shape[0]

    def turned_back(grad, first):
        span = slice(first, first + grad.shape[0])
        scaled = grad * HEAD_SIZE**-0.5
        return to_low(scaled * cosine_ref[span] - half_turn(scaled, sine_ref[span]))

    def head_block(head, first):
        column = pl.ds(pl.multiple_of(head * HEAD_SIZE, HEAD_SIZE), HEAD_SIZE)
        span = slice(first, first + QUERY_ROWS)
        extent = min(length, first + QUERY_ROWS + PIECE)
        if first == 0:
            grad_keys[...] = jnp.zeros_like(grad_keys)
            grad_values[...] = jnp.zeros_like(grad_values)
        allowed = block_mask(first, QUERY_ROWS, extent, row_piece_ref, col_piece_ref)
        query_rows = query_ref[span, column]
        keys = keys_ref[:extent, column]
        grad_rows = grad_ref[span, column]
        probs = block_probs(query_rows, keys, allowed)
        grad_probs = contract_last(grad_rows, values_ref[:extent, column])
        shift = jnp.sum(probs * grad_probs, axis=1, keepdims=True)
        grad_scores = to_low(probs * (grad_probs - shift))
        grad_values[:extent] += contract_first(to_low(probs), grad_rows)
        grad_keys[:extent] += contract_first(grad_scores, query_rows)
        grad_qkv_ref[0, span, column] = turned_back(matmul(grad_scores, keys), first)
        if first + QUERY_ROWS >= length:
            grad_qkv_ref[1, :, column] = turned_back(grad_keys[...], 0)
            grad_qkv_ref[2, :, column] = to_low(grad_values[...])

    return head_block


def attend_back_kernel(*refs):
    head_block = attend_back_steps(*refs)

    @pl.loop(0, refs[0].shape[1] // HEAD_SIZE)
    def _(head):
        for first in range(0, refs[0].shape[0], QUERY_ROWS):
            head_block(head, first)


def attend_back(query, keys, values, grads, cosine, signed_sine, row_piece, col_piece):
    length, heads_width = query.shape
    return pl.pallas_call(
        attend_back_kernel,
        out_shape=jax.ShapeDtypeStruct((3, length, heads_width), jnp.bfloat16),
        in_specs=[pl.BlockSpec(memory_space=pltpu.VMEM)] * 8,
        out_specs=pl.BlockSpec(memory_space=pltpu.VMEM),
        scratch_shapes=[pltpu.VMEM((length, HEAD_SIZE), jnp.float32)] * 2,
        compiler_params=pltpu.CompilerParams(vmem_limit_bytes=48 * 2**20),
        cost_estimate=pl.CostEstimate(
            flops=10 * length * length * heads_width,
            bytes_accessed=16 * 2**20,
            transcendentals=length * length * heads_width // HEAD_SIZE,
        ),
    )(query, keys, values, grads, cosine, signed_sine, row_piece, col_piece)


def summed_and_attended_back(wide_part, attention_inputs, number):
    if not on_line():
        return lax.psum(wide_part, "tensor"), attend_back(*attention_inputs)
    shape = wide_part.shape
    length, heads_width = attention_inputs[0].shape
    return pl.pallas_call(
        functools.partial(attend_back_sum_kernel, SUM_CHUNKS),
        out_shape=[
            jax.ShapeDtypeStruct(shape, jnp.bfloat16),
            jax.ShapeDtypeStruct((3, length, heads_width), jnp.bfloat16),
        ],
        in_specs=in_vmem(1 + len(attention_inputs)),
        out_specs=in_vmem(2),
        scratch_shapes=sum_scratch(shape) + [pltpu.VMEM((length, HEAD_SIZE), jnp.float32)] * 2,
        compiler_params=pltpu.CompilerParams(
            collective_id=number, has_side_effects=True, vmem_limit_bytes=58 * 2**20
        ),
        cost_estimate=pl.CostEstimate(flops=0, bytes_accessed=300 * 2**20, transcendentals=0),
    )(wide_part, *attention_inputs)


def hidden_step(gate_up, open_part, gate_row, extra):
    hidden = open_part.shape[0]
    gate_half, up_half = gate_up[:hidden], gate_up[hidden:]
    squashed = 1.0 / (1.0 + jnp.exp(-gate_half))
    act = to_low(gate_half * squashed * up_half)
    act_f = act.astype(jnp.float32)
    gate_grad = jnp.sum(act_f * open_part, axis=0, keepdims=True)
    grad_act = gate_row * open_part
    if extra is not None:
        grad_act = grad_act + extra
    grad_gate = to_low(grad_act * up_half * squashed * (1.0 + gate_half * (1.0 - squashed)))
    grad_up = to_low(grad_act * gate_half * squashed)
    return act, to_low(gate_row * act_f), gate_grad, grad_gate, grad_up


def experts_kernel(
    pieces,
    inputs_ref,
    gate_ref,
    mid_up_ref,
    grad_mid_ref,
    up_extra_ref,
    down_extra_ref,
    shared_up_ref,
    block_ref,
    open_ref,
    grad_ref,
    gate_grad_ref,
    mid_down_ref,
    grad_mid_up_ref,
    grad_down_a_ref,
    grad_up_b_ref,
    act_ref,
    whole_ref,
    grad_total,
    up_rows,
    open_rows,
    act_rows,
    grad_rows,
    gather_semaphores,
    semaphores,
):
    greet, _, arrive, finish, _, load, load_wait, (launch, forward, hand_over) = (
        plane_gather_steps(pieces, block_ref, whole_ref, gather_semaphores, None)
    )
    hidden = open_rows.shape[1]
    count = SHARED + EXPERTS
    each = pieces // EXPERTS

    def span(expert, rows):
        return pl.ds(pl.multiple_of(expert * rows, rows), rows)

    def load_open(expert):
        slot = expert % 2
        return pltpu.make_async_copy(
            open_ref.at[span(expert, hidden)], open_rows.at[slot], semaphores.at[1, slot]
        )

    def load_shared(expert):
        slot = expert % 2
        return pltpu.make_async_copy(
            shared_up_ref.at[span(expert, 2 * hidden)], up_rows.at[slot], semaphores.at[2, slot]
        )

    def store_act(expert):
        slot = expert % 2
        return pltpu.make_async_copy(
            act_rows.at[slot], act_ref.at[span(expert, hidden)], semaphores.at[3, slot]
        )

    def advance(expert):
        for part in range(each):
            launch(each * expert + part)
        for part in range(each):
            forward(each * (expert - 2) + part + 1)
        for part in range(each):
            hand_over(each * (expert - 3) + part + 1)

        @pl.when(expert + 1 < count)
        def _():
            load_open(expert + 1).start()

        @pl.when(expert + 1 < SHARED)
        def _():
            load_shared(expert + 1).start()

        @pl.when((expert + 1 >= SHARED) & (expert + 1 < count))
        def _():
            for part in range(each):
                arrive(each * (expert + 1 - SHARED) + part)
            slot = (expert + 1) % 2
            first = (expert + 1 - SHARED) * 2 * hidden
            for copy in load(first, 2 * hidden, up_rows.at[slot], semaphores.at[2, slot]):
                copy.start()

        load_open(expert).wait()
        load_wait(2 * hidden, up_rows.at[expert % 2], semaphores.at[2, expert % 2])

        @pl.when(expert >= 2)
        def _():
            store_act(expert - 2).wait()

    def compute(expert, shared):
        slot = expert % 2
        gate_up = matmul(up_rows[slot], inputs_ref[...])
        extra = None
        if shared:
            gate_up = gate_up + matmul(up_extra_ref[expert], mid_up_ref[...])
            extra = matmul(down_extra_ref[expert], grad_mid_ref[...])
        act, act_gated, gate_grad, grad_gate, grad_up = hidden_step(
            gate_up,
            open_rows[slot].astype(jnp.float32),
            gate_ref[pl.ds(expert, 1)],
            extra,
        )
        gate_grad_ref[pl.ds(expert, 1)] = gate_grad
        act_rows[slot] = act_gated
        grad_rows[:hidden] = grad_gate
        grad_rows[hidden:] = grad_up
        store_act(expert).start()
        grad_total[...] += contract_first(grad_rows[...], up_rows[slot])
        if shared:
            mid_down_ref[...] += contract_first(down_extra_ref[expert], act)
            grad_mid_up_ref[...] += contract_first(up_extra_ref[expert], grad_rows[...])
            grad_down_a_ref[expert] = contract_last(grad_mid_ref[...], act)
            grad_up_b_ref[expert] = ADAPTER_SCALE * contract_last(mid_up_ref[...], grad_rows[...])

    greet()
    pl.semaphore_wait(pltpu.get_barrier_semaphore(), 3)
    load_open(0).start()
    load_shared(0).start()
    grad_total[...] = jnp.zeros_like(grad_total)
    mid_down_ref[...] = jnp.zeros_like(mid_down_ref)
    grad_mid_up_ref[...] = jnp.zeros_like(grad_mid_up_ref)

    @pl.loop(0, SHARED)
    def _(expert):
        advance(expert)
        compute(expert, True)

    @pl.loop(SHARED, count)
    def _(expert):
        advance(expert)
        compute(expert, False)

    grad_ref[...] = to_low(grad_total[...])
    store_act(count - 2).wait()
    store_act(count - 1).wait()
    finish()


def experts_plain(inputs, gates, mid_up, grad_mid, up_extra, down_extra, up_rows, open_rows):
    count, length = gates.shape
    hidden = open_rows.shape[0] // count
    width = inputs.shape[0]
    grad_total = jnp.zeros((length, width), jnp.float32)
    act_parts, gate_grads, down_parts, up_parts = [], [], [], []
    mid_down = jnp.zeros((NARROW, length), jnp.float32)
    grad_mid_up = jnp.zeros((NARROW, length), jnp.float32)
    for expert in range(count):
        weights = up_rows[2 * hidden * expert : 2 * hidden * (expert + 1)]
        gate_up = matmul(weights, inputs)
        extra = None
        if expert < SHARED:
            gate_up = gate_up + matmul(up_extra[expert], mid_up)
            extra = matmul(down_extra[expert], grad_mid)
        act, act_gated, gate_grad, grad_gate, grad_up = hidden_step(
            gate_up,
            open_rows[hidden * expert : hidden * (expert + 1)].astype(jnp.float32),
            gates[expert : expert + 1],
            extra,
        )
        grad = jnp.concatenate([grad_gate, grad_up], axis=0)
        act_parts.append(act_gated)
        gate_grads.append(gate_grad)
        grad_total = grad_total + contract_first(grad, weights)
        if expert < SHARED:
            mid_down = mid_down + contract_first(down_extra[expert], act)
            grad_mid_up = grad_mid_up + contract_first(up_extra[expert], grad)
            down_parts.append(contract_last(grad_mid, act))
            up_parts.append(ADAPTER_SCALE * contract_last(mid_up, grad))
    return (
        grad_total,
        jnp.concatenate(gate_grads, axis=0),
        mid_down,
        grad_mid_up,
        jnp.stack(down_parts),
        jnp.stack(up_parts),
        jnp.concatenate(act_parts, axis=0),
    )


def experts_step(
    inputs, gates, mid_up, grad_mid, up_extra, down_extra, shared_up, block, open_rows, number
):
    width, length = inputs.shape
    count = SHARED + EXPERTS
    hidden = open_rows.shape[0] // count
    if not in_plane():
        whole = lax.all_gather(block, "dp", axis=1, tiled=True)
        up_rows = jnp.concatenate([shared_up, whole], axis=0)
        return experts_plain(
            inputs, gates, mid_up, grad_mid, up_extra, down_extra, up_rows, open_rows
        )
    pieces = HALVES * EXPERTS
    return pl.pallas_call(
        functools.partial(experts_kernel, pieces),
        in_specs=in_vmem(6) + in_hbm(3),
        out_specs=in_vmem(6) + in_hbm(2),
        out_shape=[
            jax.ShapeDtypeStruct((length, width), jnp.bfloat16),
            jax.ShapeDtypeStruct((count, length), jnp.float32),
            jax.ShapeDtypeStruct((NARROW, length), jnp.float32),
            jax.ShapeDtypeStruct((NARROW, length), jnp.float32),
            jax.ShapeDtypeStruct((SHARED, NARROW, hidden), jnp.float32),
            jax.ShapeDtypeStruct((SHARED, NARROW, 2 * hidden), jnp.float32),
            jax.ShapeDtypeStruct((count * hidden, length), jnp.bfloat16),
            jax.ShapeDtypeStruct((EXPERTS * 2 * hidden, width), jnp.bfloat16),
        ],
        scratch_shapes=[
            pltpu.VMEM((length, width), jnp.float32),
            pltpu.VMEM((2, 2 * hidden, width), jnp.bfloat16),
            pltpu.VMEM((2, hidden, length), jnp.bfloat16),
            pltpu.VMEM((2, hidden, length), jnp.bfloat16),
            pltpu.VMEM((2 * hidden, length), jnp.bfloat16),
            pltpu.SemaphoreType.DMA((18, pieces)),
            pltpu.SemaphoreType.DMA((4, 2)),
        ],
        compiler_params=pltpu.CompilerParams(
            collective_id=number, has_side_effects=True, vmem_limit_bytes=60 * 2**20
        ),
        cost_estimate=pl.CostEstimate(flops=0, bytes_accessed=600 * 2**20, transcendentals=0),
    )(inputs, gates, mid_up, grad_mid, up_extra, down_extra, shared_up, block, open_rows)[:7]


def gathered(weight):
    return lax.all_gather(weight, "dp", axis=0, tiled=True)


def body(
    tokens,
    cotangent,
    attention_norm_gain,
    query_key_value_weight,
    query_key_value_bias,
    output_projection_weight,
    feedforward_norm_gain,
    router_matrix,
    shared_expert_gate_weight,
    routed_gate_up_weight,
    routed_down_weight,
    shared_expert_gate_up_weight,
    shared_expert_down_weight,
    routes,
    sequence_adapter_index,
    picture_piece_starts,
    adapter_query_key_value_lower,
    adapter_query_key_value_upper,
    adapter_output_lower,
    adapter_output_upper,
    adapter_shared_up_lower,
    adapter_shared_up_upper,
    adapter_shared_down_lower,
    adapter_shared_down_upper,
):
    length, width = tokens.shape
    set_id = sequence_adapter_index[0]
    starts = picture_piece_starts[0]

    def selected_experts(adapter_entry):
        return lax.dynamic_index_in_dim(adapter_entry, set_id, 0, keepdims=False)

    qkv_a, qkv_b, out_a, out_b = (
        selected_experts(adapter_query_key_value_lower),
        selected_experts(adapter_query_key_value_upper),
        selected_experts(adapter_output_lower),
        selected_experts(adapter_output_upper),
    )
    up_a, up_b, down_a, down_b = (
        selected_experts(adapter_shared_up_lower),
        selected_experts(adapter_shared_up_upper),
        selected_experts(adapter_shared_down_lower),
        selected_experts(adapter_shared_down_upper),
    )
    gain_attn_f = attention_norm_gain.astype(jnp.float32)
    gain_ffn_f = feedforward_norm_gain.astype(jnp.float32)
    tokens_f = tokens.astype(jnp.float32)
    normed = to_low(rms_scale(tokens_f, gain_attn_f))
    mid_qkv = to_low(matmul(normed, qkv_a))
    attention_rows = gathered(
        jnp.concatenate([query_key_value_weight, output_projection_weight[:, None]], axis=1)
    )
    qkv_rows, output_rows = attention_rows[:, :3], attention_rows[:, 3]
    qkv_sum = jnp.einsum("tr,rsf->stf", normed, qkv_rows, preferred_element_type=jnp.float32)
    qkv_sum = qkv_sum + query_key_value_bias.astype(jnp.float32)[:, None, :]
    qkv_sum = qkv_sum + ADAPTER_SCALE * jnp.einsum(
        "tr,rsf->stf", mid_qkv, qkv_b, preferred_element_type=jnp.float32
    )
    cosine, sine_table = rope_tables(length)
    signs = jnp.where(jnp.arange(HEAD_SIZE) < HEAD_SIZE // 2, -1.0, 1.0)
    piece_ids = piece_index(jnp.arange(length, dtype=jnp.int32), starts)
    places = (cosine, sine_table * signs[None, :], piece_ids[:, None], piece_ids[None, :])
    query, keys, values, attended = attend(qkv_sum, *places)
    branch_part = contract_last(attended, output_rows)
    down_block = jnp.transpose(routed_down_weight, (1, 2, 0))
    depth = down_block.shape[2]
    down_block = jnp.concatenate(
        [shared_expert_down_weight.T, down_block.reshape(-1, depth)], axis=0
    )
    branch_here, mid_out_here_f, down_rows, open_rows = summed_and_gathered(
        branch_part,
        matmul(attended, out_a),
        down_block,
        cotangent.T,
        1,
    )
    mid_out = to_low(mid_out_here_f)
    hidden_here = tokens_f + branch_here + ADAPTER_SCALE * matmul(mid_out, out_b)
    normed_two_here_f, norm_ffn_pull = jax.vjp(
        lambda rows: rms_scale(rows, gain_ffn_f), hidden_here
    )
    normed_two_here = to_low(normed_two_here_f)
    normed_two = normed_two_here
    cot_f = cotangent.astype(jnp.float32)
    small_rows = gathered(
        jnp.concatenate(
            [
                router_matrix,
                shared_expert_gate_weight[:, None],
                jnp.full_like(shared_expert_gate_weight, set_id)[:, None],
            ],
            axis=1,
        )
    )
    router_full, gate_full = small_rows[:, :EXPERTS], small_rows[:, EXPERTS]
    router_probs = jax.nn.softmax(matmul(normed_two, router_full), axis=-1)
    shared_gate = jax.nn.sigmoid(matmul(normed_two, gate_full))
    expert_ids = jnp.arange(EXPERTS, dtype=jnp.int32)
    chosen = jnp.sum(
        (routes[:, :, None] == expert_ids[None, None, :]).astype(jnp.float32), axis=1
    )
    gates = jnp.concatenate(
        [jnp.broadcast_to(shared_gate[None], (SHARED, length)), (router_probs * chosen).T], axis=0
    )
    hidden = shared_expert_down_weight.shape[1] // SHARED
    rank = up_a.shape[1]

    def fill(rows):
        return jnp.pad(to_low(rows), ((0, NARROW - rows.shape[0]), (0, 0)))

    def fill_last(rows):
        return jnp.pad(to_low(rows), ((0, 0), (0, 0), (0, NARROW - rows.shape[2])))

    cotangent_down = ADAPTER_SCALE * contract_last(cotangent, down_b)
    mid_up = to_low(matmul(normed_two, up_a))
    grad_mid_down = shared_gate[:, None] * cotangent_down
    up_extra = ADAPTER_SCALE * up_b.reshape(rank, 2, SHARED, hidden).transpose(2, 1, 3, 0)
    shared_block = shared_expert_gate_up_weight.reshape(-1, 2, SHARED, hidden)
    shared_up = lax.all_gather(
        shared_block.transpose(2, 1, 3, 0).reshape(-1, depth), "dp", axis=1, tiled=True
    )
    up_block = jnp.transpose(routed_gate_up_weight, (1, 2, 3, 0))
    (
        normed_two_part,
        gate_grads,
        mid_down_part,
        grad_mid_up_part,
        grad_down_a_parts,
        grad_up_b_parts,
        act_rows,
    ) = experts_step(
        normed_two.T,
        gates,
        fill(mid_up.T),
        fill(grad_mid_down.T),
        fill_last(up_extra.reshape(SHARED, 2 * hidden, rank)),
        fill_last(down_a.reshape(SHARED, hidden, rank)),
        shared_up,
        up_block.reshape(-1, depth),
        open_rows,
        5,
    )
    grad_down_a_local = grad_down_a_parts[:, :rank].transpose(1, 0, 2).reshape(rank, -1)
    grad_up_b_local = (
        grad_up_b_parts[:, :rank]
        .reshape(SHARED, rank, 2, hidden)
        .transpose(1, 2, 0, 3)
        .reshape(rank, 2, -1)
    )
    narrow_part = jnp.concatenate(
        [
            gate_grads[SHARED:],
            jnp.sum(gate_grads[:SHARED], axis=0, keepdims=True),
            grad_mid_up_part[:rank],
            mid_down_part[:rank],
        ],
        axis=0,
    ).T
    grad_normed_two, narrow_sum, combined_part = summed_and_down(
        normed_two_part, narrow_part, act_rows, down_rows, 2
    )
    mid_down = to_low(narrow_sum[:, EXPERTS + 1 + rank :])
    grad_mid_up = to_low(narrow_sum[:, EXPERTS + 1 : EXPERTS + 1 + rank])
    grad_probs = chosen * narrow_sum[:, :EXPERTS]
    grad_logits = to_low(
        router_probs * (grad_probs - jnp.sum(router_probs * grad_probs, axis=1, keepdims=True))
    )
    shared_gate_grad = narrow_sum[:, EXPERTS] + jnp.sum(
        mid_down.astype(jnp.float32) * cotangent_down, axis=1
    )
    grad_gate_logit = to_low(shared_gate_grad * shared_gate * (1.0 - shared_gate))
    grad_normed_two = grad_normed_two + contract_last(
        jnp.concatenate([grad_logits, grad_gate_logit[:, None], grad_mid_up], axis=1),
        jnp.concatenate([router_full, gate_full[:, None], up_a], axis=1),
    )
    grad_hidden = cot_f + norm_ffn_pull(grad_normed_two)[0]
    grad_branch = to_low(grad_hidden)
    grad_mid_out = to_low(ADAPTER_SCALE * contract_last(grad_branch, out_b))
    grad_attended = to_low(
        matmul(grad_branch, output_rows) + contract_last(grad_mid_out, out_a)
    )
    combined_here, grad_qkv = summed_and_attended_back(
        combined_part, (query, keys, values, grad_attended) + places, 3
    )
    extra_here = ADAPTER_SCALE * matmul(mid_down, down_b)
    output = to_low(hidden_here + combined_here + shared_gate[:, None] * extra_here)
    grad_down_b_local = ADAPTER_SCALE * contract_first(
        to_low(shared_gate[:, None] * mid_down.astype(jnp.float32)), cotangent
    )
    grad_up_a_local = contract_first(grad_mid_up, normed_two)
    grad_out_b_local = ADAPTER_SCALE * contract_first(mid_out, grad_branch)
    grad_out_a_local = contract_first(grad_mid_out, attended)
    grad_mid_qkv_part = ADAPTER_SCALE * jnp.einsum(
        "stf,rsf->tr", grad_qkv, qkv_b, preferred_element_type=jnp.float32
    )
    grad_qkv_b_local = ADAPTER_SCALE * jnp.einsum(
        "tr,stf->rsf", mid_qkv, grad_qkv, preferred_element_type=jnp.float32
    )
    normed_part = jnp.einsum(
        "stf,rsf->tr",
        grad_qkv,
        qkv_rows,
        preferred_element_type=jnp.float32,
    )
    grad_normed, grad_mid_qkv_f = summed(normed_part, grad_mid_qkv_part, 4)
    grad_mid_qkv_here = to_low(grad_mid_qkv_f)
    grad_normed = grad_normed + contract_last(grad_mid_qkv_here, qkv_a)
    norm_attn_pull = jax.vjp(lambda rows: rms_scale(rows, gain_attn_f), tokens_f)[1]
    grad_tokens_here = to_low(grad_hidden + norm_attn_pull(grad_normed)[0])
    grad_tokens, grad_mid_qkv = (grad_tokens_here, grad_mid_qkv_here)
    grad_qkv_a_local = contract_first(grad_mid_qkv, normed)
    everyone = small_rows[:: small_rows.shape[0] // lax.axis_size("dp"), EXPERTS + 1]
    marker = to_low(
        jnp.arange(ADAPTER_SETS, dtype=jnp.int32)[:, None] == everyone.astype(jnp.int32)[None, :]
    )

    def adapter_sums(local_grads):
        sizes = [local_grad.shape[1] for local_grad in local_grads]
        flat = jnp.concatenate([to_low(local_grad) for local_grad in local_grads], axis=1)
        rows = lax.all_gather(flat, "dp", axis=0, tiled=False)
        totals = jnp.einsum("cj,jrn->crn", marker, rows, preferred_element_type=jnp.float32)
        results, start = [], 0
        for size in sizes:
            results.append(totals[:, :, start : start + size])
            start += size
        return results

    def flipped(total):
        return jnp.swapaxes(total, 1, 2)

    def opened(total, count):
        return total.reshape(total.shape[0], total.shape[1], count, -1)

    total_out_a, total_out_b, total_up_a, total_up_b, total_down_a, total_down_b = adapter_sums(
        [
            grad_out_a_local,
            grad_out_b_local,
            grad_up_a_local,
            grad_up_b_local.reshape(grad_up_b_local.shape[0], -1),
            grad_down_a_local,
            grad_down_b_local,
        ]
    )
    total_qkv_b, total_qkv_a = adapter_sums(
        [grad_qkv_b_local.reshape(grad_qkv_b_local.shape[0], -1), grad_qkv_a_local]
    )
    return (
        output,
        grad_tokens,
        flipped(total_qkv_a),
        opened(total_qkv_b, 3),
        flipped(total_out_a),
        total_out_b,
        flipped(total_up_a),
        opened(total_up_b, 2),
        flipped(total_down_a),
        total_down_b,
    )


def solution(mesh):
    return jax.shard_map(
        body,
        mesh=mesh,
        in_specs=(
            P("dp", None),
            P("dp", None),
            P(),
            P("dp", None, "tensor"),
            P(None, "tensor"),
            P("dp", "tensor"),
            P(),
            P("dp", None),
            P("dp"),
            P("dp", None, None, "tensor"),
            P("dp", None, "tensor"),
            P("dp", None, "tensor"),
            P("dp", "tensor"),
            P("dp", None),
            P("dp"),
            P("dp", None),
            P(),
            P(None, None, None, "tensor"),
            P(None, "tensor", None),
            P(),
            P(),
            P(None, None, None, "tensor"),
            P(None, "tensor", None),
            P(),
        ),
        out_specs=(
            P("dp", None),
            P("dp", None),
            P(),
            P(None, None, None, "tensor"),
            P(None, "tensor", None),
            P(),
            P(),
            P(None, None, None, "tensor"),
            P(None, "tensor", None),
            P(),
        ),
        check_vma=False,
    )
```

```python
import functools

import jax
import jax.numpy as jnp
from jax import lax
from jax.experimental import pallas as pl
from jax.experimental.pallas import tpu as pltpu
from jax.sharding import PartitionSpec as P

HEAD_SIZE = 128
TOP = 4
EXPERTS = 16
ADAPTER_SETS = 8
PIECE = 256


EPSILON = 1e-06
THETA = 1000000.0
ADAPTER_SCALE = 2.0
MASKED = -1e30
QUERY_ROWS = 256
NARROW = 128
MESH = pl.DeviceIdType.MESH
SUM_CHUNKS = 16
AHEAD = 1
LEAD = 2
SHARED = 4
HALVES = 1
READY = 6


def matmul(left_side, right_side):
    return jnp.dot(left_side, right_side, preferred_element_type=jnp.float32)


def contract_last(left_side, right_side):
    return lax.dot_general(
        left_side, right_side, (((1,), (1,)), ((), ())), preferred_element_type=jnp.float32
    )


def contract_first(left_side, right_side):
    return lax.dot_general(
        left_side, right_side, (((0,), (0,)), ((), ())), preferred_element_type=jnp.float32
    )


def to_low(values):
    return values.astype(jnp.bfloat16)


def rms_scale(values, gain_values):
    return (
        values * lax.rsqrt(jnp.mean(values * values, axis=1, keepdims=True) + EPSILON) * gain_values
    )


def rope_tables(length):
    half_size = HEAD_SIZE // 2
    frequency = THETA ** (-jnp.arange(half_size, dtype=jnp.float32) * 2.0 / HEAD_SIZE)
    angles = jnp.arange(length, dtype=jnp.float32)[:, None] * frequency[None, :]
    return (
        jnp.concatenate([jnp.cos(angles)] * 2, axis=1),
        jnp.concatenate([jnp.sin(angles)] * 2, axis=1),
    )


def piece_index(positions, starts):
    inside = (positions[:, None] >= starts[None, :]) & (
        positions[:, None] < starts[None, :] + PIECE
    )
    labels = jnp.arange(starts.shape[0], dtype=jnp.int32)[None, :] + 1
    return jnp.sum(jnp.where(inside, labels, 0), axis=1) - 1


def line_sum_steps(
    chunks, wide_ref, narrow_ref, total_ref, part_ref, from_end, pair_sum, from_pair, semaphores
):
    place = lax.axis_index("tensor")
    width = wide_ref.shape[1]
    rows = part_ref.shape[0] // chunks
    inner = (place == 1) | (place == 2)
    end = (place == 0) | (place == 3)
    mate = jnp.where(place < 2, 1 - place, 5 - place)
    other = jnp.where(inner, 3 - place, place)

    def span(chunk):
        return pl.ds(pl.multiple_of(chunk * rows, rows), rows)

    def copy(source, target, chunk, lane, device):
        return pltpu.make_async_remote_copy(
            source.at[span(chunk)],
            target.at[span(chunk)],
            semaphores.at[2 * lane, chunk],
            semaphores.at[2 * lane + 1, chunk],
            device_id={"tensor": device},
            device_id_type=MESH,
        )

    def inward(chunk):
        return copy(part_ref, from_end, chunk, 0, mate)

    def across(chunk):
        return copy(pair_sum, from_pair, chunk, 1, other)

    def outward(chunk):
        return copy(total_ref, total_ref, chunk, 2, mate)

    def add(left_ref, right_ref, out_ref, chunk):
        out_ref[span(chunk)] = to_low(
            left_ref[span(chunk)].astype(jnp.float32) + right_ref[span(chunk)].astype(jnp.float32)
        )

    def stage(chunk):
        part_ref[span(chunk), :width] = to_low(wide_ref[span(chunk)])
        if narrow_ref is not None:
            part_ref[span(chunk), width:] = narrow_ref[span(chunk)]

    def greet(extra):
        barrier = pltpu.get_barrier_semaphore()
        pl.semaphore_signal(barrier, inc=1, device_id={"tensor": mate}, device_id_type=MESH)

        @pl.when(inner)
        def _():
            pl.semaphore_signal(barrier, inc=1, device_id={"tensor": other}, device_id_type=MESH)
            pl.semaphore_wait(barrier, 2 + extra)

        @pl.when(end)
        def _():
            pl.semaphore_wait(barrier, 1 + extra)

    def begin():
        @pl.when(end)
        def _():
            @pl.loop(0, chunks)
            def _(chunk):
                stage(chunk)
                inward(chunk).start()

    def advance(step):
        @pl.when(inner & (step < chunks))
        def _():
            stage(step)
            inward(step).wait_recv()
            add(part_ref, from_end, pair_sum, step)
            across(step).start()

        @pl.when(inner & (step > 0) & (step <= chunks))
        def _():
            across(step - 1).wait_recv()
            add(pair_sum, from_pair, total_ref, step - 1)
            outward(step - 1).start()

    def finish():
        @pl.when(end)
        def _():
            @pl.loop(0, chunks)
            def _(chunk):
                inward(chunk).wait_send()
                outward(chunk).wait_recv()

        @pl.when(inner)
        def _():
            @pl.loop(0, chunks)
            def _(chunk):
                across(chunk).wait_send()
                outward(chunk).wait_send()

    return greet, begin, advance, finish


def plane_gather_steps(pieces, block_ref, whole_ref, semaphores, local_semaphore):
    spot = lax.axis_index("dp")
    depth = block_ref.shape[1]
    rows = block_ref.shape[0] // pieces
    core_mate = spot + 1 - 2 * (spot % 2)
    x_mate = spot + 2 - 4 * ((spot // 2) % 2)
    y_mate = spot + 4 - 8 * (spot // 4)
    x_y_mate = x_mate + 4 - 8 * (spot // 4)
    lanes = {
        "core": (spot, core_mate, 0, 1),
        "x": (spot, x_mate, 0, 1),
        "y": (spot, y_mate, 0, 1),
        "x_core": (x_mate, core_mate, 0, 1),
        "x_y": (x_mate, y_mate, 0, 2),
        "y_core": (y_mate, core_mate, 0, 1),
        "y_x": (y_mate, x_mate, 1, 2),
        "xy_core": (x_y_mate, core_mate, 0, 2),
        "yx_core": (x_y_mate, core_mate, 1, 2),
    }
    order = list(lanes)

    def send(name, piece):
        owner, device, part, parts = lanes[name]
        lane = order.index(name)
        span = pl.ds(
            pl.multiple_of(piece * rows + part * (rows // parts), rows // parts), rows // parts
        )
        columns = pl.ds(pl.multiple_of(owner * depth, depth), depth)
        target = whole_ref.at[span, columns]
        source = block_ref.at[span] if name in ("core", "x", "y") else target
        return pltpu.make_async_remote_copy(
            source,
            target,
            semaphores.at[2 * lane, piece],
            semaphores.at[2 * lane + 1, piece],
            device_id={"dp": device},
            device_id_type=MESH,
        )

    def own():
        columns = pl.ds(pl.multiple_of(spot * depth, depth), depth)
        return pltpu.make_async_copy(block_ref, whole_ref.at[:, columns], local_semaphore)

    def greet():
        barrier = pltpu.get_barrier_semaphore()
        for device in (core_mate, x_mate, y_mate):
            pl.semaphore_signal(barrier, inc=1, device_id={"dp": device}, device_id_type=MESH)

    def launch(piece):
        @pl.when((piece >= 0) & (piece < pieces))
        def _():
            for name in ("x", "y", "core"):
                send(name, piece).start()

    def forward(piece):
        @pl.when((piece >= 0) & (piece < pieces))
        def _():
            send("x", piece).wait_recv()
            send("x_y", piece).start()
            send("x_core", piece).start()
            send("y", piece).wait_recv()
            send("y_x", piece).start()
            send("y_core", piece).start()

    def hand_over(piece):
        @pl.when((piece >= 0) & (piece < pieces))
        def _():
            send("x_y", piece).wait_recv()
            send("xy_core", piece).start()
            send("y_x", piece).wait_recv()
            send("yx_core", piece).start()

    def advance(step):
        launch(step + LEAD)
        forward(step - AHEAD)
        hand_over(step - 2 * AHEAD)

    def load(first, count, target, semaphore):
        span = pl.ds(pl.multiple_of(first, rows), count)

        def columns(owner):
            return pl.ds(pl.multiple_of(owner * depth, depth), depth)

        here = columns(spot)
        copies = [pltpu.make_async_copy(block_ref.at[span], target.at[:, here], semaphore)]
        for shift in range(1, 8):
            there = columns((spot + shift) % 8)
            copies.append(
                pltpu.make_async_copy(
                    whole_ref.at[span, there], target.at[:, there], semaphore
                )
            )
        return copies

    def load_wait(count, target, semaphore):
        pltpu.make_async_copy(whole_ref.at[pl.ds(0, count)], target, semaphore).wait()

    def arrive(piece):
        for name in ("core", "x_core", "y_core", "xy_core", "yx_core"):
            send(name, piece).wait_recv()

    def finish():
        @pl.loop(0, pieces)
        def _(piece):
            for name in order:
                send(name, piece).wait_send()

    return greet, advance, arrive, finish, own, load, load_wait, (launch, forward, hand_over)


def line_sum_kernel(chunks, *refs):
    greet, begin, advance, finish = line_sum_steps(chunks, *refs)
    greet(0)
    begin()

    @pl.loop(0, chunks + 1)
    def _(step):
        advance(step)

    finish()


def sum_gather_kernel(
    chunks,
    pieces,
    wide_ref,
    narrow_ref,
    block_ref,
    cotangent_ref,
    total_ref,
    whole_ref,
    open_ref,
    *scratch,
):
    greet, begin, advance, finish = line_sum_steps(
        chunks, wide_ref, narrow_ref, total_ref, *scratch[:5]
    )
    gather_semaphores, local_semaphores, piece_rows, open_rows = scratch[5:]
    gather_greet, gather_advance, gather_arrive, gather_finish, own, load, load_wait, stages = (
        plane_gather_steps(
            pieces, block_ref, whole_ref, gather_semaphores, local_semaphores.at[0]
        )
    )
    rows = piece_rows.shape[1]

    def store(piece):
        slot = piece % 2
        span = pl.ds(pl.multiple_of(piece * rows, rows), rows)
        return pltpu.make_async_copy(
            open_rows.at[slot], open_ref.at[span], local_semaphores.at[3 + slot]
        )

    gather_greet()
    greet(3)
    begin()
    own().start()

    @pl.loop(0, LEAD)
    def _(piece):
        stages[0](piece)

    @pl.loop(0, max(chunks + 1, pieces + 3 * AHEAD + 1))
    def _(step):
        gather_advance(step)
        advance(step)

        @pl.when((step >= 3 * AHEAD) & (step < pieces + 3 * AHEAD))
        def _():
            piece = step - 3 * AHEAD
            gather_arrive(piece)
            slot = piece % 2
            for copy in load(piece * rows, rows, piece_rows.at[slot], local_semaphores.at[1 + slot]):
                copy.start()

        @pl.when((step > 3 * AHEAD) & (step <= pieces + 3 * AHEAD))
        def _():
            piece = step - 3 * AHEAD - 1
            slot = piece % 2
            load_wait(rows, piece_rows.at[slot], local_semaphores.at[1 + slot])

            @pl.when(piece >= 2)
            def _():
                store(piece - 2).wait()

            open_rows[piece % 2] = to_low(matmul(piece_rows[piece % 2], cotangent_ref[...]))
            store(piece).start()

    store(pieces - 2).wait()
    store(pieces - 1).wait()
    own().wait()
    gather_finish()
    finish()


def sum_down_kernel(
    chunks, wide_ref, narrow_ref, act_ref, down_ref, total_ref, out_ref, *scratch
):
    greet, begin, advance, finish = line_sum_steps(
        chunks, wide_ref, narrow_ref, total_ref, *scratch[:5]
    )
    semaphores, act_rows, down_rows, out_rows = scratch[5:]
    rows = act_rows.shape[1]
    blocks = down_ref.shape[0] // rows

    def loads(block):
        slot = block % 2
        span = pl.ds(pl.multiple_of(block * rows, rows), rows)
        return [
            pltpu.make_async_copy(act_ref.at[span], act_rows.at[slot], semaphores.at[0, slot]),
            pltpu.make_async_copy(down_ref.at[span], down_rows.at[slot], semaphores.at[1, slot]),
        ]

    for load in loads(0):
        load.start()
    greet(0)
    begin()
    out_rows[...] = jnp.zeros_like(out_rows)

    @pl.loop(0, max(blocks, chunks + 1))
    def _(step):
        advance(step)

        @pl.when(step < blocks)
        def _():
            @pl.when(step + 1 < blocks)
            def _():
                for load in loads(step + 1):
                    load.start()

            for load in loads(step):
                load.wait()
            tile = min(256, out_rows.shape[0])

            @pl.loop(0, out_rows.shape[0] // tile)
            def _(index):
                span = pl.ds(pl.multiple_of(index * tile, tile), tile)
                out_rows[span] += contract_first(
                    act_rows[step % 2, :, span], down_rows[step % 2]
                )

    out_ref[...] = to_low(out_rows[...])
    finish()


def attend_back_sum_kernel(chunks, wide_ref, *refs):
    inputs, (total_ref, grad_qkv_ref), scratch = refs[:8], refs[8:10], refs[10:]
    greet, begin, advance, finish = line_sum_steps(
        chunks, wide_ref, None, total_ref, *scratch[:5]
    )
    head_block = attend_back_steps(*inputs, grad_qkv_ref, *scratch[5:])
    length, heads_width = inputs[0].shape
    heads, blocks = heads_width // HEAD_SIZE, length // QUERY_ROWS
    greet(0)
    begin()

    @pl.loop(0, heads)
    def _(head):
        for block in range(blocks):
            advance(head * blocks + block)
            head_block(head, block * QUERY_ROWS)

    @pl.loop(heads * blocks, max(heads * blocks, chunks + 1))
    def _(step):
        advance(step)

    finish()


def on_line():
    return lax.axis_size("tensor") == 4


def in_plane():
    return lax.axis_size("dp") == 8


def in_vmem(count):
    return [pl.BlockSpec(memory_space=pltpu.VMEM)] * count


def in_hbm(count):
    return [pl.BlockSpec(memory_space=pltpu.HBM)] * count


def sum_scratch(shape):
    return [pltpu.VMEM(shape, jnp.bfloat16)] * 4 + [pltpu.SemaphoreType.DMA((6, SUM_CHUNKS))]


def narrowed(narrow_part):
    pad = jnp.zeros((narrow_part.shape[0], NARROW - narrow_part.shape[1]), jnp.bfloat16)
    return jnp.concatenate([to_low(narrow_part), pad], axis=1)


def parts_of(total, wide_part, narrow_part):
    width, small = wide_part.shape[1], narrow_part.shape[1]
    total = total.astype(jnp.float32)
    return total[:, :width], total[:, width : width + small]


def summed(wide_part, narrow_part, number):
    if not on_line():
        return lax.psum((wide_part, narrow_part), "tensor")
    shape = (wide_part.shape[0], wide_part.shape[1] + NARROW)
    total = pl.pallas_call(
        functools.partial(line_sum_kernel, SUM_CHUNKS),
        out_shape=jax.ShapeDtypeStruct(shape, jnp.bfloat16),
        in_specs=in_vmem(2),
        out_specs=pl.BlockSpec(memory_space=pltpu.VMEM),
        scratch_shapes=sum_scratch(shape),
        compiler_params=pltpu.CompilerParams(
            collective_id=number, has_side_effects=True, vmem_limit_bytes=48 * 2**20
        ),
        cost_estimate=pl.CostEstimate(flops=0, bytes_accessed=300 * 2**20, transcendentals=0),
    )(wide_part, narrowed(narrow_part))
    return parts_of(total, wide_part, narrow_part)


def summed_and_gathered(wide_part, narrow_part, block, cotangents, number):
    length, width = wide_part.shape
    if not (on_line() and in_plane()):
        whole = lax.all_gather(block, "dp", axis=1, tiled=True)
        open_rows = to_low(matmul(whole, cotangents))
        return summed(wide_part, narrow_part, number) + (whole, open_rows)
    shape = (length, width + NARROW)
    pieces = SHARED + EXPERTS
    rows = block.shape[0] // pieces
    total, whole, open_rows = pl.pallas_call(
        functools.partial(sum_gather_kernel, SUM_CHUNKS, pieces),
        out_shape=[
            jax.ShapeDtypeStruct(shape, jnp.bfloat16),
            jax.ShapeDtypeStruct((block.shape[0], width), jnp.bfloat16),
            jax.ShapeDtypeStruct((block.shape[0], length), jnp.bfloat16),
        ],
        in_specs=in_vmem(2) + in_hbm(1) + in_vmem(1),
        out_specs=in_vmem(1) + in_hbm(2),
        scratch_shapes=sum_scratch(shape)
        + [
            pltpu.SemaphoreType.DMA((18, pieces)),
            pltpu.SemaphoreType.DMA((5,)),
            pltpu.VMEM((2, rows, width), jnp.bfloat16),
            pltpu.VMEM((2, rows, length), jnp.bfloat16),
        ],
        compiler_params=pltpu.CompilerParams(
            collective_id=number, has_side_effects=True, vmem_limit_bytes=58 * 2**20
        ),
        cost_estimate=pl.CostEstimate(flops=0, bytes_accessed=360 * 2**20, transcendentals=0),
    )(wide_part, narrowed(narrow_part), block, cotangents)
    return parts_of(total, wide_part, narrow_part) + (whole, open_rows)


def summed_and_down(wide_part, narrow_part, act_rows, down_rows, number):
    length, width = wide_part.shape
    if not on_line():
        out = contract_first(act_rows, down_rows)
        return summed(wide_part, narrow_part, number) + (out,)
    shape = (length, width + NARROW)
    rows = 2 * down_rows.shape[0] // (SHARED + EXPERTS)
    total, out = pl.pallas_call(
        functools.partial(sum_down_kernel, SUM_CHUNKS),
        out_shape=[
            jax.ShapeDtypeStruct(shape, jnp.bfloat16),
            jax.ShapeDtypeStruct((length, width), jnp.bfloat16),
        ],
        in_specs=in_vmem(2) + in_hbm(2),
        out_specs=in_vmem(2),
        scratch_shapes=sum_scratch(shape)
        + [
            pltpu.SemaphoreType.DMA((2, 2)),
            pltpu.VMEM((2, rows, length), jnp.bfloat16),
            pltpu.VMEM((2, rows, width), jnp.bfloat16),
            pltpu.VMEM((length, width), jnp.float32),
        ],
        compiler_params=pltpu.CompilerParams(
            collective_id=number, has_side_effects=True, vmem_limit_bytes=58 * 2**20
        ),
        cost_estimate=pl.CostEstimate(flops=0, bytes_accessed=300 * 2**20, transcendentals=0),
    )(wide_part, narrowed(narrow_part), act_rows, down_rows)
    return parts_of(total, wide_part, narrow_part) + (out,)


def block_mask(first, rows, extent, row_piece_ref, col_piece_ref):
    row_place = lax.broadcasted_iota(jnp.int32, (rows, extent), 0) + first
    col_place = lax.broadcasted_iota(jnp.int32, (rows, extent), 1)
    row_piece = row_piece_ref[first : first + rows, 0:1]
    together = (row_piece == col_piece_ref[0:1, :extent]) & (row_piece >= 0)
    return (col_place <= row_place) | together


def block_probs(query_rows, keys, allowed):
    scores = jnp.where(allowed, contract_last(query_rows, keys) * HEAD_SIZE**-0.5, MASKED)
    raised = jnp.exp(scores - jnp.max(scores, axis=1, keepdims=True))
    return raised * (1.0 / jnp.sum(raised, axis=1, keepdims=True))


def half_turn(values, signed_sine):
    return pltpu.roll(values, HEAD_SIZE // 2, 1) * signed_sine


def attend_kernel(
    qkv_ref,
    cosine_ref,
    sine_ref,
    row_piece_ref,
    col_piece_ref,
    query_ref,
    keys_ref,
    values_ref,
    attended_ref,
):
    length = qkv_ref.shape[1]

    @pl.loop(0, qkv_ref.shape[2] // HEAD_SIZE)
    def _(head):
        column = pl.ds(pl.multiple_of(head * HEAD_SIZE, HEAD_SIZE), HEAD_SIZE)
        for source, target in ((0, query_ref), (1, keys_ref)):
            raw = qkv_ref[source, :, column]
            target[:, column] = to_low(raw * cosine_ref[...] + half_turn(raw, sine_ref[...]))
        values_ref[:, column] = to_low(qkv_ref[2, :, column])
        for first in range(0, length, QUERY_ROWS):
            extent = min(length, first + QUERY_ROWS + PIECE)
            allowed = block_mask(first, QUERY_ROWS, extent, row_piece_ref, col_piece_ref)
            probs = block_probs(
                query_ref[first : first + QUERY_ROWS, column], keys_ref[:extent, column], allowed
            )
            attended_ref[first : first + QUERY_ROWS, column] = to_low(
                matmul(to_low(probs), values_ref[:extent, column])
            )


def attend(qkv, cosine, signed_sine, row_piece, col_piece):
    length, heads_width = qkv.shape[1:]
    shape = jax.ShapeDtypeStruct((length, heads_width), jnp.bfloat16)
    return pl.pallas_call(
        attend_kernel,
        out_shape=[shape] * 4,
        in_specs=[pl.BlockSpec(memory_space=pltpu.VMEM)] * 5,
        out_specs=[pl.BlockSpec(memory_space=pltpu.VMEM)] * 4,
        compiler_params=pltpu.CompilerParams(vmem_limit_bytes=48 * 2**20),
        cost_estimate=pl.CostEstimate(
            flops=4 * length * length * heads_width,
            bytes_accessed=16 * 2**20,
            transcendentals=length * length * heads_width // HEAD_SIZE,
        ),
    )(qkv, cosine, signed_sine, row_piece, col_piece)


def attend_back_steps(
    query_ref,
    keys_ref,
    values_ref,
    grad_ref,
    cosine_ref,
    sine_ref,
    row_piece_ref,
    col_piece_ref,
    grad_qkv_ref,
    grad_keys,
    grad_values,
):
    length = query_ref.shape[0]

    def turned_back(grad, first):
        span = slice(first, first + grad.shape[0])
        scaled = grad * HEAD_SIZE**-0.5
        return to_low(scaled * cosine_ref[span] - half_turn(scaled, sine_ref[span]))

    def head_block(head, first):
        column = pl.ds(pl.multiple_of(head * HEAD_SIZE, HEAD_SIZE), HEAD_SIZE)
        span = slice(first, first + QUERY_ROWS)
        extent = min(length, first + QUERY_ROWS + PIECE)
        if first == 0:
            grad_keys[...] = jnp.zeros_like(grad_keys)
            grad_values[...] = jnp.zeros_like(grad_values)
        allowed = block_mask(first, QUERY_ROWS, extent, row_piece_ref, col_piece_ref)
        query_rows = query_ref[span, column]
        keys = keys_ref[:extent, column]
        grad_rows = grad_ref[span, column]
        probs = block_probs(query_rows, keys, allowed)
        grad_probs = contract_last(grad_rows, values_ref[:extent, column])
        shift = jnp.sum(probs * grad_probs, axis=1, keepdims=True)
        grad_scores = to_low(probs * (grad_probs - shift))
        grad_values[:extent] += contract_first(to_low(probs), grad_rows)
        grad_keys[:extent] += contract_first(grad_scores, query_rows)
        grad_qkv_ref[0, span, column] = turned_back(matmul(grad_scores, keys), first)
        if first + QUERY_ROWS >= length:
            grad_qkv_ref[1, :, column] = turned_back(grad_keys[...], 0)
            grad_qkv_ref[2, :, column] = to_low(grad_values[...])

    return head_block


def attend_back_kernel(*refs):
    head_block = attend_back_steps(*refs)

    @pl.loop(0, refs[0].shape[1] // HEAD_SIZE)
    def _(head):
        for first in range(0, refs[0].shape[0], QUERY_ROWS):
            head_block(head, first)


def attend_back(query, keys, values, grads, cosine, signed_sine, row_piece, col_piece):
    length, heads_width = query.shape
    return pl.pallas_call(
        attend_back_kernel,
        out_shape=jax.ShapeDtypeStruct((3, length, heads_width), jnp.bfloat16),
        in_specs=[pl.BlockSpec(memory_space=pltpu.VMEM)] * 8,
        out_specs=pl.BlockSpec(memory_space=pltpu.VMEM),
        scratch_shapes=[pltpu.VMEM((length, HEAD_SIZE), jnp.float32)] * 2,
        compiler_params=pltpu.CompilerParams(vmem_limit_bytes=48 * 2**20),
        cost_estimate=pl.CostEstimate(
            flops=10 * length * length * heads_width,
            bytes_accessed=16 * 2**20,
            transcendentals=length * length * heads_width // HEAD_SIZE,
        ),
    )(query, keys, values, grads, cosine, signed_sine, row_piece, col_piece)


def summed_and_attended_back(wide_part, attention_inputs, number):
    if not on_line():
        return lax.psum(wide_part, "tensor"), attend_back(*attention_inputs)
    shape = wide_part.shape
    length, heads_width = attention_inputs[0].shape
    return pl.pallas_call(
        functools.partial(attend_back_sum_kernel, SUM_CHUNKS),
        out_shape=[
            jax.ShapeDtypeStruct(shape, jnp.bfloat16),
            jax.ShapeDtypeStruct((3, length, heads_width), jnp.bfloat16),
        ],
        in_specs=in_vmem(1 + len(attention_inputs)),
        out_specs=in_vmem(2),
        scratch_shapes=sum_scratch(shape) + [pltpu.VMEM((length, HEAD_SIZE), jnp.float32)] * 2,
        compiler_params=pltpu.CompilerParams(
            collective_id=number, has_side_effects=True, vmem_limit_bytes=58 * 2**20
        ),
        cost_estimate=pl.CostEstimate(flops=0, bytes_accessed=300 * 2**20, transcendentals=0),
    )(wide_part, *attention_inputs)


def hidden_step(gate_up, open_part, gate_row, extra):
    hidden = open_part.shape[0]
    gate_half, up_half = gate_up[:hidden], gate_up[hidden:]
    squashed = 1.0 / (1.0 + jnp.exp(-gate_half))
    act = to_low(gate_half * squashed * up_half)
    act_f = act.astype(jnp.float32)
    gate_grad = jnp.sum(act_f * open_part, axis=0, keepdims=True)
    grad_act = gate_row * open_part
    if extra is not None:
        grad_act = grad_act + extra
    grad_gate = to_low(grad_act * up_half * squashed * (1.0 + gate_half * (1.0 - squashed)))
    grad_up = to_low(grad_act * gate_half * squashed)
    return act, to_low(gate_row * act_f), gate_grad, grad_gate, grad_up


def experts_kernel(
    pieces,
    inputs_ref,
    gate_ref,
    mid_up_ref,
    grad_mid_ref,
    up_extra_ref,
    down_extra_ref,
    ready_up_ref,
    block_ref,
    open_ref,
    grad_ref,
    gate_grad_ref,
    mid_down_ref,
    grad_mid_up_ref,
    grad_down_a_ref,
    grad_up_b_ref,
    act_ref,
    whole_ref,
    grad_total,
    up_rows,
    open_rows,
    act_rows,
    grad_rows,
    gather_semaphores,
    semaphores,
):
    greet, _, arrive, finish, _, load, load_wait, (launch, forward, hand_over) = (
        plane_gather_steps(pieces, block_ref, whole_ref, gather_semaphores, None)
    )
    hidden = open_rows.shape[1]
    count = SHARED + EXPERTS
    each = pieces // (count - READY)

    def span(expert, rows):
        return pl.ds(pl.multiple_of(expert * rows, rows), rows)

    def load_open(expert):
        slot = expert % 2
        return pltpu.make_async_copy(
            open_ref.at[span(expert, hidden)], open_rows.at[slot], semaphores.at[1, slot]
        )

    def load_ready(expert):
        slot = expert % 2
        return pltpu.make_async_copy(
            ready_up_ref.at[span(expert, 2 * hidden)], up_rows.at[slot], semaphores.at[2, slot]
        )

    def store_act(expert):
        slot = expert % 2
        return pltpu.make_async_copy(
            act_rows.at[slot], act_ref.at[span(expert, hidden)], semaphores.at[3, slot]
        )

    def advance(expert):
        for part in range(each):
            launch(each * expert + part)
        for part in range(each):
            forward(each * (expert + 3 - READY) + part + 1)
        for part in range(each):
            hand_over(each * (expert + 1 - READY) + part + 1)

        @pl.when(expert + 1 < count)
        def _():
            load_open(expert + 1).start()

        @pl.when(expert + 1 < READY)
        def _():
            load_ready(expert + 1).start()

        @pl.when((expert + 1 >= READY) & (expert + 1 < count))
        def _():
            for part in range(each):
                arrive(each * (expert + 1 - READY) + part)
            slot = (expert + 1) % 2
            first = (expert + 1 - READY) * 2 * hidden
            for copy in load(first, 2 * hidden, up_rows.at[slot], semaphores.at[2, slot]):
                copy.start()

        load_open(expert).wait()
        load_wait(2 * hidden, up_rows.at[expert % 2], semaphores.at[2, expert % 2])

        @pl.when(expert >= 2)
        def _():
            store_act(expert - 2).wait()

    def compute(expert, shared):
        slot = expert % 2
        gate_up = contract_last(up_rows[slot], inputs_ref[...])
        extra = None
        if shared:
            gate_up = gate_up + matmul(up_extra_ref[expert], mid_up_ref[...])
            extra = matmul(down_extra_ref[expert], grad_mid_ref[...])
        act, act_gated, gate_grad, grad_gate, grad_up = hidden_step(
            gate_up,
            open_rows[slot].astype(jnp.float32),
            gate_ref[pl.ds(expert, 1)],
            extra,
        )
        gate_grad_ref[pl.ds(expert, 1)] = gate_grad
        act_rows[slot] = act_gated
        grad_rows[:hidden] = grad_gate
        grad_rows[hidden:] = grad_up
        store_act(expert).start()
        grad_total[...] += contract_first(grad_rows[...], up_rows[slot])
        if shared:
            mid_down_ref[...] += contract_first(down_extra_ref[expert], act)
            grad_mid_up_ref[...] += contract_first(up_extra_ref[expert], grad_rows[...])
            grad_down_a_ref[expert] = contract_last(grad_mid_ref[...], act)
            grad_up_b_ref[expert] = ADAPTER_SCALE * contract_last(mid_up_ref[...], grad_rows[...])

    greet()
    pl.semaphore_wait(pltpu.get_barrier_semaphore(), 3)
    load_open(0).start()
    load_ready(0).start()
    grad_total[...] = jnp.zeros_like(grad_total)
    mid_down_ref[...] = jnp.zeros_like(mid_down_ref)
    grad_mid_up_ref[...] = jnp.zeros_like(grad_mid_up_ref)

    @pl.loop(0, SHARED)
    def _(expert):
        advance(expert)
        compute(expert, True)

    @pl.loop(SHARED, count)
    def _(expert):
        advance(expert)
        compute(expert, False)

    grad_ref[...] = to_low(grad_total[...])
    store_act(count - 2).wait()
    store_act(count - 1).wait()
    finish()


def experts_plain(inputs, gates, mid_up, grad_mid, up_extra, down_extra, up_rows, open_rows):
    count, length = gates.shape
    hidden = open_rows.shape[0] // count
    width = inputs.shape[1]
    grad_total = jnp.zeros((length, width), jnp.float32)
    act_parts, gate_grads, down_parts, up_parts = [], [], [], []
    mid_down = jnp.zeros((NARROW, length), jnp.float32)
    grad_mid_up = jnp.zeros((NARROW, length), jnp.float32)
    for expert in range(count):
        weights = up_rows[2 * hidden * expert : 2 * hidden * (expert + 1)]
        gate_up = contract_last(weights, inputs)
        extra = None
        if expert < SHARED:
            gate_up = gate_up + matmul(up_extra[expert], mid_up)
            extra = matmul(down_extra[expert], grad_mid)
        act, act_gated, gate_grad, grad_gate, grad_up = hidden_step(
            gate_up,
            open_rows[hidden * expert : hidden * (expert + 1)].astype(jnp.float32),
            gates[expert : expert + 1],
            extra,
        )
        grad = jnp.concatenate([grad_gate, grad_up], axis=0)
        act_parts.append(act_gated)
        gate_grads.append(gate_grad)
        grad_total = grad_total + contract_first(grad, weights)
        if expert < SHARED:
            mid_down = mid_down + contract_first(down_extra[expert], act)
            grad_mid_up = grad_mid_up + contract_first(up_extra[expert], grad)
            down_parts.append(contract_last(grad_mid, act))
            up_parts.append(ADAPTER_SCALE * contract_last(mid_up, grad))
    return (
        grad_total,
        jnp.concatenate(gate_grads, axis=0),
        mid_down,
        grad_mid_up,
        jnp.stack(down_parts),
        jnp.stack(up_parts),
        jnp.concatenate(act_parts, axis=0),
    )


def experts_step(
    inputs, gates, mid_up, grad_mid, up_extra, down_extra, ready_up, block, open_rows, number
):
    length, width = inputs.shape
    count = SHARED + EXPERTS
    hidden = open_rows.shape[0] // count
    if not in_plane():
        whole = lax.all_gather(block, "dp", axis=1, tiled=True)
        up_rows = jnp.concatenate([ready_up, whole], axis=0)
        return experts_plain(
            inputs, gates, mid_up, grad_mid, up_extra, down_extra, up_rows, open_rows
        )
    pieces = HALVES * (count - READY)
    return pl.pallas_call(
        functools.partial(experts_kernel, pieces),
        in_specs=in_vmem(6) + in_hbm(3),
        out_specs=in_vmem(6) + in_hbm(2),
        out_shape=[
            jax.ShapeDtypeStruct((length, width), jnp.bfloat16),
            jax.ShapeDtypeStruct((count, length), jnp.float32),
            jax.ShapeDtypeStruct((NARROW, length), jnp.float32),
            jax.ShapeDtypeStruct((NARROW, length), jnp.float32),
            jax.ShapeDtypeStruct((SHARED, NARROW, hidden), jnp.float32),
            jax.ShapeDtypeStruct((SHARED, NARROW, 2 * hidden), jnp.float32),
            jax.ShapeDtypeStruct((count * hidden, length), jnp.bfloat16),
            jax.ShapeDtypeStruct(((count - READY) * 2 * hidden, width), jnp.bfloat16),
        ],
        scratch_shapes=[
            pltpu.VMEM((length, width), jnp.float32),
            pltpu.VMEM((2, 2 * hidden, width), jnp.bfloat16),
            pltpu.VMEM((2, hidden, length), jnp.bfloat16),
            pltpu.VMEM((2, hidden, length), jnp.bfloat16),
            pltpu.VMEM((2 * hidden, length), jnp.bfloat16),
            pltpu.SemaphoreType.DMA((18, pieces)),
            pltpu.SemaphoreType.DMA((4, 2)),
        ],
        compiler_params=pltpu.CompilerParams(
            collective_id=number, has_side_effects=True, vmem_limit_bytes=60 * 2**20
        ),
        cost_estimate=pl.CostEstimate(flops=0, bytes_accessed=600 * 2**20, transcendentals=0),
    )(inputs, gates, mid_up, grad_mid, up_extra, down_extra, ready_up, block, open_rows)[:7]


def gathered(weight):
    return lax.all_gather(weight, "dp", axis=0, tiled=True)


def body(
    tokens,
    cotangent,
    attention_norm_gain,
    query_key_value_weight,
    query_key_value_bias,
    output_projection_weight,
    feedforward_norm_gain,
    router_matrix,
    shared_expert_gate_weight,
    routed_gate_up_weight,
    routed_down_weight,
    shared_expert_gate_up_weight,
    shared_expert_down_weight,
    routes,
    sequence_adapter_index,
    picture_piece_starts,
    adapter_query_key_value_lower,
    adapter_query_key_value_upper,
    adapter_output_lower,
    adapter_output_upper,
    adapter_shared_up_lower,
    adapter_shared_up_upper,
    adapter_shared_down_lower,
    adapter_shared_down_upper,
):
    length, width = tokens.shape
    set_id = sequence_adapter_index[0]
    starts = picture_piece_starts[0]

    def selected_experts(adapter_entry):
        return lax.dynamic_index_in_dim(adapter_entry, set_id, 0, keepdims=False)

    qkv_a, qkv_b, out_a, out_b = (
        selected_experts(adapter_query_key_value_lower),
        selected_experts(adapter_query_key_value_upper),
        selected_experts(adapter_output_lower),
        selected_experts(adapter_output_upper),
    )
    up_a, up_b, down_a, down_b = (
        selected_experts(adapter_shared_up_lower),
        selected_experts(adapter_shared_up_upper),
        selected_experts(adapter_shared_down_lower),
        selected_experts(adapter_shared_down_upper),
    )
    gain_attn_f = attention_norm_gain.astype(jnp.float32)
    gain_ffn_f = feedforward_norm_gain.astype(jnp.float32)
    tokens_f = tokens.astype(jnp.float32)
    normed = to_low(rms_scale(tokens_f, gain_attn_f))
    mid_qkv = to_low(matmul(normed, qkv_a))
    hidden = shared_expert_down_weight.shape[1] // SHARED
    rank = up_a.shape[1]

    def fill(rows):
        return jnp.pad(to_low(rows), ((0, NARROW - rows.shape[0]), (0, 0)))

    def fill_last(rows):
        return jnp.pad(to_low(rows), ((0, 0), (0, 0), (0, NARROW - rows.shape[2])))

    cotangent_down = ADAPTER_SCALE * contract_last(cotangent, down_b)
    up_extra = ADAPTER_SCALE * up_b.reshape(rank, 2, SHARED, hidden).transpose(2, 1, 3, 0)
    up_extra = fill_last(up_extra.reshape(SHARED, 2 * hidden, rank))
    down_extra = fill_last(down_a.reshape(SHARED, hidden, rank))
    depth = routed_gate_up_weight.shape[0]
    early = (READY - SHARED) * 2 * hidden
    shared_block = shared_expert_gate_up_weight.reshape(-1, 2, SHARED, hidden)
    up_block = jnp.transpose(routed_gate_up_weight, (1, 2, 3, 0)).reshape(-1, depth)
    ready_up = lax.all_gather(
        jnp.concatenate(
            [shared_block.transpose(2, 1, 3, 0).reshape(-1, depth), up_block[:early]], axis=0
        ),
        "dp",
        axis=1,
        tiled=True,
    )
    attention_rows = gathered(
        jnp.concatenate([query_key_value_weight, output_projection_weight[:, None]], axis=1)
    )
    qkv_rows, output_rows = attention_rows[:, :3], attention_rows[:, 3]
    normed, cotangent_down, up_extra, down_extra = lax.optimization_barrier(
        (normed, cotangent_down, up_extra, down_extra)
    )
    qkv_sum = jnp.einsum("tr,rsf->stf", normed, qkv_rows, preferred_element_type=jnp.float32)
    qkv_sum = qkv_sum + query_key_value_bias.astype(jnp.float32)[:, None, :]
    qkv_sum = qkv_sum + ADAPTER_SCALE * jnp.einsum(
        "tr,rsf->stf", mid_qkv, qkv_b, preferred_element_type=jnp.float32
    )
    cosine, sine_table = rope_tables(length)
    signs = jnp.where(jnp.arange(HEAD_SIZE) < HEAD_SIZE // 2, -1.0, 1.0)
    piece_ids = piece_index(jnp.arange(length, dtype=jnp.int32), starts)
    places = (cosine, sine_table * signs[None, :], piece_ids[:, None], piece_ids[None, :])
    query, keys, values, attended = attend(qkv_sum, *places)
    branch_part = contract_last(attended, output_rows)
    down_block = jnp.transpose(routed_down_weight, (1, 2, 0))
    down_block = jnp.concatenate(
        [shared_expert_down_weight.T, down_block.reshape(-1, depth)], axis=0
    )
    branch_here, mid_out_here_f, down_rows, open_rows = summed_and_gathered(
        branch_part,
        matmul(attended, out_a),
        down_block,
        cotangent.T,
        1,
    )
    mid_out = to_low(mid_out_here_f)
    hidden_here = tokens_f + branch_here + ADAPTER_SCALE * matmul(mid_out, out_b)
    normed_two_here_f, norm_ffn_pull = jax.vjp(
        lambda rows: rms_scale(rows, gain_ffn_f), hidden_here
    )
    normed_two_here = to_low(normed_two_here_f)
    normed_two = normed_two_here
    cot_f = cotangent.astype(jnp.float32)
    small_rows = gathered(
        jnp.concatenate(
            [
                router_matrix,
                shared_expert_gate_weight[:, None],
                jnp.full_like(shared_expert_gate_weight, set_id)[:, None],
            ],
            axis=1,
        )
    )
    factors = jnp.concatenate([small_rows[:, : EXPERTS + 1], up_a], axis=1)
    projected = matmul(normed_two, factors)
    router_probs = jax.nn.softmax(projected[:, :EXPERTS], axis=-1)
    shared_gate = jax.nn.sigmoid(projected[:, EXPERTS])
    mid_up = to_low(projected[:, EXPERTS + 1 :])
    expert_ids = jnp.arange(EXPERTS, dtype=jnp.int32)
    chosen = jnp.sum(
        (routes[:, :, None] == expert_ids[None, None, :]).astype(jnp.float32), axis=1
    )
    gates = jnp.concatenate(
        [jnp.broadcast_to(shared_gate[None], (SHARED, length)), (router_probs * chosen).T], axis=0
    )
    grad_mid_down = shared_gate[:, None] * cotangent_down
    (
        normed_two_part,
        gate_grads,
        mid_down_part,
        grad_mid_up_part,
        grad_down_a_parts,
        grad_up_b_parts,
        act_rows,
    ) = experts_step(
        normed_two,
        gates,
        fill(mid_up.T),
        fill(grad_mid_down.T),
        up_extra,
        down_extra,
        ready_up,
        up_block[early:],
        open_rows,
        5,
    )
    grad_down_a_local = grad_down_a_parts[:, :rank].transpose(1, 0, 2).reshape(rank, -1)
    grad_up_b_local = (
        grad_up_b_parts[:, :rank]
        .reshape(SHARED, rank, 2, hidden)
        .transpose(1, 2, 0, 3)
        .reshape(rank, 2, -1)
    )
    narrow_part = jnp.concatenate(
        [
            gate_grads[SHARED:],
            jnp.sum(gate_grads[:SHARED], axis=0, keepdims=True),
            grad_mid_up_part[:rank],
            mid_down_part[:rank],
        ],
        axis=0,
    ).T
    grad_normed_two, narrow_sum, combined_part = summed_and_down(
        normed_two_part, narrow_part, act_rows, down_rows, 2
    )
    mid_down = to_low(narrow_sum[:, EXPERTS + 1 + rank :])
    grad_mid_up = to_low(narrow_sum[:, EXPERTS + 1 : EXPERTS + 1 + rank])
    grad_probs = chosen * narrow_sum[:, :EXPERTS]
    grad_logits = to_low(
        router_probs * (grad_probs - jnp.sum(router_probs * grad_probs, axis=1, keepdims=True))
    )
    shared_gate_grad = narrow_sum[:, EXPERTS] + jnp.sum(
        mid_down.astype(jnp.float32) * cotangent_down, axis=1
    )
    grad_gate_logit = to_low(shared_gate_grad * shared_gate * (1.0 - shared_gate))
    grad_normed_two = grad_normed_two + contract_last(
        jnp.concatenate([grad_logits, grad_gate_logit[:, None], grad_mid_up], axis=1),
        factors,
    )
    grad_hidden = cot_f + norm_ffn_pull(grad_normed_two)[0]
    grad_branch = to_low(grad_hidden)
    grad_mid_out = to_low(ADAPTER_SCALE * contract_last(grad_branch, out_b))
    grad_attended = to_low(
        matmul(grad_branch, output_rows) + contract_last(grad_mid_out, out_a)
    )
    grad_down_b_local = ADAPTER_SCALE * contract_first(
        to_low(shared_gate[:, None] * mid_down.astype(jnp.float32)), cotangent
    )
    grad_up_a_local = contract_first(grad_mid_up, normed_two)
    grad_out_b_local = ADAPTER_SCALE * contract_first(mid_out, grad_branch)
    grad_out_a_local = contract_first(grad_mid_out, attended)

    def side_by_side(local_grads):
        return jnp.concatenate([to_low(local_grad) for local_grad in local_grads], axis=1)

    early_grads = [
        grad_out_a_local,
        grad_up_a_local,
        grad_up_b_local.reshape(grad_up_b_local.shape[0], -1),
        grad_down_a_local,
        grad_down_b_local,
    ]
    grad_attended, early_flat = lax.optimization_barrier(
        (grad_attended, side_by_side(early_grads))
    )
    early_rows = lax.all_gather(early_flat, "dp", axis=0, tiled=False)
    combined_here, grad_qkv = summed_and_attended_back(
        combined_part, (query, keys, values, grad_attended) + places, 3
    )
    extra_here = ADAPTER_SCALE * matmul(mid_down, down_b)
    output = to_low(hidden_here + combined_here + shared_gate[:, None] * extra_here)
    grad_qkv, early_rows = lax.optimization_barrier((grad_qkv, early_rows))
    grad_mid_qkv_part = ADAPTER_SCALE * jnp.einsum(
        "stf,rsf->tr", grad_qkv, qkv_b, preferred_element_type=jnp.float32
    )
    grad_qkv_b_local = ADAPTER_SCALE * jnp.einsum(
        "tr,stf->rsf", mid_qkv, grad_qkv, preferred_element_type=jnp.float32
    )
    normed_part = jnp.einsum(
        "stf,rsf->tr",
        grad_qkv,
        qkv_rows,
        preferred_element_type=jnp.float32,
    )
    grad_normed, grad_mid_qkv_f = summed(normed_part, grad_mid_qkv_part, 4)
    grad_mid_qkv_here = to_low(grad_mid_qkv_f)
    grad_normed = grad_normed + contract_last(grad_mid_qkv_here, qkv_a)
    norm_attn_pull = jax.vjp(lambda rows: rms_scale(rows, gain_attn_f), tokens_f)[1]
    grad_tokens_here = to_low(grad_hidden + norm_attn_pull(grad_normed)[0])
    grad_tokens, grad_mid_qkv = (grad_tokens_here, grad_mid_qkv_here)
    grad_qkv_a_local = contract_first(grad_mid_qkv, normed)
    everyone = small_rows[:: small_rows.shape[0] // lax.axis_size("dp"), EXPERTS + 1]
    marker = to_low(
        jnp.arange(ADAPTER_SETS, dtype=jnp.int32)[:, None] == everyone.astype(jnp.int32)[None, :]
    )

    def adapter_sums(local_grads, rows):
        results, start = [], 0
        for local_grad in local_grads:
            size = local_grad.shape[1]
            results.append(
                jnp.einsum(
                    "cj,jrn->crn",
                    marker,
                    rows[:, :, start : start + size],
                    preferred_element_type=jnp.float32,
                )
            )
            start += size
        return results

    def flipped(total):
        return jnp.swapaxes(total, 1, 2)

    def opened(total, count):
        return total.reshape(total.shape[0], total.shape[1], count, -1)

    total_out_a, total_up_a, total_up_b, total_down_a, total_down_b = adapter_sums(
        early_grads, early_rows
    )
    late_grads = [
        grad_qkv_b_local.reshape(grad_qkv_b_local.shape[0], -1),
        grad_qkv_a_local,
        grad_out_b_local,
    ]
    total_qkv_b, total_qkv_a, total_out_b = adapter_sums(
        late_grads, lax.all_gather(side_by_side(late_grads), "dp", axis=0, tiled=False)
    )
    return (
        output,
        grad_tokens,
        flipped(total_qkv_a),
        opened(total_qkv_b, 3),
        flipped(total_out_a),
        total_out_b,
        flipped(total_up_a),
        opened(total_up_b, 2),
        flipped(total_down_a),
        total_down_b,
    )


def solution(mesh):
    return jax.shard_map(
        body,
        mesh=mesh,
        in_specs=(
            P("dp", None),
            P("dp", None),
            P(),
            P("dp", None, "tensor"),
            P(None, "tensor"),
            P("dp", "tensor"),
            P(),
            P("dp", None),
            P("dp"),
            P("dp", None, None, "tensor"),
            P("dp", None, "tensor"),
            P("dp", None, "tensor"),
            P("dp", "tensor"),
            P("dp", None),
            P("dp"),
            P("dp", None),
            P(),
            P(None, None, None, "tensor"),
            P(None, "tensor", None),
            P(),
            P(),
            P(None, None, None, "tensor"),
            P(None, "tensor", None),
            P(),
        ),
        out_specs=(
            P("dp", None),
            P("dp", None),
            P(),
            P(None, None, None, "tensor"),
            P(None, "tensor", None),
            P(),
            P(),
            P(None, None, None, "tensor"),
            P(None, "tensor", None),
            P(),
        ),
        check_vma=False,
    )
```

```python
import functools

import jax
import jax.numpy as jnp
from jax import lax
from jax.experimental import pallas as pl
from jax.experimental.pallas import tpu as pltpu
from jax.sharding import PartitionSpec as P

HEAD_SIZE = 128
TOP = 4
EXPERTS = 16
ADAPTER_SETS = 8
PIECE = 256


EPSILON = 1e-06
THETA = 1000000.0
ADAPTER_SCALE = 2.0
MASKED = -1e30
QUERY_ROWS = 256
NARROW = 128
MESH = pl.DeviceIdType.MESH
SUM_CHUNKS = 16
AHEAD = 1
LEAD = 2
SHARED = 4
HALVES = 1
READY = 6


def matmul(left_side, right_side):
    return jnp.dot(left_side, right_side, preferred_element_type=jnp.float32)


def contract_last(left_side, right_side):
    return lax.dot_general(
        left_side, right_side, (((1,), (1,)), ((), ())), preferred_element_type=jnp.float32
    )


def contract_first(left_side, right_side):
    return lax.dot_general(
        left_side, right_side, (((0,), (0,)), ((), ())), preferred_element_type=jnp.float32
    )


def to_low(values):
    return values.astype(jnp.bfloat16)


def rms_scale(values, gain_values):
    return (
        values * lax.rsqrt(jnp.mean(values * values, axis=1, keepdims=True) + EPSILON) * gain_values
    )


def rope_tables(length):
    half_size = HEAD_SIZE // 2
    frequency = THETA ** (-jnp.arange(half_size, dtype=jnp.float32) * 2.0 / HEAD_SIZE)
    angles = jnp.arange(length, dtype=jnp.float32)[:, None] * frequency[None, :]
    return (
        jnp.concatenate([jnp.cos(angles)] * 2, axis=1),
        jnp.concatenate([jnp.sin(angles)] * 2, axis=1),
    )


def piece_index(positions, starts):
    inside = (positions[:, None] >= starts[None, :]) & (
        positions[:, None] < starts[None, :] + PIECE
    )
    labels = jnp.arange(starts.shape[0], dtype=jnp.int32)[None, :] + 1
    return jnp.sum(jnp.where(inside, labels, 0), axis=1) - 1


def line_sum_steps(
    chunks, wide_ref, narrow_ref, total_ref, part_ref, from_end, pair_sum, from_pair, semaphores
):
    place = lax.axis_index("tensor")
    width = wide_ref.shape[1]
    rows = part_ref.shape[0] // chunks
    inner = (place == 1) | (place == 2)
    end = (place == 0) | (place == 3)
    mate = jnp.where(place < 2, 1 - place, 5 - place)
    other = jnp.where(inner, 3 - place, place)

    def span(chunk):
        return pl.ds(pl.multiple_of(chunk * rows, rows), rows)

    def copy(source, target, chunk, lane, device):
        return pltpu.make_async_remote_copy(
            source.at[span(chunk)],
            target.at[span(chunk)],
            semaphores.at[2 * lane, chunk],
            semaphores.at[2 * lane + 1, chunk],
            device_id={"tensor": device},
            device_id_type=MESH,
        )

    def inward(chunk):
        return copy(part_ref, from_end, chunk, 0, mate)

    def across(chunk):
        return copy(pair_sum, from_pair, chunk, 1, other)

    def outward(chunk):
        return copy(total_ref, total_ref, chunk, 2, mate)

    def add(left_ref, right_ref, out_ref, chunk):
        out_ref[span(chunk)] = to_low(
            left_ref[span(chunk)].astype(jnp.float32) + right_ref[span(chunk)].astype(jnp.float32)
        )

    def stage(chunk):
        part_ref[span(chunk), :width] = to_low(wide_ref[span(chunk)])
        if narrow_ref is not None:
            part_ref[span(chunk), width:] = narrow_ref[span(chunk)]

    def greet(extra):
        barrier = pltpu.get_barrier_semaphore()
        pl.semaphore_signal(barrier, inc=1, device_id={"tensor": mate}, device_id_type=MESH)

        @pl.when(inner)
        def _():
            pl.semaphore_signal(barrier, inc=1, device_id={"tensor": other}, device_id_type=MESH)
            pl.semaphore_wait(barrier, 2 + extra)

        @pl.when(end)
        def _():
            pl.semaphore_wait(barrier, 1 + extra)

    def begin():
        @pl.when(end)
        def _():
            @pl.loop(0, chunks)
            def _(chunk):
                stage(chunk)
                inward(chunk).start()

    def advance(step):
        @pl.when(inner & (step < chunks))
        def _():
            stage(step)
            inward(step).wait_recv()
            add(part_ref, from_end, pair_sum, step)
            across(step).start()

        @pl.when(inner & (step > 0) & (step <= chunks))
        def _():
            across(step - 1).wait_recv()
            add(pair_sum, from_pair, total_ref, step - 1)
            outward(step - 1).start()

    def finish():
        @pl.when(end)
        def _():
            @pl.loop(0, chunks)
            def _(chunk):
                inward(chunk).wait_send()
                outward(chunk).wait_recv()

        @pl.when(inner)
        def _():
            @pl.loop(0, chunks)
            def _(chunk):
                across(chunk).wait_send()
                outward(chunk).wait_send()

    return greet, begin, advance, finish


def plane_gather_steps(pieces, block_ref, whole_ref, semaphores, local_semaphore):
    spot = lax.axis_index("dp")
    depth = block_ref.shape[1]
    rows = block_ref.shape[0] // pieces
    core_mate = spot + 1 - 2 * (spot % 2)
    x_mate = spot + 2 - 4 * ((spot // 2) % 2)
    y_mate = spot + 4 - 8 * (spot // 4)
    x_y_mate = x_mate + 4 - 8 * (spot // 4)
    lanes = {
        "core": (spot, core_mate, 0, 1),
        "x": (spot, x_mate, 0, 1),
        "y": (spot, y_mate, 0, 1),
        "x_core": (x_mate, core_mate, 0, 1),
        "x_y": (x_mate, y_mate, 0, 2),
        "y_core": (y_mate, core_mate, 0, 1),
        "y_x": (y_mate, x_mate, 1, 2),
        "xy_core": (x_y_mate, core_mate, 0, 2),
        "yx_core": (x_y_mate, core_mate, 1, 2),
    }
    order = list(lanes)

    def send(name, piece):
        owner, device, part, parts = lanes[name]
        lane = order.index(name)
        span = pl.ds(
            pl.multiple_of(piece * rows + part * (rows // parts), rows // parts), rows // parts
        )
        columns = pl.ds(pl.multiple_of(owner * depth, depth), depth)
        target = whole_ref.at[span, columns]
        source = block_ref.at[span] if name in ("core", "x", "y") else target
        return pltpu.make_async_remote_copy(
            source,
            target,
            semaphores.at[2 * lane, piece],
            semaphores.at[2 * lane + 1, piece],
            device_id={"dp": device},
            device_id_type=MESH,
        )

    def own():
        columns = pl.ds(pl.multiple_of(spot * depth, depth), depth)
        return pltpu.make_async_copy(block_ref, whole_ref.at[:, columns], local_semaphore)

    def greet():
        barrier = pltpu.get_barrier_semaphore()
        for device in (core_mate, x_mate, y_mate):
            pl.semaphore_signal(barrier, inc=1, device_id={"dp": device}, device_id_type=MESH)

    def launch(piece):
        @pl.when((piece >= 0) & (piece < pieces))
        def _():
            for name in ("x", "y", "core"):
                send(name, piece).start()

    def forward(piece):
        @pl.when((piece >= 0) & (piece < pieces))
        def _():
            send("x", piece).wait_recv()
            send("x_y", piece).start()
            send("x_core", piece).start()
            send("y", piece).wait_recv()
            send("y_x", piece).start()
            send("y_core", piece).start()

    def hand_over(piece):
        @pl.when((piece >= 0) & (piece < pieces))
        def _():
            send("x_y", piece).wait_recv()
            send("xy_core", piece).start()
            send("y_x", piece).wait_recv()
            send("yx_core", piece).start()

    def advance(step):
        launch(step + LEAD)
        forward(step - AHEAD)
        hand_over(step - 2 * AHEAD)

    def load(first, count, target, semaphore):
        span = pl.ds(pl.multiple_of(first, rows), count)

        def columns(owner):
            return pl.ds(pl.multiple_of(owner * depth, depth), depth)

        here = columns(spot)
        copies = [pltpu.make_async_copy(block_ref.at[span], target.at[:, here], semaphore)]
        for shift in range(1, 8):
            there = columns((spot + shift) % 8)
            copies.append(
                pltpu.make_async_copy(
                    whole_ref.at[span, there], target.at[:, there], semaphore
                )
            )
        return copies

    def load_wait(count, target, semaphore):
        pltpu.make_async_copy(whole_ref.at[pl.ds(0, count)], target, semaphore).wait()

    def arrive(piece):
        for name in ("core", "x_core", "y_core", "xy_core", "yx_core"):
            send(name, piece).wait_recv()

    def finish():
        @pl.loop(0, pieces)
        def _(piece):
            for name in order:
                send(name, piece).wait_send()

    return greet, advance, arrive, finish, own, load, load_wait, (launch, forward, hand_over)


def line_sum_kernel(chunks, *refs):
    greet, begin, advance, finish = line_sum_steps(chunks, *refs)
    greet(0)
    begin()

    @pl.loop(0, chunks + 1)
    def _(step):
        advance(step)

    finish()


def sum_gather_kernel(
    chunks,
    pieces,
    wide_ref,
    narrow_ref,
    block_ref,
    cotangent_ref,
    total_ref,
    whole_ref,
    open_ref,
    *scratch,
):
    greet, begin, advance, finish = line_sum_steps(
        chunks, wide_ref, narrow_ref, total_ref, *scratch[:5]
    )
    gather_semaphores, local_semaphores, piece_rows, open_rows = scratch[5:]
    gather_greet, gather_advance, gather_arrive, gather_finish, own, load, load_wait, stages = (
        plane_gather_steps(
            pieces, block_ref, whole_ref, gather_semaphores, local_semaphores.at[0]
        )
    )
    rows = piece_rows.shape[1]

    def store(piece):
        slot = piece % 2
        span = pl.ds(pl.multiple_of(piece * rows, rows), rows)
        return pltpu.make_async_copy(
            open_rows.at[slot], open_ref.at[span], local_semaphores.at[3 + slot]
        )

    gather_greet()
    greet(3)
    begin()
    own().start()

    @pl.loop(0, LEAD)
    def _(piece):
        stages[0](piece)

    @pl.loop(0, max(chunks + 1, pieces + 3 * AHEAD + 1))
    def _(step):
        gather_advance(step)
        advance(step)

        @pl.when((step >= 3 * AHEAD) & (step < pieces + 3 * AHEAD))
        def _():
            piece = step - 3 * AHEAD
            gather_arrive(piece)
            slot = piece % 2
            for copy in load(piece * rows, rows, piece_rows.at[slot], local_semaphores.at[1 + slot]):
                copy.start()

        @pl.when((step > 3 * AHEAD) & (step <= pieces + 3 * AHEAD))
        def _():
            piece = step - 3 * AHEAD - 1
            slot = piece % 2
            load_wait(rows, piece_rows.at[slot], local_semaphores.at[1 + slot])

            @pl.when(piece >= 2)
            def _():
                store(piece - 2).wait()

            open_rows[piece % 2] = to_low(matmul(piece_rows[piece % 2], cotangent_ref[...]))
            store(piece).start()

    store(pieces - 2).wait()
    store(pieces - 1).wait()
    own().wait()
    gather_finish()
    finish()


def sum_down_kernel(
    chunks, wide_ref, narrow_ref, act_ref, down_ref, total_ref, out_ref, *scratch
):
    greet, begin, advance, finish = line_sum_steps(
        chunks, wide_ref, narrow_ref, total_ref, *scratch[:5]
    )
    semaphores, act_rows, down_rows, out_rows = scratch[5:]
    rows = act_rows.shape[1]
    blocks = down_ref.shape[0] // rows

    def loads(block):
        slot = block % 2
        span = pl.ds(pl.multiple_of(block * rows, rows), rows)
        return [
            pltpu.make_async_copy(act_ref.at[span], act_rows.at[slot], semaphores.at[0, slot]),
            pltpu.make_async_copy(down_ref.at[span], down_rows.at[slot], semaphores.at[1, slot]),
        ]

    for load in loads(0):
        load.start()
    greet(0)
    begin()
    out_rows[...] = jnp.zeros_like(out_rows)

    @pl.loop(0, max(blocks, chunks + 1))
    def _(step):
        advance(step)

        @pl.when(step < blocks)
        def _():
            @pl.when(step + 1 < blocks)
            def _():
                for load in loads(step + 1):
                    load.start()

            for load in loads(step):
                load.wait()
            tile = min(256, out_rows.shape[0])

            @pl.loop(0, out_rows.shape[0] // tile)
            def _(index):
                span = pl.ds(pl.multiple_of(index * tile, tile), tile)
                out_rows[span] += contract_first(
                    act_rows[step % 2, :, span], down_rows[step % 2]
                )

    out_ref[...] = to_low(out_rows[...])
    finish()


def attend_back_sum_kernel(chunks, wide_ref, rows_ref, upper_ref, *refs):
    inputs, scratch = refs[:8], refs[12:]
    total_ref, grad_qkv_ref, normed_part_ref, mid_total_ref = refs[8:12]
    greet, begin, advance, finish = line_sum_steps(
        chunks, wide_ref, None, total_ref, *scratch[:5]
    )
    head_block = attend_back_steps(*inputs, grad_qkv_ref, *scratch[5:7])
    mid_part = scratch[7]
    _, mid_begin, mid_advance, mid_finish = line_sum_steps(
        1, mid_part, None, mid_total_ref, *scratch[8:]
    )
    length, heads_width = inputs[0].shape
    heads, blocks = heads_width // HEAD_SIZE, length // QUERY_ROWS
    each = blocks // 2
    greet(0)
    begin()

    @pl.loop(0, heads)
    def _(head):
        for step in range(each):
            advance(head * each + step)
            head_block(head, 2 * step * QUERY_ROWS)
            head_block(head, (2 * step + 1) * QUERY_ROWS)

    mid_part[...] = grad_mid_rows(grad_qkv_ref, upper_ref)
    mid_begin()
    done = heads * each

    @pl.loop(0, blocks)
    def _(block):
        advance(done + block)
        span = pl.ds(pl.multiple_of(block * QUERY_ROWS, QUERY_ROWS), QUERY_ROWS)
        normed_part_ref[span] = to_low(
            sum(contract_last(grad_qkv_ref[part, span], rows_ref[part]) for part in range(3))
        )

    mid_advance(0)

    @pl.loop(done + blocks, max(done + blocks, chunks + 1))
    def _(step):
        advance(step)

    mid_advance(1)
    mid_finish()
    finish()


def grad_mid_rows(grad_qkv_ref, upper_ref):
    return sum(contract_last(grad_qkv_ref[part], upper_ref[part]) for part in range(3))


def epilogue_kernel(
    total_ref,
    hidden_ref,
    scale_ref,
    cotangent_ref,
    gain_ref,
    probs_ref,
    chosen_ref,
    extra_ref,
    gate_ref,
    factors_ref,
    out_b_ref,
    out_a_ref,
    rows_ref,
    grad_hidden_ref,
    grad_branch_ref,
    grad_mid_ref,
    grad_attended_ref,
):
    width = hidden_ref.shape[1]
    narrow = total_ref[:, width:].astype(jnp.float32)
    lane = lax.broadcasted_iota(jnp.int32, narrow.shape, 1)
    probs = probs_ref[...]
    grad_probs = chosen_ref[...] * narrow
    grad_logits = probs * (grad_probs - jnp.sum(probs * grad_probs, axis=1, keepdims=True))
    only_gate = jnp.where(lane == EXPERTS, narrow, 0.0)
    gate_grad = jnp.sum(only_gate + narrow * extra_ref[...], axis=1, keepdims=True)
    gate = gate_ref[...]
    gate_logit = gate_grad * gate * (1.0 - gate)
    rank = extra_ref.shape[1] // 8
    rows = jnp.where(lane <= EXPERTS + rank, narrow, 0.0)
    rows = jnp.where(lane == EXPERTS, gate_logit, rows)
    rows = to_low(jnp.where(lane < EXPERTS, grad_logits, rows))
    grad_normed = total_ref[:, :width].astype(jnp.float32) + contract_last(rows, factors_ref[...])
    hidden = hidden_ref[...]
    scale = scale_ref[...]
    scaled = grad_normed * gain_ref[...]
    pull = jnp.mean(hidden * scaled, axis=1, keepdims=True)
    grad_hidden = (
        cotangent_ref[...].astype(jnp.float32)
        + scale * scaled
        - hidden * (scale * scale * scale * pull)
    )
    grad_hidden_ref[...] = grad_hidden
    grad_branch = to_low(grad_hidden)
    grad_branch_ref[...] = grad_branch
    grad_mid = to_low(ADAPTER_SCALE * contract_last(grad_branch, out_b_ref[...]))
    grad_mid_ref[...] = grad_mid
    grad_attended_ref[...] = to_low(
        matmul(grad_branch, rows_ref[...]) + contract_last(grad_mid, out_a_ref[...])
    )


def epilogue(blocked, still):
    length = blocked[0].shape[0]
    width, heads_width = still[-1].shape
    rows = min(length, 256)
    total, hidden, scale, cotangent, probs, chosen, extra, gate = blocked
    gain, factors, out_b, out_a, output_rows = still

    def block(array):
        return pl.BlockSpec((rows, array.shape[1]), lambda index: (index, 0))

    def whole(array):
        return pl.BlockSpec(array.shape, lambda index: (0, 0))

    outs = [
        jax.ShapeDtypeStruct((length, width), jnp.float32),
        jax.ShapeDtypeStruct((length, width), jnp.bfloat16),
        jax.ShapeDtypeStruct((length, NARROW), jnp.bfloat16),
        jax.ShapeDtypeStruct((length, heads_width), jnp.bfloat16),
    ]
    return pl.pallas_call(
        epilogue_kernel,
        grid=(length // rows,),
        in_specs=[block(array) for array in (total, hidden, scale, cotangent)]
        + [whole(gain)]
        + [block(array) for array in (probs, chosen, extra, gate)]
        + [whole(array) for array in (factors, out_b, out_a, output_rows)],
        out_specs=[block(out) for out in outs],
        out_shape=outs,
        compiler_params=pltpu.CompilerParams(
            vmem_limit_bytes=56 * 2**20, dimension_semantics=("arbitrary",)
        ),
        cost_estimate=pl.CostEstimate(
            flops=2 * length * width * heads_width,
            bytes_accessed=32 * 2**20,
            transcendentals=0,
        ),
    )(
        total,
        hidden,
        scale,
        cotangent,
        gain,
        probs,
        chosen,
        extra,
        gate,
        factors,
        out_b,
        out_a,
        output_rows,
    )


def on_line():
    return lax.axis_size("tensor") == 4


def in_plane():
    return lax.axis_size("dp") == 8


def in_vmem(count):
    return [pl.BlockSpec(memory_space=pltpu.VMEM)] * count


def in_hbm(count):
    return [pl.BlockSpec(memory_space=pltpu.HBM)] * count


def sum_scratch(shape):
    return [pltpu.VMEM(shape, jnp.bfloat16)] * 4 + [pltpu.SemaphoreType.DMA((6, SUM_CHUNKS))]


def narrowed(narrow_part):
    pad = jnp.zeros((narrow_part.shape[0], NARROW - narrow_part.shape[1]), jnp.bfloat16)
    return jnp.concatenate([to_low(narrow_part), pad], axis=1)


def plain_sum(wide_part, narrow_part):
    if narrow_part is not None:
        pad = jnp.zeros((narrow_part.shape[0], NARROW - narrow_part.shape[1]), jnp.float32)
        wide_part = jnp.concatenate([wide_part, narrow_part, pad], axis=1)
    return lax.psum(wide_part, "tensor")


def plain_line_sum_kernel(chunks, wide_ref, *refs):
    line_sum_kernel(chunks, wide_ref, None, *refs)


def summed(wide_part, number):
    if not on_line():
        return plain_sum(wide_part, None)
    shape = wide_part.shape
    return pl.pallas_call(
        functools.partial(plain_line_sum_kernel, SUM_CHUNKS),
        out_shape=jax.ShapeDtypeStruct(shape, jnp.bfloat16),
        in_specs=in_vmem(1),
        out_specs=pl.BlockSpec(memory_space=pltpu.VMEM),
        scratch_shapes=sum_scratch(shape),
        compiler_params=pltpu.CompilerParams(
            collective_id=number, has_side_effects=True, vmem_limit_bytes=48 * 2**20
        ),
        cost_estimate=pl.CostEstimate(flops=0, bytes_accessed=300 * 2**20, transcendentals=0),
    )(wide_part)


def summed_and_gathered(wide_part, narrow_part, block, cotangents, number):
    length, width = wide_part.shape
    if not (on_line() and in_plane()):
        whole = lax.all_gather(block, "dp", axis=1, tiled=True)
        open_rows = to_low(matmul(whole, cotangents))
        return plain_sum(wide_part, narrow_part), whole, open_rows
    shape = (length, width + NARROW)
    pieces = SHARED + EXPERTS
    rows = block.shape[0] // pieces
    total, whole, open_rows = pl.pallas_call(
        functools.partial(sum_gather_kernel, SUM_CHUNKS, pieces),
        out_shape=[
            jax.ShapeDtypeStruct(shape, jnp.bfloat16),
            jax.ShapeDtypeStruct((block.shape[0], width), jnp.bfloat16),
            jax.ShapeDtypeStruct((block.shape[0], length), jnp.bfloat16),
        ],
        in_specs=in_vmem(2) + in_hbm(1) + in_vmem(1),
        out_specs=in_vmem(1) + in_hbm(2),
        scratch_shapes=sum_scratch(shape)
        + [
            pltpu.SemaphoreType.DMA((18, pieces)),
            pltpu.SemaphoreType.DMA((5,)),
            pltpu.VMEM((2, rows, width), jnp.bfloat16),
            pltpu.VMEM((2, rows, length), jnp.bfloat16),
        ],
        compiler_params=pltpu.CompilerParams(
            collective_id=number, has_side_effects=True, vmem_limit_bytes=58 * 2**20
        ),
        cost_estimate=pl.CostEstimate(flops=0, bytes_accessed=360 * 2**20, transcendentals=0),
    )(wide_part, narrowed(narrow_part), block, cotangents)
    return total, whole, open_rows


def summed_and_down(wide_part, narrow_part, act_rows, down_rows, number):
    length, width = wide_part.shape
    if not on_line():
        out = contract_first(act_rows, down_rows)
        return plain_sum(wide_part.astype(jnp.float32), narrow_part), out
    shape = (length, width + NARROW)
    rows = 2 * down_rows.shape[0] // (SHARED + EXPERTS)
    total, out = pl.pallas_call(
        functools.partial(sum_down_kernel, SUM_CHUNKS),
        out_shape=[
            jax.ShapeDtypeStruct(shape, jnp.bfloat16),
            jax.ShapeDtypeStruct((length, width), jnp.bfloat16),
        ],
        in_specs=in_vmem(2) + in_hbm(2),
        out_specs=in_vmem(2),
        scratch_shapes=sum_scratch(shape)
        + [
            pltpu.SemaphoreType.DMA((2, 2)),
            pltpu.VMEM((2, rows, length), jnp.bfloat16),
            pltpu.VMEM((2, rows, width), jnp.bfloat16),
            pltpu.VMEM((length, width), jnp.float32),
        ],
        compiler_params=pltpu.CompilerParams(
            collective_id=number, has_side_effects=True, vmem_limit_bytes=58 * 2**20
        ),
        cost_estimate=pl.CostEstimate(flops=0, bytes_accessed=300 * 2**20, transcendentals=0),
    )(wide_part, narrowed(narrow_part), act_rows, down_rows)
    return total, out


def block_mask(first, rows, extent, row_piece_ref, col_piece_ref):
    row_place = lax.broadcasted_iota(jnp.int32, (rows, extent), 0) + first
    col_place = lax.broadcasted_iota(jnp.int32, (rows, extent), 1)
    row_piece = row_piece_ref[first : first + rows, 0:1]
    together = (row_piece == col_piece_ref[0:1, :extent]) & (row_piece >= 0)
    return (col_place <= row_place) | together


def block_probs(query_rows, keys, allowed):
    scores = jnp.where(allowed, contract_last(query_rows, keys) * HEAD_SIZE**-0.5, MASKED)
    raised = jnp.exp(scores - jnp.max(scores, axis=1, keepdims=True))
    return raised * (1.0 / jnp.sum(raised, axis=1, keepdims=True))


def half_turn(values, signed_sine):
    return pltpu.roll(values, HEAD_SIZE // 2, 1) * signed_sine


def attend_kernel(
    qkv_ref,
    cosine_ref,
    sine_ref,
    row_piece_ref,
    col_piece_ref,
    query_ref,
    keys_ref,
    values_ref,
    attended_ref,
):
    length = qkv_ref.shape[1]

    @pl.loop(0, qkv_ref.shape[2] // HEAD_SIZE)
    def _(head):
        column = pl.ds(pl.multiple_of(head * HEAD_SIZE, HEAD_SIZE), HEAD_SIZE)
        for source, target in ((0, query_ref), (1, keys_ref)):
            raw = qkv_ref[source, :, column]
            target[:, column] = to_low(raw * cosine_ref[...] + half_turn(raw, sine_ref[...]))
        values_ref[:, column] = to_low(qkv_ref[2, :, column])
        for first in range(0, length, QUERY_ROWS):
            extent = min(length, first + QUERY_ROWS + PIECE)
            allowed = block_mask(first, QUERY_ROWS, extent, row_piece_ref, col_piece_ref)
            probs = block_probs(
                query_ref[first : first + QUERY_ROWS, column], keys_ref[:extent, column], allowed
            )
            attended_ref[first : first + QUERY_ROWS, column] = to_low(
                matmul(to_low(probs), values_ref[:extent, column])
            )


def attend(qkv, cosine, signed_sine, row_piece, col_piece):
    length, heads_width = qkv.shape[1:]
    shape = jax.ShapeDtypeStruct((length, heads_width), jnp.bfloat16)
    return pl.pallas_call(
        attend_kernel,
        out_shape=[shape] * 4,
        in_specs=[pl.BlockSpec(memory_space=pltpu.VMEM)] * 5,
        out_specs=[pl.BlockSpec(memory_space=pltpu.VMEM)] * 4,
        compiler_params=pltpu.CompilerParams(vmem_limit_bytes=48 * 2**20),
        cost_estimate=pl.CostEstimate(
            flops=4 * length * length * heads_width,
            bytes_accessed=16 * 2**20,
            transcendentals=length * length * heads_width // HEAD_SIZE,
        ),
    )(qkv, cosine, signed_sine, row_piece, col_piece)


def attend_back_steps(
    query_ref,
    keys_ref,
    values_ref,
    grad_ref,
    cosine_ref,
    sine_ref,
    row_piece_ref,
    col_piece_ref,
    grad_qkv_ref,
    grad_keys,
    grad_values,
):
    length = query_ref.shape[0]

    def turned_back(grad, first):
        span = slice(first, first + grad.shape[0])
        scaled = grad * HEAD_SIZE**-0.5
        return to_low(scaled * cosine_ref[span] - half_turn(scaled, sine_ref[span]))

    def head_block(head, first):
        column = pl.ds(pl.multiple_of(head * HEAD_SIZE, HEAD_SIZE), HEAD_SIZE)
        span = slice(first, first + QUERY_ROWS)
        extent = min(length, first + QUERY_ROWS + PIECE)
        if first == 0:
            grad_keys[...] = jnp.zeros_like(grad_keys)
            grad_values[...] = jnp.zeros_like(grad_values)
        allowed = block_mask(first, QUERY_ROWS, extent, row_piece_ref, col_piece_ref)
        query_rows = query_ref[span, column]
        keys = keys_ref[:extent, column]
        grad_rows = grad_ref[span, column]
        probs = block_probs(query_rows, keys, allowed)
        grad_probs = contract_last(grad_rows, values_ref[:extent, column])
        shift = jnp.sum(probs * grad_probs, axis=1, keepdims=True)
        grad_scores = to_low(probs * (grad_probs - shift))
        grad_values[:extent] += contract_first(to_low(probs), grad_rows)
        grad_keys[:extent] += contract_first(grad_scores, query_rows)
        grad_qkv_ref[0, span, column] = turned_back(matmul(grad_scores, keys), first)
        if first + QUERY_ROWS >= length:
            grad_qkv_ref[1, :, column] = turned_back(grad_keys[...], 0)
            grad_qkv_ref[2, :, column] = to_low(grad_values[...])

    return head_block


def attend_back_kernel(*refs):
    head_block = attend_back_steps(*refs)

    @pl.loop(0, refs[0].shape[1] // HEAD_SIZE)
    def _(head):
        for first in range(0, refs[0].shape[0], QUERY_ROWS):
            head_block(head, first)


def attend_back(query, keys, values, grads, cosine, signed_sine, row_piece, col_piece):
    length, heads_width = query.shape
    return pl.pallas_call(
        attend_back_kernel,
        out_shape=jax.ShapeDtypeStruct((3, length, heads_width), jnp.bfloat16),
        in_specs=[pl.BlockSpec(memory_space=pltpu.VMEM)] * 8,
        out_specs=pl.BlockSpec(memory_space=pltpu.VMEM),
        scratch_shapes=[pltpu.VMEM((length, HEAD_SIZE), jnp.float32)] * 2,
        compiler_params=pltpu.CompilerParams(vmem_limit_bytes=48 * 2**20),
        cost_estimate=pl.CostEstimate(
            flops=10 * length * length * heads_width,
            bytes_accessed=16 * 2**20,
            transcendentals=length * length * heads_width // HEAD_SIZE,
        ),
    )(query, keys, values, grads, cosine, signed_sine, row_piece, col_piece)


def summed_and_attended_back(wide_part, rows, upper, attention_inputs, number):
    if not on_line():
        grad_qkv = attend_back(*attention_inputs)
        normed_part = sum(contract_last(grad_qkv[part], rows[part]) for part in range(3))
        mid_total = lax.psum(grad_mid_rows(grad_qkv, upper), "tensor")
        return plain_sum(wide_part, None), grad_qkv, normed_part, mid_total
    shape = wide_part.shape
    length, heads_width = attention_inputs[0].shape
    narrow_shape = (length, NARROW)
    return pl.pallas_call(
        functools.partial(attend_back_sum_kernel, SUM_CHUNKS),
        out_shape=[
            jax.ShapeDtypeStruct(shape, jnp.bfloat16),
            jax.ShapeDtypeStruct((3, length, heads_width), jnp.bfloat16),
            jax.ShapeDtypeStruct(shape, jnp.bfloat16),
            jax.ShapeDtypeStruct(narrow_shape, jnp.bfloat16),
        ],
        in_specs=in_vmem(3 + len(attention_inputs)),
        out_specs=in_vmem(4),
        scratch_shapes=sum_scratch(shape)
        + [pltpu.VMEM((length, HEAD_SIZE), jnp.float32)] * 2
        + [pltpu.VMEM(narrow_shape, jnp.float32)]
        + [pltpu.VMEM(narrow_shape, jnp.bfloat16)] * 4
        + [pltpu.SemaphoreType.DMA((6, 1))],
        compiler_params=pltpu.CompilerParams(
            collective_id=number, has_side_effects=True, vmem_limit_bytes=60 * 2**20
        ),
        cost_estimate=pl.CostEstimate(flops=0, bytes_accessed=300 * 2**20, transcendentals=0),
    )(wide_part, rows, upper, *attention_inputs)


def hidden_step(gate_up, open_part, gate_row, extra):
    hidden = open_part.shape[0]
    gate_half, up_half = gate_up[:hidden], gate_up[hidden:]
    squashed = 1.0 / (1.0 + jnp.exp(-gate_half))
    act = to_low(gate_half * squashed * up_half)
    act_f = act.astype(jnp.float32)
    gate_grad = jnp.sum(act_f * open_part, axis=0, keepdims=True)
    grad_act = gate_row * open_part
    if extra is not None:
        grad_act = grad_act + extra
    grad_gate = to_low(grad_act * up_half * squashed * (1.0 + gate_half * (1.0 - squashed)))
    grad_up = to_low(grad_act * gate_half * squashed)
    return act, to_low(gate_row * act_f), gate_grad, grad_gate, grad_up


def experts_kernel(
    pieces,
    inputs_ref,
    gate_ref,
    mid_up_ref,
    grad_mid_ref,
    up_extra_ref,
    down_extra_ref,
    ready_up_ref,
    block_ref,
    open_ref,
    grad_ref,
    gate_grad_ref,
    mid_down_ref,
    grad_mid_up_ref,
    grad_down_a_ref,
    grad_up_b_ref,
    act_ref,
    whole_ref,
    grad_total,
    up_rows,
    open_rows,
    act_rows,
    grad_rows,
    gather_semaphores,
    semaphores,
):
    greet, _, arrive, finish, _, load, load_wait, (launch, forward, hand_over) = (
        plane_gather_steps(pieces, block_ref, whole_ref, gather_semaphores, None)
    )
    hidden = open_rows.shape[1]
    count = SHARED + EXPERTS
    each = pieces // (count - READY)

    def span(expert, rows):
        return pl.ds(pl.multiple_of(expert * rows, rows), rows)

    def load_open(expert):
        slot = expert % 2
        return pltpu.make_async_copy(
            open_ref.at[span(expert, hidden)], open_rows.at[slot], semaphores.at[1, slot]
        )

    def load_ready(expert):
        slot = expert % 2
        return pltpu.make_async_copy(
            ready_up_ref.at[span(expert, 2 * hidden)], up_rows.at[slot], semaphores.at[2, slot]
        )

    def store_act(expert):
        slot = expert % 2
        return pltpu.make_async_copy(
            act_rows.at[slot], act_ref.at[span(expert, hidden)], semaphores.at[3, slot]
        )

    def advance(expert):
        for part in range(each):
            launch(each * expert + part)
        for part in range(each):
            forward(each * (expert + 3 - READY) + part + 1)
        for part in range(each):
            hand_over(each * (expert + 1 - READY) + part + 1)

        @pl.when(expert + 1 < count)
        def _():
            load_open(expert + 1).start()

        @pl.when(expert + 1 < READY)
        def _():
            load_ready(expert + 1).start()

        @pl.when((expert + 1 >= READY) & (expert + 1 < count))
        def _():
            for part in range(each):
                arrive(each * (expert + 1 - READY) + part)
            slot = (expert + 1) % 2
            first = (expert + 1 - READY) * 2 * hidden
            for copy in load(first, 2 * hidden, up_rows.at[slot], semaphores.at[2, slot]):
                copy.start()

        load_open(expert).wait()
        load_wait(2 * hidden, up_rows.at[expert % 2], semaphores.at[2, expert % 2])

        @pl.when(expert >= 2)
        def _():
            store_act(expert - 2).wait()

    def compute(expert, shared):
        slot = expert % 2
        gate_up = contract_last(up_rows[slot], inputs_ref[...])
        extra = None
        if shared:
            gate_up = gate_up + matmul(up_extra_ref[expert], mid_up_ref[...])
            extra = matmul(down_extra_ref[expert], grad_mid_ref[...])
        act, act_gated, gate_grad, grad_gate, grad_up = hidden_step(
            gate_up,
            open_rows[slot].astype(jnp.float32),
            gate_ref[pl.ds(expert, 1)],
            extra,
        )
        gate_grad_ref[pl.ds(expert, 1)] = gate_grad
        act_rows[slot] = act_gated
        grad_rows[:hidden] = grad_gate
        grad_rows[hidden:] = grad_up
        store_act(expert).start()
        grad_total[...] += contract_first(grad_rows[...], up_rows[slot])
        if shared:
            mid_down_ref[...] += contract_first(down_extra_ref[expert], act)
            grad_mid_up_ref[...] += contract_first(up_extra_ref[expert], grad_rows[...])
            grad_down_a_ref[expert] = contract_last(grad_mid_ref[...], act)
            grad_up_b_ref[expert] = ADAPTER_SCALE * contract_last(mid_up_ref[...], grad_rows[...])

    greet()
    pl.semaphore_wait(pltpu.get_barrier_semaphore(), 3)
    load_open(0).start()
    load_ready(0).start()
    grad_total[...] = jnp.zeros_like(grad_total)
    mid_down_ref[...] = jnp.zeros_like(mid_down_ref)
    grad_mid_up_ref[...] = jnp.zeros_like(grad_mid_up_ref)

    @pl.loop(0, SHARED)
    def _(expert):
        advance(expert)
        compute(expert, True)

    @pl.loop(SHARED, count)
    def _(expert):
        advance(expert)
        compute(expert, False)

    grad_ref[...] = to_low(grad_total[...])
    store_act(count - 2).wait()
    store_act(count - 1).wait()
    finish()


def experts_plain(inputs, gates, mid_up, grad_mid, up_extra, down_extra, up_rows, open_rows):
    count, length = gates.shape
    hidden = open_rows.shape[0] // count
    width = inputs.shape[1]
    grad_total = jnp.zeros((length, width), jnp.float32)
    act_parts, gate_grads, down_parts, up_parts = [], [], [], []
    mid_down = jnp.zeros((NARROW, length), jnp.float32)
    grad_mid_up = jnp.zeros((NARROW, length), jnp.float32)
    for expert in range(count):
        weights = up_rows[2 * hidden * expert : 2 * hidden * (expert + 1)]
        gate_up = contract_last(weights, inputs)
        extra = None
        if expert < SHARED:
            gate_up = gate_up + matmul(up_extra[expert], mid_up)
            extra = matmul(down_extra[expert], grad_mid)
        act, act_gated, gate_grad, grad_gate, grad_up = hidden_step(
            gate_up,
            open_rows[hidden * expert : hidden * (expert + 1)].astype(jnp.float32),
            gates[expert : expert + 1],
            extra,
        )
        grad = jnp.concatenate([grad_gate, grad_up], axis=0)
        act_parts.append(act_gated)
        gate_grads.append(gate_grad)
        grad_total = grad_total + contract_first(grad, weights)
        if expert < SHARED:
            mid_down = mid_down + contract_first(down_extra[expert], act)
            grad_mid_up = grad_mid_up + contract_first(up_extra[expert], grad)
            down_parts.append(contract_last(grad_mid, act))
            up_parts.append(ADAPTER_SCALE * contract_last(mid_up, grad))
    return (
        grad_total,
        jnp.concatenate(gate_grads, axis=0),
        mid_down,
        grad_mid_up,
        jnp.stack(down_parts),
        jnp.stack(up_parts),
        jnp.concatenate(act_parts, axis=0),
    )


def experts_step(
    inputs, gates, mid_up, grad_mid, up_extra, down_extra, ready_up, block, open_rows, number
):
    length, width = inputs.shape
    count = SHARED + EXPERTS
    hidden = open_rows.shape[0] // count
    if not in_plane():
        whole = lax.all_gather(block, "dp", axis=1, tiled=True)
        up_rows = jnp.concatenate([ready_up, whole], axis=0)
        return experts_plain(
            inputs, gates, mid_up, grad_mid, up_extra, down_extra, up_rows, open_rows
        )
    pieces = HALVES * (count - READY)
    return pl.pallas_call(
        functools.partial(experts_kernel, pieces),
        in_specs=in_vmem(6) + in_hbm(3),
        out_specs=in_vmem(6) + in_hbm(2),
        out_shape=[
            jax.ShapeDtypeStruct((length, width), jnp.bfloat16),
            jax.ShapeDtypeStruct((count, length), jnp.float32),
            jax.ShapeDtypeStruct((NARROW, length), jnp.float32),
            jax.ShapeDtypeStruct((NARROW, length), jnp.float32),
            jax.ShapeDtypeStruct((SHARED, NARROW, hidden), jnp.float32),
            jax.ShapeDtypeStruct((SHARED, NARROW, 2 * hidden), jnp.float32),
            jax.ShapeDtypeStruct((count * hidden, length), jnp.bfloat16),
            jax.ShapeDtypeStruct(((count - READY) * 2 * hidden, width), jnp.bfloat16),
        ],
        scratch_shapes=[
            pltpu.VMEM((length, width), jnp.float32),
            pltpu.VMEM((2, 2 * hidden, width), jnp.bfloat16),
            pltpu.VMEM((2, hidden, length), jnp.bfloat16),
            pltpu.VMEM((2, hidden, length), jnp.bfloat16),
            pltpu.VMEM((2 * hidden, length), jnp.bfloat16),
            pltpu.SemaphoreType.DMA((18, pieces)),
            pltpu.SemaphoreType.DMA((4, 2)),
        ],
        compiler_params=pltpu.CompilerParams(
            collective_id=number, has_side_effects=True, vmem_limit_bytes=60 * 2**20
        ),
        cost_estimate=pl.CostEstimate(flops=0, bytes_accessed=600 * 2**20, transcendentals=0),
    )(inputs, gates, mid_up, grad_mid, up_extra, down_extra, ready_up, block, open_rows)[:7]


def gathered(weight):
    return lax.all_gather(weight, "dp", axis=0, tiled=True)


def body(
    tokens,
    cotangent,
    attention_norm_gain,
    query_key_value_weight,
    query_key_value_bias,
    output_projection_weight,
    feedforward_norm_gain,
    router_matrix,
    shared_expert_gate_weight,
    routed_gate_up_weight,
    routed_down_weight,
    shared_expert_gate_up_weight,
    shared_expert_down_weight,
    routes,
    sequence_adapter_index,
    picture_piece_starts,
    adapter_query_key_value_lower,
    adapter_query_key_value_upper,
    adapter_output_lower,
    adapter_output_upper,
    adapter_shared_up_lower,
    adapter_shared_up_upper,
    adapter_shared_down_lower,
    adapter_shared_down_upper,
):
    length, width = tokens.shape
    set_id = sequence_adapter_index[0]
    starts = picture_piece_starts[0]

    def selected_experts(adapter_entry):
        return lax.dynamic_index_in_dim(adapter_entry, set_id, 0, keepdims=False)

    qkv_a, qkv_b, out_a, out_b = (
        selected_experts(adapter_query_key_value_lower),
        selected_experts(adapter_query_key_value_upper),
        selected_experts(adapter_output_lower),
        selected_experts(adapter_output_upper),
    )
    up_a, up_b, down_a, down_b = (
        selected_experts(adapter_shared_up_lower),
        selected_experts(adapter_shared_up_upper),
        selected_experts(adapter_shared_down_lower),
        selected_experts(adapter_shared_down_upper),
    )
    gain_attn_f = attention_norm_gain.astype(jnp.float32)
    gain_ffn_f = feedforward_norm_gain.astype(jnp.float32)
    tokens_f = tokens.astype(jnp.float32)
    normed = to_low(rms_scale(tokens_f, gain_attn_f))
    mid_qkv = to_low(matmul(normed, qkv_a))
    hidden = shared_expert_down_weight.shape[1] // SHARED
    rank = up_a.shape[1]

    def fill(rows):
        return jnp.pad(to_low(rows), ((0, NARROW - rows.shape[0]), (0, 0)))

    def fill_last(rows):
        return jnp.pad(to_low(rows), ((0, 0), (0, 0), (0, NARROW - rows.shape[2])))

    cotangent_down = ADAPTER_SCALE * contract_last(cotangent, down_b)
    up_extra = ADAPTER_SCALE * up_b.reshape(rank, 2, SHARED, hidden).transpose(2, 1, 3, 0)
    up_extra = fill_last(up_extra.reshape(SHARED, 2 * hidden, rank))
    down_extra = fill_last(down_a.reshape(SHARED, hidden, rank))
    depth = routed_gate_up_weight.shape[0]
    early = (READY - SHARED) * 2 * hidden
    shared_block = shared_expert_gate_up_weight.reshape(-1, 2, SHARED, hidden)
    up_block = jnp.transpose(routed_gate_up_weight, (1, 2, 3, 0)).reshape(-1, depth)
    ready_up = lax.all_gather(
        jnp.concatenate(
            [shared_block.transpose(2, 1, 3, 0).reshape(-1, depth), up_block[:early]], axis=0
        ),
        "dp",
        axis=1,
        tiled=True,
    )
    attention_rows = gathered(
        jnp.concatenate([query_key_value_weight, output_projection_weight[:, None]], axis=1)
    )
    qkv_rows, output_rows = attention_rows[:, :3], attention_rows[:, 3]
    normed, cotangent_down, up_extra, down_extra = lax.optimization_barrier(
        (normed, cotangent_down, up_extra, down_extra)
    )
    qkv_sum = jnp.einsum("tr,rsf->stf", normed, qkv_rows, preferred_element_type=jnp.float32)
    qkv_sum = qkv_sum + query_key_value_bias.astype(jnp.float32)[:, None, :]
    qkv_sum = qkv_sum + ADAPTER_SCALE * jnp.einsum(
        "tr,rsf->stf", mid_qkv, qkv_b, preferred_element_type=jnp.float32
    )
    cosine, sine_table = rope_tables(length)
    signs = jnp.where(jnp.arange(HEAD_SIZE) < HEAD_SIZE // 2, -1.0, 1.0)
    piece_ids = piece_index(jnp.arange(length, dtype=jnp.int32), starts)
    places = (cosine, sine_table * signs[None, :], piece_ids[:, None], piece_ids[None, :])
    query, keys, values, attended = attend(qkv_sum, *places)
    branch_part = contract_last(attended, output_rows)
    down_block = jnp.transpose(routed_down_weight, (1, 2, 0))
    down_block = jnp.concatenate(
        [shared_expert_down_weight.T, down_block.reshape(-1, depth)], axis=0
    )
    branch_total, down_rows, open_rows = summed_and_gathered(
        branch_part,
        matmul(attended, out_a),
        down_block,
        cotangent.T,
        1,
    )
    mid_out = to_low(branch_total[:, width : width + rank])
    hidden_here = (
        tokens_f
        + branch_total[:, :width].astype(jnp.float32)
        + ADAPTER_SCALE * matmul(mid_out, out_b)
    )
    hidden_scale = lax.rsqrt(
        jnp.mean(hidden_here * hidden_here, axis=1, keepdims=True) + EPSILON
    )
    normed_two = to_low(hidden_here * hidden_scale * gain_ffn_f)
    cot_f = cotangent.astype(jnp.float32)
    small_rows = gathered(
        jnp.concatenate(
            [
                router_matrix,
                shared_expert_gate_weight[:, None],
                jnp.full_like(shared_expert_gate_weight, set_id)[:, None],
            ],
            axis=1,
        )
    )
    factors = jnp.concatenate([small_rows[:, : EXPERTS + 1], up_a], axis=1)
    projected = matmul(normed_two, factors)
    router_probs = jax.nn.softmax(projected[:, :EXPERTS], axis=-1)
    shared_gate = jax.nn.sigmoid(projected[:, EXPERTS])
    mid_up = to_low(projected[:, EXPERTS + 1 :])
    expert_ids = jnp.arange(EXPERTS, dtype=jnp.int32)
    chosen = jnp.sum(
        (routes[:, :, None] == expert_ids[None, None, :]).astype(jnp.float32), axis=1
    )
    gates = jnp.concatenate(
        [jnp.broadcast_to(shared_gate[None], (SHARED, length)), (router_probs * chosen).T], axis=0
    )
    grad_mid_down = shared_gate[:, None] * cotangent_down
    (
        normed_two_part,
        gate_grads,
        mid_down_part,
        grad_mid_up_part,
        grad_down_a_parts,
        grad_up_b_parts,
        act_rows,
    ) = experts_step(
        normed_two,
        gates,
        fill(mid_up.T),
        fill(grad_mid_down.T),
        up_extra,
        down_extra,
        ready_up,
        up_block[early:],
        open_rows,
        5,
    )
    grad_down_a_local = grad_down_a_parts[:, :rank].transpose(1, 0, 2).reshape(rank, -1)
    grad_up_b_local = (
        grad_up_b_parts[:, :rank]
        .reshape(SHARED, rank, 2, hidden)
        .transpose(1, 2, 0, 3)
        .reshape(rank, 2, -1)
    )
    narrow_part = jnp.concatenate(
        [
            gate_grads[SHARED:],
            jnp.sum(gate_grads[:SHARED], axis=0, keepdims=True),
            grad_mid_up_part[:rank],
            mid_down_part[:rank],
        ],
        axis=0,
    ).T
    second_total, combined_part = summed_and_down(
        normed_two_part, narrow_part, act_rows, down_rows, 2
    )
    up_from = width + EXPERTS + 1
    grad_mid_up = to_low(second_total[:, up_from : up_from + rank])
    mid_down = to_low(second_total[:, up_from + rank : up_from + 2 * rank])

    def lanes(columns, first):
        return jnp.pad(columns, ((0, 0), (first, NARROW - first - columns.shape[1])))

    grad_hidden, grad_branch, grad_mid_out, grad_attended = epilogue(
        (
            second_total,
            hidden_here,
            hidden_scale,
            cotangent,
            lanes(router_probs, 0),
            lanes(chosen, 0),
            lanes(cotangent_down, EXPERTS + 1 + rank),
            shared_gate[:, None],
        ),
        (gain_ffn_f[None], lanes(factors, 0), fill(out_b), lanes(out_a, 0), output_rows),
    )
    grad_mid_out = grad_mid_out[:, :rank]
    grad_down_b_local = ADAPTER_SCALE * contract_first(
        to_low(shared_gate[:, None] * mid_down.astype(jnp.float32)), cotangent
    )
    grad_up_a_local = contract_first(grad_mid_up, normed_two)
    grad_out_b_local = ADAPTER_SCALE * contract_first(mid_out, grad_branch)
    grad_out_a_local = contract_first(grad_mid_out, attended)

    def side_by_side(local_grads):
        return jnp.concatenate([to_low(local_grad) for local_grad in local_grads], axis=1)

    early_grads = [
        grad_out_a_local,
        grad_up_a_local,
        grad_up_b_local.reshape(grad_up_b_local.shape[0], -1),
        grad_down_a_local,
        grad_down_b_local,
    ]
    grad_attended, early_flat = lax.optimization_barrier(
        (grad_attended, side_by_side(early_grads))
    )
    early_rows = lax.all_gather(early_flat, "dp", axis=0, tiled=False)
    upper = jnp.pad(
        ADAPTER_SCALE * qkv_b.transpose(1, 0, 2), ((0, 0), (0, NARROW - rank), (0, 0))
    )
    combined_here, grad_qkv, normed_part, mid_total = summed_and_attended_back(
        combined_part,
        qkv_rows.transpose(1, 0, 2),
        upper,
        (query, keys, values, grad_attended) + places,
        3,
    )
    mid_total, early_rows = lax.optimization_barrier((mid_total, early_rows))
    grad_mid_qkv = to_low(mid_total[:, :rank])
    late_grads = [
        (
            ADAPTER_SCALE
            * jnp.einsum("tr,stf->rsf", mid_qkv, grad_qkv, preferred_element_type=jnp.float32)
        ).reshape(rank, -1),
        contract_first(grad_mid_qkv, normed),
        grad_out_b_local,
    ]
    normed_part, late_flat = lax.optimization_barrier((normed_part, side_by_side(late_grads)))
    late_rows = lax.all_gather(late_flat, "dp", axis=0, tiled=False)
    extra_here = ADAPTER_SCALE * matmul(mid_down, down_b)
    output = to_low(hidden_here + combined_here + shared_gate[:, None] * extra_here)
    last_total = summed(normed_part, 4)
    last_total, late_rows = lax.optimization_barrier((last_total, late_rows))
    grad_normed = last_total.astype(jnp.float32) + contract_last(grad_mid_qkv, qkv_a)
    norm_attn_pull = jax.vjp(lambda rows: rms_scale(rows, gain_attn_f), tokens_f)[1]
    grad_tokens = to_low(grad_hidden + norm_attn_pull(grad_normed)[0])
    everyone = small_rows[:: small_rows.shape[0] // lax.axis_size("dp"), EXPERTS + 1]
    marker = to_low(
        jnp.arange(ADAPTER_SETS, dtype=jnp.int32)[:, None] == everyone.astype(jnp.int32)[None, :]
    )

    def adapter_sums(local_grads, rows):
        results, start = [], 0
        for local_grad in local_grads:
            size = local_grad.shape[1]
            results.append(
                jnp.einsum(
                    "cj,jrn->crn",
                    marker,
                    rows[:, :, start : start + size],
                    preferred_element_type=jnp.float32,
                )
            )
            start += size
        return results

    def flipped(total):
        return jnp.swapaxes(total, 1, 2)

    def opened(total, count):
        return total.reshape(total.shape[0], total.shape[1], count, -1)

    total_out_a, total_up_a, total_up_b, total_down_a, total_down_b = adapter_sums(
        early_grads, early_rows
    )
    total_qkv_b, total_qkv_a, total_out_b = adapter_sums(late_grads, late_rows)
    return (
        output,
        grad_tokens,
        flipped(total_qkv_a),
        opened(total_qkv_b, 3),
        flipped(total_out_a),
        total_out_b,
        flipped(total_up_a),
        opened(total_up_b, 2),
        flipped(total_down_a),
        total_down_b,
    )


def solution(mesh):
    return jax.shard_map(
        body,
        mesh=mesh,
        in_specs=(
            P("dp", None),
            P("dp", None),
            P(),
            P("dp", None, "tensor"),
            P(None, "tensor"),
            P("dp", "tensor"),
            P(),
            P("dp", None),
            P("dp"),
            P("dp", None, None, "tensor"),
            P("dp", None, "tensor"),
            P("dp", None, "tensor"),
            P("dp", "tensor"),
            P("dp", None),
            P("dp"),
            P("dp", None),
            P(),
            P(None, None, None, "tensor"),
            P(None, "tensor", None),
            P(),
            P(),
            P(None, None, None, "tensor"),
            P(None, "tensor", None),
            P(),
        ),
        out_specs=(
            P("dp", None),
            P("dp", None),
            P(),
            P(None, None, None, "tensor"),
            P(None, "tensor", None),
            P(),
            P(),
            P(None, None, None, "tensor"),
            P(None, "tensor", None),
            P(),
        ),
        check_vma=False,
    )
```

```python
import functools

import jax
import jax.numpy as jnp
from jax import lax
from jax.experimental import pallas as pl
from jax.experimental.pallas import tpu as pltpu
from jax.sharding import PartitionSpec as P

HEAD_SIZE = 128
TOP = 4
EXPERTS = 16
ADAPTER_SETS = 8
PIECE = 256


EPSILON = 1e-06
THETA = 1000000.0
ADAPTER_SCALE = 2.0
MASKED = -1e30
QUERY_ROWS = 256
NARROW = 128
MESH = pl.DeviceIdType.MESH
SUM_CHUNKS = 16
LAG = 1
AHEAD = 1
LEAD = 2
SHARED = 4
HALVES = 1
READY = 6


def matmul(left_side, right_side):
    return jnp.dot(left_side, right_side, preferred_element_type=jnp.float32)


def contract_last(left_side, right_side):
    return lax.dot_general(
        left_side, right_side, (((1,), (1,)), ((), ())), preferred_element_type=jnp.float32
    )


def contract_first(left_side, right_side):
    return lax.dot_general(
        left_side, right_side, (((0,), (0,)), ((), ())), preferred_element_type=jnp.float32
    )


def to_low(values):
    return values.astype(jnp.bfloat16)


def rms_scale(values, gain_values):
    return (
        values * lax.rsqrt(jnp.mean(values * values, axis=1, keepdims=True) + EPSILON) * gain_values
    )


def rope_tables(length):
    half_size = HEAD_SIZE // 2
    frequency = THETA ** (-jnp.arange(half_size, dtype=jnp.float32) * 2.0 / HEAD_SIZE)
    angles = jnp.arange(length, dtype=jnp.float32)[:, None] * frequency[None, :]
    return (
        jnp.concatenate([jnp.cos(angles)] * 2, axis=1),
        jnp.concatenate([jnp.sin(angles)] * 2, axis=1),
    )


def piece_index(positions, starts):
    inside = (positions[:, None] >= starts[None, :]) & (
        positions[:, None] < starts[None, :] + PIECE
    )
    labels = jnp.arange(starts.shape[0], dtype=jnp.int32)[None, :] + 1
    return jnp.sum(jnp.where(inside, labels, 0), axis=1) - 1


def line_sum_steps(
    chunks,
    lag,
    wide_ref,
    narrow_ref,
    total_ref,
    part_ref,
    from_end,
    pair_sum,
    from_pair,
    semaphores,
):
    place = lax.axis_index("tensor")
    width = wide_ref.shape[1]
    rows = part_ref.shape[0] // chunks
    inner = (place == 1) | (place == 2)
    end = (place == 0) | (place == 3)
    mate = jnp.where(place < 2, 1 - place, 5 - place)
    other = jnp.where(inner, 3 - place, place)

    def span(chunk):
        return pl.ds(pl.multiple_of(chunk * rows, rows), rows)

    def copy(source, target, chunk, lane, device):
        return pltpu.make_async_remote_copy(
            source.at[span(chunk)],
            target.at[span(chunk)],
            semaphores.at[2 * lane, chunk],
            semaphores.at[2 * lane + 1, chunk],
            device_id={"tensor": device},
            device_id_type=MESH,
        )

    def inward(chunk):
        return copy(part_ref, from_end, chunk, 0, mate)

    def across(chunk):
        return copy(pair_sum, from_pair, chunk, 1, other)

    def outward(chunk):
        return copy(total_ref, total_ref, chunk, 2, mate)

    def add(left_ref, right_ref, out_ref, chunk):
        out_ref[span(chunk)] = to_low(
            left_ref[span(chunk)].astype(jnp.float32) + right_ref[span(chunk)].astype(jnp.float32)
        )

    def stage(chunk):
        part_ref[span(chunk), :width] = to_low(wide_ref[span(chunk)])
        if narrow_ref is not None:
            part_ref[span(chunk), width:] = narrow_ref[span(chunk)]

    def greet(extra):
        barrier = pltpu.get_barrier_semaphore()
        pl.semaphore_signal(barrier, inc=1, device_id={"tensor": mate}, device_id_type=MESH)

        @pl.when(inner)
        def _():
            pl.semaphore_signal(barrier, inc=1, device_id={"tensor": other}, device_id_type=MESH)
            pl.semaphore_wait(barrier, 2 + extra)

        @pl.when(end)
        def _():
            pl.semaphore_wait(barrier, 1 + extra)

    def begin(first=0, last=chunks):
        @pl.when(end)
        def _():
            @pl.loop(first, last)
            def _(chunk):
                stage(chunk)
                inward(chunk).start()

    def advance(step):
        @pl.when(inner & (step < chunks))
        def _():
            stage(step)
            inward(step).wait_recv()
            add(part_ref, from_end, pair_sum, step)
            across(step).start()

        @pl.when(inner & (step >= lag) & (step < chunks + lag))
        def _():
            across(step - lag).wait_recv()
            add(pair_sum, from_pair, total_ref, step - lag)
            outward(step - lag).start()

    def finish():
        @pl.when(end)
        def _():
            @pl.loop(0, chunks)
            def _(chunk):
                inward(chunk).wait_send()
                outward(chunk).wait_recv()

        @pl.when(inner)
        def _():
            @pl.loop(0, chunks)
            def _(chunk):
                across(chunk).wait_send()
                outward(chunk).wait_send()

    return greet, begin, advance, finish


def plane_gather_steps(pieces, block_ref, whole_ref, semaphores, local_semaphore):
    spot = lax.axis_index("dp")
    depth = block_ref.shape[1]
    rows = block_ref.shape[0] // pieces
    core_mate = spot + 1 - 2 * (spot % 2)
    x_mate = spot + 2 - 4 * ((spot // 2) % 2)
    y_mate = spot + 4 - 8 * (spot // 4)
    x_y_mate = x_mate + 4 - 8 * (spot // 4)
    lanes = {
        "core": (spot, core_mate, 0, 1),
        "x": (spot, x_mate, 0, 1),
        "y": (spot, y_mate, 0, 1),
        "x_core": (x_mate, core_mate, 0, 1),
        "x_y": (x_mate, y_mate, 0, 2),
        "y_core": (y_mate, core_mate, 0, 1),
        "y_x": (y_mate, x_mate, 1, 2),
        "xy_core": (x_y_mate, core_mate, 0, 2),
        "yx_core": (x_y_mate, core_mate, 1, 2),
    }
    order = list(lanes)

    def send(name, piece):
        owner, device, part, parts = lanes[name]
        lane = order.index(name)
        span = pl.ds(
            pl.multiple_of(piece * rows + part * (rows // parts), rows // parts), rows // parts
        )
        columns = pl.ds(pl.multiple_of(owner * depth, depth), depth)
        target = whole_ref.at[span, columns]
        source = block_ref.at[span] if name in ("core", "x", "y") else target
        return pltpu.make_async_remote_copy(
            source,
            target,
            semaphores.at[2 * lane, piece],
            semaphores.at[2 * lane + 1, piece],
            device_id={"dp": device},
            device_id_type=MESH,
        )

    def own():
        columns = pl.ds(pl.multiple_of(spot * depth, depth), depth)
        return pltpu.make_async_copy(block_ref, whole_ref.at[:, columns], local_semaphore)

    def greet():
        barrier = pltpu.get_barrier_semaphore()
        for device in (core_mate, x_mate, y_mate):
            pl.semaphore_signal(barrier, inc=1, device_id={"dp": device}, device_id_type=MESH)

    def launch(piece):
        @pl.when((piece >= 0) & (piece < pieces))
        def _():
            for name in ("x", "y", "core"):
                send(name, piece).start()

    def forward(piece):
        @pl.when((piece >= 0) & (piece < pieces))
        def _():
            send("x", piece).wait_recv()
            send("x_y", piece).start()
            send("x_core", piece).start()
            send("y", piece).wait_recv()
            send("y_x", piece).start()
            send("y_core", piece).start()

    def hand_over(piece):
        @pl.when((piece >= 0) & (piece < pieces))
        def _():
            send("x_y", piece).wait_recv()
            send("xy_core", piece).start()
            send("y_x", piece).wait_recv()
            send("yx_core", piece).start()

    def advance(step):
        launch(step + LEAD)
        forward(step - AHEAD)
        hand_over(step - 2 * AHEAD)

    def load(first, count, target, semaphore):
        span = pl.ds(pl.multiple_of(first, rows), count)

        def columns(owner):
            return pl.ds(pl.multiple_of(owner * depth, depth), depth)

        here = columns(spot)
        copies = [pltpu.make_async_copy(block_ref.at[span], target.at[:, here], semaphore)]
        for shift in range(1, 8):
            there = columns((spot + shift) % 8)
            copies.append(
                pltpu.make_async_copy(
                    whole_ref.at[span, there], target.at[:, there], semaphore
                )
            )
        return copies

    def load_wait(count, target, semaphore):
        pltpu.make_async_copy(whole_ref.at[pl.ds(0, count)], target, semaphore).wait()

    def arrive(piece):
        for name in ("core", "x_core", "y_core", "xy_core", "yx_core"):
            send(name, piece).wait_recv()

    def finish():
        @pl.loop(0, pieces)
        def _(piece):
            for name in order:
                send(name, piece).wait_send()

    return greet, advance, arrive, finish, own, load, load_wait, (launch, forward, hand_over)


def line_sum_kernel(chunks, *refs):
    greet, begin, advance, finish = line_sum_steps(chunks, 1, *refs)
    greet(0)
    begin()

    @pl.loop(0, chunks + 1)
    def _(step):
        advance(step)

    finish()


def sum_gather_kernel(
    chunks,
    pieces,
    wide_ref,
    narrow_ref,
    block_ref,
    cotangent_ref,
    total_ref,
    whole_ref,
    open_ref,
    *scratch,
):
    greet, begin, advance, finish = line_sum_steps(
        chunks, LAG, wide_ref, narrow_ref, total_ref, *scratch[:5]
    )
    gather_semaphores, local_semaphores, piece_rows, open_rows = scratch[5:]
    gather_greet, gather_advance, gather_arrive, gather_finish, own, load, load_wait, stages = (
        plane_gather_steps(
            pieces, block_ref, whole_ref, gather_semaphores, local_semaphores.at[0]
        )
    )
    rows = piece_rows.shape[1]

    def store(piece):
        slot = piece % 2
        span = pl.ds(pl.multiple_of(piece * rows, rows), rows)
        return pltpu.make_async_copy(
            open_rows.at[slot], open_ref.at[span], local_semaphores.at[3 + slot]
        )

    gather_greet()
    greet(3)
    begin()
    own().start()

    @pl.loop(0, LEAD)
    def _(piece):
        stages[0](piece)

    @pl.loop(0, max(chunks + LAG, pieces + 3 * AHEAD + 1))
    def _(step):
        gather_advance(step)
        advance(step)

        @pl.when((step >= 3 * AHEAD) & (step < pieces + 3 * AHEAD))
        def _():
            piece = step - 3 * AHEAD
            gather_arrive(piece)
            slot = piece % 2
            for copy in load(piece * rows, rows, piece_rows.at[slot], local_semaphores.at[1 + slot]):
                copy.start()

        @pl.when((step > 3 * AHEAD) & (step <= pieces + 3 * AHEAD))
        def _():
            piece = step - 3 * AHEAD - 1
            slot = piece % 2
            load_wait(rows, piece_rows.at[slot], local_semaphores.at[1 + slot])

            @pl.when(piece >= 2)
            def _():
                store(piece - 2).wait()

            open_rows[piece % 2] = to_low(matmul(piece_rows[piece % 2], cotangent_ref[...]))
            store(piece).start()

    store(pieces - 2).wait()
    store(pieces - 1).wait()
    own().wait()
    gather_finish()
    finish()


def sum_down_kernel(
    chunks, wide_ref, narrow_ref, act_ref, down_ref, total_ref, out_ref, *scratch
):
    greet, begin, advance, finish = line_sum_steps(
        chunks, LAG, wide_ref, narrow_ref, total_ref, *scratch[:5]
    )
    semaphores, act_rows, down_rows, out_rows = scratch[5:]
    rows = act_rows.shape[1]
    blocks = down_ref.shape[0] // rows

    def loads(block):
        slot = block % 2
        span = pl.ds(pl.multiple_of(block * rows, rows), rows)
        return [
            pltpu.make_async_copy(act_ref.at[span], act_rows.at[slot], semaphores.at[0, slot]),
            pltpu.make_async_copy(down_ref.at[span], down_rows.at[slot], semaphores.at[1, slot]),
        ]

    for load in loads(0):
        load.start()
    greet(0)
    begin()
    out_rows[...] = jnp.zeros_like(out_rows)

    @pl.loop(0, max(blocks, chunks + LAG))
    def _(step):
        advance(step)

        @pl.when(step < blocks)
        def _():
            @pl.when(step + 1 < blocks)
            def _():
                for load in loads(step + 1):
                    load.start()

            for load in loads(step):
                load.wait()
            tile = min(256, out_rows.shape[0])

            @pl.loop(0, out_rows.shape[0] // tile)
            def _(index):
                span = pl.ds(pl.multiple_of(index * tile, tile), tile)
                out_rows[span] += contract_first(
                    act_rows[step % 2, :, span], down_rows[step % 2]
                )

    out_ref[...] = to_low(out_rows[...])
    finish()


def attend_back_sum_kernel(chunks, wide_ref, rows_ref, upper_ref, *refs):
    inputs, scratch = refs[:8], refs[12:]
    total_ref, grad_qkv_ref, normed_part_ref, mid_total_ref = refs[8:12]
    greet, begin, advance, finish = line_sum_steps(
        chunks, LAG, wide_ref, None, total_ref, *scratch[:5]
    )
    head_block = attend_back_steps(*inputs, grad_qkv_ref, *scratch[5:7])
    mid_part = scratch[7]
    _, mid_begin, mid_advance, mid_finish = line_sum_steps(
        1, 1, mid_part, None, mid_total_ref, *scratch[8:13]
    )
    length, heads_width = inputs[0].shape
    heads, blocks = heads_width // HEAD_SIZE, length // QUERY_ROWS
    each = blocks // 2
    rows = scratch[-2]
    load = pltpu.make_async_copy(rows_ref.at[:3], rows, scratch[-1].at[0])
    load.start()
    done = heads * each
    greet(0)
    begin(0, done + blocks)

    @pl.loop(0, heads)
    def _(head):
        for step in range(each):
            advance(head * each + step)
            head_block(head, 2 * step * QUERY_ROWS)
            head_block(head, (2 * step + 1) * QUERY_ROWS)

    mid_part[...] = grad_mid_rows(grad_qkv_ref, upper_ref)
    mid_begin()
    begin(done + blocks, chunks)
    load.wait()

    @pl.loop(0, blocks)
    def _(block):
        advance(done + block)
        span = pl.ds(pl.multiple_of(block * QUERY_ROWS, QUERY_ROWS), QUERY_ROWS)
        normed_part_ref[span] = to_low(
            sum(contract_last(grad_qkv_ref[part, span], rows[part]) for part in range(3))
        )

    mid_advance(0)

    advance(done + blocks)
    mid_advance(1)

    @pl.loop(done + blocks + 1, max(done + blocks + 1, chunks + LAG))
    def _(step):
        advance(step)

    mid_finish()
    finish()


def grad_mid_rows(grad_qkv_ref, upper_ref):
    return sum(contract_last(grad_qkv_ref[part], upper_ref[part]) for part in range(3))


def epilogue_kernel(
    total_ref,
    hidden_ref,
    scale_ref,
    cotangent_ref,
    gain_ref,
    probs_ref,
    chosen_ref,
    extra_ref,
    gate_ref,
    factors_ref,
    out_b_ref,
    out_a_ref,
    rows_ref,
    grad_hidden_ref,
    grad_branch_ref,
    grad_mid_ref,
    grad_attended_ref,
):
    width = hidden_ref.shape[1]
    narrow = total_ref[:, width:].astype(jnp.float32)
    lane = lax.broadcasted_iota(jnp.int32, narrow.shape, 1)
    probs = probs_ref[...]
    grad_probs = chosen_ref[...] * narrow
    grad_logits = probs * (grad_probs - jnp.sum(probs * grad_probs, axis=1, keepdims=True))
    only_gate = jnp.where(lane == EXPERTS, narrow, 0.0)
    gate_grad = jnp.sum(only_gate + narrow * extra_ref[...], axis=1, keepdims=True)
    gate = gate_ref[...]
    gate_logit = gate_grad * gate * (1.0 - gate)
    rank = extra_ref.shape[1] // 8
    rows = jnp.where(lane <= EXPERTS + rank, narrow, 0.0)
    rows = jnp.where(lane == EXPERTS, gate_logit, rows)
    rows = to_low(jnp.where(lane < EXPERTS, grad_logits, rows))
    grad_normed = total_ref[:, :width].astype(jnp.float32) + contract_last(rows, factors_ref[...])
    hidden = hidden_ref[...]
    scale = scale_ref[...]
    scaled = grad_normed * gain_ref[...]
    pull = jnp.mean(hidden * scaled, axis=1, keepdims=True)
    grad_hidden = (
        cotangent_ref[...].astype(jnp.float32)
        + scale * scaled
        - hidden * (scale * scale * scale * pull)
    )
    grad_hidden_ref[...] = grad_hidden
    grad_branch = to_low(grad_hidden)
    grad_branch_ref[...] = grad_branch
    grad_mid = to_low(ADAPTER_SCALE * contract_last(grad_branch, out_b_ref[...]))
    grad_mid_ref[...] = grad_mid
    grad_attended_ref[...] = to_low(
        matmul(grad_branch, rows_ref[0]) + contract_last(grad_mid, out_a_ref[...])
    )


def epilogue(blocked, still):
    length = blocked[0].shape[0]
    width, heads_width = still[-1].shape[1:]
    rows = min(length, 256)
    total, hidden, scale, cotangent, probs, chosen, extra, gate = blocked
    gain, factors, out_b, out_a, row_stack = still

    def block(array):
        return pl.BlockSpec((rows, array.shape[1]), lambda index: (index, 0))

    def whole(array):
        return pl.BlockSpec(array.shape, lambda index: (0, 0))

    outs = [
        jax.ShapeDtypeStruct((length, width), jnp.float32),
        jax.ShapeDtypeStruct((length, width), jnp.bfloat16),
        jax.ShapeDtypeStruct((length, NARROW), jnp.bfloat16),
        jax.ShapeDtypeStruct((length, heads_width), jnp.bfloat16),
    ]
    return pl.pallas_call(
        epilogue_kernel,
        grid=(length // rows,),
        in_specs=[block(array) for array in (total, hidden, scale, cotangent)]
        + [whole(gain)]
        + [block(array) for array in (probs, chosen, extra, gate)]
        + [whole(array) for array in (factors, out_b, out_a)]
        + [pl.BlockSpec((1, width, heads_width), lambda index: (3, 0, 0))],
        out_specs=[block(out) for out in outs],
        out_shape=outs,
        compiler_params=pltpu.CompilerParams(
            vmem_limit_bytes=56 * 2**20, dimension_semantics=("arbitrary",)
        ),
        cost_estimate=pl.CostEstimate(
            flops=2 * length * width * heads_width,
            bytes_accessed=32 * 2**20,
            transcendentals=0,
        ),
    )(
        total,
        hidden,
        scale,
        cotangent,
        gain,
        probs,
        chosen,
        extra,
        gate,
        factors,
        out_b,
        out_a,
        row_stack,
    )


def on_line():
    return lax.axis_size("tensor") == 4


def in_plane():
    return lax.axis_size("dp") == 8


def in_vmem(count):
    return [pl.BlockSpec(memory_space=pltpu.VMEM)] * count


def in_hbm(count):
    return [pl.BlockSpec(memory_space=pltpu.HBM)] * count


def sum_scratch(shape):
    return [pltpu.VMEM(shape, jnp.bfloat16)] * 4 + [pltpu.SemaphoreType.DMA((6, SUM_CHUNKS))]


def narrowed(narrow_part):
    pad = jnp.zeros((narrow_part.shape[0], NARROW - narrow_part.shape[1]), jnp.bfloat16)
    return jnp.concatenate([to_low(narrow_part), pad], axis=1)


def plain_sum(wide_part, narrow_part):
    if narrow_part is not None:
        pad = jnp.zeros((narrow_part.shape[0], NARROW - narrow_part.shape[1]), jnp.float32)
        wide_part = jnp.concatenate([wide_part, narrow_part, pad], axis=1)
    return lax.psum(wide_part, "tensor")


def plain_line_sum_kernel(chunks, wide_ref, *refs):
    line_sum_kernel(chunks, wide_ref, None, *refs)


def summed(wide_part, number):
    if not on_line():
        return plain_sum(wide_part, None)
    shape = wide_part.shape
    return pl.pallas_call(
        functools.partial(plain_line_sum_kernel, SUM_CHUNKS),
        out_shape=jax.ShapeDtypeStruct(shape, jnp.bfloat16),
        in_specs=in_vmem(1),
        out_specs=pl.BlockSpec(memory_space=pltpu.VMEM),
        scratch_shapes=sum_scratch(shape),
        compiler_params=pltpu.CompilerParams(
            collective_id=number, has_side_effects=True, vmem_limit_bytes=48 * 2**20
        ),
        cost_estimate=pl.CostEstimate(flops=0, bytes_accessed=300 * 2**20, transcendentals=0),
    )(wide_part)


def summed_and_gathered(wide_part, narrow_part, block, cotangents, number):
    length, width = wide_part.shape
    if not (on_line() and in_plane()):
        whole = lax.all_gather(block, "dp", axis=1, tiled=True)
        open_rows = to_low(matmul(whole, cotangents))
        return plain_sum(wide_part, narrow_part), whole, open_rows
    shape = (length, width + NARROW)
    pieces = SHARED + EXPERTS
    rows = block.shape[0] // pieces
    total, whole, open_rows = pl.pallas_call(
        functools.partial(sum_gather_kernel, SUM_CHUNKS, pieces),
        out_shape=[
            jax.ShapeDtypeStruct(shape, jnp.bfloat16),
            jax.ShapeDtypeStruct((block.shape[0], width), jnp.bfloat16),
            jax.ShapeDtypeStruct((block.shape[0], length), jnp.bfloat16),
        ],
        in_specs=in_vmem(2) + in_hbm(1) + in_vmem(1),
        out_specs=in_vmem(1) + in_hbm(2),
        scratch_shapes=sum_scratch(shape)
        + [
            pltpu.SemaphoreType.DMA((18, pieces)),
            pltpu.SemaphoreType.DMA((5,)),
            pltpu.VMEM((2, rows, width), jnp.bfloat16),
            pltpu.VMEM((2, rows, length), jnp.bfloat16),
        ],
        compiler_params=pltpu.CompilerParams(
            collective_id=number, has_side_effects=True, vmem_limit_bytes=58 * 2**20
        ),
        cost_estimate=pl.CostEstimate(flops=0, bytes_accessed=360 * 2**20, transcendentals=0),
    )(wide_part, narrowed(narrow_part), block, cotangents)
    return total, whole, open_rows


def summed_and_down(wide_part, narrow_part, act_rows, down_rows, number):
    length, width = wide_part.shape
    if not on_line():
        out = contract_first(act_rows, down_rows)
        return plain_sum(wide_part.astype(jnp.float32), narrow_part), out
    shape = (length, width + NARROW)
    rows = 2 * down_rows.shape[0] // (SHARED + EXPERTS)
    total, out = pl.pallas_call(
        functools.partial(sum_down_kernel, SUM_CHUNKS),
        out_shape=[
            jax.ShapeDtypeStruct(shape, jnp.bfloat16),
            jax.ShapeDtypeStruct((length, width), jnp.bfloat16),
        ],
        in_specs=in_vmem(2) + in_hbm(2),
        out_specs=in_vmem(2),
        scratch_shapes=sum_scratch(shape)
        + [
            pltpu.SemaphoreType.DMA((2, 2)),
            pltpu.VMEM((2, rows, length), jnp.bfloat16),
            pltpu.VMEM((2, rows, width), jnp.bfloat16),
            pltpu.VMEM((length, width), jnp.float32),
        ],
        compiler_params=pltpu.CompilerParams(
            collective_id=number, has_side_effects=True, vmem_limit_bytes=58 * 2**20
        ),
        cost_estimate=pl.CostEstimate(flops=0, bytes_accessed=300 * 2**20, transcendentals=0),
    )(wide_part, narrowed(narrow_part), act_rows, down_rows)
    return total, out


def block_mask(first, rows, extent, row_piece_ref, col_piece_ref):
    row_place = lax.broadcasted_iota(jnp.int32, (rows, extent), 0) + first
    col_place = lax.broadcasted_iota(jnp.int32, (rows, extent), 1)
    row_piece = row_piece_ref[first : first + rows, 0:1]
    together = (row_piece == col_piece_ref[0:1, :extent]) & (row_piece >= 0)
    return (col_place <= row_place) | together


def block_probs(query_rows, keys, allowed):
    scores = jnp.where(allowed, contract_last(query_rows, keys) * HEAD_SIZE**-0.5, MASKED)
    raised = jnp.exp(scores - jnp.max(scores, axis=1, keepdims=True))
    return raised * (1.0 / jnp.sum(raised, axis=1, keepdims=True))


def half_turn(values, signed_sine):
    return pltpu.roll(values, HEAD_SIZE // 2, 1) * signed_sine


def attend_kernel(
    qkv_ref,
    cosine_ref,
    sine_ref,
    row_piece_ref,
    col_piece_ref,
    query_ref,
    keys_ref,
    values_ref,
    attended_ref,
):
    length = qkv_ref.shape[1]

    @pl.loop(0, qkv_ref.shape[2] // HEAD_SIZE)
    def _(head):
        column = pl.ds(pl.multiple_of(head * HEAD_SIZE, HEAD_SIZE), HEAD_SIZE)
        for source, target in ((0, query_ref), (1, keys_ref)):
            raw = qkv_ref[source, :, column]
            target[:, column] = to_low(raw * cosine_ref[...] + half_turn(raw, sine_ref[...]))
        values_ref[:, column] = to_low(qkv_ref[2, :, column])
        for first in range(0, length, QUERY_ROWS):
            extent = min(length, first + QUERY_ROWS + PIECE)
            allowed = block_mask(first, QUERY_ROWS, extent, row_piece_ref, col_piece_ref)
            probs = block_probs(
                query_ref[first : first + QUERY_ROWS, column], keys_ref[:extent, column], allowed
            )
            attended_ref[first : first + QUERY_ROWS, column] = to_low(
                matmul(to_low(probs), values_ref[:extent, column])
            )


def attend(qkv, cosine, signed_sine, row_piece, col_piece):
    length, heads_width = qkv.shape[1:]
    shape = jax.ShapeDtypeStruct((length, heads_width), jnp.bfloat16)
    return pl.pallas_call(
        attend_kernel,
        out_shape=[shape] * 4,
        in_specs=[pl.BlockSpec(memory_space=pltpu.VMEM)] * 5,
        out_specs=[pl.BlockSpec(memory_space=pltpu.VMEM)] * 4,
        compiler_params=pltpu.CompilerParams(vmem_limit_bytes=48 * 2**20),
        cost_estimate=pl.CostEstimate(
            flops=4 * length * length * heads_width,
            bytes_accessed=16 * 2**20,
            transcendentals=length * length * heads_width // HEAD_SIZE,
        ),
    )(qkv, cosine, signed_sine, row_piece, col_piece)


def attend_back_steps(
    query_ref,
    keys_ref,
    values_ref,
    grad_ref,
    cosine_ref,
    sine_ref,
    row_piece_ref,
    col_piece_ref,
    grad_qkv_ref,
    grad_keys,
    grad_values,
):
    length = query_ref.shape[0]

    def turned_back(grad, first):
        span = slice(first, first + grad.shape[0])
        scaled = grad * HEAD_SIZE**-0.5
        return to_low(scaled * cosine_ref[span] - half_turn(scaled, sine_ref[span]))

    def head_block(head, first):
        column = pl.ds(pl.multiple_of(head * HEAD_SIZE, HEAD_SIZE), HEAD_SIZE)
        span = slice(first, first + QUERY_ROWS)
        extent = min(length, first + QUERY_ROWS + PIECE)
        if first == 0:
            grad_keys[...] = jnp.zeros_like(grad_keys)
            grad_values[...] = jnp.zeros_like(grad_values)
        allowed = block_mask(first, QUERY_ROWS, extent, row_piece_ref, col_piece_ref)
        query_rows = query_ref[span, column]
        keys = keys_ref[:extent, column]
        grad_rows = grad_ref[span, column]
        probs = block_probs(query_rows, keys, allowed)
        grad_probs = contract_last(grad_rows, values_ref[:extent, column])
        shift = jnp.sum(probs * grad_probs, axis=1, keepdims=True)
        grad_scores = to_low(probs * (grad_probs - shift))
        grad_values[:extent] += contract_first(to_low(probs), grad_rows)
        grad_keys[:extent] += contract_first(grad_scores, query_rows)
        grad_qkv_ref[0, span, column] = turned_back(matmul(grad_scores, keys), first)
        if first + QUERY_ROWS >= length:
            grad_qkv_ref[1, :, column] = turned_back(grad_keys[...], 0)
            grad_qkv_ref[2, :, column] = to_low(grad_values[...])

    return head_block


def attend_back_kernel(*refs):
    head_block = attend_back_steps(*refs)

    @pl.loop(0, refs[0].shape[1] // HEAD_SIZE)
    def _(head):
        for first in range(0, refs[0].shape[0], QUERY_ROWS):
            head_block(head, first)


def attend_back(query, keys, values, grads, cosine, signed_sine, row_piece, col_piece):
    length, heads_width = query.shape
    return pl.pallas_call(
        attend_back_kernel,
        out_shape=jax.ShapeDtypeStruct((3, length, heads_width), jnp.bfloat16),
        in_specs=[pl.BlockSpec(memory_space=pltpu.VMEM)] * 8,
        out_specs=pl.BlockSpec(memory_space=pltpu.VMEM),
        scratch_shapes=[pltpu.VMEM((length, HEAD_SIZE), jnp.float32)] * 2,
        compiler_params=pltpu.CompilerParams(vmem_limit_bytes=48 * 2**20),
        cost_estimate=pl.CostEstimate(
            flops=10 * length * length * heads_width,
            bytes_accessed=16 * 2**20,
            transcendentals=length * length * heads_width // HEAD_SIZE,
        ),
    )(query, keys, values, grads, cosine, signed_sine, row_piece, col_piece)


def summed_and_attended_back(wide_part, rows, upper, attention_inputs, number):
    if not on_line():
        grad_qkv = attend_back(*attention_inputs)
        normed_part = sum(contract_last(grad_qkv[part], rows[part]) for part in range(3))
        mid_total = lax.psum(grad_mid_rows(grad_qkv, upper), "tensor")
        return plain_sum(wide_part, None), grad_qkv, normed_part, mid_total
    shape = wide_part.shape
    length, heads_width = attention_inputs[0].shape
    narrow_shape = (length, NARROW)
    return pl.pallas_call(
        functools.partial(attend_back_sum_kernel, SUM_CHUNKS),
        out_shape=[
            jax.ShapeDtypeStruct(shape, jnp.bfloat16),
            jax.ShapeDtypeStruct((3, length, heads_width), jnp.bfloat16),
            jax.ShapeDtypeStruct(shape, jnp.bfloat16),
            jax.ShapeDtypeStruct(narrow_shape, jnp.bfloat16),
        ],
        in_specs=in_vmem(1) + in_hbm(1) + in_vmem(1 + len(attention_inputs)),
        out_specs=in_vmem(4),
        scratch_shapes=sum_scratch(shape)
        + [pltpu.VMEM((length, HEAD_SIZE), jnp.float32)] * 2
        + [pltpu.VMEM(narrow_shape, jnp.float32)]
        + [pltpu.VMEM(narrow_shape, jnp.bfloat16)] * 4
        + [pltpu.SemaphoreType.DMA((6, 1))]
        + [pltpu.VMEM((3,) + rows.shape[1:], jnp.bfloat16), pltpu.SemaphoreType.DMA((1,))],
        compiler_params=pltpu.CompilerParams(
            collective_id=number, has_side_effects=True, vmem_limit_bytes=60 * 2**20
        ),
        cost_estimate=pl.CostEstimate(flops=0, bytes_accessed=300 * 2**20, transcendentals=0),
    )(wide_part, rows, upper, *attention_inputs)


def hidden_step(gate_up, open_part, gate_row, extra):
    hidden = open_part.shape[0]
    gate_half, up_half = gate_up[:hidden], gate_up[hidden:]
    squashed = 1.0 / (1.0 + jnp.exp(-gate_half))
    act = to_low(gate_half * squashed * up_half)
    act_f = act.astype(jnp.float32)
    gate_grad = jnp.sum(act_f * open_part, axis=0, keepdims=True)
    grad_act = gate_row * open_part
    if extra is not None:
        grad_act = grad_act + extra
    grad_gate = to_low(grad_act * up_half * squashed * (1.0 + gate_half * (1.0 - squashed)))
    grad_up = to_low(grad_act * gate_half * squashed)
    return act, to_low(gate_row * act_f), gate_grad, grad_gate, grad_up


def experts_kernel(
    pieces,
    inputs_ref,
    gate_ref,
    mid_up_ref,
    grad_mid_ref,
    up_extra_ref,
    down_extra_ref,
    ready_up_ref,
    block_ref,
    open_ref,
    grad_ref,
    gate_grad_ref,
    mid_down_ref,
    grad_mid_up_ref,
    grad_down_a_ref,
    grad_up_b_ref,
    act_ref,
    whole_ref,
    grad_total,
    up_rows,
    open_rows,
    act_rows,
    grad_rows,
    gather_semaphores,
    semaphores,
):
    greet, _, arrive, finish, _, load, load_wait, (launch, forward, hand_over) = (
        plane_gather_steps(pieces, block_ref, whole_ref, gather_semaphores, None)
    )
    hidden = open_rows.shape[1]
    count = SHARED + EXPERTS
    each = pieces // (count - READY)

    def span(expert, rows):
        return pl.ds(pl.multiple_of(expert * rows, rows), rows)

    def load_open(expert):
        slot = expert % 2
        return pltpu.make_async_copy(
            open_ref.at[span(expert, hidden)], open_rows.at[slot], semaphores.at[1, slot]
        )

    def load_ready(expert):
        slot = expert % 2
        return pltpu.make_async_copy(
            ready_up_ref.at[span(expert, 2 * hidden)], up_rows.at[slot], semaphores.at[2, slot]
        )

    def store_act(expert):
        slot = expert % 2
        return pltpu.make_async_copy(
            act_rows.at[slot], act_ref.at[span(expert, hidden)], semaphores.at[3, slot]
        )

    def advance(expert):
        for part in range(each):
            launch(each * expert + part)
        for part in range(each):
            forward(each * (expert + 3 - READY) + part + 1)
        for part in range(each):
            hand_over(each * (expert + 1 - READY) + part + 1)

        @pl.when(expert + 1 < count)
        def _():
            load_open(expert + 1).start()

        @pl.when(expert + 1 < READY)
        def _():
            load_ready(expert + 1).start()

        @pl.when((expert + 1 >= READY) & (expert + 1 < count))
        def _():
            for part in range(each):
                arrive(each * (expert + 1 - READY) + part)
            slot = (expert + 1) % 2
            first = (expert + 1 - READY) * 2 * hidden
            for copy in load(first, 2 * hidden, up_rows.at[slot], semaphores.at[2, slot]):
                copy.start()

        load_open(expert).wait()
        load_wait(2 * hidden, up_rows.at[expert % 2], semaphores.at[2, expert % 2])

        @pl.when(expert >= 2)
        def _():
            store_act(expert - 2).wait()

    def compute(expert, shared):
        slot = expert % 2
        gate_up = contract_last(up_rows[slot], inputs_ref[...])
        extra = None
        if shared:
            gate_up = gate_up + matmul(up_extra_ref[expert], mid_up_ref[...])
            extra = matmul(down_extra_ref[expert], grad_mid_ref[...])
        act, act_gated, gate_grad, grad_gate, grad_up = hidden_step(
            gate_up,
            open_rows[slot].astype(jnp.float32),
            gate_ref[pl.ds(expert, 1)],
            extra,
        )
        gate_grad_ref[pl.ds(expert, 1)] = gate_grad
        act_rows[slot] = act_gated
        grad_rows[:hidden] = grad_gate
        grad_rows[hidden:] = grad_up
        store_act(expert).start()
        grad_total[...] += contract_first(grad_rows[...], up_rows[slot])
        if shared:
            mid_down_ref[...] += contract_first(down_extra_ref[expert], act)
            grad_mid_up_ref[...] += contract_first(up_extra_ref[expert], grad_rows[...])
            grad_down_a_ref[expert] = contract_last(grad_mid_ref[...], act)
            grad_up_b_ref[expert] = ADAPTER_SCALE * contract_last(mid_up_ref[...], grad_rows[...])

    greet()
    pl.semaphore_wait(pltpu.get_barrier_semaphore(), 3)
    load_open(0).start()
    load_ready(0).start()
    grad_total[...] = jnp.zeros_like(grad_total)
    mid_down_ref[...] = jnp.zeros_like(mid_down_ref)
    grad_mid_up_ref[...] = jnp.zeros_like(grad_mid_up_ref)

    @pl.loop(0, SHARED)
    def _(expert):
        advance(expert)
        compute(expert, True)

    @pl.loop(SHARED, count)
    def _(expert):
        advance(expert)
        compute(expert, False)

    grad_ref[...] = to_low(grad_total[...])
    store_act(count - 2).wait()
    store_act(count - 1).wait()
    finish()


def experts_plain(inputs, gates, mid_up, grad_mid, up_extra, down_extra, up_rows, open_rows):
    count, length = gates.shape
    hidden = open_rows.shape[0] // count
    width = inputs.shape[1]
    grad_total = jnp.zeros((length, width), jnp.float32)
    act_parts, gate_grads, down_parts, up_parts = [], [], [], []
    mid_down = jnp.zeros((NARROW, length), jnp.float32)
    grad_mid_up = jnp.zeros((NARROW, length), jnp.float32)
    for expert in range(count):
        weights = up_rows[2 * hidden * expert : 2 * hidden * (expert + 1)]
        gate_up = contract_last(weights, inputs)
        extra = None
        if expert < SHARED:
            gate_up = gate_up + matmul(up_extra[expert], mid_up)
            extra = matmul(down_extra[expert], grad_mid)
        act, act_gated, gate_grad, grad_gate, grad_up = hidden_step(
            gate_up,
            open_rows[hidden * expert : hidden * (expert + 1)].astype(jnp.float32),
            gates[expert : expert + 1],
            extra,
        )
        grad = jnp.concatenate([grad_gate, grad_up], axis=0)
        act_parts.append(act_gated)
        gate_grads.append(gate_grad)
        grad_total = grad_total + contract_first(grad, weights)
        if expert < SHARED:
            mid_down = mid_down + contract_first(down_extra[expert], act)
            grad_mid_up = grad_mid_up + contract_first(up_extra[expert], grad)
            down_parts.append(contract_last(grad_mid, act))
            up_parts.append(ADAPTER_SCALE * contract_last(mid_up, grad))
    return (
        grad_total,
        jnp.concatenate(gate_grads, axis=0),
        mid_down,
        grad_mid_up,
        jnp.stack(down_parts),
        jnp.stack(up_parts),
        jnp.concatenate(act_parts, axis=0),
    )


def experts_step(
    inputs, gates, mid_up, grad_mid, up_extra, down_extra, ready_up, block, open_rows, number
):
    length, width = inputs.shape
    count = SHARED + EXPERTS
    hidden = open_rows.shape[0] // count
    if not in_plane():
        whole = lax.all_gather(block, "dp", axis=1, tiled=True)
        up_rows = jnp.concatenate([ready_up, whole], axis=0)
        return experts_plain(
            inputs, gates, mid_up, grad_mid, up_extra, down_extra, up_rows, open_rows
        )
    pieces = HALVES * (count - READY)
    return pl.pallas_call(
        functools.partial(experts_kernel, pieces),
        in_specs=in_vmem(6) + in_hbm(3),
        out_specs=in_vmem(6) + in_hbm(2),
        out_shape=[
            jax.ShapeDtypeStruct((length, width), jnp.bfloat16),
            jax.ShapeDtypeStruct((count, length), jnp.float32),
            jax.ShapeDtypeStruct((NARROW, length), jnp.float32),
            jax.ShapeDtypeStruct((NARROW, length), jnp.float32),
            jax.ShapeDtypeStruct((SHARED, NARROW, hidden), jnp.float32),
            jax.ShapeDtypeStruct((SHARED, NARROW, 2 * hidden), jnp.float32),
            jax.ShapeDtypeStruct((count * hidden, length), jnp.bfloat16),
            jax.ShapeDtypeStruct(((count - READY) * 2 * hidden, width), jnp.bfloat16),
        ],
        scratch_shapes=[
            pltpu.VMEM((length, width), jnp.float32),
            pltpu.VMEM((2, 2 * hidden, width), jnp.bfloat16),
            pltpu.VMEM((2, hidden, length), jnp.bfloat16),
            pltpu.VMEM((2, hidden, length), jnp.bfloat16),
            pltpu.VMEM((2 * hidden, length), jnp.bfloat16),
            pltpu.SemaphoreType.DMA((18, pieces)),
            pltpu.SemaphoreType.DMA((4, 2)),
        ],
        compiler_params=pltpu.CompilerParams(
            collective_id=number, has_side_effects=True, vmem_limit_bytes=60 * 2**20
        ),
        cost_estimate=pl.CostEstimate(flops=0, bytes_accessed=600 * 2**20, transcendentals=0),
    )(inputs, gates, mid_up, grad_mid, up_extra, down_extra, ready_up, block, open_rows)[:7]


def gathered(weight):
    return lax.all_gather(weight, "dp", axis=0, tiled=True)


def body(
    tokens,
    cotangent,
    attention_norm_gain,
    query_key_value_weight,
    query_key_value_bias,
    output_projection_weight,
    feedforward_norm_gain,
    router_matrix,
    shared_expert_gate_weight,
    routed_gate_up_weight,
    routed_down_weight,
    shared_expert_gate_up_weight,
    shared_expert_down_weight,
    routes,
    sequence_adapter_index,
    picture_piece_starts,
    adapter_query_key_value_lower,
    adapter_query_key_value_upper,
    adapter_output_lower,
    adapter_output_upper,
    adapter_shared_up_lower,
    adapter_shared_up_upper,
    adapter_shared_down_lower,
    adapter_shared_down_upper,
):
    length, width = tokens.shape
    set_id = sequence_adapter_index[0]
    starts = picture_piece_starts[0]

    def selected_experts(adapter_entry):
        return lax.dynamic_index_in_dim(adapter_entry, set_id, 0, keepdims=False)

    qkv_a, qkv_b, out_a, out_b = (
        selected_experts(adapter_query_key_value_lower),
        selected_experts(adapter_query_key_value_upper),
        selected_experts(adapter_output_lower),
        selected_experts(adapter_output_upper),
    )
    up_a, up_b, down_a, down_b = (
        selected_experts(adapter_shared_up_lower),
        selected_experts(adapter_shared_up_upper),
        selected_experts(adapter_shared_down_lower),
        selected_experts(adapter_shared_down_upper),
    )
    gain_attn_f = attention_norm_gain.astype(jnp.float32)
    gain_ffn_f = feedforward_norm_gain.astype(jnp.float32)
    tokens_f = tokens.astype(jnp.float32)
    normed = to_low(rms_scale(tokens_f, gain_attn_f))
    mid_qkv = to_low(matmul(normed, qkv_a))
    hidden = shared_expert_down_weight.shape[1] // SHARED
    rank = up_a.shape[1]

    def fill(rows):
        return jnp.pad(to_low(rows), ((0, NARROW - rows.shape[0]), (0, 0)))

    def fill_last(rows):
        return jnp.pad(to_low(rows), ((0, 0), (0, 0), (0, NARROW - rows.shape[2])))

    cotangent_down = ADAPTER_SCALE * contract_last(cotangent, down_b)
    up_extra = ADAPTER_SCALE * up_b.reshape(rank, 2, SHARED, hidden).transpose(2, 1, 3, 0)
    up_extra = fill_last(up_extra.reshape(SHARED, 2 * hidden, rank))
    down_extra = fill_last(down_a.reshape(SHARED, hidden, rank))
    depth = routed_gate_up_weight.shape[0]
    early = (READY - SHARED) * 2 * hidden
    shared_block = shared_expert_gate_up_weight.reshape(-1, 2, SHARED, hidden)
    up_block = jnp.transpose(routed_gate_up_weight, (1, 2, 3, 0)).reshape(-1, depth)
    ready_up = lax.all_gather(
        jnp.concatenate(
            [shared_block.transpose(2, 1, 3, 0).reshape(-1, depth), up_block[:early]], axis=0
        ),
        "dp",
        axis=1,
        tiled=True,
    )
    attention_rows = gathered(
        jnp.concatenate([query_key_value_weight, output_projection_weight[:, None]], axis=1)
    )
    qkv_rows, output_rows = attention_rows[:, :3], attention_rows[:, 3]
    row_stack = attention_rows.transpose(1, 0, 2)
    normed, cotangent_down, up_extra, down_extra = lax.optimization_barrier(
        (normed, cotangent_down, up_extra, down_extra)
    )
    qkv_sum = jnp.einsum("tr,rsf->stf", normed, qkv_rows, preferred_element_type=jnp.float32)
    qkv_sum = qkv_sum + query_key_value_bias.astype(jnp.float32)[:, None, :]
    qkv_sum = qkv_sum + ADAPTER_SCALE * jnp.einsum(
        "tr,rsf->stf", mid_qkv, qkv_b, preferred_element_type=jnp.float32
    )
    cosine, sine_table = rope_tables(length)
    signs = jnp.where(jnp.arange(HEAD_SIZE) < HEAD_SIZE // 2, -1.0, 1.0)
    piece_ids = piece_index(jnp.arange(length, dtype=jnp.int32), starts)
    places = (cosine, sine_table * signs[None, :], piece_ids[:, None], piece_ids[None, :])
    query, keys, values, attended = attend(qkv_sum, *places)
    branch_part = contract_last(attended, output_rows)
    down_block = jnp.transpose(routed_down_weight, (1, 2, 0))
    down_block = jnp.concatenate(
        [shared_expert_down_weight.T, down_block.reshape(-1, depth)], axis=0
    )
    branch_total, down_rows, open_rows = summed_and_gathered(
        branch_part,
        matmul(attended, out_a),
        down_block,
        cotangent.T,
        1,
    )
    mid_out = to_low(branch_total[:, width : width + rank])
    hidden_here = (
        tokens_f
        + branch_total[:, :width].astype(jnp.float32)
        + ADAPTER_SCALE * matmul(mid_out, out_b)
    )
    hidden_scale = lax.rsqrt(
        jnp.mean(hidden_here * hidden_here, axis=1, keepdims=True) + EPSILON
    )
    normed_two = to_low(hidden_here * hidden_scale * gain_ffn_f)
    cot_f = cotangent.astype(jnp.float32)
    small_rows = gathered(
        jnp.concatenate(
            [
                router_matrix,
                shared_expert_gate_weight[:, None],
                jnp.full_like(shared_expert_gate_weight, set_id)[:, None],
            ],
            axis=1,
        )
    )
    factors = jnp.concatenate([small_rows[:, : EXPERTS + 1], up_a], axis=1)
    projected = matmul(normed_two, factors)
    router_probs = jax.nn.softmax(projected[:, :EXPERTS], axis=-1)
    shared_gate = jax.nn.sigmoid(projected[:, EXPERTS])
    mid_up = to_low(projected[:, EXPERTS + 1 :])
    expert_ids = jnp.arange(EXPERTS, dtype=jnp.int32)
    chosen = jnp.sum(
        (routes[:, :, None] == expert_ids[None, None, :]).astype(jnp.float32), axis=1
    )
    gates = jnp.concatenate(
        [jnp.broadcast_to(shared_gate[None], (SHARED, length)), (router_probs * chosen).T], axis=0
    )
    grad_mid_down = shared_gate[:, None] * cotangent_down
    (
        normed_two_part,
        gate_grads,
        mid_down_part,
        grad_mid_up_part,
        grad_down_a_parts,
        grad_up_b_parts,
        act_rows,
    ) = experts_step(
        normed_two,
        gates,
        fill(mid_up.T),
        fill(grad_mid_down.T),
        up_extra,
        down_extra,
        ready_up,
        up_block[early:],
        open_rows,
        5,
    )
    grad_down_a_local = grad_down_a_parts[:, :rank].transpose(1, 0, 2).reshape(rank, -1)
    grad_up_b_local = (
        grad_up_b_parts[:, :rank]
        .reshape(SHARED, rank, 2, hidden)
        .transpose(1, 2, 0, 3)
        .reshape(rank, 2, -1)
    )
    narrow_part = jnp.concatenate(
        [
            gate_grads[SHARED:],
            jnp.sum(gate_grads[:SHARED], axis=0, keepdims=True),
            grad_mid_up_part[:rank],
            mid_down_part[:rank],
        ],
        axis=0,
    ).T
    second_total, combined_part = summed_and_down(
        normed_two_part, narrow_part, act_rows, down_rows, 2
    )
    up_from = width + EXPERTS + 1
    grad_mid_up = to_low(second_total[:, up_from : up_from + rank])
    mid_down = to_low(second_total[:, up_from + rank : up_from + 2 * rank])

    def lanes(columns, first):
        return jnp.pad(columns, ((0, 0), (first, NARROW - first - columns.shape[1])))

    grad_hidden, grad_branch, grad_mid_out, grad_attended = epilogue(
        (
            second_total,
            hidden_here,
            hidden_scale,
            cotangent,
            lanes(router_probs, 0),
            lanes(chosen, 0),
            lanes(cotangent_down, EXPERTS + 1 + rank),
            shared_gate[:, None],
        ),
        (gain_ffn_f[None], lanes(factors, 0), fill(out_b), lanes(out_a, 0), row_stack),
    )
    grad_mid_out = grad_mid_out[:, :rank]
    grad_down_b_local = ADAPTER_SCALE * contract_first(
        to_low(shared_gate[:, None] * mid_down.astype(jnp.float32)), cotangent
    )
    grad_up_a_local = contract_first(grad_mid_up, normed_two)
    grad_out_b_local = ADAPTER_SCALE * contract_first(mid_out, grad_branch)
    grad_out_a_local = contract_first(grad_mid_out, attended)

    def side_by_side(local_grads):
        return jnp.concatenate([to_low(local_grad) for local_grad in local_grads], axis=1)

    early_grads = [
        grad_out_a_local,
        grad_up_a_local,
        grad_up_b_local.reshape(grad_up_b_local.shape[0], -1),
        grad_down_a_local,
        grad_down_b_local,
    ]
    grad_attended, early_flat = lax.optimization_barrier(
        (grad_attended, side_by_side(early_grads))
    )
    early_rows = lax.all_gather(early_flat, "dp", axis=0, tiled=True)
    upper = jnp.pad(
        ADAPTER_SCALE * qkv_b.transpose(1, 0, 2), ((0, 0), (0, NARROW - rank), (0, 0))
    )
    combined_here, grad_qkv, normed_part, mid_total = summed_and_attended_back(
        combined_part,
        row_stack,
        upper,
        (query, keys, values, grad_attended) + places,
        3,
    )
    mid_total, early_rows = lax.optimization_barrier((mid_total, early_rows))
    grad_mid_qkv = to_low(mid_total[:, :rank])
    late_grads = [
        (
            ADAPTER_SCALE
            * jnp.einsum("tr,stf->rsf", mid_qkv, grad_qkv, preferred_element_type=jnp.float32)
        ).reshape(rank, -1),
        contract_first(grad_mid_qkv, normed),
        grad_out_b_local,
    ]
    normed_part, late_flat = lax.optimization_barrier((normed_part, side_by_side(late_grads)))
    late_rows = lax.all_gather(late_flat, "dp", axis=0, tiled=True)
    extra_here = ADAPTER_SCALE * matmul(mid_down, down_b)
    output = to_low(hidden_here + combined_here + shared_gate[:, None] * extra_here)
    last_total = summed(normed_part, 4)
    last_total, late_rows = lax.optimization_barrier((last_total, late_rows))
    grad_normed = last_total.astype(jnp.float32) + contract_last(grad_mid_qkv, qkv_a)
    norm_attn_pull = jax.vjp(lambda rows: rms_scale(rows, gain_attn_f), tokens_f)[1]
    grad_tokens = to_low(grad_hidden + norm_attn_pull(grad_normed)[0])
    everyone = small_rows[:: small_rows.shape[0] // lax.axis_size("dp"), EXPERTS + 1]
    hits = jnp.arange(ADAPTER_SETS, dtype=jnp.int32)[:, None] == everyone.astype(jnp.int32)
    same = jnp.arange(rank)[:, None] == jnp.arange(rank)[None, :]
    chooser = to_low(hits[:, None, :, None] & same[None, :, None, :])
    chooser = chooser.reshape(ADAPTER_SETS * rank, -1)

    def adapter_sums(local_grads, rows):
        results, start = [], 0
        for local_grad in local_grads:
            size = local_grad.shape[1]
            total = matmul(chooser, rows[:, start : start + size])
            results.append(total.reshape(ADAPTER_SETS, rank, size))
            start += size
        return results

    def flipped(total):
        return jnp.swapaxes(total, 1, 2)

    def opened(total, count):
        return total.reshape(total.shape[0], total.shape[1], count, -1)

    total_out_a, total_up_a, total_up_b, total_down_a, total_down_b = adapter_sums(
        early_grads, early_rows
    )
    total_qkv_b, total_qkv_a, total_out_b = adapter_sums(late_grads, late_rows)
    return (
        output,
        grad_tokens,
        flipped(total_qkv_a),
        opened(total_qkv_b, 3),
        flipped(total_out_a),
        total_out_b,
        flipped(total_up_a),
        opened(total_up_b, 2),
        flipped(total_down_a),
        total_down_b,
    )


def solution(mesh):
    return jax.shard_map(
        body,
        mesh=mesh,
        in_specs=(
            P("dp", None),
            P("dp", None),
            P(),
            P("dp", None, "tensor"),
            P(None, "tensor"),
            P("dp", "tensor"),
            P(),
            P("dp", None),
            P("dp"),
            P("dp", None, None, "tensor"),
            P("dp", None, "tensor"),
            P("dp", None, "tensor"),
            P("dp", "tensor"),
            P("dp", None),
            P("dp"),
            P("dp", None),
            P(),
            P(None, None, None, "tensor"),
            P(None, "tensor", None),
            P(),
            P(),
            P(None, None, None, "tensor"),
            P(None, "tensor", None),
            P(),
        ),
        out_specs=(
            P("dp", None),
            P("dp", None),
            P(),
            P(None, None, None, "tensor"),
            P(None, "tensor", None),
            P(),
            P(),
            P(None, None, None, "tensor"),
            P(None, "tensor", None),
            P(),
        ),
        check_vma=False,
    )
```

```python
import functools

import jax
import jax.numpy as jnp
from jax import lax
from jax.experimental import pallas as pl
from jax.experimental.pallas import tpu as pltpu
from jax.sharding import PartitionSpec as P

HEAD_SIZE = 128
TOP = 4
EXPERTS = 16
ADAPTER_SETS = 8
PIECE = 256


EPSILON = 1e-06
THETA = 1000000.0
ADAPTER_SCALE = 2.0
MASKED = -1e30
QUERY_ROWS = 256
NARROW = 128
MESH = pl.DeviceIdType.MESH
SUM_CHUNKS = 16
LAG = 1
AHEAD = 1
LEAD = 2
SHARED = 4
HALVES = 1
READY = 4


def matmul(left_side, right_side):
    return jnp.dot(left_side, right_side, preferred_element_type=jnp.float32)


def contract_last(left_side, right_side):
    return lax.dot_general(
        left_side, right_side, (((1,), (1,)), ((), ())), preferred_element_type=jnp.float32
    )


def contract_first(left_side, right_side):
    return lax.dot_general(
        left_side, right_side, (((0,), (0,)), ((), ())), preferred_element_type=jnp.float32
    )


def to_low(values):
    return values.astype(jnp.bfloat16)


def rms_scale(values, gain_values):
    return (
        values * lax.rsqrt(jnp.mean(values * values, axis=1, keepdims=True) + EPSILON) * gain_values
    )


def rope_tables(length):
    half_size = HEAD_SIZE // 2
    frequency = THETA ** (-jnp.arange(half_size, dtype=jnp.float32) * 2.0 / HEAD_SIZE)
    angles = jnp.arange(length, dtype=jnp.float32)[:, None] * frequency[None, :]
    return (
        jnp.concatenate([jnp.cos(angles)] * 2, axis=1),
        jnp.concatenate([jnp.sin(angles)] * 2, axis=1),
    )


def piece_index(positions, starts):
    inside = (positions[:, None] >= starts[None, :]) & (
        positions[:, None] < starts[None, :] + PIECE
    )
    labels = jnp.arange(starts.shape[0], dtype=jnp.int32)[None, :] + 1
    return jnp.sum(jnp.where(inside, labels, 0), axis=1) - 1


def line_sum_steps(
    chunks,
    lag,
    wide_ref,
    narrow_ref,
    total_ref,
    part_ref,
    from_end,
    pair_sum,
    from_pair,
    semaphores,
    on_total=None,
):
    place = lax.axis_index("tensor")
    width = wide_ref.shape[1]
    rows = part_ref.shape[0] // chunks
    inner = (place == 1) | (place == 2)
    end = (place == 0) | (place == 3)
    mate = jnp.where(place < 2, 1 - place, 5 - place)
    other = jnp.where(inner, 3 - place, place)

    def span(chunk):
        return pl.ds(pl.multiple_of(chunk * rows, rows), rows)

    def copy(source, target, chunk, lane, device):
        return pltpu.make_async_remote_copy(
            source.at[span(chunk)],
            target.at[span(chunk)],
            semaphores.at[2 * lane, chunk],
            semaphores.at[2 * lane + 1, chunk],
            device_id={"tensor": device},
            device_id_type=MESH,
        )

    def inward(chunk):
        return copy(part_ref, from_end, chunk, 0, mate)

    def across(chunk):
        return copy(pair_sum, from_pair, chunk, 1, other)

    def outward(chunk):
        return copy(total_ref, total_ref, chunk, 2, mate)

    def add(left_ref, right_ref, out_ref, chunk):
        out_ref[span(chunk)] = to_low(
            left_ref[span(chunk)].astype(jnp.float32) + right_ref[span(chunk)].astype(jnp.float32)
        )

    def stage(chunk):
        part_ref[span(chunk), :width] = to_low(wide_ref[span(chunk)])
        if narrow_ref is not None:
            part_ref[span(chunk), width:] = narrow_ref[span(chunk)]

    def greet(extra):
        barrier = pltpu.get_barrier_semaphore()
        pl.semaphore_signal(barrier, inc=1, device_id={"tensor": mate}, device_id_type=MESH)

        @pl.when(inner)
        def _():
            pl.semaphore_signal(barrier, inc=1, device_id={"tensor": other}, device_id_type=MESH)
            pl.semaphore_wait(barrier, 2 + extra)

        @pl.when(end)
        def _():
            pl.semaphore_wait(barrier, 1 + extra)

    def begin(first=0, last=chunks):
        @pl.when(end)
        def _():
            @pl.loop(first, last)
            def _(chunk):
                stage(chunk)
                inward(chunk).start()

    def advance(step):
        @pl.when(inner & (step < chunks))
        def _():
            stage(step)
            inward(step).wait_recv()
            add(part_ref, from_end, pair_sum, step)
            across(step).start()

        @pl.when(inner & (step >= lag) & (step < chunks + lag))
        def _():
            across(step - lag).wait_recv()
            add(pair_sum, from_pair, total_ref, step - lag)
            outward(step - lag).start()
            if on_total is not None:
                on_total(step - lag)

    def finish():
        @pl.when(end)
        def _():
            @pl.loop(0, chunks)
            def _(chunk):
                inward(chunk).wait_send()
                outward(chunk).wait_recv()
                if on_total is not None:
                    on_total(chunk)

        @pl.when(inner)
        def _():
            @pl.loop(0, chunks)
            def _(chunk):
                across(chunk).wait_send()
                outward(chunk).wait_send()

    return greet, begin, advance, finish


def plane_gather_steps(pieces, block_ref, whole_ref, semaphores, local_semaphore):
    spot = lax.axis_index("dp")
    depth = block_ref.shape[1]
    rows = block_ref.shape[0] // pieces
    core_mate = spot + 1 - 2 * (spot % 2)
    x_mate = spot + 2 - 4 * ((spot // 2) % 2)
    y_mate = spot + 4 - 8 * (spot // 4)
    x_y_mate = x_mate + 4 - 8 * (spot // 4)
    lanes = {
        "core": (spot, core_mate, 0, 1),
        "x": (spot, x_mate, 0, 1),
        "y": (spot, y_mate, 0, 1),
        "x_core": (x_mate, core_mate, 0, 1),
        "x_y": (x_mate, y_mate, 0, 2),
        "y_core": (y_mate, core_mate, 0, 1),
        "y_x": (y_mate, x_mate, 1, 2),
        "xy_core": (x_y_mate, core_mate, 0, 2),
        "yx_core": (x_y_mate, core_mate, 1, 2),
    }
    order = list(lanes)

    def send(name, piece):
        owner, device, part, parts = lanes[name]
        lane = order.index(name)
        span = pl.ds(
            pl.multiple_of(piece * rows + part * (rows // parts), rows // parts), rows // parts
        )
        columns = pl.ds(pl.multiple_of(owner * depth, depth), depth)
        target = whole_ref.at[span, columns]
        source = block_ref.at[span] if name in ("core", "x", "y") else target
        return pltpu.make_async_remote_copy(
            source,
            target,
            semaphores.at[2 * lane, piece],
            semaphores.at[2 * lane + 1, piece],
            device_id={"dp": device},
            device_id_type=MESH,
        )

    def own():
        columns = pl.ds(pl.multiple_of(spot * depth, depth), depth)
        return pltpu.make_async_copy(block_ref, whole_ref.at[:, columns], local_semaphore)

    def greet():
        barrier = pltpu.get_barrier_semaphore()
        for device in (core_mate, x_mate, y_mate):
            pl.semaphore_signal(barrier, inc=1, device_id={"dp": device}, device_id_type=MESH)

    def launch(piece):
        @pl.when((piece >= 0) & (piece < pieces))
        def _():
            for name in ("x", "y", "core"):
                send(name, piece).start()

    def forward(piece):
        @pl.when((piece >= 0) & (piece < pieces))
        def _():
            send("x", piece).wait_recv()
            send("x_y", piece).start()
            send("x_core", piece).start()
            send("y", piece).wait_recv()
            send("y_x", piece).start()
            send("y_core", piece).start()

    def hand_over(piece):
        @pl.when((piece >= 0) & (piece < pieces))
        def _():
            send("x_y", piece).wait_recv()
            send("xy_core", piece).start()
            send("y_x", piece).wait_recv()
            send("yx_core", piece).start()

    def advance(step):
        launch(step + LEAD)
        forward(step - AHEAD)
        hand_over(step - 2 * AHEAD)

    def load(first, count, target, semaphore):
        span = pl.ds(pl.multiple_of(first, rows), count)

        def columns(owner):
            return pl.ds(pl.multiple_of(owner * depth, depth), depth)

        here = columns(spot)
        copies = [pltpu.make_async_copy(block_ref.at[span], target.at[:, here], semaphore)]
        for shift in range(1, 8):
            there = columns((spot + shift) % 8)
            copies.append(
                pltpu.make_async_copy(
                    whole_ref.at[span, there], target.at[:, there], semaphore
                )
            )
        return copies

    def load_wait(count, target, semaphore):
        pltpu.make_async_copy(whole_ref.at[pl.ds(0, count)], target, semaphore).wait()

    def arrive(piece):
        for name in ("core", "x_core", "y_core", "xy_core", "yx_core"):
            send(name, piece).wait_recv()

    def finish():
        @pl.loop(0, pieces)
        def _(piece):
            for name in order:
                send(name, piece).wait_send()

    return greet, advance, arrive, finish, own, load, load_wait, (launch, forward, hand_over)


def sum_gather_kernel(
    chunks,
    pieces,
    wide_ref,
    narrow_ref,
    block_ref,
    cotangent_ref,
    total_ref,
    whole_ref,
    open_ref,
    *scratch,
):
    greet, begin, advance, finish = line_sum_steps(
        chunks, LAG, wide_ref, narrow_ref, total_ref, *scratch[:5]
    )
    gather_semaphores, local_semaphores, piece_rows, open_rows = scratch[5:]
    gather_greet, gather_advance, gather_arrive, gather_finish, own, load, load_wait, stages = (
        plane_gather_steps(
            pieces, block_ref, whole_ref, gather_semaphores, local_semaphores.at[0]
        )
    )
    rows = piece_rows.shape[1]

    def store(piece):
        slot = piece % 2
        span = pl.ds(pl.multiple_of(piece * rows, rows), rows)
        return pltpu.make_async_copy(
            open_rows.at[slot], open_ref.at[span], local_semaphores.at[3 + slot]
        )

    gather_greet()
    greet(3)
    begin()
    own().start()

    @pl.loop(0, LEAD)
    def _(piece):
        stages[0](piece)

    @pl.loop(0, max(chunks + LAG, pieces + 3 * AHEAD + 1))
    def _(step):
        gather_advance(step)
        advance(step)

        @pl.when((step >= 3 * AHEAD) & (step < pieces + 3 * AHEAD))
        def _():
            piece = step - 3 * AHEAD
            gather_arrive(piece)
            slot = piece % 2
            for copy in load(piece * rows, rows, piece_rows.at[slot], local_semaphores.at[1 + slot]):
                copy.start()

        @pl.when((step > 3 * AHEAD) & (step <= pieces + 3 * AHEAD))
        def _():
            piece = step - 3 * AHEAD - 1
            slot = piece % 2
            load_wait(rows, piece_rows.at[slot], local_semaphores.at[1 + slot])

            @pl.when(piece >= 2)
            def _():
                store(piece - 2).wait()

            open_rows[piece % 2] = to_low(matmul(piece_rows[piece % 2], cotangent_ref[...]))
            store(piece).start()

    store(pieces - 2).wait()
    store(pieces - 1).wait()
    own().wait()
    gather_finish()
    finish()


def sum_down_kernel(
    chunks, wide_ref, narrow_ref, act_ref, down_ref, total_ref, out_ref, *scratch
):
    greet, begin, advance, finish = line_sum_steps(
        chunks, LAG, wide_ref, narrow_ref, total_ref, *scratch[:5]
    )
    semaphores, act_rows, down_rows, out_rows = scratch[5:]
    rows = act_rows.shape[1]
    blocks = down_ref.shape[0] // rows

    def loads(block):
        slot = block % 2
        span = pl.ds(pl.multiple_of(block * rows, rows), rows)
        return [
            pltpu.make_async_copy(act_ref.at[span], act_rows.at[slot], semaphores.at[0, slot]),
            pltpu.make_async_copy(down_ref.at[span], down_rows.at[slot], semaphores.at[1, slot]),
        ]

    for load in loads(0):
        load.start()
    greet(0)
    begin()
    out_rows[...] = jnp.zeros_like(out_rows)

    @pl.loop(0, max(blocks, chunks + LAG))
    def _(step):
        advance(step)

        @pl.when(step < blocks)
        def _():
            @pl.when(step + 1 < blocks)
            def _():
                for load in loads(step + 1):
                    load.start()

            for load in loads(step):
                load.wait()
            tile = min(256, out_rows.shape[0])

            @pl.loop(0, out_rows.shape[0] // tile)
            def _(index):
                span = pl.ds(pl.multiple_of(index * tile, tile), tile)
                out_rows[span] += contract_first(
                    act_rows[step % 2, :, span], down_rows[step % 2]
                )

    out_ref[...] = to_low(out_rows[...])
    finish()


def last_sum_kernel(
    chunks,
    wide_ref,
    streamed_refs,
    mid_ref,
    qkv_a_ref,
    gain_ref,
    mid_down_ref,
    down_b_ref,
    gate_ref,
    grad_tokens_ref,
    output_ref,
    total_ref,
    *scratch,
):
    buffers, load_semaphores = scratch[5:-1], scratch[-1]
    rows = wide_ref.shape[0] // chunks

    def span(chunk):
        return pl.ds(pl.multiple_of(chunk * rows, rows), rows)

    def loads(chunk):
        slot = chunk % 2
        return [
            pltpu.make_async_copy(
                source.at[span(chunk)], target.at[slot], load_semaphores.at[number, slot]
            )
            for number, (source, target) in enumerate(zip(streamed_refs, buffers))
        ]

    def on_total(chunk):
        for load in loads(chunk):
            load.wait()

        @pl.when(chunk + 1 < chunks)
        def _():
            for load in loads(chunk + 1):
                load.start()

        here = span(chunk)
        grad_hidden, tokens, hidden, combined = [buffer[chunk % 2] for buffer in buffers]
        grad_normed = total_ref[here].astype(jnp.float32) + contract_last(
            mid_ref[here], qkv_a_ref[...]
        )
        grad_tokens_ref[here] = last_grad(grad_normed, tokens, gain_ref[...], grad_hidden)
        extra = ADAPTER_SCALE * matmul(mid_down_ref[here], down_b_ref[...])
        output_ref[here] = to_low(hidden + combined.astype(jnp.float32) + gate_ref[here] * extra)

    greet, begin, advance, finish = line_sum_steps(
        chunks, 1, wide_ref, None, total_ref, *scratch[:5], on_total=on_total
    )
    for load in loads(0):
        load.start()
    greet(0)
    begin()

    @pl.loop(0, chunks + 1)
    def _(step):
        advance(step)

    finish()


def last_grad(grad_normed, tokens, gain, grad_hidden):
    tokens_f = tokens.astype(jnp.float32)
    scale = lax.rsqrt(jnp.mean(tokens_f * tokens_f, axis=1, keepdims=True) + EPSILON)
    scaled = grad_normed * gain
    pull = jnp.mean(tokens_f * scaled, axis=1, keepdims=True)
    return to_low(grad_hidden + scale * scaled - tokens_f * (scale * scale * scale * pull))


def attend_back_sum_kernel(chunks, wide_ref, rows_ref, upper_ref, *refs):
    inputs, scratch = refs[:8], refs[12:]
    total_ref, grad_qkv_ref, normed_part_ref, mid_total_ref = refs[8:12]
    greet, begin, advance, finish = line_sum_steps(
        chunks, LAG, wide_ref, None, total_ref, *scratch[:5]
    )
    head_block = attend_back_steps(*inputs, grad_qkv_ref, *scratch[5:7])
    mid_part = scratch[7]
    _, mid_begin, mid_advance, mid_finish = line_sum_steps(
        1, 1, mid_part, None, mid_total_ref, *scratch[8:13]
    )
    length, heads_width = inputs[0].shape
    heads, blocks = heads_width // HEAD_SIZE, length // QUERY_ROWS
    each = blocks // 2
    rows = scratch[-2]
    load = pltpu.make_async_copy(rows_ref.at[:3], rows, scratch[-1].at[0])
    load.start()
    done = heads * each
    greet(0)
    begin(0, done + blocks)

    @pl.loop(0, heads)
    def _(head):
        for step in range(each):
            advance(head * each + step)
            head_block(head, 2 * step * QUERY_ROWS)
            head_block(head, (2 * step + 1) * QUERY_ROWS)

    mid_part[...] = grad_mid_rows(grad_qkv_ref, upper_ref)
    mid_begin()
    begin(done + blocks, chunks)
    load.wait()

    @pl.loop(0, blocks)
    def _(block):
        advance(done + block)
        span = pl.ds(pl.multiple_of(block * QUERY_ROWS, QUERY_ROWS), QUERY_ROWS)
        normed_part_ref[span] = to_low(
            sum(contract_last(grad_qkv_ref[part, span], rows[part]) for part in range(3))
        )

    mid_advance(0)

    advance(done + blocks)
    mid_advance(1)

    @pl.loop(done + blocks + 1, max(done + blocks + 1, chunks + LAG))
    def _(step):
        advance(step)

    mid_finish()
    finish()


def grad_mid_rows(grad_qkv_ref, upper_ref):
    return sum(contract_last(grad_qkv_ref[part], upper_ref[part]) for part in range(3))


def epilogue_kernel(
    total_ref,
    hidden_ref,
    scale_ref,
    cotangent_ref,
    gain_ref,
    probs_ref,
    chosen_ref,
    extra_ref,
    gate_ref,
    factors_ref,
    out_b_ref,
    out_a_ref,
    rows_ref,
    grad_hidden_ref,
    grad_branch_ref,
    grad_mid_ref,
    grad_attended_ref,
):
    width = hidden_ref.shape[1]
    narrow = total_ref[:, width:].astype(jnp.float32)
    lane = lax.broadcasted_iota(jnp.int32, narrow.shape, 1)
    probs = probs_ref[...]
    grad_probs = chosen_ref[...] * narrow
    grad_logits = probs * (grad_probs - jnp.sum(probs * grad_probs, axis=1, keepdims=True))
    only_gate = jnp.where(lane == EXPERTS, narrow, 0.0)
    gate_grad = jnp.sum(only_gate + narrow * extra_ref[...], axis=1, keepdims=True)
    gate = gate_ref[...]
    gate_logit = gate_grad * gate * (1.0 - gate)
    rank = extra_ref.shape[1] // 8
    rows = jnp.where(lane <= EXPERTS + rank, narrow, 0.0)
    rows = jnp.where(lane == EXPERTS, gate_logit, rows)
    rows = to_low(jnp.where(lane < EXPERTS, grad_logits, rows))
    grad_normed = total_ref[:, :width].astype(jnp.float32) + contract_last(rows, factors_ref[...])
    hidden = hidden_ref[...]
    scale = scale_ref[...]
    scaled = grad_normed * gain_ref[...]
    pull = jnp.mean(hidden * scaled, axis=1, keepdims=True)
    grad_hidden = (
        cotangent_ref[...].astype(jnp.float32)
        + scale * scaled
        - hidden * (scale * scale * scale * pull)
    )
    grad_hidden_ref[...] = grad_hidden
    grad_branch = to_low(grad_hidden)
    grad_branch_ref[...] = grad_branch
    grad_mid = to_low(ADAPTER_SCALE * contract_last(grad_branch, out_b_ref[...]))
    grad_mid_ref[...] = grad_mid
    grad_attended_ref[...] = to_low(
        matmul(grad_branch, rows_ref[0]) + contract_last(grad_mid, out_a_ref[...])
    )


def epilogue(blocked, still):
    length = blocked[0].shape[0]
    width, heads_width = still[-1].shape[1:]
    rows = min(length, 256)
    total, hidden, scale, cotangent, probs, chosen, extra, gate = blocked
    gain, factors, out_b, out_a, row_stack = still

    def block(array):
        return pl.BlockSpec((rows, array.shape[1]), lambda index: (index, 0))

    def whole(array):
        return pl.BlockSpec(array.shape, lambda index: (0, 0))

    outs = [
        jax.ShapeDtypeStruct((length, width), jnp.float32),
        jax.ShapeDtypeStruct((length, width), jnp.bfloat16),
        jax.ShapeDtypeStruct((length, NARROW), jnp.bfloat16),
        jax.ShapeDtypeStruct((length, heads_width), jnp.bfloat16),
    ]
    return pl.pallas_call(
        epilogue_kernel,
        grid=(length // rows,),
        in_specs=[block(array) for array in (total, hidden, scale, cotangent)]
        + [whole(gain)]
        + [block(array) for array in (probs, chosen, extra, gate)]
        + [whole(array) for array in (factors, out_b, out_a)]
        + [pl.BlockSpec((1, width, heads_width), lambda index: (3, 0, 0))],
        out_specs=[block(out) for out in outs],
        out_shape=outs,
        compiler_params=pltpu.CompilerParams(
            vmem_limit_bytes=56 * 2**20, dimension_semantics=("arbitrary",)
        ),
        cost_estimate=pl.CostEstimate(
            flops=2 * length * width * heads_width,
            bytes_accessed=32 * 2**20,
            transcendentals=0,
        ),
    )(
        total,
        hidden,
        scale,
        cotangent,
        gain,
        probs,
        chosen,
        extra,
        gate,
        factors,
        out_b,
        out_a,
        row_stack,
    )


def on_line():
    return lax.axis_size("tensor") == 4


def in_plane():
    return lax.axis_size("dp") == 8


def in_vmem(count):
    return [pl.BlockSpec(memory_space=pltpu.VMEM)] * count


def in_hbm(count):
    return [pl.BlockSpec(memory_space=pltpu.HBM)] * count


def sum_scratch(shape):
    return [pltpu.VMEM(shape, jnp.bfloat16)] * 4 + [pltpu.SemaphoreType.DMA((6, SUM_CHUNKS))]


def narrowed(narrow_part):
    pad = jnp.zeros((narrow_part.shape[0], NARROW - narrow_part.shape[1]), jnp.bfloat16)
    return jnp.concatenate([to_low(narrow_part), pad], axis=1)


def plain_sum(wide_part, narrow_part):
    if narrow_part is not None:
        pad = jnp.zeros((narrow_part.shape[0], NARROW - narrow_part.shape[1]), jnp.float32)
        wide_part = jnp.concatenate([wide_part, narrow_part, pad], axis=1)
    return lax.psum(wide_part, "tensor")


def last_step(wide_part, streamed, still, number):
    length, width = wide_part.shape
    mid, qkv_a, gain, mid_down, down_b, gate = still
    if not on_line():
        grad_hidden, tokens, hidden, combined = streamed
        grad_normed = plain_sum(wide_part, None).astype(jnp.float32) + contract_last(mid, qkv_a)
        extra = ADAPTER_SCALE * matmul(mid_down, down_b)
        return (
            last_grad(grad_normed, tokens, gain, grad_hidden),
            to_low(hidden + combined.astype(jnp.float32) + gate * extra),
        )
    rows = length // SUM_CHUNKS

    def kernel(wide_ref, *refs):
        last_sum_kernel(SUM_CHUNKS, wide_ref, refs[:4], *refs[4:])

    return pl.pallas_call(
        kernel,
        out_shape=[jax.ShapeDtypeStruct((length, width), jnp.bfloat16)] * 2,
        in_specs=in_vmem(1) + in_hbm(4) + in_vmem(6),
        out_specs=in_vmem(2),
        scratch_shapes=[pltpu.VMEM((length, width), jnp.bfloat16)]
        + sum_scratch((length, width))
        + [pltpu.VMEM((2, rows, width), array.dtype) for array in streamed]
        + [pltpu.SemaphoreType.DMA((4, 2))],
        compiler_params=pltpu.CompilerParams(
            collective_id=number, has_side_effects=True, vmem_limit_bytes=58 * 2**20
        ),
        cost_estimate=pl.CostEstimate(flops=0, bytes_accessed=300 * 2**20, transcendentals=0),
    )(wide_part, *streamed, *still)


def summed_and_gathered(wide_part, narrow_part, block, cotangents, number):
    length, width = wide_part.shape
    if not (on_line() and in_plane()):
        whole = lax.all_gather(block, "dp", axis=1, tiled=True)
        open_rows = to_low(matmul(whole, cotangents))
        return plain_sum(wide_part, narrow_part), whole, open_rows
    shape = (length, width + NARROW)
    pieces = SHARED + EXPERTS
    rows = block.shape[0] // pieces
    total, whole, open_rows = pl.pallas_call(
        functools.partial(sum_gather_kernel, SUM_CHUNKS, pieces),
        out_shape=[
            jax.ShapeDtypeStruct(shape, jnp.bfloat16),
            jax.ShapeDtypeStruct((block.shape[0], width), jnp.bfloat16),
            jax.ShapeDtypeStruct((block.shape[0], length), jnp.bfloat16),
        ],
        in_specs=in_vmem(2) + in_hbm(1) + in_vmem(1),
        out_specs=in_vmem(1) + in_hbm(2),
        scratch_shapes=sum_scratch(shape)
        + [
            pltpu.SemaphoreType.DMA((18, pieces)),
            pltpu.SemaphoreType.DMA((5,)),
            pltpu.VMEM((2, rows, width), jnp.bfloat16),
            pltpu.VMEM((2, rows, length), jnp.bfloat16),
        ],
        compiler_params=pltpu.CompilerParams(
            collective_id=number, has_side_effects=True, vmem_limit_bytes=58 * 2**20
        ),
        cost_estimate=pl.CostEstimate(flops=0, bytes_accessed=360 * 2**20, transcendentals=0),
    )(wide_part, narrowed(narrow_part), block, cotangents)
    return total, whole, open_rows


def summed_and_down(wide_part, narrow_part, act_rows, down_rows, number):
    length, width = wide_part.shape
    if not on_line():
        out = contract_first(act_rows, down_rows)
        return plain_sum(wide_part.astype(jnp.float32), narrow_part), out
    shape = (length, width + NARROW)
    rows = 2 * down_rows.shape[0] // (SHARED + EXPERTS)
    total, out = pl.pallas_call(
        functools.partial(sum_down_kernel, SUM_CHUNKS),
        out_shape=[
            jax.ShapeDtypeStruct(shape, jnp.bfloat16),
            jax.ShapeDtypeStruct((length, width), jnp.bfloat16),
        ],
        in_specs=in_vmem(2) + in_hbm(2),
        out_specs=in_vmem(2),
        scratch_shapes=sum_scratch(shape)
        + [
            pltpu.SemaphoreType.DMA((2, 2)),
            pltpu.VMEM((2, rows, length), jnp.bfloat16),
            pltpu.VMEM((2, rows, width), jnp.bfloat16),
            pltpu.VMEM((length, width), jnp.float32),
        ],
        compiler_params=pltpu.CompilerParams(
            collective_id=number, has_side_effects=True, vmem_limit_bytes=58 * 2**20
        ),
        cost_estimate=pl.CostEstimate(flops=0, bytes_accessed=300 * 2**20, transcendentals=0),
    )(wide_part, narrowed(narrow_part), act_rows, down_rows)
    return total, out


def block_mask(first, rows, extent, row_piece_ref, col_piece_ref):
    row_place = lax.broadcasted_iota(jnp.int32, (rows, extent), 0) + first
    col_place = lax.broadcasted_iota(jnp.int32, (rows, extent), 1)
    row_piece = row_piece_ref[first : first + rows, 0:1]
    together = (row_piece == col_piece_ref[0:1, :extent]) & (row_piece >= 0)
    return (col_place <= row_place) | together


def block_probs(query_rows, keys, allowed):
    scores = jnp.where(allowed, contract_last(query_rows, keys) * HEAD_SIZE**-0.5, MASKED)
    raised = jnp.exp(scores - jnp.max(scores, axis=1, keepdims=True))
    return raised * (1.0 / jnp.sum(raised, axis=1, keepdims=True))


def half_turn(values, signed_sine):
    return pltpu.roll(values, HEAD_SIZE // 2, 1) * signed_sine


def attend_kernel(
    qkv_ref,
    cosine_ref,
    sine_ref,
    row_piece_ref,
    col_piece_ref,
    query_ref,
    keys_ref,
    values_ref,
    attended_ref,
):
    length = qkv_ref.shape[1]

    @pl.loop(0, qkv_ref.shape[2] // HEAD_SIZE)
    def _(head):
        column = pl.ds(pl.multiple_of(head * HEAD_SIZE, HEAD_SIZE), HEAD_SIZE)
        for source, target in ((0, query_ref), (1, keys_ref)):
            raw = qkv_ref[source, :, column]
            target[:, column] = to_low(raw * cosine_ref[...] + half_turn(raw, sine_ref[...]))
        values_ref[:, column] = to_low(qkv_ref[2, :, column])
        for first in range(0, length, QUERY_ROWS):
            extent = min(length, first + QUERY_ROWS + PIECE)
            allowed = block_mask(first, QUERY_ROWS, extent, row_piece_ref, col_piece_ref)
            probs = block_probs(
                query_ref[first : first + QUERY_ROWS, column], keys_ref[:extent, column], allowed
            )
            attended_ref[first : first + QUERY_ROWS, column] = to_low(
                matmul(to_low(probs), values_ref[:extent, column])
            )


def attend(qkv, cosine, signed_sine, row_piece, col_piece):
    length, heads_width = qkv.shape[1:]
    shape = jax.ShapeDtypeStruct((length, heads_width), jnp.bfloat16)
    return pl.pallas_call(
        attend_kernel,
        out_shape=[shape] * 4,
        in_specs=[pl.BlockSpec(memory_space=pltpu.VMEM)] * 5,
        out_specs=[pl.BlockSpec(memory_space=pltpu.VMEM)] * 4,
        compiler_params=pltpu.CompilerParams(vmem_limit_bytes=48 * 2**20),
        cost_estimate=pl.CostEstimate(
            flops=4 * length * length * heads_width,
            bytes_accessed=16 * 2**20,
            transcendentals=length * length * heads_width // HEAD_SIZE,
        ),
    )(qkv, cosine, signed_sine, row_piece, col_piece)


def attend_back_steps(
    query_ref,
    keys_ref,
    values_ref,
    grad_ref,
    cosine_ref,
    sine_ref,
    row_piece_ref,
    col_piece_ref,
    grad_qkv_ref,
    grad_keys,
    grad_values,
):
    length = query_ref.shape[0]

    def turned_back(grad, first):
        span = slice(first, first + grad.shape[0])
        scaled = grad * HEAD_SIZE**-0.5
        return to_low(scaled * cosine_ref[span] - half_turn(scaled, sine_ref[span]))

    def head_block(head, first):
        column = pl.ds(pl.multiple_of(head * HEAD_SIZE, HEAD_SIZE), HEAD_SIZE)
        span = slice(first, first + QUERY_ROWS)
        extent = min(length, first + QUERY_ROWS + PIECE)
        if first == 0:
            grad_keys[...] = jnp.zeros_like(grad_keys)
            grad_values[...] = jnp.zeros_like(grad_values)
        allowed = block_mask(first, QUERY_ROWS, extent, row_piece_ref, col_piece_ref)
        query_rows = query_ref[span, column]
        keys = keys_ref[:extent, column]
        grad_rows = grad_ref[span, column]
        probs = block_probs(query_rows, keys, allowed)
        grad_probs = contract_last(grad_rows, values_ref[:extent, column])
        shift = jnp.sum(probs * grad_probs, axis=1, keepdims=True)
        grad_scores = to_low(probs * (grad_probs - shift))
        grad_values[:extent] += contract_first(to_low(probs), grad_rows)
        grad_keys[:extent] += contract_first(grad_scores, query_rows)
        grad_qkv_ref[0, span, column] = turned_back(matmul(grad_scores, keys), first)
        if first + QUERY_ROWS >= length:
            grad_qkv_ref[1, :, column] = turned_back(grad_keys[...], 0)
            grad_qkv_ref[2, :, column] = to_low(grad_values[...])

    return head_block


def attend_back_kernel(*refs):
    head_block = attend_back_steps(*refs)

    @pl.loop(0, refs[0].shape[1] // HEAD_SIZE)
    def _(head):
        for first in range(0, refs[0].shape[0], QUERY_ROWS):
            head_block(head, first)


def attend_back(query, keys, values, grads, cosine, signed_sine, row_piece, col_piece):
    length, heads_width = query.shape
    return pl.pallas_call(
        attend_back_kernel,
        out_shape=jax.ShapeDtypeStruct((3, length, heads_width), jnp.bfloat16),
        in_specs=[pl.BlockSpec(memory_space=pltpu.VMEM)] * 8,
        out_specs=pl.BlockSpec(memory_space=pltpu.VMEM),
        scratch_shapes=[pltpu.VMEM((length, HEAD_SIZE), jnp.float32)] * 2,
        compiler_params=pltpu.CompilerParams(vmem_limit_bytes=48 * 2**20),
        cost_estimate=pl.CostEstimate(
            flops=10 * length * length * heads_width,
            bytes_accessed=16 * 2**20,
            transcendentals=length * length * heads_width // HEAD_SIZE,
        ),
    )(query, keys, values, grads, cosine, signed_sine, row_piece, col_piece)


def summed_and_attended_back(wide_part, rows, upper, attention_inputs, number):
    if not on_line():
        grad_qkv = attend_back(*attention_inputs)
        normed_part = sum(contract_last(grad_qkv[part], rows[part]) for part in range(3))
        mid_total = lax.psum(grad_mid_rows(grad_qkv, upper), "tensor")
        return plain_sum(wide_part, None), grad_qkv, normed_part, mid_total
    shape = wide_part.shape
    length, heads_width = attention_inputs[0].shape
    narrow_shape = (length, NARROW)
    return pl.pallas_call(
        functools.partial(attend_back_sum_kernel, SUM_CHUNKS),
        out_shape=[
            jax.ShapeDtypeStruct(shape, jnp.bfloat16),
            jax.ShapeDtypeStruct((3, length, heads_width), jnp.bfloat16),
            jax.ShapeDtypeStruct(shape, jnp.bfloat16),
            jax.ShapeDtypeStruct(narrow_shape, jnp.bfloat16),
        ],
        in_specs=in_vmem(1) + in_hbm(1) + in_vmem(1 + len(attention_inputs)),
        out_specs=in_vmem(4),
        scratch_shapes=sum_scratch(shape)
        + [pltpu.VMEM((length, HEAD_SIZE), jnp.float32)] * 2
        + [pltpu.VMEM(narrow_shape, jnp.float32)]
        + [pltpu.VMEM(narrow_shape, jnp.bfloat16)] * 4
        + [pltpu.SemaphoreType.DMA((6, 1))]
        + [pltpu.VMEM((3,) + rows.shape[1:], jnp.bfloat16), pltpu.SemaphoreType.DMA((1,))],
        compiler_params=pltpu.CompilerParams(
            collective_id=number, has_side_effects=True, vmem_limit_bytes=60 * 2**20
        ),
        cost_estimate=pl.CostEstimate(flops=0, bytes_accessed=300 * 2**20, transcendentals=0),
    )(wide_part, rows, upper, *attention_inputs)


def hidden_step(gate_up, open_part, gate_row, extra):
    hidden = open_part.shape[0]
    gate_half, up_half = gate_up[:hidden], gate_up[hidden:]
    squashed = 1.0 / (1.0 + jnp.exp(-gate_half))
    act = to_low(gate_half * squashed * up_half)
    act_f = act.astype(jnp.float32)
    gate_grad = jnp.sum(act_f * open_part, axis=0, keepdims=True)
    grad_act = gate_row * open_part
    if extra is not None:
        grad_act = grad_act + extra
    grad_gate = to_low(grad_act * up_half * squashed * (1.0 + gate_half * (1.0 - squashed)))
    grad_up = to_low(grad_act * gate_half * squashed)
    return act, to_low(gate_row * act_f), gate_grad, grad_gate, grad_up


def experts_kernel(
    pieces,
    inputs_ref,
    gate_ref,
    mid_up_ref,
    grad_mid_ref,
    up_extra_ref,
    down_extra_ref,
    ready_up_ref,
    block_ref,
    open_ref,
    grad_ref,
    gate_grad_ref,
    mid_down_ref,
    grad_mid_up_ref,
    grad_down_a_ref,
    grad_up_b_ref,
    act_ref,
    whole_ref,
    grad_total,
    up_rows,
    open_rows,
    act_rows,
    grad_rows,
    gather_semaphores,
    semaphores,
):
    greet, _, arrive, finish, _, load, load_wait, (launch, forward, hand_over) = (
        plane_gather_steps(pieces, block_ref, whole_ref, gather_semaphores, None)
    )
    hidden = open_rows.shape[1]
    count = SHARED + EXPERTS
    each = pieces // (count - READY)

    def span(expert, rows):
        return pl.ds(pl.multiple_of(expert * rows, rows), rows)

    def load_open(expert):
        slot = expert % 2
        return pltpu.make_async_copy(
            open_ref.at[span(expert, hidden)], open_rows.at[slot], semaphores.at[1, slot]
        )

    def load_ready(expert):
        slot = expert % 2
        return pltpu.make_async_copy(
            ready_up_ref.at[span(expert, 2 * hidden)], up_rows.at[slot], semaphores.at[2, slot]
        )

    def store_act(expert):
        slot = expert % 2
        return pltpu.make_async_copy(
            act_rows.at[slot], act_ref.at[span(expert, hidden)], semaphores.at[3, slot]
        )

    def advance(expert):
        for part in range(each):
            launch(each * (expert + 1) + part)
        for part in range(each):
            forward(each * (expert + 2 - READY) + part + 1)
        for part in range(each):
            hand_over(each * (expert + 1 - READY) + part + 1)

        @pl.when(expert + 1 < count)
        def _():
            load_open(expert + 1).start()

        @pl.when(expert + 1 < READY)
        def _():
            load_ready(expert + 1).start()

        @pl.when((expert + 1 >= READY) & (expert + 1 < count))
        def _():
            for part in range(each):
                arrive(each * (expert + 1 - READY) + part)
            slot = (expert + 1) % 2
            first = (expert + 1 - READY) * 2 * hidden
            for copy in load(first, 2 * hidden, up_rows.at[slot], semaphores.at[2, slot]):
                copy.start()

        load_open(expert).wait()
        load_wait(2 * hidden, up_rows.at[expert % 2], semaphores.at[2, expert % 2])

        @pl.when(expert >= 2)
        def _():
            store_act(expert - 2).wait()

    def compute(expert, shared):
        slot = expert % 2
        gate_up = contract_last(up_rows[slot], inputs_ref[...])
        extra = None
        if shared:
            gate_up = gate_up + matmul(up_extra_ref[expert], mid_up_ref[...])
            extra = matmul(down_extra_ref[expert], grad_mid_ref[...])
        act, act_gated, gate_grad, grad_gate, grad_up = hidden_step(
            gate_up,
            open_rows[slot].astype(jnp.float32),
            gate_ref[pl.ds(expert, 1)],
            extra,
        )
        gate_grad_ref[pl.ds(expert, 1)] = gate_grad
        act_rows[slot] = act_gated
        grad_rows[:hidden] = grad_gate
        grad_rows[hidden:] = grad_up
        store_act(expert).start()
        grad_total[...] += contract_first(grad_rows[...], up_rows[slot])
        if shared:
            mid_down_ref[...] += contract_first(down_extra_ref[expert], act)
            grad_mid_up_ref[...] += contract_first(up_extra_ref[expert], grad_rows[...])
            grad_down_a_ref[expert] = contract_last(grad_mid_ref[...], act)
            grad_up_b_ref[expert] = ADAPTER_SCALE * contract_last(mid_up_ref[...], grad_rows[...])

    greet()
    pl.semaphore_wait(pltpu.get_barrier_semaphore(), 3)
    load_open(0).start()
    load_ready(0).start()

    @pl.loop(0, each)
    def _(piece):
        launch(piece)

    grad_total[...] = jnp.zeros_like(grad_total)
    mid_down_ref[...] = jnp.zeros_like(mid_down_ref)
    grad_mid_up_ref[...] = jnp.zeros_like(grad_mid_up_ref)

    @pl.loop(0, SHARED)
    def _(expert):
        advance(expert)
        compute(expert, True)

    @pl.loop(SHARED, count)
    def _(expert):
        advance(expert)
        compute(expert, False)

    grad_ref[...] = to_low(grad_total[...])
    store_act(count - 2).wait()
    store_act(count - 1).wait()
    finish()


def experts_plain(inputs, gates, mid_up, grad_mid, up_extra, down_extra, up_rows, open_rows):
    count, length = gates.shape
    hidden = open_rows.shape[0] // count
    width = inputs.shape[1]
    grad_total = jnp.zeros((length, width), jnp.float32)
    act_parts, gate_grads, down_parts, up_parts = [], [], [], []
    mid_down = jnp.zeros((NARROW, length), jnp.float32)
    grad_mid_up = jnp.zeros((NARROW, length), jnp.float32)
    for expert in range(count):
        weights = up_rows[2 * hidden * expert : 2 * hidden * (expert + 1)]
        gate_up = contract_last(weights, inputs)
        extra = None
        if expert < SHARED:
            gate_up = gate_up + matmul(up_extra[expert], mid_up)
            extra = matmul(down_extra[expert], grad_mid)
        act, act_gated, gate_grad, grad_gate, grad_up = hidden_step(
            gate_up,
            open_rows[hidden * expert : hidden * (expert + 1)].astype(jnp.float32),
            gates[expert : expert + 1],
            extra,
        )
        grad = jnp.concatenate([grad_gate, grad_up], axis=0)
        act_parts.append(act_gated)
        gate_grads.append(gate_grad)
        grad_total = grad_total + contract_first(grad, weights)
        if expert < SHARED:
            mid_down = mid_down + contract_first(down_extra[expert], act)
            grad_mid_up = grad_mid_up + contract_first(up_extra[expert], grad)
            down_parts.append(contract_last(grad_mid, act))
            up_parts.append(ADAPTER_SCALE * contract_last(mid_up, grad))
    return (
        grad_total,
        jnp.concatenate(gate_grads, axis=0),
        mid_down,
        grad_mid_up,
        jnp.stack(down_parts),
        jnp.stack(up_parts),
        jnp.concatenate(act_parts, axis=0),
    )


def experts_step(
    inputs, gates, mid_up, grad_mid, up_extra, down_extra, ready_up, block, open_rows, number
):
    length, width = inputs.shape
    count = SHARED + EXPERTS
    hidden = open_rows.shape[0] // count
    if not in_plane():
        whole = lax.all_gather(block, "dp", axis=1, tiled=True)
        up_rows = jnp.concatenate([ready_up, whole], axis=0)
        return experts_plain(
            inputs, gates, mid_up, grad_mid, up_extra, down_extra, up_rows, open_rows
        )
    pieces = HALVES * (count - READY)
    return pl.pallas_call(
        functools.partial(experts_kernel, pieces),
        in_specs=in_vmem(6) + in_hbm(3),
        out_specs=in_vmem(6) + in_hbm(2),
        out_shape=[
            jax.ShapeDtypeStruct((length, width), jnp.bfloat16),
            jax.ShapeDtypeStruct((count, length), jnp.float32),
            jax.ShapeDtypeStruct((NARROW, length), jnp.float32),
            jax.ShapeDtypeStruct((NARROW, length), jnp.float32),
            jax.ShapeDtypeStruct((SHARED, NARROW, hidden), jnp.float32),
            jax.ShapeDtypeStruct((SHARED, NARROW, 2 * hidden), jnp.float32),
            jax.ShapeDtypeStruct((count * hidden, length), jnp.bfloat16),
            jax.ShapeDtypeStruct(((count - READY) * 2 * hidden, width), jnp.bfloat16),
        ],
        scratch_shapes=[
            pltpu.VMEM((length, width), jnp.float32),
            pltpu.VMEM((2, 2 * hidden, width), jnp.bfloat16),
            pltpu.VMEM((2, hidden, length), jnp.bfloat16),
            pltpu.VMEM((2, hidden, length), jnp.bfloat16),
            pltpu.VMEM((2 * hidden, length), jnp.bfloat16),
            pltpu.SemaphoreType.DMA((18, pieces)),
            pltpu.SemaphoreType.DMA((4, 2)),
        ],
        compiler_params=pltpu.CompilerParams(
            collective_id=number, has_side_effects=True, vmem_limit_bytes=60 * 2**20
        ),
        cost_estimate=pl.CostEstimate(flops=0, bytes_accessed=600 * 2**20, transcendentals=0),
    )(inputs, gates, mid_up, grad_mid, up_extra, down_extra, ready_up, block, open_rows)[:7]


def gathered(weight):
    return lax.all_gather(weight, "dp", axis=0, tiled=True)


def body(
    tokens,
    cotangent,
    attention_norm_gain,
    query_key_value_weight,
    query_key_value_bias,
    output_projection_weight,
    feedforward_norm_gain,
    router_matrix,
    shared_expert_gate_weight,
    routed_gate_up_weight,
    routed_down_weight,
    shared_expert_gate_up_weight,
    shared_expert_down_weight,
    routes,
    sequence_adapter_index,
    picture_piece_starts,
    adapter_query_key_value_lower,
    adapter_query_key_value_upper,
    adapter_output_lower,
    adapter_output_upper,
    adapter_shared_up_lower,
    adapter_shared_up_upper,
    adapter_shared_down_lower,
    adapter_shared_down_upper,
):
    length, width = tokens.shape
    set_id = sequence_adapter_index[0]
    starts = picture_piece_starts[0]

    def selected_experts(adapter_entry):
        return lax.dynamic_index_in_dim(adapter_entry, set_id, 0, keepdims=False)

    qkv_a, qkv_b, out_a, out_b = (
        selected_experts(adapter_query_key_value_lower),
        selected_experts(adapter_query_key_value_upper),
        selected_experts(adapter_output_lower),
        selected_experts(adapter_output_upper),
    )
    up_a, up_b, down_a, down_b = (
        selected_experts(adapter_shared_up_lower),
        selected_experts(adapter_shared_up_upper),
        selected_experts(adapter_shared_down_lower),
        selected_experts(adapter_shared_down_upper),
    )
    gain_attn_f = attention_norm_gain.astype(jnp.float32)
    gain_ffn_f = feedforward_norm_gain.astype(jnp.float32)
    tokens_f = tokens.astype(jnp.float32)
    normed = to_low(rms_scale(tokens_f, gain_attn_f))
    mid_qkv = to_low(matmul(normed, qkv_a))
    hidden = shared_expert_down_weight.shape[1] // SHARED
    rank = up_a.shape[1]

    def fill(rows):
        return jnp.pad(to_low(rows), ((0, NARROW - rows.shape[0]), (0, 0)))

    def fill_last(rows):
        return jnp.pad(to_low(rows), ((0, 0), (0, 0), (0, NARROW - rows.shape[2])))

    cotangent_down = ADAPTER_SCALE * contract_last(cotangent, down_b)
    up_extra = ADAPTER_SCALE * up_b.reshape(rank, 2, SHARED, hidden).transpose(2, 1, 3, 0)
    up_extra = fill_last(up_extra.reshape(SHARED, 2 * hidden, rank))
    down_extra = fill_last(down_a.reshape(SHARED, hidden, rank))
    depth = routed_gate_up_weight.shape[0]
    early = (READY - SHARED) * 2 * hidden
    shared_block = shared_expert_gate_up_weight.reshape(-1, 2, SHARED, hidden)
    up_block = jnp.transpose(routed_gate_up_weight, (1, 2, 3, 0)).reshape(-1, depth)
    ready_up = lax.all_gather(
        jnp.concatenate(
            [shared_block.transpose(2, 1, 3, 0).reshape(-1, depth), up_block[:early]], axis=0
        ),
        "dp",
        axis=1,
        tiled=True,
    )
    attention_rows = gathered(
        jnp.concatenate([query_key_value_weight, output_projection_weight[:, None]], axis=1)
    )
    qkv_rows, output_rows = attention_rows[:, :3], attention_rows[:, 3]
    row_stack = attention_rows.transpose(1, 0, 2)
    normed, cotangent_down, up_extra, down_extra = lax.optimization_barrier(
        (normed, cotangent_down, up_extra, down_extra)
    )
    qkv_sum = jnp.einsum("tr,rsf->stf", normed, qkv_rows, preferred_element_type=jnp.float32)
    qkv_sum = qkv_sum + query_key_value_bias.astype(jnp.float32)[:, None, :]
    qkv_sum = qkv_sum + ADAPTER_SCALE * jnp.einsum(
        "tr,rsf->stf", mid_qkv, qkv_b, preferred_element_type=jnp.float32
    )
    cosine, sine_table = rope_tables(length)
    signs = jnp.where(jnp.arange(HEAD_SIZE) < HEAD_SIZE // 2, -1.0, 1.0)
    piece_ids = piece_index(jnp.arange(length, dtype=jnp.int32), starts)
    places = (cosine, sine_table * signs[None, :], piece_ids[:, None], piece_ids[None, :])
    query, keys, values, attended = attend(qkv_sum, *places)
    branch_part = contract_last(attended, output_rows)
    down_block = jnp.transpose(routed_down_weight, (1, 2, 0))
    down_block = jnp.concatenate(
        [shared_expert_down_weight.T, down_block.reshape(-1, depth)], axis=0
    )
    branch_total, down_rows, open_rows = summed_and_gathered(
        branch_part,
        matmul(attended, out_a),
        down_block,
        cotangent.T,
        1,
    )
    mid_out = to_low(branch_total[:, width : width + rank])
    hidden_here = (
        tokens_f
        + branch_total[:, :width].astype(jnp.float32)
        + ADAPTER_SCALE * matmul(mid_out, out_b)
    )
    hidden_scale = lax.rsqrt(
        jnp.mean(hidden_here * hidden_here, axis=1, keepdims=True) + EPSILON
    )
    normed_two = to_low(hidden_here * hidden_scale * gain_ffn_f)
    cot_f = cotangent.astype(jnp.float32)
    small_rows = gathered(
        jnp.concatenate(
            [
                router_matrix,
                shared_expert_gate_weight[:, None],
                jnp.full_like(shared_expert_gate_weight, set_id)[:, None],
            ],
            axis=1,
        )
    )
    factors = jnp.concatenate([small_rows[:, : EXPERTS + 1], up_a], axis=1)
    projected = matmul(normed_two, factors)
    router_probs = jax.nn.softmax(projected[:, :EXPERTS], axis=-1)
    shared_gate = jax.nn.sigmoid(projected[:, EXPERTS])
    mid_up = to_low(projected[:, EXPERTS + 1 :])
    expert_ids = jnp.arange(EXPERTS, dtype=jnp.int32)
    chosen = jnp.sum(
        (routes[:, :, None] == expert_ids[None, None, :]).astype(jnp.float32), axis=1
    )
    gates = jnp.concatenate(
        [jnp.broadcast_to(shared_gate[None], (SHARED, length)), (router_probs * chosen).T], axis=0
    )
    grad_mid_down = shared_gate[:, None] * cotangent_down
    (
        normed_two_part,
        gate_grads,
        mid_down_part,
        grad_mid_up_part,
        grad_down_a_parts,
        grad_up_b_parts,
        act_rows,
    ) = experts_step(
        normed_two,
        gates,
        fill(mid_up.T),
        fill(grad_mid_down.T),
        up_extra,
        down_extra,
        ready_up,
        up_block[early:],
        open_rows,
        5,
    )
    grad_down_a_local = grad_down_a_parts[:, :rank].transpose(1, 0, 2).reshape(rank, -1)
    grad_up_b_local = (
        grad_up_b_parts[:, :rank]
        .reshape(SHARED, rank, 2, hidden)
        .transpose(1, 2, 0, 3)
        .reshape(rank, 2, -1)
    )
    narrow_part = jnp.concatenate(
        [
            gate_grads[SHARED:],
            jnp.sum(gate_grads[:SHARED], axis=0, keepdims=True),
            grad_mid_up_part[:rank],
            mid_down_part[:rank],
        ],
        axis=0,
    ).T
    second_total, combined_part = summed_and_down(
        normed_two_part, narrow_part, act_rows, down_rows, 2
    )
    up_from = width + EXPERTS + 1
    grad_mid_up = to_low(second_total[:, up_from : up_from + rank])
    mid_down = to_low(second_total[:, up_from + rank : up_from + 2 * rank])

    def lanes(columns, first):
        return jnp.pad(columns, ((0, 0), (first, NARROW - first - columns.shape[1])))

    grad_hidden, grad_branch, grad_mid_out, grad_attended = epilogue(
        (
            second_total,
            hidden_here,
            hidden_scale,
            cotangent,
            lanes(router_probs, 0),
            lanes(chosen, 0),
            lanes(cotangent_down, EXPERTS + 1 + rank),
            shared_gate[:, None],
        ),
        (gain_ffn_f[None], lanes(factors, 0), fill(out_b), lanes(out_a, 0), row_stack),
    )
    grad_mid_out = grad_mid_out[:, :rank]
    grad_down_b_local = ADAPTER_SCALE * contract_first(
        to_low(shared_gate[:, None] * mid_down.astype(jnp.float32)), cotangent
    )
    grad_up_a_local = contract_first(grad_mid_up, normed_two)
    grad_out_b_local = ADAPTER_SCALE * contract_first(mid_out, grad_branch)
    grad_out_a_local = contract_first(grad_mid_out, attended)

    def side_by_side(local_grads):
        return jnp.concatenate([to_low(local_grad) for local_grad in local_grads], axis=1)

    early_grads = [
        grad_out_a_local,
        grad_up_a_local,
        grad_up_b_local.reshape(grad_up_b_local.shape[0], -1),
        grad_down_a_local,
        grad_down_b_local,
    ]
    grad_attended, early_flat = lax.optimization_barrier(
        (grad_attended, side_by_side(early_grads))
    )
    early_rows = lax.all_gather(early_flat, "dp", axis=0, tiled=True)
    upper = jnp.pad(
        ADAPTER_SCALE * qkv_b.transpose(1, 0, 2), ((0, 0), (0, NARROW - rank), (0, 0))
    )
    combined_here, grad_qkv, normed_part, mid_total = summed_and_attended_back(
        combined_part,
        row_stack,
        upper,
        (query, keys, values, grad_attended) + places,
        3,
    )
    mid_total, early_rows = lax.optimization_barrier((to_low(mid_total), early_rows))
    grad_mid_qkv = mid_total[:, :rank]
    late_grads = [
        (
            ADAPTER_SCALE
            * jnp.einsum("tr,stf->rsf", mid_qkv, grad_qkv, preferred_element_type=jnp.float32)
        ).reshape(rank, -1),
        contract_first(grad_mid_qkv, normed),
        grad_out_b_local,
    ]
    normed_part, late_flat = lax.optimization_barrier((normed_part, side_by_side(late_grads)))
    late_rows = lax.all_gather(late_flat, "dp", axis=0, tiled=True)
    grad_tokens, output = last_step(
        normed_part,
        (grad_hidden, tokens, hidden_here, combined_here),
        (
            mid_total,
            lanes(qkv_a, 0),
            gain_attn_f[None],
            lanes(mid_down, 0),
            fill(down_b),
            shared_gate[:, None],
        ),
        4,
    )
    output, late_rows = lax.optimization_barrier((output, late_rows))
    everyone = small_rows[:: small_rows.shape[0] // lax.axis_size("dp"), EXPERTS + 1]
    hits = jnp.arange(ADAPTER_SETS, dtype=jnp.int32)[:, None] == everyone.astype(jnp.int32)
    same = jnp.arange(rank)[:, None] == jnp.arange(rank)[None, :]
    chooser = to_low(hits[:, None, :, None] & same[None, :, None, :])
    chooser = chooser.reshape(ADAPTER_SETS * rank, -1)

    def adapter_sums(local_grads, rows):
        results, start = [], 0
        for local_grad in local_grads:
            size = local_grad.shape[1]
            total = matmul(chooser, rows[:, start : start + size])
            results.append(total.reshape(ADAPTER_SETS, rank, size))
            start += size
        return results

    def flipped(total):
        return jnp.swapaxes(total, 1, 2)

    def opened(total, count):
        return total.reshape(total.shape[0], total.shape[1], count, -1)

    total_out_a, total_up_a, total_up_b, total_down_a, total_down_b = adapter_sums(
        early_grads, early_rows
    )
    total_qkv_b, total_qkv_a, total_out_b = adapter_sums(late_grads, late_rows)
    return (
        output,
        grad_tokens,
        flipped(total_qkv_a),
        opened(total_qkv_b, 3),
        flipped(total_out_a),
        total_out_b,
        flipped(total_up_a),
        opened(total_up_b, 2),
        flipped(total_down_a),
        total_down_b,
    )


def solution(mesh):
    return jax.shard_map(
        body,
        mesh=mesh,
        in_specs=(
            P("dp", None),
            P("dp", None),
            P(),
            P("dp", None, "tensor"),
            P(None, "tensor"),
            P("dp", "tensor"),
            P(),
            P("dp", None),
            P("dp"),
            P("dp", None, None, "tensor"),
            P("dp", None, "tensor"),
            P("dp", None, "tensor"),
            P("dp", "tensor"),
            P("dp", None),
            P("dp"),
            P("dp", None),
            P(),
            P(None, None, None, "tensor"),
            P(None, "tensor", None),
            P(),
            P(),
            P(None, None, None, "tensor"),
            P(None, "tensor", None),
            P(),
        ),
        out_specs=(
            P("dp", None),
            P("dp", None),
            P(),
            P(None, None, None, "tensor"),
            P(None, "tensor", None),
            P(),
            P(),
            P(None, None, None, "tensor"),
            P(None, "tensor", None),
            P(),
        ),
        check_vma=False,
    )
```

```python
import functools

import jax
import jax.numpy as jnp
from jax import lax
from jax.experimental import pallas as pl
from jax.experimental.pallas import tpu as pltpu
from jax.sharding import PartitionSpec as P

HEAD_SIZE = 128
TOP = 4
EXPERTS = 16
ADAPTER_SETS = 8
PIECE = 256


EPSILON = 1e-06
THETA = 1000000.0
ADAPTER_SCALE = 2.0
MASKED = -1e30
QUERY_ROWS = 256
NARROW = 128
MESH = pl.DeviceIdType.MESH
SUM_CHUNKS = 16
LAG = 1
AHEAD = 1
LEAD = 2
SHARED = 4
HALVES = 1
READY = 4


def matmul(left_side, right_side):
    return jnp.dot(left_side, right_side, preferred_element_type=jnp.float32)


def contract_last(left_side, right_side):
    return lax.dot_general(
        left_side, right_side, (((1,), (1,)), ((), ())), preferred_element_type=jnp.float32
    )


def contract_first(left_side, right_side):
    return lax.dot_general(
        left_side, right_side, (((0,), (0,)), ((), ())), preferred_element_type=jnp.float32
    )


def to_low(values):
    return values.astype(jnp.bfloat16)


def rms_scale(values, gain_values):
    return (
        values * lax.rsqrt(jnp.mean(values * values, axis=1, keepdims=True) + EPSILON) * gain_values
    )


def rope_tables(length):
    half_size = HEAD_SIZE // 2
    frequency = THETA ** (-jnp.arange(half_size, dtype=jnp.float32) * 2.0 / HEAD_SIZE)
    angles = jnp.arange(length, dtype=jnp.float32)[:, None] * frequency[None, :]
    return (
        jnp.concatenate([jnp.cos(angles)] * 2, axis=1),
        jnp.concatenate([jnp.sin(angles)] * 2, axis=1),
    )


def piece_index(positions, starts):
    inside = (positions[:, None] >= starts[None, :]) & (
        positions[:, None] < starts[None, :] + PIECE
    )
    labels = jnp.arange(starts.shape[0], dtype=jnp.int32)[None, :] + 1
    return jnp.sum(jnp.where(inside, labels, 0), axis=1) - 1


def line_sum_steps(
    chunks,
    lag,
    wide_ref,
    narrow_ref,
    total_ref,
    part_ref,
    from_end,
    pair_sum,
    from_pair,
    semaphores,
    on_total=None,
):
    place = lax.axis_index("tensor")
    width = wide_ref.shape[1]
    rows = part_ref.shape[0] // chunks
    inner = (place == 1) | (place == 2)
    end = (place == 0) | (place == 3)
    mate = jnp.where(place < 2, 1 - place, 5 - place)
    other = jnp.where(inner, 3 - place, place)

    def span(chunk):
        return pl.ds(pl.multiple_of(chunk * rows, rows), rows)

    def copy(source, target, chunk, lane, device):
        return pltpu.make_async_remote_copy(
            source.at[span(chunk)],
            target.at[span(chunk)],
            semaphores.at[2 * lane, chunk],
            semaphores.at[2 * lane + 1, chunk],
            device_id={"tensor": device},
            device_id_type=MESH,
        )

    def inward(chunk):
        return copy(part_ref, from_end, chunk, 0, mate)

    def across(chunk):
        return copy(pair_sum, from_pair, chunk, 1, other)

    def outward(chunk):
        return copy(total_ref, total_ref, chunk, 2, mate)

    def add(left_ref, right_ref, out_ref, chunk):
        out_ref[span(chunk)] = to_low(
            left_ref[span(chunk)].astype(jnp.float32) + right_ref[span(chunk)].astype(jnp.float32)
        )

    def stage(chunk):
        part_ref[span(chunk), :width] = to_low(wide_ref[span(chunk)])
        if narrow_ref is not None:
            part_ref[span(chunk), width:] = narrow_ref[span(chunk)]

    def greet(extra):
        barrier = pltpu.get_barrier_semaphore()
        pl.semaphore_signal(barrier, inc=1, device_id={"tensor": mate}, device_id_type=MESH)

        @pl.when(inner)
        def _():
            pl.semaphore_signal(barrier, inc=1, device_id={"tensor": other}, device_id_type=MESH)
            pl.semaphore_wait(barrier, 2 + extra)

        @pl.when(end)
        def _():
            pl.semaphore_wait(barrier, 1 + extra)

    def begin(first=0, last=chunks):
        @pl.when(end)
        def _():
            @pl.loop(first, last)
            def _(chunk):
                stage(chunk)
                inward(chunk).start()

    def advance(step):
        @pl.when(inner & (step < chunks))
        def _():
            stage(step)
            inward(step).wait_recv()
            add(part_ref, from_end, pair_sum, step)
            across(step).start()

        @pl.when(inner & (step >= lag) & (step < chunks + lag))
        def _():
            across(step - lag).wait_recv()
            add(pair_sum, from_pair, total_ref, step - lag)
            outward(step - lag).start()
            if on_total is not None:
                on_total(step - lag)

    def finish():
        @pl.when(end)
        def _():
            @pl.loop(0, chunks)
            def _(chunk):
                inward(chunk).wait_send()
                outward(chunk).wait_recv()
                if on_total is not None:
                    on_total(chunk)

        @pl.when(inner)
        def _():
            @pl.loop(0, chunks)
            def _(chunk):
                across(chunk).wait_send()
                outward(chunk).wait_send()

    return greet, begin, advance, finish


def plane_gather_steps(pieces, block_ref, whole_ref, semaphores, local_semaphore):
    spot = lax.axis_index("dp")
    depth = block_ref.shape[1]
    rows = block_ref.shape[0] // pieces
    core_mate = spot + 1 - 2 * (spot % 2)
    x_mate = spot + 2 - 4 * ((spot // 2) % 2)
    y_mate = spot + 4 - 8 * (spot // 4)
    x_y_mate = x_mate + 4 - 8 * (spot // 4)
    lanes = {
        "core": (spot, core_mate, 0, 1),
        "x": (spot, x_mate, 0, 1),
        "y": (spot, y_mate, 0, 1),
        "x_core": (x_mate, core_mate, 0, 1),
        "x_y": (x_mate, y_mate, 0, 2),
        "y_core": (y_mate, core_mate, 0, 1),
        "y_x": (y_mate, x_mate, 1, 2),
        "xy_core": (x_y_mate, core_mate, 0, 2),
        "yx_core": (x_y_mate, core_mate, 1, 2),
    }
    order = list(lanes)

    def send(name, piece):
        owner, device, part, parts = lanes[name]
        lane = order.index(name)
        span = pl.ds(
            pl.multiple_of(piece * rows + part * (rows // parts), rows // parts), rows // parts
        )
        columns = pl.ds(pl.multiple_of(owner * depth, depth), depth)
        target = whole_ref.at[span, columns]
        source = block_ref.at[span] if name in ("core", "x", "y") else target
        return pltpu.make_async_remote_copy(
            source,
            target,
            semaphores.at[2 * lane, piece],
            semaphores.at[2 * lane + 1, piece],
            device_id={"dp": device},
            device_id_type=MESH,
        )

    def own():
        columns = pl.ds(pl.multiple_of(spot * depth, depth), depth)
        return pltpu.make_async_copy(block_ref, whole_ref.at[:, columns], local_semaphore)

    def greet():
        barrier = pltpu.get_barrier_semaphore()
        for device in (core_mate, x_mate, y_mate):
            pl.semaphore_signal(barrier, inc=1, device_id={"dp": device}, device_id_type=MESH)

    def launch(piece):
        @pl.when((piece >= 0) & (piece < pieces))
        def _():
            for name in ("x", "y", "core"):
                send(name, piece).start()

    def forward(piece):
        @pl.when((piece >= 0) & (piece < pieces))
        def _():
            send("x", piece).wait_recv()
            send("x_y", piece).start()
            send("x_core", piece).start()
            send("y", piece).wait_recv()
            send("y_x", piece).start()
            send("y_core", piece).start()

    def hand_over(piece):
        @pl.when((piece >= 0) & (piece < pieces))
        def _():
            send("x_y", piece).wait_recv()
            send("xy_core", piece).start()
            send("y_x", piece).wait_recv()
            send("yx_core", piece).start()

    def advance(step):
        launch(step + LEAD)
        forward(step - AHEAD)
        hand_over(step - 2 * AHEAD)

    def load(first, count, target, semaphore):
        span = pl.ds(pl.multiple_of(first, rows), count)

        def columns(owner):
            return pl.ds(pl.multiple_of(owner * depth, depth), depth)

        here = columns(spot)
        copies = [pltpu.make_async_copy(block_ref.at[span], target.at[:, here], semaphore)]
        for shift in range(1, 8):
            there = columns((spot + shift) % 8)
            copies.append(
                pltpu.make_async_copy(
                    whole_ref.at[span, there], target.at[:, there], semaphore
                )
            )
        return copies

    def load_wait(count, target, semaphore):
        pltpu.make_async_copy(whole_ref.at[pl.ds(0, count)], target, semaphore).wait()

    def arrive(piece):
        for name in ("core", "x_core", "y_core", "xy_core", "yx_core"):
            send(name, piece).wait_recv()

    def finish():
        @pl.loop(0, pieces)
        def _(piece):
            for name in order:
                send(name, piece).wait_send()

    return greet, advance, arrive, finish, own, load, load_wait, (launch, forward, hand_over)


def sum_gather_kernel(
    chunks,
    pieces,
    attended_ref,
    narrow_ref,
    row_stack_ref,
    block_ref,
    cotangent_ref,
    total_ref,
    whole_ref,
    open_ref,
    *scratch,
):
    wide_ref, projection, projection_semaphore = scratch[-3:]
    greet, begin, advance, finish = line_sum_steps(
        chunks, LAG, wide_ref, narrow_ref, total_ref, *scratch[:5]
    )
    gather_semaphores, local_semaphores, piece_rows, open_rows = scratch[5:-3]
    gather_greet, gather_advance, gather_arrive, gather_finish, own, load, load_wait, stages = (
        plane_gather_steps(
            pieces, block_ref, whole_ref, gather_semaphores, local_semaphores.at[0]
        )
    )
    rows = piece_rows.shape[1]

    def store(piece):
        slot = piece % 2
        span = pl.ds(pl.multiple_of(piece * rows, rows), rows)
        return pltpu.make_async_copy(
            open_rows.at[slot], open_ref.at[span], local_semaphores.at[3 + slot]
        )

    load_projection = pltpu.make_async_copy(
        row_stack_ref.at[3], projection, projection_semaphore.at[0]
    )
    load_projection.start()
    gather_greet()
    greet(3)

    @pl.loop(0, LEAD)
    def _(piece):
        stages[0](piece)

    load_projection.wait()
    blocks = 4
    size = wide_ref.shape[0] // blocks
    for block in range(blocks):
        span = slice(block * size, (block + 1) * size)
        wide_ref[span] = contract_last(attended_ref[span], projection[...])
        begin(block * chunks // blocks, (block + 1) * chunks // blocks)
    own().start()

    @pl.loop(0, max(chunks + LAG, pieces + 3 * AHEAD + 1))
    def _(step):
        gather_advance(step)
        advance(step)

        @pl.when((step >= 3 * AHEAD) & (step < pieces + 3 * AHEAD))
        def _():
            piece = step - 3 * AHEAD
            gather_arrive(piece)
            slot = piece % 2
            for copy in load(piece * rows, rows, piece_rows.at[slot], local_semaphores.at[1 + slot]):
                copy.start()

        @pl.when((step > 3 * AHEAD) & (step <= pieces + 3 * AHEAD))
        def _():
            piece = step - 3 * AHEAD - 1
            slot = piece % 2
            load_wait(rows, piece_rows.at[slot], local_semaphores.at[1 + slot])

            @pl.when(piece >= 2)
            def _():
                store(piece - 2).wait()

            open_rows[piece % 2] = to_low(matmul(piece_rows[piece % 2], cotangent_ref[...]))
            store(piece).start()

    store(pieces - 2).wait()
    store(pieces - 1).wait()
    own().wait()
    gather_finish()
    finish()


def sum_down_kernel(
    chunks, wide_ref, narrow_ref, act_ref, down_ref, total_ref, out_ref, *scratch
):
    greet, begin, advance, finish = line_sum_steps(
        chunks, LAG, wide_ref, narrow_ref, total_ref, *scratch[:5]
    )
    semaphores, act_rows, down_rows, out_rows = scratch[5:]
    rows = act_rows.shape[1]
    blocks = down_ref.shape[0] // rows

    def loads(block):
        slot = block % 2
        span = pl.ds(pl.multiple_of(block * rows, rows), rows)
        return [
            pltpu.make_async_copy(act_ref.at[span], act_rows.at[slot], semaphores.at[0, slot]),
            pltpu.make_async_copy(down_ref.at[span], down_rows.at[slot], semaphores.at[1, slot]),
        ]

    for load in loads(0):
        load.start()
    greet(0)
    begin()
    out_rows[...] = jnp.zeros_like(out_rows)

    @pl.loop(0, max(blocks, chunks + LAG))
    def _(step):
        advance(step)

        @pl.when(step < blocks)
        def _():
            @pl.when(step + 1 < blocks)
            def _():
                for load in loads(step + 1):
                    load.start()

            for load in loads(step):
                load.wait()
            tile = min(256, out_rows.shape[0])

            @pl.loop(0, out_rows.shape[0] // tile)
            def _(index):
                span = pl.ds(pl.multiple_of(index * tile, tile), tile)
                out_rows[span] += contract_first(
                    act_rows[step % 2, :, span], down_rows[step % 2]
                )

    out_ref[...] = to_low(out_rows[...])
    finish()


def last_sum_kernel(
    chunks,
    wide_ref,
    streamed_refs,
    mid_ref,
    qkv_a_ref,
    gain_ref,
    mid_down_ref,
    down_b_ref,
    gate_ref,
    grad_tokens_ref,
    output_ref,
    total_ref,
    *scratch,
):
    buffers, load_semaphores = scratch[5:-1], scratch[-1]
    rows = wide_ref.shape[0] // chunks

    def span(chunk):
        return pl.ds(pl.multiple_of(chunk * rows, rows), rows)

    def loads(chunk):
        slot = chunk % 2
        return [
            pltpu.make_async_copy(
                source.at[span(chunk)], target.at[slot], load_semaphores.at[number, slot]
            )
            for number, (source, target) in enumerate(zip(streamed_refs, buffers))
        ]

    def on_total(chunk):
        for load in loads(chunk):
            load.wait()

        @pl.when(chunk + 1 < chunks)
        def _():
            for load in loads(chunk + 1):
                load.start()

        here = span(chunk)
        grad_hidden, tokens, hidden, combined = [buffer[chunk % 2] for buffer in buffers]
        grad_normed = total_ref[here].astype(jnp.float32) + contract_last(
            mid_ref[here], qkv_a_ref[...]
        )
        grad_tokens_ref[here] = last_grad(grad_normed, tokens, gain_ref[...], grad_hidden)
        extra = ADAPTER_SCALE * matmul(mid_down_ref[here], down_b_ref[...])
        output_ref[here] = to_low(hidden + combined.astype(jnp.float32) + gate_ref[here] * extra)

    greet, begin, advance, finish = line_sum_steps(
        chunks, 1, wide_ref, None, total_ref, *scratch[:5], on_total=on_total
    )
    for load in loads(0):
        load.start()
    greet(0)
    begin()

    @pl.loop(0, chunks + 1)
    def _(step):
        advance(step)

    finish()


def last_grad(grad_normed, tokens, gain, grad_hidden):
    tokens_f = tokens.astype(jnp.float32)
    scale = lax.rsqrt(jnp.mean(tokens_f * tokens_f, axis=1, keepdims=True) + EPSILON)
    scaled = grad_normed * gain
    pull = jnp.mean(tokens_f * scaled, axis=1, keepdims=True)
    return to_low(grad_hidden + scale * scaled - tokens_f * (scale * scale * scale * pull))


def attend_back_sum_kernel(chunks, wide_ref, rows_ref, upper_ref, *refs):
    inputs, scratch = refs[:8], refs[12:]
    total_ref, grad_qkv_ref, normed_part_ref, mid_total_ref = refs[8:12]
    greet, begin, advance, finish = line_sum_steps(
        chunks, LAG, wide_ref, None, total_ref, *scratch[:5]
    )
    head_block = attend_back_steps(*inputs, grad_qkv_ref, *scratch[5:7])
    mid_part = scratch[7]
    _, mid_begin, mid_advance, mid_finish = line_sum_steps(
        1, 1, mid_part, None, mid_total_ref, *scratch[8:13]
    )
    length, heads_width = inputs[0].shape
    heads, blocks = heads_width // HEAD_SIZE, length // QUERY_ROWS
    each = blocks // 2
    rows = scratch[-2]
    load = pltpu.make_async_copy(rows_ref.at[:3], rows, scratch[-1].at[0])
    load.start()
    done = heads * each
    greet(0)
    begin(0, done + blocks)

    @pl.loop(0, heads)
    def _(head):
        for step in range(each):
            advance(head * each + step)
            head_block(head, 2 * step * QUERY_ROWS)
            head_block(head, (2 * step + 1) * QUERY_ROWS)

    mid_part[...] = grad_mid_rows(grad_qkv_ref, upper_ref)
    mid_begin()
    begin(done + blocks, chunks)
    load.wait()

    @pl.loop(0, blocks)
    def _(block):
        advance(done + block)
        span = pl.ds(pl.multiple_of(block * QUERY_ROWS, QUERY_ROWS), QUERY_ROWS)
        normed_part_ref[span] = to_low(
            sum(contract_last(grad_qkv_ref[part, span], rows[part]) for part in range(3))
        )

    mid_advance(0)

    advance(done + blocks)
    mid_advance(1)

    @pl.loop(done + blocks + 1, max(done + blocks + 1, chunks + LAG))
    def _(step):
        advance(step)

    mid_finish()
    finish()


def grad_mid_rows(grad_qkv_ref, upper_ref):
    return sum(contract_last(grad_qkv_ref[part], upper_ref[part]) for part in range(3))


def hidden_kernel(
    total_ref,
    tokens_ref,
    out_b_ref,
    gain_ref,
    factors_ref,
    hidden_ref,
    scale_ref,
    normed_ref,
    projected_ref,
):
    width = tokens_ref.shape[1]
    total = total_ref[...]
    hidden = (
        tokens_ref[...].astype(jnp.float32)
        + total[:, :width].astype(jnp.float32)
        + ADAPTER_SCALE * matmul(to_low(total[:, width:]), out_b_ref[...])
    )
    scale = lax.rsqrt(jnp.mean(hidden * hidden, axis=1, keepdims=True) + EPSILON)
    normed = to_low(hidden * scale * gain_ref[...])
    hidden_ref[...] = hidden
    scale_ref[...] = scale
    normed_ref[...] = normed
    projected_ref[...] = matmul(normed, factors_ref[...])


def hidden_rows(total, tokens, out_b, gain, factors):
    length, width = tokens.shape
    rows = min(length, 128)

    def block(columns):
        return pl.BlockSpec((rows, columns), lambda index: (index, 0))

    def whole(array):
        return pl.BlockSpec(array.shape, lambda index: (0, 0))

    return pl.pallas_call(
        hidden_kernel,
        grid=(length // rows,),
        in_specs=[block(total.shape[1]), block(width), whole(out_b), whole(gain), whole(factors)],
        out_specs=[block(width), block(1), block(width), block(NARROW)],
        out_shape=[
            jax.ShapeDtypeStruct((length, width), jnp.float32),
            jax.ShapeDtypeStruct((length, 1), jnp.float32),
            jax.ShapeDtypeStruct((length, width), jnp.bfloat16),
            jax.ShapeDtypeStruct((length, NARROW), jnp.float32),
        ],
        compiler_params=pltpu.CompilerParams(
            vmem_limit_bytes=40 * 2**20, dimension_semantics=("arbitrary",)
        ),
        cost_estimate=pl.CostEstimate(
            flops=4 * length * width * NARROW, bytes_accessed=20 * 2**20, transcendentals=0
        ),
    )(total, tokens, out_b, gain, factors)


def epilogue_kernel(
    total_ref,
    hidden_ref,
    scale_ref,
    cotangent_ref,
    gain_ref,
    probs_ref,
    chosen_ref,
    extra_ref,
    gate_ref,
    factors_ref,
    out_b_ref,
    out_a_ref,
    rows_ref,
    grad_hidden_ref,
    grad_branch_ref,
    grad_mid_ref,
    grad_attended_ref,
):
    width = hidden_ref.shape[1]
    narrow = total_ref[:, width:].astype(jnp.float32)
    lane = lax.broadcasted_iota(jnp.int32, narrow.shape, 1)
    probs = probs_ref[...]
    grad_probs = chosen_ref[...] * narrow
    grad_logits = probs * (grad_probs - jnp.sum(probs * grad_probs, axis=1, keepdims=True))
    only_gate = jnp.where(lane == EXPERTS, narrow, 0.0)
    gate_grad = jnp.sum(only_gate + narrow * extra_ref[...], axis=1, keepdims=True)
    gate = gate_ref[...]
    gate_logit = gate_grad * gate * (1.0 - gate)
    rank = extra_ref.shape[1] // 8
    rows = jnp.where(lane <= EXPERTS + rank, narrow, 0.0)
    rows = jnp.where(lane == EXPERTS, gate_logit, rows)
    rows = to_low(jnp.where(lane < EXPERTS, grad_logits, rows))
    grad_normed = total_ref[:, :width].astype(jnp.float32) + contract_last(rows, factors_ref[...])
    hidden = hidden_ref[...]
    scale = scale_ref[...]
    scaled = grad_normed * gain_ref[...]
    pull = jnp.mean(hidden * scaled, axis=1, keepdims=True)
    grad_hidden = (
        cotangent_ref[...].astype(jnp.float32)
        + scale * scaled
        - hidden * (scale * scale * scale * pull)
    )
    grad_hidden_ref[...] = grad_hidden
    grad_branch = to_low(grad_hidden)
    grad_branch_ref[...] = grad_branch
    grad_mid = to_low(ADAPTER_SCALE * contract_last(grad_branch, out_b_ref[...]))
    grad_mid_ref[...] = grad_mid
    grad_attended_ref[...] = to_low(
        matmul(grad_branch, rows_ref[0]) + contract_last(grad_mid, out_a_ref[...])
    )


def epilogue(blocked, still):
    length = blocked[0].shape[0]
    width, heads_width = still[-1].shape[1:]
    rows = min(length, 256)
    total, hidden, scale, cotangent, probs, chosen, extra, gate = blocked
    gain, factors, out_b, out_a, row_stack = still

    def block(array):
        return pl.BlockSpec((rows, array.shape[1]), lambda index: (index, 0))

    def whole(array):
        return pl.BlockSpec(array.shape, lambda index: (0, 0))

    outs = [
        jax.ShapeDtypeStruct((length, width), jnp.float32),
        jax.ShapeDtypeStruct((length, width), jnp.bfloat16),
        jax.ShapeDtypeStruct((length, NARROW), jnp.bfloat16),
        jax.ShapeDtypeStruct((length, heads_width), jnp.bfloat16),
    ]
    return pl.pallas_call(
        epilogue_kernel,
        grid=(length // rows,),
        in_specs=[block(array) for array in (total, hidden, scale, cotangent)]
        + [whole(gain)]
        + [block(array) for array in (probs, chosen, extra, gate)]
        + [whole(array) for array in (factors, out_b, out_a)]
        + [pl.BlockSpec((1, width, heads_width), lambda index: (3, 0, 0))],
        out_specs=[block(out) for out in outs],
        out_shape=outs,
        compiler_params=pltpu.CompilerParams(
            vmem_limit_bytes=56 * 2**20, dimension_semantics=("arbitrary",)
        ),
        cost_estimate=pl.CostEstimate(
            flops=2 * length * width * heads_width,
            bytes_accessed=32 * 2**20,
            transcendentals=0,
        ),
    )(
        total,
        hidden,
        scale,
        cotangent,
        gain,
        probs,
        chosen,
        extra,
        gate,
        factors,
        out_b,
        out_a,
        row_stack,
    )


def on_line():
    return lax.axis_size("tensor") == 4


def in_plane():
    return lax.axis_size("dp") == 8


def in_vmem(count):
    return [pl.BlockSpec(memory_space=pltpu.VMEM)] * count


def in_hbm(count):
    return [pl.BlockSpec(memory_space=pltpu.HBM)] * count


def sum_scratch(shape):
    return [pltpu.VMEM(shape, jnp.bfloat16)] * 4 + [pltpu.SemaphoreType.DMA((6, SUM_CHUNKS))]


def narrowed(narrow_part):
    pad = jnp.zeros((narrow_part.shape[0], NARROW - narrow_part.shape[1]), jnp.bfloat16)
    return jnp.concatenate([to_low(narrow_part), pad], axis=1)


def plain_sum(wide_part, narrow_part):
    if narrow_part is not None:
        pad = jnp.zeros((narrow_part.shape[0], NARROW - narrow_part.shape[1]), jnp.float32)
        wide_part = jnp.concatenate([wide_part, narrow_part, pad], axis=1)
    return lax.psum(wide_part, "tensor")


def last_step(wide_part, streamed, still, number):
    length, width = wide_part.shape
    mid, qkv_a, gain, mid_down, down_b, gate = still
    if not on_line():
        grad_hidden, tokens, hidden, combined = streamed
        grad_normed = plain_sum(wide_part, None).astype(jnp.float32) + contract_last(mid, qkv_a)
        extra = ADAPTER_SCALE * matmul(mid_down, down_b)
        return (
            last_grad(grad_normed, tokens, gain, grad_hidden),
            to_low(hidden + combined.astype(jnp.float32) + gate * extra),
        )
    rows = length // SUM_CHUNKS

    def kernel(wide_ref, *refs):
        last_sum_kernel(SUM_CHUNKS, wide_ref, refs[:4], *refs[4:])

    return pl.pallas_call(
        kernel,
        out_shape=[jax.ShapeDtypeStruct((length, width), jnp.bfloat16)] * 2,
        in_specs=in_vmem(1) + in_hbm(4) + in_vmem(6),
        out_specs=in_vmem(2),
        scratch_shapes=[pltpu.VMEM((length, width), jnp.bfloat16)]
        + sum_scratch((length, width))
        + [pltpu.VMEM((2, rows, width), array.dtype) for array in streamed]
        + [pltpu.SemaphoreType.DMA((4, 2))],
        compiler_params=pltpu.CompilerParams(
            collective_id=number, has_side_effects=True, vmem_limit_bytes=58 * 2**20
        ),
        cost_estimate=pl.CostEstimate(flops=0, bytes_accessed=300 * 2**20, transcendentals=0),
    )(wide_part, *streamed, *still)


def summed_and_gathered(attended, narrow_part, row_stack, block, cotangents, number):
    length, width = attended.shape[0], row_stack.shape[1]
    if not (on_line() and in_plane()):
        whole = lax.all_gather(block, "dp", axis=1, tiled=True)
        open_rows = to_low(matmul(whole, cotangents))
        wide_part = contract_last(attended, row_stack[3])
        return plain_sum(wide_part, narrow_part), whole, open_rows
    shape = (length, width + NARROW)
    pieces = SHARED + EXPERTS
    rows = block.shape[0] // pieces
    total, whole, open_rows = pl.pallas_call(
        functools.partial(sum_gather_kernel, SUM_CHUNKS, pieces),
        out_shape=[
            jax.ShapeDtypeStruct(shape, jnp.bfloat16),
            jax.ShapeDtypeStruct((block.shape[0], width), jnp.bfloat16),
            jax.ShapeDtypeStruct((block.shape[0], length), jnp.bfloat16),
        ],
        in_specs=in_vmem(2) + in_hbm(2) + in_vmem(1),
        out_specs=in_vmem(1) + in_hbm(2),
        scratch_shapes=sum_scratch(shape)
        + [
            pltpu.SemaphoreType.DMA((18, pieces)),
            pltpu.SemaphoreType.DMA((5,)),
            pltpu.VMEM((2, rows, width), jnp.bfloat16),
            pltpu.VMEM((2, rows, length), jnp.bfloat16),
            pltpu.VMEM((length, width), jnp.float32),
            pltpu.VMEM(row_stack.shape[1:], jnp.bfloat16),
            pltpu.SemaphoreType.DMA((1,)),
        ],
        compiler_params=pltpu.CompilerParams(
            collective_id=number, has_side_effects=True, vmem_limit_bytes=58 * 2**20
        ),
        cost_estimate=pl.CostEstimate(flops=0, bytes_accessed=360 * 2**20, transcendentals=0),
    )(attended, narrowed(narrow_part), row_stack, block, cotangents)
    return total, whole, open_rows


def summed_and_down(wide_part, narrow_part, act_rows, down_rows, number):
    length, width = wide_part.shape
    if not on_line():
        out = contract_first(act_rows, down_rows)
        return plain_sum(wide_part.astype(jnp.float32), narrow_part), out
    shape = (length, width + NARROW)
    rows = 2 * down_rows.shape[0] // (SHARED + EXPERTS)
    total, out = pl.pallas_call(
        functools.partial(sum_down_kernel, SUM_CHUNKS),
        out_shape=[
            jax.ShapeDtypeStruct(shape, jnp.bfloat16),
            jax.ShapeDtypeStruct((length, width), jnp.bfloat16),
        ],
        in_specs=in_vmem(2) + in_hbm(2),
        out_specs=in_vmem(2),
        scratch_shapes=sum_scratch(shape)
        + [
            pltpu.SemaphoreType.DMA((2, 2)),
            pltpu.VMEM((2, rows, length), jnp.bfloat16),
            pltpu.VMEM((2, rows, width), jnp.bfloat16),
            pltpu.VMEM((length, width), jnp.float32),
        ],
        compiler_params=pltpu.CompilerParams(
            collective_id=number, has_side_effects=True, vmem_limit_bytes=58 * 2**20
        ),
        cost_estimate=pl.CostEstimate(flops=0, bytes_accessed=300 * 2**20, transcendentals=0),
    )(wide_part, narrowed(narrow_part), act_rows, down_rows)
    return total, out


def block_mask(first, rows, extent, row_piece_ref, col_piece_ref):
    row_place = lax.broadcasted_iota(jnp.int32, (rows, extent), 0) + first
    col_place = lax.broadcasted_iota(jnp.int32, (rows, extent), 1)
    row_piece = row_piece_ref[first : first + rows, 0:1]
    together = (row_piece == col_piece_ref[0:1, :extent]) & (row_piece >= 0)
    return (col_place <= row_place) | together


def block_probs(query_rows, keys, allowed):
    scores = jnp.where(allowed, contract_last(query_rows, keys) * HEAD_SIZE**-0.5, MASKED)
    raised = jnp.exp(scores - jnp.max(scores, axis=1, keepdims=True))
    return raised * (1.0 / jnp.sum(raised, axis=1, keepdims=True))


def half_turn(values, signed_sine):
    return pltpu.roll(values, HEAD_SIZE // 2, 1) * signed_sine


def attend_kernel(
    qkv_ref,
    mid_ref,
    upper_ref,
    bias_ref,
    cosine_ref,
    sine_ref,
    row_piece_ref,
    col_piece_ref,
    query_ref,
    keys_ref,
    values_ref,
    attended_ref,
):
    length = qkv_ref.shape[1]

    def whole(source, column):
        extra = matmul(mid_ref[...], upper_ref[source, :, column])
        return qkv_ref[source, :, column] + extra + bias_ref[source, :, column]

    @pl.loop(0, qkv_ref.shape[2] // HEAD_SIZE)
    def _(head):
        column = pl.ds(pl.multiple_of(head * HEAD_SIZE, HEAD_SIZE), HEAD_SIZE)
        for source, target in ((0, query_ref), (1, keys_ref)):
            raw = whole(source, column)
            target[:, column] = to_low(raw * cosine_ref[...] + half_turn(raw, sine_ref[...]))
        values_ref[:, column] = to_low(whole(2, column))
        for first in range(0, length, QUERY_ROWS):
            extent = min(length, first + QUERY_ROWS + PIECE)
            allowed = block_mask(first, QUERY_ROWS, extent, row_piece_ref, col_piece_ref)
            probs = block_probs(
                query_ref[first : first + QUERY_ROWS, column], keys_ref[:extent, column], allowed
            )
            attended_ref[first : first + QUERY_ROWS, column] = to_low(
                matmul(to_low(probs), values_ref[:extent, column])
            )


def attend(qkv, mid, upper, bias, cosine, signed_sine, row_piece, col_piece):
    length, heads_width = qkv.shape[1:]
    shape = jax.ShapeDtypeStruct((length, heads_width), jnp.bfloat16)
    return pl.pallas_call(
        attend_kernel,
        out_shape=[shape] * 4,
        in_specs=[pl.BlockSpec(memory_space=pltpu.VMEM)] * 8,
        out_specs=[pl.BlockSpec(memory_space=pltpu.VMEM)] * 4,
        compiler_params=pltpu.CompilerParams(vmem_limit_bytes=48 * 2**20),
        cost_estimate=pl.CostEstimate(
            flops=4 * length * length * heads_width,
            bytes_accessed=16 * 2**20,
            transcendentals=length * length * heads_width // HEAD_SIZE,
        ),
    )(qkv, mid, upper, bias, cosine, signed_sine, row_piece, col_piece)


def attend_back_steps(
    query_ref,
    keys_ref,
    values_ref,
    grad_ref,
    cosine_ref,
    sine_ref,
    row_piece_ref,
    col_piece_ref,
    grad_qkv_ref,
    grad_keys,
    grad_values,
):
    length = query_ref.shape[0]

    def turned_back(grad, first):
        span = slice(first, first + grad.shape[0])
        scaled = grad * HEAD_SIZE**-0.5
        return to_low(scaled * cosine_ref[span] - half_turn(scaled, sine_ref[span]))

    def head_block(head, first):
        column = pl.ds(pl.multiple_of(head * HEAD_SIZE, HEAD_SIZE), HEAD_SIZE)
        span = slice(first, first + QUERY_ROWS)
        extent = min(length, first + QUERY_ROWS + PIECE)
        if first == 0:
            grad_keys[...] = jnp.zeros_like(grad_keys)
            grad_values[...] = jnp.zeros_like(grad_values)
        allowed = block_mask(first, QUERY_ROWS, extent, row_piece_ref, col_piece_ref)
        query_rows = query_ref[span, column]
        keys = keys_ref[:extent, column]
        grad_rows = grad_ref[span, column]
        probs = block_probs(query_rows, keys, allowed)
        grad_probs = contract_last(grad_rows, values_ref[:extent, column])
        shift = jnp.sum(probs * grad_probs, axis=1, keepdims=True)
        grad_scores = to_low(probs * (grad_probs - shift))
        grad_values[:extent] += contract_first(to_low(probs), grad_rows)
        grad_keys[:extent] += contract_first(grad_scores, query_rows)
        grad_qkv_ref[0, span, column] = turned_back(matmul(grad_scores, keys), first)
        if first + QUERY_ROWS >= length:
            grad_qkv_ref[1, :, column] = turned_back(grad_keys[...], 0)
            grad_qkv_ref[2, :, column] = to_low(grad_values[...])

    return head_block


def attend_back_kernel(*refs):
    head_block = attend_back_steps(*refs)

    @pl.loop(0, refs[0].shape[1] // HEAD_SIZE)
    def _(head):
        for first in range(0, refs[0].shape[0], QUERY_ROWS):
            head_block(head, first)


def attend_back(query, keys, values, grads, cosine, signed_sine, row_piece, col_piece):
    length, heads_width = query.shape
    return pl.pallas_call(
        attend_back_kernel,
        out_shape=jax.ShapeDtypeStruct((3, length, heads_width), jnp.bfloat16),
        in_specs=[pl.BlockSpec(memory_space=pltpu.VMEM)] * 8,
        out_specs=pl.BlockSpec(memory_space=pltpu.VMEM),
        scratch_shapes=[pltpu.VMEM((length, HEAD_SIZE), jnp.float32)] * 2,
        compiler_params=pltpu.CompilerParams(vmem_limit_bytes=48 * 2**20),
        cost_estimate=pl.CostEstimate(
            flops=10 * length * length * heads_width,
            bytes_accessed=16 * 2**20,
            transcendentals=length * length * heads_width // HEAD_SIZE,
        ),
    )(query, keys, values, grads, cosine, signed_sine, row_piece, col_piece)


def summed_and_attended_back(wide_part, rows, upper, attention_inputs, number):
    if not on_line():
        grad_qkv = attend_back(*attention_inputs)
        normed_part = sum(contract_last(grad_qkv[part], rows[part]) for part in range(3))
        mid_total = lax.psum(grad_mid_rows(grad_qkv, upper), "tensor")
        return plain_sum(wide_part, None), grad_qkv, normed_part, mid_total
    shape = wide_part.shape
    length, heads_width = attention_inputs[0].shape
    narrow_shape = (length, NARROW)
    return pl.pallas_call(
        functools.partial(attend_back_sum_kernel, SUM_CHUNKS),
        out_shape=[
            jax.ShapeDtypeStruct(shape, jnp.bfloat16),
            jax.ShapeDtypeStruct((3, length, heads_width), jnp.bfloat16),
            jax.ShapeDtypeStruct(shape, jnp.bfloat16),
            jax.ShapeDtypeStruct(narrow_shape, jnp.bfloat16),
        ],
        in_specs=in_vmem(1) + in_hbm(1) + in_vmem(1 + len(attention_inputs)),
        out_specs=in_vmem(4),
        scratch_shapes=sum_scratch(shape)
        + [pltpu.VMEM((length, HEAD_SIZE), jnp.float32)] * 2
        + [pltpu.VMEM(narrow_shape, jnp.float32)]
        + [pltpu.VMEM(narrow_shape, jnp.bfloat16)] * 4
        + [pltpu.SemaphoreType.DMA((6, 1))]
        + [pltpu.VMEM((3,) + rows.shape[1:], jnp.bfloat16), pltpu.SemaphoreType.DMA((1,))],
        compiler_params=pltpu.CompilerParams(
            collective_id=number, has_side_effects=True, vmem_limit_bytes=60 * 2**20
        ),
        cost_estimate=pl.CostEstimate(flops=0, bytes_accessed=300 * 2**20, transcendentals=0),
    )(wide_part, rows, upper, *attention_inputs)


def hidden_step(gate_up, open_part, gate_row, extra):
    hidden = open_part.shape[0]
    gate_half, up_half = gate_up[:hidden], gate_up[hidden:]
    squashed = 1.0 / (1.0 + jnp.exp(-gate_half))
    act = to_low(gate_half * squashed * up_half)
    act_f = act.astype(jnp.float32)
    gate_grad = jnp.sum(act_f * open_part, axis=0, keepdims=True)
    grad_act = gate_row * open_part
    if extra is not None:
        grad_act = grad_act + extra
    grad_gate = to_low(grad_act * up_half * squashed * (1.0 + gate_half * (1.0 - squashed)))
    grad_up = to_low(grad_act * gate_half * squashed)
    return act, to_low(gate_row * act_f), gate_grad, grad_gate, grad_up


def experts_kernel(
    pieces,
    inputs_ref,
    gate_ref,
    mid_up_ref,
    grad_mid_ref,
    up_extra_ref,
    down_extra_ref,
    ready_up_ref,
    block_ref,
    open_ref,
    grad_ref,
    gate_grad_ref,
    mid_down_ref,
    grad_mid_up_ref,
    grad_down_a_ref,
    grad_up_b_ref,
    act_ref,
    whole_ref,
    grad_total,
    up_rows,
    open_rows,
    act_rows,
    grad_rows,
    gather_semaphores,
    semaphores,
):
    greet, _, arrive, finish, _, load, load_wait, (launch, forward, hand_over) = (
        plane_gather_steps(pieces, block_ref, whole_ref, gather_semaphores, None)
    )
    hidden = open_rows.shape[1]
    count = SHARED + EXPERTS
    each = pieces // (count - READY)

    def span(expert, rows):
        return pl.ds(pl.multiple_of(expert * rows, rows), rows)

    def load_open(expert):
        slot = expert % 2
        return pltpu.make_async_copy(
            open_ref.at[span(expert, hidden)], open_rows.at[slot], semaphores.at[1, slot]
        )

    def load_ready(expert):
        slot = expert % 2
        return pltpu.make_async_copy(
            ready_up_ref.at[span(expert, 2 * hidden)], up_rows.at[slot], semaphores.at[2, slot]
        )

    def store_act(expert):
        slot = expert % 2
        return pltpu.make_async_copy(
            act_rows.at[slot], act_ref.at[span(expert, hidden)], semaphores.at[3, slot]
        )

    def advance(expert):
        for part in range(each):
            launch(each * (expert + 1) + part)
        for part in range(each):
            forward(each * (expert + 2 - READY) + part + 1)
        for part in range(each):
            hand_over(each * (expert + 1 - READY) + part + 1)

        @pl.when(expert + 1 < count)
        def _():
            load_open(expert + 1).start()

        @pl.when(expert + 1 < READY)
        def _():
            load_ready(expert + 1).start()

        @pl.when((expert + 1 >= READY) & (expert + 1 < count))
        def _():
            for part in range(each):
                arrive(each * (expert + 1 - READY) + part)
            slot = (expert + 1) % 2
            first = (expert + 1 - READY) * 2 * hidden
            for copy in load(first, 2 * hidden, up_rows.at[slot], semaphores.at[2, slot]):
                copy.start()

        load_open(expert).wait()
        load_wait(2 * hidden, up_rows.at[expert % 2], semaphores.at[2, expert % 2])

        @pl.when(expert >= 2)
        def _():
            store_act(expert - 2).wait()

    def compute(expert, shared):
        slot = expert % 2
        gate_up = contract_last(up_rows[slot], inputs_ref[...])
        extra = None
        if shared:
            gate_up = gate_up + matmul(up_extra_ref[expert], mid_up_ref[...])
            extra = matmul(down_extra_ref[expert], grad_mid_ref[...])
        act, act_gated, gate_grad, grad_gate, grad_up = hidden_step(
            gate_up,
            open_rows[slot].astype(jnp.float32),
            gate_ref[pl.ds(expert, 1)],
            extra,
        )
        gate_grad_ref[pl.ds(expert, 1)] = gate_grad
        act_rows[slot] = act_gated
        grad_rows[:hidden] = grad_gate
        grad_rows[hidden:] = grad_up
        store_act(expert).start()
        grad_total[...] += contract_first(grad_rows[...], up_rows[slot])
        if shared:
            mid_down_ref[...] += contract_first(down_extra_ref[expert], act)
            grad_mid_up_ref[...] += contract_first(up_extra_ref[expert], grad_rows[...])
            grad_down_a_ref[expert] = contract_last(grad_mid_ref[...], act)
            grad_up_b_ref[expert] = ADAPTER_SCALE * contract_last(mid_up_ref[...], grad_rows[...])

    greet()
    pl.semaphore_wait(pltpu.get_barrier_semaphore(), 3)
    load_open(0).start()
    load_ready(0).start()

    @pl.loop(0, each)
    def _(piece):
        launch(piece)

    grad_total[...] = jnp.zeros_like(grad_total)
    mid_down_ref[...] = jnp.zeros_like(mid_down_ref)
    grad_mid_up_ref[...] = jnp.zeros_like(grad_mid_up_ref)

    @pl.loop(0, SHARED)
    def _(expert):
        advance(expert)
        compute(expert, True)

    @pl.loop(SHARED, count)
    def _(expert):
        advance(expert)
        compute(expert, False)

    grad_ref[...] = to_low(grad_total[...])
    store_act(count - 2).wait()
    store_act(count - 1).wait()
    finish()


def experts_plain(inputs, gates, mid_up, grad_mid, up_extra, down_extra, up_rows, open_rows):
    count, length = gates.shape
    hidden = open_rows.shape[0] // count
    width = inputs.shape[1]
    grad_total = jnp.zeros((length, width), jnp.float32)
    act_parts, gate_grads, down_parts, up_parts = [], [], [], []
    mid_down = jnp.zeros((NARROW, length), jnp.float32)
    grad_mid_up = jnp.zeros((NARROW, length), jnp.float32)
    for expert in range(count):
        weights = up_rows[2 * hidden * expert : 2 * hidden * (expert + 1)]
        gate_up = contract_last(weights, inputs)
        extra = None
        if expert < SHARED:
            gate_up = gate_up + matmul(up_extra[expert], mid_up)
            extra = matmul(down_extra[expert], grad_mid)
        act, act_gated, gate_grad, grad_gate, grad_up = hidden_step(
            gate_up,
            open_rows[hidden * expert : hidden * (expert + 1)].astype(jnp.float32),
            gates[expert : expert + 1],
            extra,
        )
        grad = jnp.concatenate([grad_gate, grad_up], axis=0)
        act_parts.append(act_gated)
        gate_grads.append(gate_grad)
        grad_total = grad_total + contract_first(grad, weights)
        if expert < SHARED:
            mid_down = mid_down + contract_first(down_extra[expert], act)
            grad_mid_up = grad_mid_up + contract_first(up_extra[expert], grad)
            down_parts.append(contract_last(grad_mid, act))
            up_parts.append(ADAPTER_SCALE * contract_last(mid_up, grad))
    return (
        grad_total,
        jnp.concatenate(gate_grads, axis=0),
        mid_down,
        grad_mid_up,
        jnp.stack(down_parts),
        jnp.stack(up_parts),
        jnp.concatenate(act_parts, axis=0),
    )


def experts_step(
    inputs, gates, mid_up, grad_mid, up_extra, down_extra, ready_up, block, open_rows, number
):
    length, width = inputs.shape
    count = SHARED + EXPERTS
    hidden = open_rows.shape[0] // count
    if not in_plane():
        whole = lax.all_gather(block, "dp", axis=1, tiled=True)
        up_rows = jnp.concatenate([ready_up, whole], axis=0)
        return experts_plain(
            inputs, gates, mid_up, grad_mid, up_extra, down_extra, up_rows, open_rows
        )
    pieces = HALVES * (count - READY)
    return pl.pallas_call(
        functools.partial(experts_kernel, pieces),
        in_specs=in_vmem(6) + in_hbm(3),
        out_specs=in_vmem(6) + in_hbm(2),
        out_shape=[
            jax.ShapeDtypeStruct((length, width), jnp.bfloat16),
            jax.ShapeDtypeStruct((count, length), jnp.float32),
            jax.ShapeDtypeStruct((NARROW, length), jnp.float32),
            jax.ShapeDtypeStruct((NARROW, length), jnp.float32),
            jax.ShapeDtypeStruct((SHARED, NARROW, hidden), jnp.float32),
            jax.ShapeDtypeStruct((SHARED, NARROW, 2 * hidden), jnp.float32),
            jax.ShapeDtypeStruct((count * hidden, length), jnp.bfloat16),
            jax.ShapeDtypeStruct(((count - READY) * 2 * hidden, width), jnp.bfloat16),
        ],
        scratch_shapes=[
            pltpu.VMEM((length, width), jnp.float32),
            pltpu.VMEM((2, 2 * hidden, width), jnp.bfloat16),
            pltpu.VMEM((2, hidden, length), jnp.bfloat16),
            pltpu.VMEM((2, hidden, length), jnp.bfloat16),
            pltpu.VMEM((2 * hidden, length), jnp.bfloat16),
            pltpu.SemaphoreType.DMA((18, pieces)),
            pltpu.SemaphoreType.DMA((4, 2)),
        ],
        compiler_params=pltpu.CompilerParams(
            collective_id=number, has_side_effects=True, vmem_limit_bytes=60 * 2**20
        ),
        cost_estimate=pl.CostEstimate(flops=0, bytes_accessed=600 * 2**20, transcendentals=0),
    )(inputs, gates, mid_up, grad_mid, up_extra, down_extra, ready_up, block, open_rows)[:7]


def gathered(weight):
    return lax.all_gather(weight, "dp", axis=0, tiled=True)


def body(
    tokens,
    cotangent,
    attention_norm_gain,
    query_key_value_weight,
    query_key_value_bias,
    output_projection_weight,
    feedforward_norm_gain,
    router_matrix,
    shared_expert_gate_weight,
    routed_gate_up_weight,
    routed_down_weight,
    shared_expert_gate_up_weight,
    shared_expert_down_weight,
    routes,
    sequence_adapter_index,
    picture_piece_starts,
    adapter_query_key_value_lower,
    adapter_query_key_value_upper,
    adapter_output_lower,
    adapter_output_upper,
    adapter_shared_up_lower,
    adapter_shared_up_upper,
    adapter_shared_down_lower,
    adapter_shared_down_upper,
):
    length, width = tokens.shape
    set_id = sequence_adapter_index[0]
    starts = picture_piece_starts[0]

    def selected_experts(adapter_entry):
        return lax.dynamic_index_in_dim(adapter_entry, set_id, 0, keepdims=False)

    qkv_a, qkv_b, out_a, out_b = (
        selected_experts(adapter_query_key_value_lower),
        selected_experts(adapter_query_key_value_upper),
        selected_experts(adapter_output_lower),
        selected_experts(adapter_output_upper),
    )
    up_a, up_b, down_a, down_b = (
        selected_experts(adapter_shared_up_lower),
        selected_experts(adapter_shared_up_upper),
        selected_experts(adapter_shared_down_lower),
        selected_experts(adapter_shared_down_upper),
    )
    gain_attn_f = attention_norm_gain.astype(jnp.float32)
    gain_ffn_f = feedforward_norm_gain.astype(jnp.float32)
    tokens_f = tokens.astype(jnp.float32)
    normed = to_low(rms_scale(tokens_f, gain_attn_f))
    mid_qkv = to_low(matmul(normed, qkv_a))
    hidden = shared_expert_down_weight.shape[1] // SHARED
    rank = up_a.shape[1]

    def fill(rows):
        return jnp.pad(to_low(rows), ((0, NARROW - rows.shape[0]), (0, 0)))

    def fill_last(rows):
        return jnp.pad(to_low(rows), ((0, 0), (0, 0), (0, NARROW - rows.shape[2])))

    cotangent_down = ADAPTER_SCALE * contract_last(cotangent, down_b)
    up_extra = ADAPTER_SCALE * up_b.reshape(rank, 2, SHARED, hidden).transpose(2, 1, 3, 0)
    up_extra = fill_last(up_extra.reshape(SHARED, 2 * hidden, rank))
    down_extra = fill_last(down_a.reshape(SHARED, hidden, rank))
    def lanes(columns, first):
        return jnp.pad(columns, ((0, 0), (first, NARROW - first - columns.shape[1])))

    upper = jnp.pad(
        ADAPTER_SCALE * qkv_b.transpose(1, 0, 2), ((0, 0), (0, NARROW - rank), (0, 0))
    )
    depth = routed_gate_up_weight.shape[0]
    early = (READY - SHARED) * 2 * hidden
    shared_block = shared_expert_gate_up_weight.reshape(-1, 2, SHARED, hidden)
    up_block = jnp.transpose(routed_gate_up_weight, (1, 2, 3, 0)).reshape(-1, depth)
    ready_up = lax.all_gather(
        jnp.concatenate(
            [shared_block.transpose(2, 1, 3, 0).reshape(-1, depth), up_block[:early]], axis=0
        ),
        "dp",
        axis=1,
        tiled=True,
    )
    attention_rows = gathered(
        jnp.concatenate([query_key_value_weight, output_projection_weight[:, None]], axis=1)
    )
    qkv_rows = attention_rows[:, :3]
    row_stack = attention_rows.transpose(1, 0, 2)
    normed, cotangent_down, up_extra, down_extra = lax.optimization_barrier(
        (normed, cotangent_down, up_extra, down_extra)
    )
    qkv_sum = jnp.einsum("tr,rsf->stf", normed, qkv_rows, preferred_element_type=jnp.float32)
    cosine, sine_table = rope_tables(length)
    signs = jnp.where(jnp.arange(HEAD_SIZE) < HEAD_SIZE // 2, -1.0, 1.0)
    piece_ids = piece_index(jnp.arange(length, dtype=jnp.int32), starts)
    places = (cosine, sine_table * signs[None, :], piece_ids[:, None], piece_ids[None, :])
    query, keys, values, attended = attend(
        qkv_sum,
        lanes(mid_qkv, 0),
        upper,
        query_key_value_bias.astype(jnp.float32)[:, None, :],
        *places,
    )
    down_block = jnp.transpose(routed_down_weight, (1, 2, 0))
    down_block = jnp.concatenate(
        [shared_expert_down_weight.T, down_block.reshape(-1, depth)], axis=0
    )
    branch_total, down_rows, open_rows = summed_and_gathered(
        attended,
        matmul(attended, out_a),
        row_stack,
        down_block,
        cotangent.T,
        1,
    )
    mid_out = to_low(branch_total[:, width : width + rank])
    small_rows = gathered(
        jnp.concatenate(
            [
                router_matrix,
                shared_expert_gate_weight[:, None],
                jnp.full_like(shared_expert_gate_weight, set_id)[:, None],
            ],
            axis=1,
        )
    )
    factors = jnp.concatenate([small_rows[:, : EXPERTS + 1], up_a], axis=1)
    hidden_here, hidden_scale, normed_two, projected = hidden_rows(
        branch_total, tokens, fill(out_b), gain_ffn_f[None], lanes(factors, 0)
    )
    router_probs = jax.nn.softmax(projected[:, :EXPERTS], axis=-1)
    shared_gate = jax.nn.sigmoid(projected[:, EXPERTS])
    mid_up = to_low(projected[:, EXPERTS + 1 : EXPERTS + 1 + rank])
    expert_ids = jnp.arange(EXPERTS, dtype=jnp.int32)
    chosen = jnp.sum(
        (routes[:, :, None] == expert_ids[None, None, :]).astype(jnp.float32), axis=1
    )
    gates = jnp.concatenate(
        [jnp.broadcast_to(shared_gate[None], (SHARED, length)), (router_probs * chosen).T], axis=0
    )
    grad_mid_down = shared_gate[:, None] * cotangent_down
    (
        normed_two_part,
        gate_grads,
        mid_down_part,
        grad_mid_up_part,
        grad_down_a_parts,
        grad_up_b_parts,
        act_rows,
    ) = experts_step(
        normed_two,
        gates,
        fill(mid_up.T),
        fill(grad_mid_down.T),
        up_extra,
        down_extra,
        ready_up,
        up_block[early:],
        open_rows,
        5,
    )
    grad_down_a_local = grad_down_a_parts[:, :rank].transpose(1, 0, 2).reshape(rank, -1)
    grad_up_b_local = (
        grad_up_b_parts[:, :rank]
        .reshape(SHARED, rank, 2, hidden)
        .transpose(1, 2, 0, 3)
        .reshape(rank, 2, -1)
    )
    narrow_part = jnp.concatenate(
        [
            gate_grads[SHARED:],
            jnp.sum(gate_grads[:SHARED], axis=0, keepdims=True),
            grad_mid_up_part[:rank],
            mid_down_part[:rank],
        ],
        axis=0,
    ).T
    second_total, combined_part = summed_and_down(
        normed_two_part, narrow_part, act_rows, down_rows, 2
    )
    up_from = width + EXPERTS + 1
    grad_mid_up = to_low(second_total[:, up_from : up_from + rank])
    mid_down = to_low(second_total[:, up_from + rank : up_from + 2 * rank])

    grad_hidden, grad_branch, grad_mid_out, grad_attended = epilogue(
        (
            second_total,
            hidden_here,
            hidden_scale,
            cotangent,
            lanes(router_probs, 0),
            lanes(chosen, 0),
            lanes(cotangent_down, EXPERTS + 1 + rank),
            shared_gate[:, None],
        ),
        (gain_ffn_f[None], lanes(factors, 0), fill(out_b), lanes(out_a, 0), row_stack),
    )
    grad_mid_out = grad_mid_out[:, :rank]
    grad_down_b_local = ADAPTER_SCALE * contract_first(
        to_low(shared_gate[:, None] * mid_down.astype(jnp.float32)), cotangent
    )
    grad_up_a_local = contract_first(grad_mid_up, normed_two)
    grad_out_b_local = ADAPTER_SCALE * contract_first(mid_out, grad_branch)
    grad_out_a_local = contract_first(grad_mid_out, attended)

    def side_by_side(local_grads):
        return jnp.concatenate([to_low(local_grad) for local_grad in local_grads], axis=1)

    early_grads = [
        grad_out_a_local,
        grad_up_a_local,
        grad_up_b_local.reshape(grad_up_b_local.shape[0], -1),
        grad_down_a_local,
        grad_down_b_local,
    ]
    grad_attended, early_flat = lax.optimization_barrier(
        (grad_attended, side_by_side(early_grads))
    )
    early_rows = lax.all_gather(early_flat, "dp", axis=0, tiled=True)
    combined_here, grad_qkv, normed_part, mid_total = summed_and_attended_back(
        combined_part,
        row_stack,
        upper,
        (query, keys, values, grad_attended) + places,
        3,
    )
    mid_total, early_rows = lax.optimization_barrier((to_low(mid_total), early_rows))
    grad_mid_qkv = mid_total[:, :rank]
    late_grads = [
        (
            ADAPTER_SCALE
            * jnp.einsum("tr,stf->rsf", mid_qkv, grad_qkv, preferred_element_type=jnp.float32)
        ).reshape(rank, -1),
        contract_first(grad_mid_qkv, normed),
        grad_out_b_local,
    ]
    normed_part, late_flat = lax.optimization_barrier((normed_part, side_by_side(late_grads)))
    late_rows = lax.all_gather(late_flat, "dp", axis=0, tiled=True)
    grad_tokens, output = last_step(
        normed_part,
        (grad_hidden, tokens, hidden_here, combined_here),
        (
            mid_total,
            lanes(qkv_a, 0),
            gain_attn_f[None],
            lanes(mid_down, 0),
            fill(down_b),
            shared_gate[:, None],
        ),
        4,
    )
    output, late_rows = lax.optimization_barrier((output, late_rows))
    everyone = small_rows[:: small_rows.shape[0] // lax.axis_size("dp"), EXPERTS + 1]
    hits = jnp.arange(ADAPTER_SETS, dtype=jnp.int32)[:, None] == everyone.astype(jnp.int32)
    same = jnp.arange(rank)[:, None] == jnp.arange(rank)[None, :]
    chooser = to_low(hits[:, None, :, None] & same[None, :, None, :])
    chooser = chooser.reshape(ADAPTER_SETS * rank, -1)

    def adapter_sums(local_grads, rows):
        results, start = [], 0
        for local_grad in local_grads:
            size = local_grad.shape[1]
            total = matmul(chooser, rows[:, start : start + size])
            results.append(total.reshape(ADAPTER_SETS, rank, size))
            start += size
        return results

    def flipped(total):
        return jnp.swapaxes(total, 1, 2)

    def opened(total, count):
        return total.reshape(total.shape[0], total.shape[1], count, -1)

    total_out_a, total_up_a, total_up_b, total_down_a, total_down_b = adapter_sums(
        early_grads, early_rows
    )
    total_qkv_b, total_qkv_a, total_out_b = adapter_sums(late_grads, late_rows)
    return (
        output,
        grad_tokens,
        flipped(total_qkv_a),
        opened(total_qkv_b, 3),
        flipped(total_out_a),
        total_out_b,
        flipped(total_up_a),
        opened(total_up_b, 2),
        flipped(total_down_a),
        total_down_b,
    )


def solution(mesh):
    return jax.shard_map(
        body,
        mesh=mesh,
        in_specs=(
            P("dp", None),
            P("dp", None),
            P(),
            P("dp", None, "tensor"),
            P(None, "tensor"),
            P("dp", "tensor"),
            P(),
            P("dp", None),
            P("dp"),
            P("dp", None, None, "tensor"),
            P("dp", None, "tensor"),
            P("dp", None, "tensor"),
            P("dp", "tensor"),
            P("dp", None),
            P("dp"),
            P("dp", None),
            P(),
            P(None, None, None, "tensor"),
            P(None, "tensor", None),
            P(),
            P(),
            P(None, None, None, "tensor"),
            P(None, "tensor", None),
            P(),
        ),
        out_specs=(
            P("dp", None),
            P("dp", None),
            P(),
            P(None, None, None, "tensor"),
            P(None, "tensor", None),
            P(),
            P(),
            P(None, None, None, "tensor"),
            P(None, "tensor", None),
            P(),
        ),
        check_vma=False,
    )
```
